32 devices in a mesh: row: 8 (over z, x), col: 4 (over y, core).
Axes of the slice: x: 2, y: 2, z: 4, core: 2. Of those that a mesh axis runs over, the one named last changes fastest.
Arguments:
- objective: float32 [128, 8192], P('row', 'col'), may hold values from -6 to 6
- center: bfloat16 [128, 8192], P('row', 'col'), may hold values from -5 to 5
- radius: bfloat16 [128, 8192], P('row', 'col'), may hold values from 0.049804688 to 1
- lower_gap: bfloat16 [3, 128, 8192], P(None, 'row', 'col'), may hold values from 0.19921875 to 3
- upper_gap: bfloat16 [3, 128, 8192], P(None, 'row', 'col'), may hold values from 0.19921875 to 3
- kernels: float32 [4, 3, 3, 64, 64], replicated, may hold values from -0.25 to 0.25
- biases: float32 [4, 64], replicated, may hold values from -3 to 3
- step_sizes: float32 [3], replicated, may hold values from 0.2 to 1
Outputs:
- bounds: float32 [3], replicated
- final_duals: float32 [3, 128, 8192], P(None, 'row', 'col')
- final_multipliers: float32 [3, 128, 8192], P(None, 'row', 'col')
The draws below stay inside these ranges and needn't reach their ends.
All inputs are finite; a program needn't handle non-finite values.
Results may differ from the reference program's by a relative error of at most 0.0003.
Values sent between devices are 32-bit elements; how exact they have to be, the bound alone decides.
No kernel may reach another device: no remote copies, remote signals or barrier semaphores. Data moves between devices by JAX's collectives and lax.ppermute only.
A program may use at most 128 MiB of HBM per device.

```python
import math
import jax
import jax.numpy as jnp
from jax import lax

CH = 64
LAYERS = 4
ITERS = 3
H = 128
W = 128
WC = 8192


def steps_of(rng, extent, split, low, top_value):
    def one(dim, blocks):
        steps = jax.random.uniform(jax.random.fold_in(jax.random.fold_in(rng, 6), dim), (blocks,), jnp.float32, low / len(split), top_value / len(split))
        return jnp.repeat(jnp.exp(steps), extent[dim] // blocks).reshape((-1,) + (1,) * (len(extent) - dim - 1))

    level = one(*split[0])
    for cut in split[1:]:
        level = level * one(*cut)
    return level


def noise(rng, extent, deviation, bound, cuts=(), dtype=jnp.bfloat16):
    gain = steps_of(rng, extent, cuts, -0.22, 0.18) if cuts else 1.0
    entries = jax.random.normal(rng, extent, jnp.float32) * deviation * gain
    return jnp.minimum(jnp.maximum(entries, -bound), bound).astype(dtype)


def setup_inputs(seed: int = 0) -> dict:
    key_of = jax.random.split(jax.random.key(seed), 9)
    objective = noise(key_of[0], (H, WC), 1.0, 6.0, ((0, 8), (1, 4)), jnp.float32)
    center = noise(key_of[1], (H, WC), 1.0, 5.0, ((0, 8), (1, 4)))
    radius = jnp.clip(jnp.exp(math.log(1.0) - 2.9996462 * jax.random.uniform(key_of[2], (H, WC), jnp.float32) ** steps_of(key_of[2], (H, WC), ((0, 8), (1, 4)), -0.2, 0.2)), 0.049804688, 1.0).astype(jnp.bfloat16)
    lower_gap = jnp.clip(jnp.exp(math.log(3.0) - 2.7119641 * jax.random.uniform(key_of[3], (LAYERS - 1, H, WC), jnp.float32) ** steps_of(key_of[3], (LAYERS - 1, H, WC), ((1, 8), (2, 4)), -0.2, 0.2)), 0.19921875, 3.0).astype(jnp.bfloat16)
    upper_gap = jnp.clip(jnp.exp(math.log(3.0) - 2.7119641 * jax.random.uniform(key_of[4], (LAYERS - 1, H, WC), jnp.float32) ** steps_of(key_of[4], (LAYERS - 1, H, WC), ((1, 8), (2, 4)), -0.2, 0.2)), 0.19921875, 3.0).astype(jnp.bfloat16)
    kernels = noise(key_of[5], (LAYERS, 3, 3, CH, CH), (9 * CH) ** -0.5, 0.25, (), jnp.float32)
    biases = noise(key_of[6], (LAYERS, CH), 0.5, 3.0, (), jnp.float32)
    step_sizes = jnp.clip(jnp.exp(jax.random.uniform(key_of[7], (ITERS,), jnp.float32, math.log(0.2), math.log(1.0))), 0.2, 1.0)
    return dict(objective=objective, center=center, radius=radius, lower_gap=lower_gap, upper_gap=upper_gap, kernels=kernels, biases=biases, step_sizes=step_sizes)


TEMP = 0.5
EPS = 1e-06

def soft_value(coef, low, high):
    return coef * low - TEMP * jax.nn.softplus(coef * (low - high) / TEMP)

def soft_point(coef, low, high):
    return low + (high - low) * jax.nn.sigmoid(coef * (low - high) / TEMP)

def flipped(kernel):
    return jnp.transpose(kernel[::-1, ::-1], (0, 1, 3, 2))

def conv_same(maps, kernel):
    result = lax.conv_general_dilated(maps[None], kernel, (1, 1), 'SAME', dimension_numbers=('NHWC', 'HWIO', 'NHWC'), precision=lax.Precision.HIGHEST)
    return result[0]

def reference(objective, center, radius, lower_gap, upper_gap, kernels, biases, step_sizes):
    depth = LAYERS - 1
    target = objective.reshape(H, W, CH)
    middle = center.astype(jnp.float32).reshape(H, W, CH)
    half = radius.astype(jnp.float32).reshape(H, W, CH)
    below = lower_gap.astype(jnp.float32).reshape(depth, H, W, CH)
    above = upper_gap.astype(jnp.float32).reshape(depth, H, W, CH)
    zero_map = jnp.zeros((H, W, CH), jnp.float32)
    lows = [middle - half] + [zero_map] * depth
    highs = [middle + half] + [above[j] for j in range(depth)]
    target_back = conv_same(target, flipped(kernels[LAYERS - 1]))
    fixed_part = jnp.sum(target * biases[LAYERS - 1])
    duals = [zero_map] * depth
    multipliers = [zero_map] * depth
    total_cells = H * W * CH
    bounds = []
    for step in range(ITERS):
        value = fixed_part
        points = []
        for layer in range(LAYERS):
            if layer < depth:
                coef = -conv_same(duals[layer], flipped(kernels[layer]))
            else:
                coef = target_back
            if layer > 0:
                coef = coef + multipliers[layer - 1]
            value = value + jnp.sum(soft_value(coef, lows[layer], highs[layer]))
            points.append(soft_point(coef, lows[layer], highs[layer]))
        slope_duals = []
        slope_mults = []
        squares = jnp.zeros((), jnp.float32)
        for j in range(depth):
            pos_coef = duals[j] - multipliers[j]
            neg_coef = -duals[j]
            value = value + jnp.sum(soft_value(pos_coef, zero_map, above[j]))
            value = value + jnp.sum(soft_value(neg_coef, zero_map, below[j]))
            value = value - jnp.sum(duals[j] * biases[j])
            positive = soft_point(pos_coef, zero_map, above[j])
            negative = soft_point(neg_coef, zero_map, below[j])
            slope_dual = positive - negative - conv_same(points[j], kernels[j]) - biases[j]
            slope_mult = points[j + 1] - positive
            squares = squares + jnp.sum(slope_dual * slope_dual) + jnp.sum(slope_mult * slope_mult)
            slope_duals.append(slope_dual)
            slope_mults.append(slope_mult)
        scale = step_sizes[step] / jnp.sqrt(squares / (2 * depth * total_cells) + EPS)
        duals = [duals[j] + scale * slope_duals[j] for j in range(depth)]
        multipliers = [multipliers[j] + scale * slope_mults[j] for j in range(depth)]
        bounds.append(value / total_cells)
    final_duals = jnp.stack(duals).reshape(depth, H, W * CH)
    final_multipliers = jnp.stack(multipliers).reshape(depth, H, W * CH)
    return (jnp.stack(bounds), final_duals, final_multipliers)
```

```python
import functools
import math

import jax
import jax.numpy as jnp
from jax import lax
from jax.experimental import pallas as pl
from jax.experimental.pallas import tpu as pltpu
from jax.sharding import PartitionSpec as P

CH = 64
LAYERS = 4
ITERS = 3
EPS = 1e-06
LANES = 2 * CH
HALO_PAIRS = 3
WIDE = 5
EDGE = 4
F32 = jnp.float32
BF16 = jnp.bfloat16

ROWS_SENT = (5, 5, 5, 4, 4, 4, 4, 3, 3)
ROW_START = tuple(sum(ROWS_SENT[:m]) for m in range(9))
SENT = 40

VMEM = pl.BlockSpec(memory_space=pltpu.VMEM)
SMEM = pl.BlockSpec(memory_space=pltpu.SMEM)


def call(body, outs, scratch, operands, flops, mem=24, scalars=()):
    return pl.pallas_call(
        body,
        out_shape=outs,
        in_specs=[SMEM if j in scalars else VMEM for j in range(len(operands))],
        out_specs=jax.tree.map(lambda _: VMEM, outs),
        scratch_shapes=scratch,
        compiler_params=pltpu.CompilerParams(vmem_limit_bytes=mem << 20),
        cost_estimate=pl.CostEstimate(flops=flops, bytes_accessed=4 << 20, transcendentals=0),
    )(*operands)


def shape(*dims, dtype=F32):
    return jax.ShapeDtypeStruct(dims, dtype)


def split(value):
    high = value.astype(BF16)
    return high, (value - high.astype(F32)).astype(BF16)


def weights_body(kernels, biases, fwd_hi, fwd_lo, bwd_hi, bwd_lo, bias2):
    zero = jnp.zeros((CH, CH), F32)

    def put(hi, lo, k, j, dh, first, second):
        block = jnp.concatenate([first, second], axis=1)
        high, low = split(block)
        where = (k, pl.ds(CH * j, CH), pl.ds(LANES * dh, LANES))
        hi[where] = high
        lo[where] = low

    for k in range(LAYERS):
        for dh in range(3):
            taps = [kernels[k * 9 + dh * 3 + dw] for dw in range(3)]
            if k < LAYERS - 1:
                for j in range(4):
                    put(fwd_hi, fwd_lo, k, j, dh, taps[j] if j < 3 else zero, taps[j - 1] if j > 0 else zero)
            flips = [tap.T for tap in taps]
            for j in range(4):
                put(bwd_hi, bwd_lo, k, j, 2 - dh, flips[2 - j] if j < 3 else zero, flips[3 - j] if j > 0 else zero)
    for k in range(LAYERS):
        row = biases[k : k + 1, :]
        bias2[k : k + 1, :] = jnp.concatenate([row, row], axis=1)


def weights(kernels, biases):
    n = 4 * CH
    outs = (
        shape(LAYERS - 1, n, 3 * LANES, dtype=BF16),
        shape(LAYERS - 1, n, 3 * LANES, dtype=BF16),
        shape(LAYERS, n, 3 * LANES, dtype=BF16),
        shape(LAYERS, n, 3 * LANES, dtype=BF16),
        shape(8, LANES),
    )
    return call(weights_body, outs, [], (kernels.reshape(LAYERS * 9, CH, CH), biases), 1 << 22)


def sources(objective, center, radius, lower, upper):
    return [
        lambda cols: center[:, cols].astype(F32),
        lambda cols: upper[0, :, cols].astype(F32),
        lambda cols: upper[1, :, cols].astype(F32),
        lambda cols: upper[2, :, cols].astype(F32),
        lambda cols: lower[0, :, cols].astype(F32),
        lambda cols: lower[1, :, cols].astype(F32),
        lambda cols: lower[2, :, cols].astype(F32),
        lambda cols: radius[:, cols].astype(F32),
        lambda cols: objective[:, cols],
    ]


def sides_body(objective, center, radius, lower, upper, head, tail):
    rows, cols = objective.shape
    strip = HALO_PAIRS * LANES
    for m, read in enumerate(sources(objective, center, radius, lower, upper)):
        here = pl.ds(m * rows, rows)
        head[here, :] = read(pl.ds(0, strip))
        tail[here, :] = read(pl.ds(cols - strip, strip))


def column(reads, left, right, rows, pairs, m, q):
    if q < HALO_PAIRS:
        return left[m * rows : (m + 1) * rows, q * LANES : (q + 1) * LANES]
    if q >= HALO_PAIRS + pairs:
        q -= HALO_PAIRS + pairs
        return right[m * rows : (m + 1) * rows, q * LANES : (q + 1) * LANES]
    return reads[m](pl.ds((q - HALO_PAIRS) * LANES, LANES))


def ends_body(objective, center, radius, lower, upper, left, right, top, bottom):
    rows, cols = objective.shape
    pairs = cols // LANES
    reads = sources(objective, center, radius, lower, upper)
    for m in range(9):
        sent = ROWS_SENT[m]
        here = slice(ROW_START[m], ROW_START[m] + sent)
        for q in range(pairs + 2 * HALO_PAIRS):
            value = column(reads, left, right, rows, pairs, m, q)
            top[q, here, :] = value[:sent]
            bottom[q, here, :] = value[rows - sent :]
    spare = slice(sum(ROWS_SENT), SENT)
    top[:, spare, :] = jnp.zeros((pairs + 2 * HALO_PAIRS, SENT - sum(ROWS_SENT), LANES), F32)
    bottom[:, spare, :] = jnp.zeros((pairs + 2 * HALO_PAIRS, SENT - sum(ROWS_SENT), LANES), F32)


def neighbours(head, tail, axis):
    count = lax.axis_size(axis)
    before = lax.ppermute(tail, axis, [(i, i + 1) for i in range(count - 1)])
    after = lax.ppermute(head, axis, [(i + 1, i) for i in range(count - 1)])
    return before, after


def roll_rows(value, shift):
    return pltpu.roll(value, shift % value.shape[0], 0)


def slide(maps, count, store, produce):
    rows = store.shape[2]
    early = lax.broadcasted_iota(jnp.int32, (rows, LANES), 1) < CH
    zero = jnp.zeros((rows, LANES), F32)

    def step(q, carry):
        fresh = [pltpu.roll(value, CH, 1) for value in produce(q)]
        for k in range(maps):
            store[k, q] = jnp.where(early, carry[k], fresh[k])
        return tuple(fresh)

    last = lax.fori_loop(0, count, step, (zero,) * maps)
    for k in range(maps):
        store[k, count] = jnp.where(early, last[k], zero)


def multiply(store, k, first, count, hi, lo, layer, sums, exact=False):
    rows = store.shape[2]
    left = store[k, pl.ds(first, count)].reshape(count * rows, LANES)
    right = store[k, pl.ds(first + 1, count)].reshape(count * rows, LANES)
    window = jnp.concatenate([left, right], axis=1)
    dot = functools.partial(jnp.dot, preferred_element_type=F32)
    if exact:
        high = window.astype(BF16)
        result = dot(high, hi[layer]) + dot(high, lo[layer])
    else:
        high, low = split(window)
        result = dot(high, hi[layer]) + dot(high, lo[layer]) + dot(low, hi[layer])
    for d in range(3):
        sums[k, d, pl.ds(0, count)] = result[:, d * LANES : (d + 1) * LANES].reshape(count, rows, LANES)


def gathered(sums, k, q):
    return roll_rows(sums[k, 0, q], 1) + sums[k, 1, q] + roll_rows(sums[k, 2, q], -1)


def scale_of(total, step, cells):
    squares = jnp.sum(total[0:1, :], axis=1, keepdims=True)
    return step / jnp.sqrt(squares / (2 * (LAYERS - 1) * cells) + EPS)


def soft(top, t):
    return 0.5 * top * (1.0 - jnp.tanh(t))


class Bound:
    def __init__(self, start):
        self.linear = start
        self.factor = None

    def add(self, t):
        self.linear = self.linear - jnp.maximum(-t, 0.0)
        factor = 1.0 + jnp.exp(-2.0 * jnp.abs(t))
        self.factor = factor if self.factor is None else self.factor * factor

    def total(self):
        return self.linear - 0.5 * jnp.log(self.factor)


def own_rows(value):
    rows = value.shape[0]
    row = lax.broadcasted_iota(jnp.int32, value.shape, 0)
    kept = jnp.where((row >= EDGE) & (row < rows - EDGE), value, 0.0)
    return jnp.sum(kept, axis=0, keepdims=True)


def stats(rows):
    blank = [jnp.zeros((1, LANES), F32)] * (8 - len(rows))
    return jnp.concatenate(list(rows) + blank, axis=0)


def first_body(
    objective, center, radius, lower, upper, left, right, above, below,
    fwd_hi, fwd_lo, bwd_hi, bwd_lo, bias,
    box, back, slope, mult, stat, value,
    raw, target, store, sums,
):
    rows, cols = objective.shape
    pairs = cols // LANES
    frame = rows + 2 * EDGE
    wide = pairs + 4
    reads = sources(objective, center, radius, lower, upper)
    for m in range(9):
        sent = ROWS_SENT[m]
        here = slice(ROW_START[m], ROW_START[m] + sent)
        for q in range(pairs + 2 * HALO_PAIRS):
            if m >= 3 and not 1 <= q < wide + 1:
                continue
            own = column(reads, left, right, rows, pairs, m, q)
            if m < 3:
                dest, at, edge = raw.at[m, q], 0, WIDE
            else:
                dest, at, edge = (target.at[q - 1] if m == 8 else box.at[m, q - 1]), EDGE - sent, EDGE
                if at:
                    dest[0:EDGE, :] = jnp.zeros((EDGE, LANES), F32)
                    dest[EDGE + rows : frame, :] = jnp.zeros((EDGE, LANES), F32)
            dest[at : at + sent, :] = above[q, here, :]
            dest[edge : edge + rows, :] = own
            dest[edge + rows : edge + rows + sent, :] = below[q, here, :]
    raw[:, :, rows + 2 * WIDE :, :] = jnp.zeros((3, wide + 2, raw.shape[2] - rows - 2 * WIDE, LANES), F32)
    for m in range(3):
        for q in range(wide):
            box[m, q] = raw[m, q + 1, 1 : 1 + frame, :]

    tall = raw.shape[2]
    early = lax.broadcasted_iota(jnp.int32, (tall, LANES), 1) < CH

    def middle(q):
        return [raw[0, q], 0.5 * raw[1, q], 0.5 * raw[2, q]]

    slide(3, wide + 2, store, middle)
    for k in range(3):
        multiply(store, k, 1, wide, fwd_hi, fwd_lo, k, sums, exact=True)

    def slopes(q, carry):
        for k in range(3):
            conv = (
                sums[k, 0, q][:frame]
                + roll_rows(sums[k, 1, q], -1)[:frame]
                + roll_rows(sums[k, 2, q], -2)[:frame]
            )
            gap = box[1 + k, q]
            dl = 0.5 * (gap - box[4 + k, q]) - conv - bias[k : k + 1, :]
            slope[k, q] = jnp.where(gap > 0.0, dl, 0.0)
        return carry

    lax.fori_loop(0, wide, slopes, 0)

    early = lax.broadcasted_iota(jnp.int32, (frame, LANES), 1) < CH
    zero = jnp.zeros((frame, LANES), F32)

    def shift(q, carry):
        fresh = pltpu.roll(target[q], CH, 1)
        store[0, q, 0:frame, :] = jnp.where(early, carry, fresh)
        return fresh

    last = lax.fori_loop(0, wide, shift, zero)
    store[0, wide, 0:frame, :] = jnp.where(early, last, zero)
    lhs = jnp.concatenate(
        [
            store[0, 0:wide, 0:frame, :].reshape(wide * frame, LANES),
            store[0, 1 : wide + 1, 0:frame, :].reshape(wide * frame, LANES),
        ],
        axis=1,
    )
    high, low = split(lhs)
    dot = functools.partial(jnp.dot, preferred_element_type=F32)
    k = LAYERS - 1
    result = dot(high, bwd_hi[k]) + dot(high, bwd_lo[k]) + dot(low, bwd_hi[k])
    for d in range(3):
        sums[0, d, 0:wide, 0:frame, :] = result[:, d * LANES : (d + 1) * LANES].reshape(wide, frame, LANES)

    def pulls(q, carry):
        squares, worth, fixed = carry
        pull = (
            roll_rows(sums[0, 0, q][:frame], 1)
            + sums[0, 1, q][:frame]
            + roll_rows(sums[0, 2, q][:frame], -1)
        )
        back[q] = pull
        gap = box[3, q]
        t = pull * gap
        dm = -0.5 * gap * jnp.tanh(t)
        mult[q] = dm
        new = dm * dm
        for k in range(3):
            dl = slope[k, q]
            new = new + dl * dl
        bound = Bound(jnp.full((frame, LANES), -4.5 * math.log(2.0), F32))
        bound.add(t)
        own = (q >= 2) & (q < wide - 2)
        squares = squares + jnp.where(own, new, 0.0)
        worth = worth + jnp.where(own, bound.total(), 0.0)
        fixed = fixed + jnp.where(own, target[q] * bias[3:4, :], 0.0)
        return squares, worth, fixed

    squares, worth, fixed = lax.fori_loop(0, wide, pulls, (zero, zero, zero))
    fixed = own_rows(fixed)
    stat[...] = stats([own_rows(squares)])
    value[...] = stats([own_rows(worth) + fixed, fixed])


def second_pull_body(slope, bwd_hi, bwd_lo, back, store, sums):
    count = slope.shape[1]
    slide(3, count, store, lambda q: [slope[k, q] for k in range(3)])
    for k in range(3):
        multiply(store, k, 0, count, bwd_hi, bwd_lo, k, sums)

    def step(q, carry):
        for k in range(3):
            back[k, q] = gathered(sums, k, q)
        return carry

    lax.fori_loop(0, count, step, 0)


def second_body(
    total, steps, box, back, slope, mult, pull, fwd_hi, fwd_lo, bias,
    slope_out, mult_out, stat, value,
    points, store, sums, *, cells,
):
    wide = box.shape[1]
    frame = box.shape[2]
    scale = jnp.broadcast_to(scale_of(total, steps[0], cells), (frame, LANES))
    zero = jnp.zeros((frame, LANES), F32)

    def produce(q):
        radius = box[7, q]
        outs = [box[0, q] - radius * jnp.tanh(-2.0 * radius * (scale * pull[0, q]))]
        for k in (1, 2):
            gap = box[k, q]
            x = soft(gap, -(scale * pull[k, q]) * gap)
            points[k - 1, q] = x
            outs.append(x)
        return outs

    slide(3, wide, store, produce)
    for k in range(3):
        multiply(store, k, 1, wide - 2, fwd_hi, fwd_lo, k, sums)

    def step(j, carry):
        squares, worth = carry
        q = j + 1
        new = zero
        g = -(scale * pull[0, q])
        radius = box[7, q]
        bound = Bound(g * (box[0, q] - radius))
        bound.add(2.0 * g * radius)
        for k in range(3):
            gap = box[1 + k, q]
            low = box[4 + k, q]
            lam = scale * slope[k, q]
            if k < 2:
                x = points[k, q]
                bound.add(-(scale * pull[k + 1, q]) * gap)
                tp = lam * gap
            else:
                mu = scale * mult[q]
                t = (back[q] + mu) * gap
                x = soft(gap, t)
                bound.add(t)
                tp = (lam - mu) * gap
            tn = -lam * low
            bound.add(tp)
            bound.add(tn)
            bound.linear = bound.linear - lam * bias[k : k + 1, :]
            positive = soft(gap, tp)
            dl = positive - soft(low, tn) - gathered(sums, k, j) - bias[k : k + 1, :]
            dl = jnp.where(gap > 0.0, dl, 0.0)
            dm = x - positive
            slope_out[k, j] = dl
            mult_out[k, j] = dm
            new = new + dl * dl + dm * dm
        own = (q >= 2) & (q < wide - 2)
        return squares + jnp.where(own, new, 0.0), worth + jnp.where(own, bound.total(), 0.0)

    squares, worth = lax.fori_loop(0, wide - 2, step, (zero, zero))
    stat[...] = stats([own_rows(squares)])
    value[...] = stats([own_rows(worth)])


def third_body(
    total0, total1, steps, box, back, slope0, mult0, pull0, slope1, mult1, pull1, fwd_hi, fwd_lo, bias,
    value0, value1,
    duals, multipliers, slope_out, mult_out, stat,
    points, store, sums, *, cells,
):
    wide = box.shape[1]
    frame = box.shape[2]
    rows = frame - 2 * EDGE
    s0 = jnp.broadcast_to(scale_of(total0, steps[0], cells), (frame, LANES))
    s1 = jnp.broadcast_to(scale_of(total1, steps[1], cells), (frame, LANES))
    zero = jnp.zeros((frame, LANES), F32)

    def pull_of(k, j):
        g = -(s0 * pull0[k, j + 1] + s1 * pull1[k, j])
        return g if k == 0 else g + s1 * mult1[k - 1, j]

    def produce(j):
        q = j + 1
        radius = box[7, q]
        outs = [box[0, q] - radius * jnp.tanh(2.0 * radius * pull_of(0, j))]
        for k in (1, 2):
            gap = box[k, q]
            x = soft(gap, pull_of(k, j) * gap)
            points[k - 1, j] = x
            outs.append(x)
        return outs

    slide(3, wide - 2, store, produce)
    for k in range(3):
        multiply(store, k, 1, wide - 4, fwd_hi, fwd_lo, k, sums)

    def step(i, carry):
        squares, worth = carry
        j = i + 1
        q = i + 2
        new = zero
        g = pull_of(0, j)
        radius = box[7, q]
        bound = Bound(g * (box[0, q] - radius))
        bound.add(2.0 * g * radius)
        here = pl.ds(pl.multiple_of(i * LANES, LANES), LANES)
        for k in range(3):
            gap = box[1 + k, q]
            low = box[4 + k, q]
            lam = s0 * slope0[k, q] + s1 * slope1[k, j]
            mu = s1 * mult1[k, j]
            if k < 2:
                x = points[k, j]
                bound.add(pull_of(k + 1, j) * gap)
            else:
                mu = mu + s0 * mult0[q]
                t = (back[q] + mu) * gap
                x = soft(gap, t)
                bound.add(t)
            tp = (lam - mu) * gap
            tn = -lam * low
            bound.add(tp)
            bound.add(tn)
            bound.linear = bound.linear - lam * bias[k : k + 1, :]
            positive = soft(gap, tp)
            dl = positive - soft(low, tn) - gathered(sums, k, i) - bias[k : k + 1, :]
            dm = x - positive
            duals[k, :, here] = lam[EDGE : EDGE + rows]
            multipliers[k, :, here] = mu[EDGE : EDGE + rows]
            slope_out[k, :, here] = dl[EDGE : EDGE + rows]
            mult_out[k, :, here] = dm[EDGE : EDGE + rows]
            new = new + dl * dl + dm * dm
        return squares + new, worth + bound.total()

    squares, worth = lax.fori_loop(0, wide - 4, step, (zero, zero))
    fixed = value0[1:2, :]
    stat[...] = stats([own_rows(squares), value0[0:1, :], value1[0:1, :] + fixed, own_rows(worth) + fixed])


def last_body(total, steps, duals, multipliers, slope, mult, bounds, duals_out, mult_out, *, cells):
    scale = jnp.broadcast_to(scale_of(total, steps[2], cells), (duals.shape[1], duals.shape[2]))
    for k in range(LAYERS - 1):
        duals_out[k] = duals[k] + scale * slope[k]
        mult_out[k] = multipliers[k] + scale * mult[k]
    sums = jnp.sum(total[...], axis=1, keepdims=True) / cells
    bounds[...] = jnp.broadcast_to(sums, bounds.shape)


def everyone(partial):
    return lax.psum(partial, ("row", "col"))


def shards(objective, center, radius, lower, upper, kernels, biases, steps):
    rows, cols = objective.shape
    pairs = cols // LANES
    wide = pairs + 4
    frame = rows + 2 * EDGE
    tall = -(-(rows + 2 * WIDE) // 8) * 8
    cells = rows * cols * lax.axis_size("row") * lax.axis_size("col")
    inputs = (objective, center, radius, lower, upper)
    flops = 3 * 2 * 3 * wide * frame * 4 * CH * 3 * LANES

    strip = shape(9 * rows, HALO_PAIRS * LANES)
    head, tail = call(sides_body, (strip, strip), [], inputs, 1 << 20)
    left, right = neighbours(head, tail, "col")
    fwd_hi, fwd_lo, bwd_hi, bwd_lo, bias = weights(kernels, biases)
    strip = shape(pairs + 2 * HALO_PAIRS, SENT, LANES)
    top, bottom = call(ends_body, (strip, strip), [], inputs + (left, right), 1 << 20)
    above, below = neighbours(top, bottom, "row")

    stat_shape = shape(8, LANES)
    box, back, slope0, mult0, stat0, value0 = call(
        first_body,
        (
            shape(8, wide, frame, LANES),
            shape(wide, frame, LANES),
            shape(3, wide, frame, LANES),
            shape(wide, frame, LANES),
            stat_shape,
            stat_shape,
        ),
        [
            pltpu.VMEM((3, wide + 2, tall, LANES), F32),
            pltpu.VMEM((wide, frame, LANES), F32),
            pltpu.VMEM((3, wide + 3, tall, LANES), F32),
            pltpu.VMEM((3, 3, wide, tall, LANES), F32),
        ],
        inputs + (left, right, above, below, fwd_hi, fwd_lo, bwd_hi, bwd_lo, bias),
        2 * flops,
    )

    def pulled(slope):
        count = slope.shape[1]
        return call(
            second_pull_body,
            shape(3, count, frame, LANES),
            [
                pltpu.VMEM((3, count + 1, frame, LANES), F32),
                pltpu.VMEM((3, 3, count, frame, LANES), F32),
            ],
            (slope, bwd_hi, bwd_lo),
            flops,
        )

    total0 = everyone(stat0)
    pull0 = pulled(slope0)
    slope1, mult1, stat1, value1 = call(
        functools.partial(second_body, cells=cells),
        (shape(3, wide - 2, frame, LANES), shape(3, wide - 2, frame, LANES), stat_shape, stat_shape),
        [
            pltpu.VMEM((2, wide, frame, LANES), F32),
            pltpu.VMEM((3, wide + 1, frame, LANES), F32),
            pltpu.VMEM((3, 3, wide - 2, frame, LANES), F32),
        ],
        (total0, steps, box, back, slope0, mult0, pull0, fwd_hi, fwd_lo, bias),
        flops,
        scalars=(1,),
    )
    total1 = everyone(stat1)
    pull1 = pulled(slope1)
    out = shape(3, rows, cols)
    duals, multipliers, slope2, mult2, stat2 = call(
        functools.partial(third_body, cells=cells),
        (out, out, out, out, stat_shape),
        [
            pltpu.VMEM((2, wide - 2, frame, LANES), F32),
            pltpu.VMEM((3, wide - 1, frame, LANES), F32),
            pltpu.VMEM((3, 3, wide - 4, frame, LANES), F32),
        ],
        (
            total0, total1, steps, box, back, slope0, mult0, pull0, slope1, mult1, pull1,
            fwd_hi, fwd_lo, bias, value0, value1,
        ),
        flops,
        scalars=(2,),
    )
    total2 = everyone(stat2)
    bounds, final_duals, final_multipliers = call(
        functools.partial(last_body, cells=cells),
        (stat_shape, out, out),
        [],
        (total2, steps, duals, multipliers, slope2, mult2),
        1 << 20,
        scalars=(1,),
    )
    return bounds[1 : 1 + ITERS, 0], final_duals, final_multipliers


def solution(mesh):
    placed = (
        P("row", "col"),
        P("row", "col"),
        P("row", "col"),
        P(None, "row", "col"),
        P(None, "row", "col"),
        P(),
        P(),
        P(),
    )
    return jax.shard_map(
        shards,
        mesh=mesh,
        in_specs=placed,
        out_specs=(P(), P(None, "row", "col"), P(None, "row", "col")),
        check_vma=False,
    )
```

```python
import functools
import math

import jax
import jax.numpy as jnp
from jax import lax
from jax.experimental import pallas as pl
from jax.experimental.pallas import tpu as pltpu
from jax.sharding import PartitionSpec as P

CH = 64
LAYERS = 4
ITERS = 3
EPS = 1e-06
LANES = 2 * CH
HALO_PAIRS = 3
WIDE = 5
EDGE = 4
F32 = jnp.float32
BF16 = jnp.bfloat16

ROWS_SENT = (5, 5, 5, 4, 4, 4, 4, 3, 3)
ROW_START = tuple(sum(ROWS_SENT[:m]) for m in range(9))
SENT = 40

VMEM = pl.BlockSpec(memory_space=pltpu.VMEM)
SMEM = pl.BlockSpec(memory_space=pltpu.SMEM)


def call(body, outs, scratch, operands, flops, mem=24, scalars=()):
    return pl.pallas_call(
        body,
        out_shape=outs,
        in_specs=[SMEM if j in scalars else VMEM for j in range(len(operands))],
        out_specs=jax.tree.map(lambda _: VMEM, outs),
        scratch_shapes=scratch,
        compiler_params=pltpu.CompilerParams(vmem_limit_bytes=mem << 20),
        cost_estimate=pl.CostEstimate(flops=flops, bytes_accessed=4 << 20, transcendentals=0),
    )(*operands)


def shape(*dims, dtype=F32):
    return jax.ShapeDtypeStruct(dims, dtype)


def split(value):
    high = value.astype(BF16)
    return high, (value - high.astype(F32)).astype(BF16)


def weights_body(kernels, biases, fwd_hi, fwd_lo, bwd_hi, bwd_lo, bias2):
    zero = jnp.zeros((CH, CH), F32)

    def put(hi, lo, k, j, dh, first, second):
        block = jnp.concatenate([first, second], axis=1)
        high, low = split(block)
        where = (k, pl.ds(CH * j, CH), pl.ds(LANES * dh, LANES))
        hi[where] = high
        lo[where] = low

    for k in range(LAYERS):
        for dh in range(3):
            taps = [kernels[k * 9 + dh * 3 + dw] for dw in range(3)]
            if k < LAYERS - 1:
                for j in range(4):
                    put(fwd_hi, fwd_lo, k, j, dh, taps[j] if j < 3 else zero, taps[j - 1] if j > 0 else zero)
            flips = [tap.T for tap in taps]
            for j in range(4):
                put(bwd_hi, bwd_lo, k, j, 2 - dh, flips[2 - j] if j < 3 else zero, flips[3 - j] if j > 0 else zero)
    for k in range(LAYERS):
        row = biases[k : k + 1, :]
        bias2[k : k + 1, :] = jnp.concatenate([row, row], axis=1)


def weights(kernels, biases):
    n = 4 * CH
    outs = (
        shape(LAYERS - 1, n, 3 * LANES, dtype=BF16),
        shape(LAYERS - 1, n, 3 * LANES, dtype=BF16),
        shape(LAYERS, n, 3 * LANES, dtype=BF16),
        shape(LAYERS, n, 3 * LANES, dtype=BF16),
        shape(8, LANES),
    )
    return call(weights_body, outs, [], (kernels.reshape(LAYERS * 9, CH, CH), biases), 1 << 22)


def sources(objective, center, radius, lower, upper):
    return [
        lambda cols: center[:, cols].astype(F32),
        lambda cols: upper[0, :, cols].astype(F32),
        lambda cols: upper[1, :, cols].astype(F32),
        lambda cols: upper[2, :, cols].astype(F32),
        lambda cols: lower[0, :, cols].astype(F32),
        lambda cols: lower[1, :, cols].astype(F32),
        lambda cols: lower[2, :, cols].astype(F32),
        lambda cols: radius[:, cols].astype(F32),
        lambda cols: objective[:, cols],
    ]


def sides_body(objective, center, radius, lower, upper, head, tail):
    rows, cols = objective.shape
    strip = HALO_PAIRS * LANES
    for m, read in enumerate(sources(objective, center, radius, lower, upper)):
        here = pl.ds(m * rows, rows)
        head[here, :] = read(pl.ds(0, strip))
        tail[here, :] = read(pl.ds(cols - strip, strip))


def column(reads, left, right, rows, pairs, m, q):
    if q < HALO_PAIRS:
        return left[m * rows : (m + 1) * rows, q * LANES : (q + 1) * LANES]
    if q >= HALO_PAIRS + pairs:
        q -= HALO_PAIRS + pairs
        return right[m * rows : (m + 1) * rows, q * LANES : (q + 1) * LANES]
    return reads[m](pl.ds((q - HALO_PAIRS) * LANES, LANES))


def ends_body(objective, center, radius, lower, upper, left, right, top, bottom):
    rows, cols = objective.shape
    pairs = cols // LANES
    reads = sources(objective, center, radius, lower, upper)
    for m in range(9):
        sent = ROWS_SENT[m]
        here = slice(ROW_START[m], ROW_START[m] + sent)
        for q in range(pairs + 2 * HALO_PAIRS):
            value = column(reads, left, right, rows, pairs, m, q)
            top[q, here, :] = value[:sent]
            bottom[q, here, :] = value[rows - sent :]
    spare = slice(sum(ROWS_SENT), SENT)
    top[:, spare, :] = jnp.zeros((pairs + 2 * HALO_PAIRS, SENT - sum(ROWS_SENT), LANES), F32)
    bottom[:, spare, :] = jnp.zeros((pairs + 2 * HALO_PAIRS, SENT - sum(ROWS_SENT), LANES), F32)


def neighbours(head, tail, axis):
    count = lax.axis_size(axis)
    before = lax.ppermute(tail, axis, [(i, i + 1) for i in range(count - 1)])
    after = lax.ppermute(head, axis, [(i + 1, i) for i in range(count - 1)])
    return before, after


def roll_rows(value, shift):
    return pltpu.roll(value, shift % value.shape[0], 0)


def slide(maps, count, store, produce):
    rows = store.shape[2]
    early = lax.broadcasted_iota(jnp.int32, (rows, LANES), 1) < CH
    zero = jnp.zeros((rows, LANES), F32)

    def step(q, carry):
        fresh = [pltpu.roll(value, CH, 1) for value in produce(q)]
        for k in range(maps):
            store[k, q] = jnp.where(early, carry[k], fresh[k])
        return tuple(fresh)

    last = lax.fori_loop(0, count, step, (zero,) * maps)
    for k in range(maps):
        store[k, count] = jnp.where(early, last[k], zero)


def multiply(store, k, first, count, hi, lo, layer, sums, exact=False):
    rows = store.shape[2]
    left = store[k, pl.ds(first, count)].reshape(count * rows, LANES)
    right = store[k, pl.ds(first + 1, count)].reshape(count * rows, LANES)
    window = jnp.concatenate([left, right], axis=1)
    dot = functools.partial(jnp.dot, preferred_element_type=F32)
    if exact:
        high = window.astype(BF16)
        result = dot(high, hi[layer]) + dot(high, lo[layer])
    else:
        high, low = split(window)
        result = dot(high, hi[layer]) + dot(high, lo[layer]) + dot(low, hi[layer])
    for d in range(3):
        sums[k, d, pl.ds(0, count)] = result[:, d * LANES : (d + 1) * LANES].reshape(count, rows, LANES)


def gathered(sums, k, q):
    return roll_rows(sums[k, 0, q], 1) + sums[k, 1, q] + roll_rows(sums[k, 2, q], -1)


def summed(total):
    return jnp.sum(total[...], axis=0, keepdims=True)


def scale_of(total, step, cells):
    squares = summed(total)[:, 0:1]
    return step / jnp.sqrt(squares / (2 * (LAYERS - 1) * cells) + EPS)


def soft(top, t):
    return 0.5 * top * (1.0 - jnp.tanh(t))


class Bound:
    def __init__(self, start):
        self.linear = start
        self.factor = None

    def add(self, t):
        self.linear = self.linear - jnp.maximum(-t, 0.0)
        factor = 1.0 + jnp.exp(-2.0 * jnp.abs(t))
        self.factor = factor if self.factor is None else self.factor * factor

    def total(self):
        return self.linear - 0.5 * jnp.log(self.factor)


def own_rows(value):
    rows = value.shape[0]
    row = lax.broadcasted_iota(jnp.int32, value.shape, 0)
    kept = jnp.where((row >= EDGE) & (row < rows - EDGE), value, 0.0)
    return jnp.sum(kept, axis=0, keepdims=True)


def stats(out, rows):
    lane = lax.broadcasted_iota(jnp.int32, (1, LANES), 1)
    packed = jnp.zeros((1, LANES), F32)
    for j, row in enumerate(rows):
        packed = jnp.where(lane == j, jnp.sum(row, axis=1, keepdims=True), packed)
    out[...] = jnp.broadcast_to(packed, out.shape)


def first_body(
    objective, center, radius, lower, upper, left, right, above, below,
    fwd_hi, fwd_lo, bwd_hi, bwd_lo, bias,
    box, back, slope, mult, stat, value,
    raw, target, store, sums,
):
    rows, cols = objective.shape
    pairs = cols // LANES
    frame = rows + 2 * EDGE
    wide = pairs + 4
    reads = sources(objective, center, radius, lower, upper)
    for m in range(9):
        sent = ROWS_SENT[m]
        here = slice(ROW_START[m], ROW_START[m] + sent)
        for q in range(pairs + 2 * HALO_PAIRS):
            if m >= 3 and not 1 <= q < wide + 1:
                continue
            own = column(reads, left, right, rows, pairs, m, q)
            if m < 3:
                dest, at, edge = raw.at[m, q], 0, WIDE
            else:
                dest, at, edge = (target.at[q - 1] if m == 8 else box.at[m, q - 1]), EDGE - sent, EDGE
                if at:
                    dest[0:EDGE, :] = jnp.zeros((EDGE, LANES), F32)
                    dest[EDGE + rows : frame, :] = jnp.zeros((EDGE, LANES), F32)
            dest[at : at + sent, :] = above[q, here, :]
            dest[edge : edge + rows, :] = own
            dest[edge + rows : edge + rows + sent, :] = below[q, here, :]
    raw[:, :, rows + 2 * WIDE :, :] = jnp.zeros((3, wide + 2, raw.shape[2] - rows - 2 * WIDE, LANES), F32)
    for m in range(3):
        for q in range(wide):
            box[m, q] = raw[m, q + 1, 1 : 1 + frame, :]

    tall = raw.shape[2]
    early = lax.broadcasted_iota(jnp.int32, (tall, LANES), 1) < CH

    def middle(q):
        return [raw[0, q], 0.5 * raw[1, q], 0.5 * raw[2, q]]

    slide(3, wide + 2, store, middle)
    for k in range(3):
        multiply(store, k, 1, wide, fwd_hi, fwd_lo, k, sums, exact=True)

    def slopes(q, carry):
        for k in range(3):
            conv = (
                sums[k, 0, q][:frame]
                + roll_rows(sums[k, 1, q], -1)[:frame]
                + roll_rows(sums[k, 2, q], -2)[:frame]
            )
            gap = box[1 + k, q]
            dl = 0.5 * (gap - box[4 + k, q]) - conv - bias[k : k + 1, :]
            slope[k, q] = jnp.where(gap > 0.0, dl, 0.0)
        return carry

    lax.fori_loop(0, wide, slopes, 0)

    early = lax.broadcasted_iota(jnp.int32, (frame, LANES), 1) < CH
    zero = jnp.zeros((frame, LANES), F32)

    def shift(q, carry):
        fresh = pltpu.roll(target[q], CH, 1)
        store[0, q, 0:frame, :] = jnp.where(early, carry, fresh)
        return fresh

    last = lax.fori_loop(0, wide, shift, zero)
    store[0, wide, 0:frame, :] = jnp.where(early, last, zero)
    lhs = jnp.concatenate(
        [
            store[0, 0:wide, 0:frame, :].reshape(wide * frame, LANES),
            store[0, 1 : wide + 1, 0:frame, :].reshape(wide * frame, LANES),
        ],
        axis=1,
    )
    high, low = split(lhs)
    dot = functools.partial(jnp.dot, preferred_element_type=F32)
    k = LAYERS - 1
    result = dot(high, bwd_hi[k]) + dot(high, bwd_lo[k]) + dot(low, bwd_hi[k])
    for d in range(3):
        sums[0, d, 0:wide, 0:frame, :] = result[:, d * LANES : (d + 1) * LANES].reshape(wide, frame, LANES)

    def pulls(q, carry):
        squares, worth, fixed = carry
        pull = (
            roll_rows(sums[0, 0, q][:frame], 1)
            + sums[0, 1, q][:frame]
            + roll_rows(sums[0, 2, q][:frame], -1)
        )
        back[q] = pull
        gap = box[3, q]
        t = pull * gap
        dm = -0.5 * gap * jnp.tanh(t)
        mult[q] = dm
        new = dm * dm
        for k in range(3):
            dl = slope[k, q]
            new = new + dl * dl
        bound = Bound(jnp.full((frame, LANES), -4.5 * math.log(2.0), F32))
        bound.add(t)
        own = (q >= 2) & (q < wide - 2)
        squares = squares + jnp.where(own, new, 0.0)
        worth = worth + jnp.where(own, bound.total(), 0.0)
        fixed = fixed + jnp.where(own, target[q] * bias[3:4, :], 0.0)
        return squares, worth, fixed

    squares, worth, fixed = lax.fori_loop(0, wide, pulls, (zero, zero, zero))
    fixed = own_rows(fixed)
    stats(stat, [own_rows(squares)])
    stats(value, [own_rows(worth) + fixed, fixed])


def second_pull_body(slope, bwd_hi, bwd_lo, back, store, sums):
    count = slope.shape[1]
    slide(3, count, store, lambda q: [slope[k, q] for k in range(3)])
    for k in range(3):
        multiply(store, k, 0, count, bwd_hi, bwd_lo, k, sums)

    def step(q, carry):
        for k in range(3):
            back[k, q] = gathered(sums, k, q)
        return carry

    lax.fori_loop(0, count, step, 0)


def second_body(
    total, steps, box, back, slope, mult, pull, fwd_hi, fwd_lo, bias,
    slope_out, mult_out, stat, value,
    points, store, sums, *, cells,
):
    wide = box.shape[1]
    frame = box.shape[2]
    scale = jnp.broadcast_to(scale_of(total, steps[0], cells), (frame, LANES))
    zero = jnp.zeros((frame, LANES), F32)

    def produce(q):
        radius = box[7, q]
        outs = [box[0, q] - radius * jnp.tanh(-2.0 * radius * (scale * pull[0, q]))]
        for k in (1, 2):
            gap = box[k, q]
            x = soft(gap, -(scale * pull[k, q]) * gap)
            points[k - 1, q] = x
            outs.append(x)
        return outs

    slide(3, wide, store, produce)
    for k in range(3):
        multiply(store, k, 1, wide - 2, fwd_hi, fwd_lo, k, sums)

    def step(j, carry):
        squares, worth = carry
        q = j + 1
        new = zero
        g = -(scale * pull[0, q])
        radius = box[7, q]
        bound = Bound(g * (box[0, q] - radius))
        bound.add(2.0 * g * radius)
        for k in range(3):
            gap = box[1 + k, q]
            low = box[4 + k, q]
            lam = scale * slope[k, q]
            if k < 2:
                x = points[k, q]
                bound.add(-(scale * pull[k + 1, q]) * gap)
                tp = lam * gap
            else:
                mu = scale * mult[q]
                t = (back[q] + mu) * gap
                x = soft(gap, t)
                bound.add(t)
                tp = (lam - mu) * gap
            tn = -lam * low
            bound.add(tp)
            bound.add(tn)
            bound.linear = bound.linear - lam * bias[k : k + 1, :]
            positive = soft(gap, tp)
            dl = positive - soft(low, tn) - gathered(sums, k, j) - bias[k : k + 1, :]
            dl = jnp.where(gap > 0.0, dl, 0.0)
            dm = x - positive
            slope_out[k, j] = dl
            mult_out[k, j] = dm
            new = new + dl * dl + dm * dm
        own = (q >= 2) & (q < wide - 2)
        return squares + jnp.where(own, new, 0.0), worth + jnp.where(own, bound.total(), 0.0)

    squares, worth = lax.fori_loop(0, wide - 2, step, (zero, zero))
    stats(stat, [own_rows(squares)])
    stats(value, [own_rows(worth)])


def third_body(
    total0, total1, steps, box, back, slope0, mult0, pull0, slope1, mult1, pull1, fwd_hi, fwd_lo, bias,
    value0, value1,
    duals, multipliers, slope_out, mult_out, stat,
    points, store, sums, *, cells,
):
    wide = box.shape[1]
    frame = box.shape[2]
    rows = frame - 2 * EDGE
    s0 = jnp.broadcast_to(scale_of(total0, steps[0], cells), (frame, LANES))
    s1 = jnp.broadcast_to(scale_of(total1, steps[1], cells), (frame, LANES))
    zero = jnp.zeros((frame, LANES), F32)

    def pull_of(k, j):
        g = -(s0 * pull0[k, j + 1] + s1 * pull1[k, j])
        return g if k == 0 else g + s1 * mult1[k - 1, j]

    def produce(j):
        q = j + 1
        radius = box[7, q]
        outs = [box[0, q] - radius * jnp.tanh(2.0 * radius * pull_of(0, j))]
        for k in (1, 2):
            gap = box[k, q]
            x = soft(gap, pull_of(k, j) * gap)
            points[k - 1, j] = x
            outs.append(x)
        return outs

    slide(3, wide - 2, store, produce)
    for k in range(3):
        multiply(store, k, 1, wide - 4, fwd_hi, fwd_lo, k, sums)

    def step(i, carry):
        squares, worth = carry
        j = i + 1
        q = i + 2
        new = zero
        g = pull_of(0, j)
        radius = box[7, q]
        bound = Bound(g * (box[0, q] - radius))
        bound.add(2.0 * g * radius)
        here = pl.ds(pl.multiple_of(i * LANES, LANES), LANES)
        for k in range(3):
            gap = box[1 + k, q]
            low = box[4 + k, q]
            lam = s0 * slope0[k, q] + s1 * slope1[k, j]
            mu = s1 * mult1[k, j]
            if k < 2:
                x = points[k, j]
                bound.add(pull_of(k + 1, j) * gap)
            else:
                mu = mu + s0 * mult0[q]
                t = (back[q] + mu) * gap
                x = soft(gap, t)
                bound.add(t)
            tp = (lam - mu) * gap
            tn = -lam * low
            bound.add(tp)
            bound.add(tn)
            bound.linear = bound.linear - lam * bias[k : k + 1, :]
            positive = soft(gap, tp)
            dl = positive - soft(low, tn) - gathered(sums, k, i) - bias[k : k + 1, :]
            dm = x - positive
            duals[k, :, here] = lam[EDGE : EDGE + rows]
            multipliers[k, :, here] = mu[EDGE : EDGE + rows]
            slope_out[k, :, here] = dl[EDGE : EDGE + rows]
            mult_out[k, :, here] = dm[EDGE : EDGE + rows]
            new = new + dl * dl + dm * dm
        return squares + new, worth + bound.total()

    squares, worth = lax.fori_loop(0, wide - 4, step, (zero, zero))
    lane = lax.broadcasted_iota(jnp.int32, (1, LANES), 1)
    first, fixed = (jnp.where(lane == j, value0[0:1, :], 0.0) for j in range(2))
    second = jnp.where(lane == 0, value1[0:1, :], 0.0)
    stats(stat, [own_rows(squares), first, second + fixed, own_rows(worth) + fixed])


def last_body(total, steps, duals, multipliers, slope, mult, bounds, duals_out, mult_out, *, cells):
    scale = jnp.broadcast_to(scale_of(total, steps[2], cells), (duals.shape[1], duals.shape[2]))
    for k in range(LAYERS - 1):
        duals_out[k] = duals[k] + scale * slope[k]
        mult_out[k] = multipliers[k] + scale * mult[k]
    bounds[...] = jnp.broadcast_to(summed(total) / cells, bounds.shape)


def everyone(partial):
    return lax.all_to_all(partial, ("row", "col"), 0, 0, tiled=True)


def shards(objective, center, radius, lower, upper, kernels, biases, steps):
    rows, cols = objective.shape
    pairs = cols // LANES
    wide = pairs + 4
    frame = rows + 2 * EDGE
    tall = -(-(rows + 2 * WIDE) // 8) * 8
    cells = rows * cols * lax.axis_size("row") * lax.axis_size("col")
    inputs = (objective, center, radius, lower, upper)
    flops = 3 * 2 * 3 * wide * frame * 4 * CH * 3 * LANES

    strip = shape(9 * rows, HALO_PAIRS * LANES)
    head, tail = call(sides_body, (strip, strip), [], inputs, 1 << 20)
    left, right = neighbours(head, tail, "col")
    fwd_hi, fwd_lo, bwd_hi, bwd_lo, bias = weights(kernels, biases)
    strip = shape(pairs + 2 * HALO_PAIRS, SENT, LANES)
    top, bottom = call(ends_body, (strip, strip), [], inputs + (left, right), 1 << 20)
    above, below = neighbours(top, bottom, "row")

    stat_shape = shape(8, LANES)
    spread = shape(lax.axis_size("row") * lax.axis_size("col"), LANES)
    box, back, slope0, mult0, stat0, value0 = call(
        first_body,
        (
            shape(8, wide, frame, LANES),
            shape(wide, frame, LANES),
            shape(3, wide, frame, LANES),
            shape(wide, frame, LANES),
            spread,
            stat_shape,
        ),
        [
            pltpu.VMEM((3, wide + 2, tall, LANES), F32),
            pltpu.VMEM((wide, frame, LANES), F32),
            pltpu.VMEM((3, wide + 3, tall, LANES), F32),
            pltpu.VMEM((3, 3, wide, tall, LANES), F32),
        ],
        inputs + (left, right, above, below, fwd_hi, fwd_lo, bwd_hi, bwd_lo, bias),
        2 * flops,
    )

    def pulled(slope):
        count = slope.shape[1]
        return call(
            second_pull_body,
            shape(3, count, frame, LANES),
            [
                pltpu.VMEM((3, count + 1, frame, LANES), F32),
                pltpu.VMEM((3, 3, count, frame, LANES), F32),
            ],
            (slope, bwd_hi, bwd_lo),
            flops,
        )

    total0 = everyone(stat0)
    pull0 = pulled(slope0)
    slope1, mult1, stat1, value1 = call(
        functools.partial(second_body, cells=cells),
        (shape(3, wide - 2, frame, LANES), shape(3, wide - 2, frame, LANES), spread, stat_shape),
        [
            pltpu.VMEM((2, wide, frame, LANES), F32),
            pltpu.VMEM((3, wide + 1, frame, LANES), F32),
            pltpu.VMEM((3, 3, wide - 2, frame, LANES), F32),
        ],
        (total0, steps, box, back, slope0, mult0, pull0, fwd_hi, fwd_lo, bias),
        flops,
        scalars=(1,),
    )
    total1 = everyone(stat1)
    pull1 = pulled(slope1)
    out = shape(3, rows, cols)
    duals, multipliers, slope2, mult2, stat2 = call(
        functools.partial(third_body, cells=cells),
        (out, out, out, out, spread),
        [
            pltpu.VMEM((2, wide - 2, frame, LANES), F32),
            pltpu.VMEM((3, wide - 1, frame, LANES), F32),
            pltpu.VMEM((3, 3, wide - 4, frame, LANES), F32),
        ],
        (
            total0, total1, steps, box, back, slope0, mult0, pull0, slope1, mult1, pull1,
            fwd_hi, fwd_lo, bias, value0, value1,
        ),
        flops,
        scalars=(2,),
    )
    total2 = everyone(stat2)
    bounds, final_duals, final_multipliers = call(
        functools.partial(last_body, cells=cells),
        (stat_shape, out, out),
        [],
        (total2, steps, duals, multipliers, slope2, mult2),
        1 << 20,
        scalars=(1,),
    )
    return bounds[0, 1 : 1 + ITERS], final_duals, final_multipliers


def solution(mesh):
    placed = (
        P("row", "col"),
        P("row", "col"),
        P("row", "col"),
        P(None, "row", "col"),
        P(None, "row", "col"),
        P(),
        P(),
        P(),
    )
    return jax.shard_map(
        shards,
        mesh=mesh,
        in_specs=placed,
        out_specs=(P(), P(None, "row", "col"), P(None, "row", "col")),
        check_vma=False,
    )
```

```python
import functools
import math

import jax
import jax.numpy as jnp
from jax import lax
from jax.experimental import pallas as pl
from jax.experimental.pallas import tpu as pltpu
from jax.sharding import PartitionSpec as P

CH = 64
LAYERS = 4
ITERS = 3
EPS = 1e-06
LANES = 2 * CH
HALO_PAIRS = 3
WIDE = 5
EDGE = 4
F32 = jnp.float32
BF16 = jnp.bfloat16

ROWS_SENT = (5, 5, 5, 4, 4, 4, 4, 3, 3)
ROW_START = tuple(sum(ROWS_SENT[:m]) for m in range(9))
SENT = 40
NEAR = (0, 1, 2, 8)

VMEM = pl.BlockSpec(memory_space=pltpu.VMEM)
SMEM = pl.BlockSpec(memory_space=pltpu.SMEM)
HBM = pl.BlockSpec(memory_space=pltpu.HBM)


def call(body, outs, scratch, operands, flops, mem=20, scalars=(), far=(), far_outs=()):
    specs = [SMEM if j in scalars else HBM if j in far else VMEM for j in range(len(operands))]
    out_specs = tuple(HBM if j in far_outs else VMEM for j in range(len(outs)))
    return pl.pallas_call(
        body,
        out_shape=outs,
        in_specs=specs,
        out_specs=out_specs,
        scratch_shapes=scratch,
        compiler_params=pltpu.CompilerParams(vmem_limit_bytes=mem << 20),
        cost_estimate=pl.CostEstimate(flops=flops, bytes_accessed=4 << 20, transcendentals=0),
    )(*operands)


def shape(*dims, dtype=F32):
    return jax.ShapeDtypeStruct(dims, dtype)


def copies(pairs, sem):
    made = [pltpu.make_async_copy(src, dst, sem.at[j]) for j, (src, dst) in enumerate(pairs)]
    for one in made:
        one.start()
    return made


def finish(made):
    for one in made:
        one.wait()


def split(value):
    high = value.astype(BF16)
    return high, (value - high.astype(F32)).astype(BF16)


def weights_body(kernels, biases, fwd_out, bwd_out, bias2, fwd, bwd, sem):
    zero = jnp.zeros((CH, CH), F32)

    def put(dest, k, j, dh, first, second):
        block = jnp.concatenate([first, second], axis=1)
        for part, value in enumerate(split(block)):
            dest[part, k, pl.ds(CH * j, CH), pl.ds(LANES * dh, LANES)] = value

    for k in range(LAYERS):
        for dh in range(3):
            taps = [kernels[k * 9 + dh * 3 + dw] for dw in range(3)]
            if k < LAYERS - 1:
                for j in range(4):
                    put(fwd, k, j, dh, taps[j] if j < 3 else zero, taps[j - 1] if j > 0 else zero)
            flips = [tap.T for tap in taps]
            for j in range(4):
                put(bwd, k, j, 2 - dh, flips[2 - j] if j < 3 else zero, flips[3 - j] if j > 0 else zero)
    for k in range(LAYERS):
        row = biases[k : k + 1, :]
        bias2[k : k + 1, :] = jnp.concatenate([row, row], axis=1)
    finish(copies([(fwd, fwd_out), (bwd, bwd_out)], sem))


FWD = (2, LAYERS - 1, 4 * CH, 3 * LANES)
BWD = (2, LAYERS, 4 * CH, 3 * LANES)


def weights(kernels, biases):
    return call(
        weights_body,
        (shape(*FWD, dtype=BF16), shape(*BWD, dtype=BF16), shape(8, LANES)),
        [pltpu.VMEM(FWD, BF16), pltpu.VMEM(BWD, BF16), pltpu.SemaphoreType.DMA((2,))],
        (kernels.reshape(LAYERS * 9, CH, CH), biases),
        1 << 22,
        far_outs=(0, 1),
    )


def sources(objective, center, radius, lower, upper):
    return [
        lambda cols: center[:, cols].astype(F32),
        lambda cols: upper[0, :, cols].astype(F32),
        lambda cols: upper[1, :, cols].astype(F32),
        lambda cols: upper[2, :, cols].astype(F32),
        lambda cols: lower[0, :, cols].astype(F32),
        lambda cols: lower[1, :, cols].astype(F32),
        lambda cols: lower[2, :, cols].astype(F32),
        lambda cols: radius[:, cols].astype(F32),
        lambda cols: objective[:, cols],
    ]


def sides_body(objective, center, radius, lower, upper, head, tail, *rest):
    rows, cols = objective.shape
    strip = HALO_PAIRS * LANES
    ends, sem = rest[:-1], rest[-1]
    moves = []
    for side, at in enumerate((0, cols - strip)):
        here = pl.ds(at, strip)
        five = ends[5 * side : 5 * side + 5]
        moves += [
            (objective.at[:, here], five[0]),
            (center.at[:, here], five[1]),
            (radius.at[:, here], five[2]),
            (lower.at[:, :, here], five[3]),
            (upper.at[:, :, here], five[4]),
        ]
    finish(copies(moves, sem))
    for side, out in enumerate((head, tail)):
        for m, read in enumerate(sources(*ends[5 * side : 5 * side + 5])):
            out[pl.ds(m * rows, rows), :] = read(slice(None))


def column(reads, left, right, rows, pairs, m, q):
    if q < HALO_PAIRS:
        return left[m * rows : (m + 1) * rows, q * LANES : (q + 1) * LANES]
    if q >= HALO_PAIRS + pairs:
        q -= HALO_PAIRS + pairs
        return right[m * rows : (m + 1) * rows, q * LANES : (q + 1) * LANES]
    return reads[m](pl.ds((q - HALO_PAIRS) * LANES, LANES))


def ends_body(objective, center, radius, lower, upper, left, right, near_top, near_bottom, top, bottom):
    rows, cols = objective.shape
    pairs = cols // LANES
    reads = sources(objective, center, radius, lower, upper)
    for m in range(9):
        sent = ROWS_SENT[m]
        here = slice(ROW_START[m], ROW_START[m] + sent)
        for q in range(pairs + 2 * HALO_PAIRS):
            value = column(reads, left, right, rows, pairs, m, q)
            top[q, here, :] = value[:sent]
            bottom[q, here, :] = value[rows - sent :]
            if m in NEAR and HALO_PAIRS - 1 <= q <= HALO_PAIRS + pairs:
                row = NEAR.index(m)
                near_top[q - HALO_PAIRS + 1, row : row + 1, :] = value[:1]
                near_bottom[q - HALO_PAIRS + 1, row : row + 1, :] = value[rows - 1 :]
    spare = slice(sum(ROWS_SENT), SENT)
    blank = jnp.zeros((pairs + 2 * HALO_PAIRS, SENT - sum(ROWS_SENT), LANES), F32)
    top[:, spare, :] = blank
    bottom[:, spare, :] = blank


def neighbours(head, tail, axis):
    count = lax.axis_size(axis)
    before = lax.ppermute(tail, axis, [(i, i + 1) for i in range(count - 1)])
    after = lax.ppermute(head, axis, [(i + 1, i) for i in range(count - 1)])
    return before, after


def roll_rows(value, shift):
    return pltpu.roll(value, shift % value.shape[0], 0)


def slide(maps, count, store, produce):
    rows = store.shape[2]
    early = lax.broadcasted_iota(jnp.int32, (rows, LANES), 1) < CH
    zero = jnp.zeros((rows, LANES), F32)

    def step(q, carry):
        fresh = [pltpu.roll(value, CH, 1) for value in produce(q)]
        for k in range(maps):
            store[k, q] = jnp.where(early, carry[k], fresh[k])
        return tuple(fresh)

    last = lax.fori_loop(0, count, step, (zero,) * maps)
    for k in range(maps):
        store[k, count] = jnp.where(early, last[k], zero)


def multiply(store, k, first, count, weight, layer, sums, exact=False):
    rows = store.shape[2]
    left = store[k, pl.ds(first, count)].reshape(count * rows, LANES)
    right = store[k, pl.ds(first + 1, count)].reshape(count * rows, LANES)
    window = jnp.concatenate([left, right], axis=1)
    dot = functools.partial(jnp.dot, preferred_element_type=F32)
    high, low = split(window)
    result = dot(high, weight[0, layer]) + dot(high, weight[1, layer])
    if not exact:
        result = result + dot(low, weight[0, layer])
    for d in range(3):
        sums[k, d, pl.ds(0, count)] = result[:, d * LANES : (d + 1) * LANES].reshape(count, rows, LANES)


def gathered(sums, k, q):
    return roll_rows(sums[k, 0, q], 1) + sums[k, 1, q] + roll_rows(sums[k, 2, q], -1)


def inner(sums, k, q, first, rows):
    parts = [roll_rows(sums[k, d, q], 1 - d - first)[:rows] for d in range(3)]
    return parts[0] + parts[1] + parts[2]


def summed(total):
    return jnp.sum(total[...], axis=0, keepdims=True)


def scale_of(total, step, cells, dims):
    squares = summed(total)[:, 0:1]
    return jnp.broadcast_to(step / jnp.sqrt(squares / (2 * (LAYERS - 1) * cells) + EPS), dims)


def soft(top, t):
    return 0.5 * top * (1.0 - jnp.tanh(t))


class Bound:
    def __init__(self, start):
        self.linear = start
        self.factor = None

    def add(self, t):
        self.linear = self.linear - jnp.maximum(-t, 0.0)
        factor = 1.0 + jnp.exp(-2.0 * jnp.abs(t))
        self.factor = factor if self.factor is None else self.factor * factor

    def total(self):
        return self.linear - 0.5 * jnp.log(self.factor)


def folded(value):
    return jnp.sum(value, axis=0, keepdims=True)


def own_rows(value):
    rows = value.shape[0]
    row = lax.broadcasted_iota(jnp.int32, value.shape, 0)
    return folded(jnp.where((row >= EDGE) & (row < rows - EDGE), value, 0.0))


def stats(out, rows):
    lane = lax.broadcasted_iota(jnp.int32, (1, LANES), 1)
    packed = jnp.zeros((1, LANES), F32)
    for j, row in enumerate(rows):
        packed = jnp.where(lane == j, jnp.sum(row, axis=1, keepdims=True), packed)
    out[...] = jnp.broadcast_to(packed, out.shape)


def own_body(
    objective, center, radius, lower, upper, left, right, above, below, fwd_far, bwd_far, bias,
    stat,
    raw, store, sums, fwd, bwd, sem,
):
    arrivals = copies([(fwd_far, fwd), (bwd_far.at[:, LAYERS - 1], bwd.at[:, 0])], sem)
    rows, cols = objective.shape
    pairs = cols // LANES
    frame = raw.shape[2]
    reads = sources(objective, center, radius, lower, upper)
    for row, m in enumerate(NEAR):
        for q in range(pairs + 2):
            raw[row, q, 0:1, :] = above[q, row : row + 1, :]
            raw[row, q, 1 : rows + 1, :] = column(reads, left, right, rows, pairs, m, q + HALO_PAIRS - 1)
            raw[row, q, rows + 1 : rows + 2, :] = below[q, row : row + 1, :]
    raw[:, :, rows + 2 :, :] = jnp.zeros((4, pairs + 2, frame - rows - 2, LANES), F32)
    slide(4, pairs + 2, store, lambda q: [raw[0, q], 0.5 * raw[1, q], 0.5 * raw[2, q], raw[3, q]])
    finish(arrivals)
    for k in range(3):
        multiply(store, k, 1, pairs, fwd, k, sums, exact=True)
    multiply(store, 3, 1, pairs, bwd, 0, sums)

    def step(q, squares):
        here = pl.ds(pl.multiple_of(q * LANES, LANES), LANES)
        for k in range(3):
            gap = upper[k, :, here].astype(F32)
            low = lower[k, :, here].astype(F32)
            dl = 0.5 * (gap - low) - inner(sums, k, q, 1, rows) - bias[k : k + 1, :]
            squares = squares + dl * dl
        dm = 0.5 * gap * jnp.tanh(inner(sums, 3, q, 1, rows) * gap)
        return squares + dm * dm

    squares = lax.fori_loop(0, pairs, step, jnp.zeros((rows, LANES), F32))
    stats(stat, [folded(squares)])


def wide_body(
    objective, center, radius, lower, upper, left, right, above, below, fwd_far, bwd_far, bias, after,
    near_box, far_box, back, slope_out, mult, pull, value,
    raw, gaps, target, slope, store, sums, fwd, bwd, sem,
):
    del after
    arrivals = copies([(fwd_far, fwd), (bwd_far, bwd)], sem)
    rows, cols = objective.shape
    pairs = cols // LANES
    frame = rows + 2 * EDGE
    wide = pairs + 4
    reads = sources(objective, center, radius, lower, upper)
    for m in range(9):
        sent = ROWS_SENT[m]
        here = slice(ROW_START[m], ROW_START[m] + sent)
        for q in range(pairs + 2 * HALO_PAIRS):
            if m >= 3 and not 1 <= q < wide + 1:
                continue
            own = column(reads, left, right, rows, pairs, m, q)
            if m < 3:
                dest, at, edge = raw.at[m, q], 0, WIDE
            else:
                dest, at, edge = (target.at[q - 1] if m == 8 else gaps.at[m - 3, q - 1]), EDGE - sent, EDGE
                if at:
                    dest[0:EDGE, :] = jnp.zeros((EDGE, LANES), F32)
                    dest[EDGE + rows : frame, :] = jnp.zeros((EDGE, LANES), F32)
            dest[at : at + sent, :] = above[q, here, :]
            dest[edge : edge + rows, :] = own
            dest[edge + rows : edge + rows + sent, :] = below[q, here, :]
    raw[:, :, rows + 2 * WIDE :, :] = jnp.zeros((3, wide + 2, raw.shape[2] - rows - 2 * WIDE, LANES), F32)

    slide(3, wide + 2, store, lambda q: [raw[0, q], 0.5 * raw[1, q], 0.5 * raw[2, q]])
    finish(arrivals)
    for k in range(3):
        multiply(store, k, 1, wide, fwd, k, sums, exact=True)

    def slopes(q, carry):
        near = [raw[m, q + 1][1 : 1 + frame] for m in range(3)] + [gaps[4, q]]
        far = [gaps[m, q] for m in range(4)]
        for m in range(4):
            near_box[m, q] = near[m].astype(BF16)
            far_box[m, q] = far[m].astype(BF16)
        for k in range(3):
            gap = near[1 + k] if k < 2 else far[0]
            dl = 0.5 * (gap - far[1 + k]) - inner(sums, k, q, 1, frame) - bias[k : k + 1, :]
            slope[k, q] = jnp.where(gap > 0.0, dl, 0.0)
        return carry

    lax.fori_loop(0, wide, slopes, 0)
    slope_out[...] = slope[:, 1 : wide - 1]

    def produce(q):
        return [slope[k, q] for k in range(3)] + [target[q]]

    window = store.at[:, :, 0:frame, :]
    slide(4, wide, window, produce)
    short = sums.at[:, :, :, 0:frame, :]
    for k in range(4):
        multiply(window, k, 0, wide, bwd, k, short)

    zero = jnp.zeros((frame, LANES), F32)

    def pulls(q, carry):
        worth, fixed = carry
        for k in range(3):
            pull[k, q] = gathered(short, k, q)
        tug = gathered(short, 3, q)
        back[q] = tug
        gap = gaps[0, q]
        t = tug * gap
        mult[q] = -0.5 * gap * jnp.tanh(t)
        bound = Bound(jnp.full((frame, LANES), -4.5 * math.log(2.0), F32))
        bound.add(t)
        own = (q >= 2) & (q < wide - 2)
        worth = worth + jnp.where(own, bound.total(), 0.0)
        fixed = fixed + jnp.where(own, target[q] * bias[3:4, :], 0.0)
        return worth, fixed

    worth, fixed = lax.fori_loop(0, wide, pulls, (zero, zero))
    fixed = own_rows(fixed)
    stats(value, [own_rows(worth) + fixed, fixed])


def second_body(
    total, steps, near_box, far_box, back, slope, mult, pull, fwd_far, bias,
    base, slope_out, mult_out, duals, last_mult, last_slope, last_pull, stat,
    points, store, sums, fwd, sem, *, cells,
):
    arrivals = copies([(fwd_far, fwd)], sem)
    wide, frame = near_box.shape[1:3]
    inside = slice(EDGE, frame - EDGE)
    scale = scale_of(total, steps[0], cells, (frame, LANES))
    zero = jnp.zeros((frame, LANES), F32)

    def produce(q):
        center, radius = near_box[0, q].astype(F32), near_box[3, q].astype(F32)
        g = -(scale * pull[0, q])
        base[0, q] = g
        outs = [center - radius * jnp.tanh(2.0 * radius * g)]
        for k in (1, 2):
            gap = near_box[k, q].astype(F32)
            g = -(scale * pull[k, q])
            base[k, q] = g
            x = soft(gap, g * gap)
            points[k - 1, q] = x
            outs.append(x)
        return outs

    slide(3, wide, store, produce)
    finish(arrivals)
    for k in range(3):
        multiply(store, k, 1, wide - 2, fwd, k, sums)

    def step(j, squares):
        q = j + 1
        new = zero
        for k in range(3):
            gap = (near_box[1 + k, q] if k < 2 else far_box[0, q]).astype(F32)
            low = far_box[1 + k, q].astype(F32)
            lam = scale * slope[k, j]
            if k < 2:
                x = points[k, q]
                positive = soft(gap, lam * gap)
            else:
                mu = scale * mult[q]
                g = back[q] + mu
                x = soft(gap, g * gap)
                positive = soft(gap, (lam - mu) * gap)
            dl = positive - soft(low, -lam * low) - gathered(sums, k, j) - bias[k : k + 1, :]
            dl = jnp.where(gap > 0.0, dl, 0.0)
            dm = x - positive
            slope_out[k, j] = dl
            duals[k, j] = lam[inside]
            if k < 2:
                mult_out[k, j] = dm
            else:
                last_mult[j] = mu[inside]
                last_slope[j] = dm[inside]
                last_pull[j] = g[inside]
            new = new + dl * dl + dm * dm
        own = (q >= 2) & (q < wide - 2)
        return squares + jnp.where(own, new, 0.0)

    squares = lax.fori_loop(0, wide - 2, step, zero)
    stats(stat, [own_rows(squares)])


def pulled_body(
    slope, bwd_far, center_far, radius_far, lower_far, upper_far, base, duals, last_mult, last_pull, bias,
    pull, value,
    store, sums, bwd, center, radius, lower, upper, sem,
):
    arrivals = copies(
        [
            (bwd_far.at[:, 0 : LAYERS - 1], bwd),
            (center_far, center),
            (radius_far, radius),
            (lower_far, lower),
            (upper_far, upper),
        ],
        sem,
    )
    count, frame = slope.shape[1:3]
    rows = frame - 2 * EDGE
    inside = slice(EDGE, frame - EDGE)
    slide(3, count, store, lambda q: [slope[k, q] for k in range(3)])
    finish(arrivals)
    for k in range(3):
        multiply(store, k, 0, count, bwd, k, sums)

    def step(q, carry):
        for k in range(3):
            pull[k, q] = gathered(sums, k, q)
        return carry

    lax.fori_loop(0, count, step, 0)

    def worth_of(i, worth):
        j, q = i + 1, i + 2
        here = pl.ds(pl.multiple_of(i * LANES, LANES), LANES)
        spread = radius[:, here].astype(F32)
        g = base[0, q, inside, :]
        bound = Bound(g * (center[:, here].astype(F32) - spread))
        bound.add(2.0 * g * spread)
        for k in range(3):
            gap = upper[k, :, here].astype(F32)
            lam = duals[k, j]
            if k < 2:
                bound.add(base[k + 1, q, inside, :] * gap)
                bound.add(lam * gap)
            else:
                bound.add(last_pull[j] * gap)
                bound.add((lam - last_mult[j]) * gap)
            bound.add(-lam * lower[k, :, here].astype(F32))
            bound.linear = bound.linear - lam * bias[k : k + 1, :]
        return worth + bound.total()

    worth = lax.fori_loop(0, count - 2, worth_of, jnp.zeros((rows, LANES), F32))
    stats(value, [folded(worth)])


def third_body(
    total, steps, near_box, base, pull, mult, slope, duals1, last_mult, last_slope, last_pull,
    fwd_far, lower_far, upper_far, bias, value0, value1,
    duals, multipliers, slope_out, mult_out, stat,
    points, store, sums, fwd, lower, upper, sem, *, cells,
):
    arrivals = copies([(fwd_far, fwd), (lower_far, lower), (upper_far, upper)], sem)
    wide, frame = near_box.shape[1:3]
    rows = frame - 2 * EDGE
    inside = slice(EDGE, frame - EDGE)
    scale = scale_of(total, steps[1], cells, (frame, LANES))
    zero = jnp.zeros((frame, LANES), F32)

    def body(j, worth):
        q = j + 1
        center, radius = near_box[0, q].astype(F32), near_box[3, q].astype(F32)
        g = base[0, q] - scale * pull[0, j]
        bound = Bound(g * (center - radius))
        t = 2.0 * radius * g
        bound.add(t)
        outs = [center - radius * jnp.tanh(t)]
        for k in (1, 2):
            gap = near_box[k, q].astype(F32)
            t = (base[k, q] + scale * (mult[k - 1, j] - pull[k, j])) * gap
            bound.add(t)
            x = soft(gap, t)
            points[k - 1, j] = x
            outs.append(x)
        own = (q >= 2) & (q < wide - 2)
        return outs, worth + jnp.where(own, bound.total(), 0.0)

    early = lax.broadcasted_iota(jnp.int32, (frame, LANES), 1) < CH

    def first(j, carry):
        outs, worth = body(j, carry[3])
        fresh = [pltpu.roll(value, CH, 1) for value in outs]
        for k in range(3):
            store[k, j] = jnp.where(early, carry[k], fresh[k])
        return tuple(fresh) + (worth,)

    framed = lax.fori_loop(0, wide - 2, first, (zero,) * 4)[3]
    finish(arrivals)
    for k in range(3):
        multiply(store, k, 1, wide - 4, fwd, k, sums)

    scale = scale[:rows]

    def step(i, carry):
        squares, worth = carry
        j = i + 1
        here = pl.ds(pl.multiple_of(i * LANES, LANES), LANES)
        bound = None
        for k in range(3):
            gap = upper[k, :, here].astype(F32)
            low = lower[k, :, here].astype(F32)
            lam = duals1[k, j] + scale * slope[k, j, inside, :]
            if bound is None:
                bound = Bound(-lam * bias[k : k + 1, :])
            else:
                bound.linear = bound.linear - lam * bias[k : k + 1, :]
            if k < 2:
                x = points[k, j, inside, :]
                mu = scale * mult[k, j, inside, :]
            else:
                change = scale * last_slope[j]
                mu = last_mult[j] + change
                t = (last_pull[j] + change) * gap
                x = soft(gap, t)
                bound.add(t)
            tp = (lam - mu) * gap
            tn = -lam * low
            bound.add(tp)
            bound.add(tn)
            positive = soft(gap, tp)
            dl = positive - soft(low, tn) - inner(sums, k, i, EDGE, rows) - bias[k : k + 1, :]
            dm = x - positive
            duals[k, :, here] = lam
            multipliers[k, :, here] = mu
            slope_out[k, :, here] = dl
            mult_out[k, :, here] = dm
            squares = squares + dl * dl + dm * dm
        return squares, worth + bound.total()

    zero = jnp.zeros((rows, LANES), F32)
    squares, worth = lax.fori_loop(0, wide - 4, step, (zero, zero))
    lane = lax.broadcasted_iota(jnp.int32, (1, LANES), 1)
    start, fixed = (jnp.where(lane == j, value0[0:1, :], 0.0) for j in range(2))
    middle = jnp.where(lane == 0, value1[0:1, :], 0.0)
    stats(stat, [folded(squares), start, middle + fixed, folded(worth) + own_rows(framed) + fixed])


def last_body(total, steps, duals, multipliers, slope, mult, bounds, duals_out, mult_out, *, cells):
    scale = scale_of(total, steps[2], cells, duals.shape[1:])
    for k in range(LAYERS - 1):
        duals_out[k] = duals[k] + scale * slope[k]
        mult_out[k] = multipliers[k] + scale * mult[k]
    bounds[...] = jnp.broadcast_to(summed(total) / cells, bounds.shape)


def everyone(partial):
    return lax.all_to_all(partial, ("row", "col"), 0, 0, tiled=True)


def shards(objective, center, radius, lower, upper, kernels, biases, steps):
    rows, cols = objective.shape
    pairs = cols // LANES
    wide = pairs + 4
    frame = rows + 2 * EDGE
    tall = -(-(rows + 2 * WIDE) // 8) * 8
    low = -(-(rows + 2) // 8) * 8
    cells = rows * cols * lax.axis_size("row") * lax.axis_size("col")
    inputs = (objective, center, radius, lower, upper)
    flops = 3 * 2 * 3 * wide * frame * 4 * CH * 3 * LANES
    dma = pltpu.SemaphoreType.DMA
    spread = shape(lax.axis_size("row") * lax.axis_size("col"), LANES)
    small = shape(8, LANES)

    strip = HALO_PAIRS * LANES
    five = [
        pltpu.VMEM((rows, strip), F32),
        pltpu.VMEM((rows, strip), BF16),
        pltpu.VMEM((rows, strip), BF16),
        pltpu.VMEM((3, rows, strip), BF16),
        pltpu.VMEM((3, rows, strip), BF16),
    ]
    head, tail = call(
        sides_body,
        (shape(9 * rows, strip), shape(9 * rows, strip)),
        five + five + [dma((10,))],
        inputs,
        1 << 20,
        far=range(5),
    )
    left, right = neighbours(head, tail, "col")
    fwd, bwd, bias = weights(kernels, biases)
    near = shape(pairs + 2, len(NEAR), LANES)
    strip = shape(pairs + 2 * HALO_PAIRS, SENT, LANES)
    near_top, near_bottom, top, bottom = call(
        ends_body, (near, near, strip, strip), [], inputs + (left, right), 1 << 20
    )
    near_above, near_below = neighbours(near_top, near_bottom, "row")
    above, below = neighbours(top, bottom, "row")

    (stat0,) = call(
        own_body,
        (spread,),
        [
            pltpu.VMEM((4, pairs + 2, low, LANES), F32),
            pltpu.VMEM((4, pairs + 3, low, LANES), F32),
            pltpu.VMEM((4, 3, pairs, low, LANES), F32),
            pltpu.VMEM(FWD, BF16),
            pltpu.VMEM((2, 1) + BWD[2:], BF16),
            dma((2,)),
        ],
        inputs + (left, right, near_above, near_below, fwd, bwd, bias),
        flops,
        far=(9, 10),
    )
    total0 = everyone(stat0)
    near_box, far_box, back, slope0, mult0, pull0, value0 = call(
        wide_body,
        (
            shape(4, wide, frame, LANES, dtype=BF16),
            shape(4, wide, frame, LANES, dtype=BF16),
            shape(wide, frame, LANES),
            shape(3, wide - 2, frame, LANES),
            shape(wide, frame, LANES),
            shape(3, wide, frame, LANES),
            small,
        ),
        [
            pltpu.VMEM((3, wide + 2, tall, LANES), F32),
            pltpu.VMEM((5, wide, frame, LANES), F32),
            pltpu.VMEM((wide, frame, LANES), F32),
            pltpu.VMEM((3, wide, frame, LANES), F32),
            pltpu.VMEM((4, wide + 3, tall, LANES), F32),
            pltpu.VMEM((4, 3, wide, tall, LANES), F32),
            pltpu.VMEM(FWD, BF16),
            pltpu.VMEM(BWD, BF16),
            dma((2,)),
        ],
        inputs + (left, right, above, below, fwd, bwd, bias, stat0),
        2 * flops,
        mem=30,
        far=(9, 10),
    )

    tile = shape(wide - 2, rows, LANES)
    base, slope1, mult1, duals1, last_mult, last_slope, last_pull, stat1 = call(
        functools.partial(second_body, cells=cells),
        (
            shape(3, wide, frame, LANES),
            shape(3, wide - 2, frame, LANES),
            shape(2, wide - 2, frame, LANES),
            shape(3, wide - 2, rows, LANES),
            tile,
            tile,
            tile,
            spread,
        ),
        [
            pltpu.VMEM((2, wide, frame, LANES), F32),
            pltpu.VMEM((3, wide + 1, frame, LANES), F32),
            pltpu.VMEM((3, 3, wide - 2, frame, LANES), F32),
            pltpu.VMEM(FWD, BF16),
            dma((1,)),
        ],
        (total0, steps, near_box, far_box, back, slope0, mult0, pull0, fwd, bias),
        flops,
        scalars=(1,),
        far=(8,),
    )
    total1 = everyone(stat1)
    gaps = pltpu.VMEM((3, rows, cols), BF16)
    pull1, value1 = call(
        pulled_body,
        (shape(3, wide - 2, frame, LANES), small),
        [
            pltpu.VMEM((3, wide - 1, frame, LANES), F32),
            pltpu.VMEM((3, 3, wide - 2, frame, LANES), F32),
            pltpu.VMEM(FWD, BF16),
            pltpu.VMEM((rows, cols), BF16),
            pltpu.VMEM((rows, cols), BF16),
            gaps,
            gaps,
            dma((5,)),
        ],
        (slope1, bwd, center, radius, lower, upper, base, duals1, last_mult, last_pull, bias),
        flops,
        far=(1, 2, 3, 4, 5),
    )
    out = shape(3, rows, cols)
    duals, multipliers, slope2, mult2, stat2 = call(
        functools.partial(third_body, cells=cells),
        (out, out, out, out, spread),
        [
            pltpu.VMEM((2, wide - 2, frame, LANES), F32),
            pltpu.VMEM((3, wide - 1, frame, LANES), F32),
            pltpu.VMEM((3, 3, wide - 4, frame, LANES), F32),
            pltpu.VMEM(FWD, BF16),
            gaps,
            gaps,
            dma((3,)),
        ],
        (
            total1, steps, near_box, base, pull1, mult1, slope1, duals1, last_mult, last_slope, last_pull,
            fwd, lower, upper, bias, value0, value1,
        ),
        flops,
        scalars=(1,),
        far=(11, 12, 13),
    )
    total2 = everyone(stat2)
    bounds, final_duals, final_multipliers = call(
        functools.partial(last_body, cells=cells),
        (small, out, out),
        [],
        (total2, steps, duals, multipliers, slope2, mult2),
        1 << 20,
        scalars=(1,),
    )
    return bounds[0, 1 : 1 + ITERS], final_duals, final_multipliers


def solution(mesh):
    placed = (
        P("row", "col"),
        P("row", "col"),
        P("row", "col"),
        P(None, "row", "col"),
        P(None, "row", "col"),
        P(),
        P(),
        P(),
    )
    return jax.shard_map(
        shards,
        mesh=mesh,
        in_specs=placed,
        out_specs=(P(), P(None, "row", "col"), P(None, "row", "col")),
        check_vma=False,
    )
```

```python
import functools
import math

import jax
import jax.numpy as jnp
from jax import lax
from jax.experimental import pallas as pl
from jax.experimental.pallas import tpu as pltpu
from jax.sharding import PartitionSpec as P

CH = 64
LAYERS = 4
ITERS = 3
EPS = 1e-06
LANES = 2 * CH
HALO_PAIRS = 3
WIDE = 5
EDGE = 4
F32 = jnp.float32
BF16 = jnp.bfloat16

ROWS_SENT = (5, 5, 5, 4, 4, 4, 4, 3, 3)
ROW_START = tuple(sum(ROWS_SENT[:m]) for m in range(9))
SENT = 40

VMEM = pl.BlockSpec(memory_space=pltpu.VMEM)
SMEM = pl.BlockSpec(memory_space=pltpu.SMEM)


def call(body, outs, scratch, operands, flops, mem=24, scalars=()):
    return pl.pallas_call(
        body,
        out_shape=outs,
        in_specs=[SMEM if j in scalars else VMEM for j in range(len(operands))],
        out_specs=jax.tree.map(lambda _: VMEM, outs),
        scratch_shapes=scratch,
        compiler_params=pltpu.CompilerParams(vmem_limit_bytes=mem << 20),
        cost_estimate=pl.CostEstimate(flops=flops, bytes_accessed=4 << 20, transcendentals=0),
    )(*operands)


def shape(*dims, dtype=F32):
    return jax.ShapeDtypeStruct(dims, dtype)


def split(value):
    high = value.astype(BF16)
    return high, (value - high.astype(F32)).astype(BF16)


def weights_body(kernels, biases, fwd_hi, fwd_lo, bwd_hi, bwd_lo, bias2):
    zero = jnp.zeros((CH, CH), F32)

    def put(hi, lo, k, j, dh, first, second):
        block = jnp.concatenate([first, second], axis=1)
        high, low = split(block)
        where = (k, pl.ds(CH * j, CH), pl.ds(LANES * dh, LANES))
        hi[where] = high
        lo[where] = low

    for k in range(LAYERS):
        for dh in range(3):
            taps = [kernels[k * 9 + dh * 3 + dw] for dw in range(3)]
            if k < LAYERS - 1:
                for j in range(4):
                    put(fwd_hi, fwd_lo, k, j, dh, taps[j] if j < 3 else zero, taps[j - 1] if j > 0 else zero)
            flips = [tap.T for tap in taps]
            for j in range(4):
                put(bwd_hi, bwd_lo, k, j, 2 - dh, flips[2 - j] if j < 3 else zero, flips[3 - j] if j > 0 else zero)
    for k in range(LAYERS):
        row = biases[k : k + 1, :]
        bias2[k : k + 1, :] = jnp.concatenate([row, row], axis=1)


def weights(kernels, biases):
    n = 4 * CH
    outs = (
        shape(LAYERS - 1, n, 3 * LANES, dtype=BF16),
        shape(LAYERS - 1, n, 3 * LANES, dtype=BF16),
        shape(LAYERS, n, 3 * LANES, dtype=BF16),
        shape(LAYERS, n, 3 * LANES, dtype=BF16),
        shape(8, LANES),
    )
    return call(weights_body, outs, [], (kernels.reshape(LAYERS * 9, CH, CH), biases), 1 << 22)


def sources(objective, center, radius, lower, upper):
    return [
        lambda cols: center[:, cols].astype(F32),
        lambda cols: upper[0, :, cols].astype(F32),
        lambda cols: upper[1, :, cols].astype(F32),
        lambda cols: upper[2, :, cols].astype(F32),
        lambda cols: lower[0, :, cols].astype(F32),
        lambda cols: lower[1, :, cols].astype(F32),
        lambda cols: lower[2, :, cols].astype(F32),
        lambda cols: radius[:, cols].astype(F32),
        lambda cols: objective[:, cols],
    ]


def sides_body(objective, center, radius, lower, upper, head, tail):
    rows, cols = objective.shape
    strip = HALO_PAIRS * LANES
    for m, read in enumerate(sources(objective, center, radius, lower, upper)):
        here = pl.ds(m * rows, rows)
        head[here, :] = read(pl.ds(0, strip))
        tail[here, :] = read(pl.ds(cols - strip, strip))


def column(reads, left, right, rows, pairs, m, q):
    if q < HALO_PAIRS:
        return left[m * rows : (m + 1) * rows, q * LANES : (q + 1) * LANES]
    if q >= HALO_PAIRS + pairs:
        q -= HALO_PAIRS + pairs
        return right[m * rows : (m + 1) * rows, q * LANES : (q + 1) * LANES]
    return reads[m](pl.ds((q - HALO_PAIRS) * LANES, LANES))


def ends_body(objective, center, radius, lower, upper, left, right, top, bottom):
    rows, cols = objective.shape
    pairs = cols // LANES
    reads = sources(objective, center, radius, lower, upper)
    for m in range(9):
        sent = ROWS_SENT[m]
        here = slice(ROW_START[m], ROW_START[m] + sent)
        for q in range(pairs + 2 * HALO_PAIRS):
            value = column(reads, left, right, rows, pairs, m, q)
            top[q, here, :] = value[:sent]
            bottom[q, here, :] = value[rows - sent :]
    spare = slice(sum(ROWS_SENT), SENT)
    top[:, spare, :] = jnp.zeros((pairs + 2 * HALO_PAIRS, SENT - sum(ROWS_SENT), LANES), F32)
    bottom[:, spare, :] = jnp.zeros((pairs + 2 * HALO_PAIRS, SENT - sum(ROWS_SENT), LANES), F32)


def neighbours(head, tail, axis):
    count = lax.axis_size(axis)
    before = lax.ppermute(tail, axis, [(i, i + 1) for i in range(count - 1)])
    after = lax.ppermute(head, axis, [(i + 1, i) for i in range(count - 1)])
    return before, after


def roll_rows(value, shift):
    return pltpu.roll(value, shift % value.shape[0], 0)


def slide(maps, count, store, produce):
    rows = store.shape[2]
    early = lax.broadcasted_iota(jnp.int32, (rows, LANES), 1) < CH
    zero = jnp.zeros((rows, LANES), F32)

    def step(q, carry):
        fresh = [pltpu.roll(value, CH, 1) for value in produce(q)]
        for k in range(maps):
            store[k, q] = jnp.where(early, carry[k], fresh[k])
        return tuple(fresh)

    last = lax.fori_loop(0, count, step, (zero,) * maps)
    for k in range(maps):
        store[k, count] = jnp.where(early, last[k], zero)


def multiply(store, k, first, count, hi, lo, layer, sums, exact=False):
    rows = store.shape[2]
    left = store[k, pl.ds(first, count)].reshape(count * rows, LANES)
    right = store[k, pl.ds(first + 1, count)].reshape(count * rows, LANES)
    window = jnp.concatenate([left, right], axis=1)
    dot = functools.partial(jnp.dot, preferred_element_type=F32)
    if exact:
        high = window.astype(BF16)
        result = dot(high, hi[layer]) + dot(high, lo[layer])
    else:
        high, low = split(window)
        result = dot(high, hi[layer]) + dot(high, lo[layer]) + dot(low, hi[layer])
    for d in range(3):
        sums[k, d, pl.ds(0, count)] = result[:, d * LANES : (d + 1) * LANES].reshape(count, rows, LANES)


def gathered(sums, k, q):
    return roll_rows(sums[k, 0, q], 1) + sums[k, 1, q] + roll_rows(sums[k, 2, q], -1)


def summed(total):
    return jnp.sum(total[...], axis=0, keepdims=True)


def scale_of(total, step, cells):
    squares = summed(total)[:, 0:1]
    return step / jnp.sqrt(squares / (2 * (LAYERS - 1) * cells) + EPS)


def soft(top, t):
    return 0.5 * top * (1.0 - jnp.tanh(t))


class Bound:
    def __init__(self, start):
        self.linear = start
        self.factor = None

    def add(self, t):
        self.linear = self.linear - jnp.maximum(-t, 0.0)
        factor = 1.0 + jnp.exp(-2.0 * jnp.abs(t))
        self.factor = factor if self.factor is None else self.factor * factor

    def total(self):
        return self.linear - 0.5 * jnp.log(self.factor)


def own_rows(value):
    rows = value.shape[0]
    row = lax.broadcasted_iota(jnp.int32, value.shape, 0)
    kept = jnp.where((row >= EDGE) & (row < rows - EDGE), value, 0.0)
    return jnp.sum(kept, axis=0, keepdims=True)


def stats(out, rows):
    lane = lax.broadcasted_iota(jnp.int32, (1, LANES), 1)
    packed = jnp.zeros((1, LANES), F32)
    for j, row in enumerate(rows):
        packed = jnp.where(lane == j, jnp.sum(row, axis=1, keepdims=True), packed)
    out[...] = jnp.broadcast_to(packed, out.shape)


def first_body(
    objective, center, radius, lower, upper, left, right, above, below,
    fwd_hi, fwd_lo, bwd_hi, bwd_lo, bias,
    box, back, slope, mult, stat, value,
    raw, target, store, sums,
):
    rows, cols = objective.shape
    pairs = cols // LANES
    frame = rows + 2 * EDGE
    wide = pairs + 4
    reads = sources(objective, center, radius, lower, upper)
    for m in range(9):
        sent = ROWS_SENT[m]
        here = slice(ROW_START[m], ROW_START[m] + sent)
        for q in range(pairs + 2 * HALO_PAIRS):
            if m >= 3 and not 1 <= q < wide + 1:
                continue
            own = column(reads, left, right, rows, pairs, m, q)
            if m < 3:
                dest, at, edge = raw.at[m, q], 0, WIDE
            else:
                dest, at, edge = (target.at[q - 1] if m == 8 else box.at[m, q - 1]), EDGE - sent, EDGE
                if at:
                    dest[0:EDGE, :] = jnp.zeros((EDGE, LANES), F32)
                    dest[EDGE + rows : frame, :] = jnp.zeros((EDGE, LANES), F32)
            dest[at : at + sent, :] = above[q, here, :]
            dest[edge : edge + rows, :] = own
            dest[edge + rows : edge + rows + sent, :] = below[q, here, :]
    raw[:, :, rows + 2 * WIDE :, :] = jnp.zeros((3, wide + 2, raw.shape[2] - rows - 2 * WIDE, LANES), F32)
    for m in range(3):
        for q in range(wide):
            box[m, q] = raw[m, q + 1, 1 : 1 + frame, :]

    tall = raw.shape[2]
    early = lax.broadcasted_iota(jnp.int32, (tall, LANES), 1) < CH

    def middle(q):
        return [raw[0, q], 0.5 * raw[1, q], 0.5 * raw[2, q]]

    slide(3, wide + 2, store, middle)
    for k in range(3):
        multiply(store, k, 1, wide, fwd_hi, fwd_lo, k, sums, exact=True)

    def slopes(q, carry):
        for k in range(3):
            conv = (
                sums[k, 0, q][:frame]
                + roll_rows(sums[k, 1, q], -1)[:frame]
                + roll_rows(sums[k, 2, q], -2)[:frame]
            )
            gap = box[1 + k, q]
            dl = 0.5 * (gap - box[4 + k, q]) - conv - bias[k : k + 1, :]
            slope[k, q] = jnp.where(gap > 0.0, dl, 0.0)
        return carry

    lax.fori_loop(0, wide, slopes, 0)

    early = lax.broadcasted_iota(jnp.int32, (frame, LANES), 1) < CH
    zero = jnp.zeros((frame, LANES), F32)

    def shift(q, carry):
        fresh = pltpu.roll(target[q], CH, 1)
        store[0, q, 0:frame, :] = jnp.where(early, carry, fresh)
        return fresh

    last = lax.fori_loop(0, wide, shift, zero)
    store[0, wide, 0:frame, :] = jnp.where(early, last, zero)
    lhs = jnp.concatenate(
        [
            store[0, 0:wide, 0:frame, :].reshape(wide * frame, LANES),
            store[0, 1 : wide + 1, 0:frame, :].reshape(wide * frame, LANES),
        ],
        axis=1,
    )
    high, low = split(lhs)
    dot = functools.partial(jnp.dot, preferred_element_type=F32)
    k = LAYERS - 1
    result = dot(high, bwd_hi[k]) + dot(high, bwd_lo[k]) + dot(low, bwd_hi[k])
    for d in range(3):
        sums[0, d, 0:wide, 0:frame, :] = result[:, d * LANES : (d + 1) * LANES].reshape(wide, frame, LANES)

    def pulls(q, carry):
        squares, worth, fixed = carry
        pull = (
            roll_rows(sums[0, 0, q][:frame], 1)
            + sums[0, 1, q][:frame]
            + roll_rows(sums[0, 2, q][:frame], -1)
        )
        back[q] = pull
        gap = box[3, q]
        t = pull * gap
        dm = -0.5 * gap * jnp.tanh(t)
        mult[q] = dm
        new = dm * dm
        for k in range(3):
            dl = slope[k, q]
            new = new + dl * dl
        bound = Bound(jnp.full((frame, LANES), -4.5 * math.log(2.0), F32))
        bound.add(t)
        own = (q >= 2) & (q < wide - 2)
        squares = squares + jnp.where(own, new, 0.0)
        worth = worth + jnp.where(own, bound.total(), 0.0)
        fixed = fixed + jnp.where(own, target[q] * bias[3:4, :], 0.0)
        return squares, worth, fixed

    squares, worth, fixed = lax.fori_loop(0, wide, pulls, (zero, zero, zero))
    fixed = own_rows(fixed)
    stats(stat, [own_rows(squares)])
    stats(value, [own_rows(worth) + fixed, fixed])


def second_pull_body(slope, bwd_hi, bwd_lo, back, store, sums):
    count = slope.shape[1]
    slide(3, count, store, lambda q: [slope[k, q] for k in range(3)])
    for k in range(3):
        multiply(store, k, 0, count, bwd_hi, bwd_lo, k, sums)

    def step(q, carry):
        for k in range(3):
            back[k, q] = gathered(sums, k, q)
        return carry

    lax.fori_loop(0, count, step, 0)


def second_body(
    total, steps, box, back, slope, mult, pull, fwd_hi, fwd_lo, bias,
    slope_out, mult_out, stat, value,
    points, store, sums, *, cells,
):
    wide = box.shape[1]
    frame = box.shape[2]
    scale = jnp.broadcast_to(scale_of(total, steps[0], cells), (frame, LANES))
    zero = jnp.zeros((frame, LANES), F32)

    def produce(q):
        radius = box[7, q]
        outs = [box[0, q] - radius * jnp.tanh(-2.0 * radius * (scale * pull[0, q]))]
        for k in (1, 2):
            gap = box[k, q]
            x = soft(gap, -(scale * pull[k, q]) * gap)
            points[k - 1, q] = x
            outs.append(x)
        return outs

    slide(3, wide, store, produce)
    for k in range(3):
        multiply(store, k, 1, wide - 2, fwd_hi, fwd_lo, k, sums)

    def step(j, carry):
        squares, worth = carry
        q = j + 1
        new = zero
        g = -(scale * pull[0, q])
        radius = box[7, q]
        bound = Bound(g * (box[0, q] - radius))
        bound.add(2.0 * g * radius)
        for k in range(3):
            gap = box[1 + k, q]
            low = box[4 + k, q]
            lam = scale * slope[k, q]
            if k < 2:
                x = points[k, q]
                bound.add(-(scale * pull[k + 1, q]) * gap)
                tp = lam * gap
            else:
                mu = scale * mult[q]
                t = (back[q] + mu) * gap
                x = soft(gap, t)
                bound.add(t)
                tp = (lam - mu) * gap
            tn = -lam * low
            bound.add(tp)
            bound.add(tn)
            bound.linear = bound.linear - lam * bias[k : k + 1, :]
            positive = soft(gap, tp)
            dl = positive - soft(low, tn) - gathered(sums, k, j) - bias[k : k + 1, :]
            dl = jnp.where(gap > 0.0, dl, 0.0)
            dm = x - positive
            slope_out[k, j] = dl
            mult_out[k, j] = dm
            new = new + dl * dl + dm * dm
        own = (q >= 2) & (q < wide - 2)
        return squares + jnp.where(own, new, 0.0), worth + jnp.where(own, bound.total(), 0.0)

    squares, worth = lax.fori_loop(0, wide - 2, step, (zero, zero))
    stats(stat, [own_rows(squares)])
    stats(value, [own_rows(worth)])


def third_body(
    total0, total1, steps, box, back, slope0, mult0, pull0, slope1, mult1, pull1, fwd_hi, fwd_lo, bias,
    value0, value1,
    duals, multipliers, slope_out, mult_out, stat,
    points, store, sums, *, cells,
):
    wide = box.shape[1]
    frame = box.shape[2]
    rows = frame - 2 * EDGE
    s0 = jnp.broadcast_to(scale_of(total0, steps[0], cells), (frame, LANES))
    s1 = jnp.broadcast_to(scale_of(total1, steps[1], cells), (frame, LANES))
    zero = jnp.zeros((frame, LANES), F32)

    def pull_of(k, j):
        g = -(s0 * pull0[k, j + 1] + s1 * pull1[k, j])
        return g if k == 0 else g + s1 * mult1[k - 1, j]

    def produce(j):
        q = j + 1
        radius = box[7, q]
        outs = [box[0, q] - radius * jnp.tanh(2.0 * radius * pull_of(0, j))]
        for k in (1, 2):
            gap = box[k, q]
            x = soft(gap, pull_of(k, j) * gap)
            points[k - 1, j] = x
            outs.append(x)
        return outs

    slide(3, wide - 2, store, produce)
    for k in range(3):
        multiply(store, k, 1, wide - 4, fwd_hi, fwd_lo, k, sums)

    def step(i, carry):
        squares, worth = carry
        j = i + 1
        q = i + 2
        new = zero
        g = pull_of(0, j)
        radius = box[7, q]
        bound = Bound(g * (box[0, q] - radius))
        bound.add(2.0 * g * radius)
        here = pl.ds(pl.multiple_of(i * LANES, LANES), LANES)
        for k in range(3):
            gap = box[1 + k, q]
            low = box[4 + k, q]
            lam = s0 * slope0[k, q] + s1 * slope1[k, j]
            mu = s1 * mult1[k, j]
            if k < 2:
                x = points[k, j]
                bound.add(pull_of(k + 1, j) * gap)
            else:
                mu = mu + s0 * mult0[q]
                t = (back[q] + mu) * gap
                x = soft(gap, t)
                bound.add(t)
            tp = (lam - mu) * gap
            tn = -lam * low
            bound.add(tp)
            bound.add(tn)
            bound.linear = bound.linear - lam * bias[k : k + 1, :]
            positive = soft(gap, tp)
            dl = positive - soft(low, tn) - gathered(sums, k, i) - bias[k : k + 1, :]
            dm = x - positive
            duals[k, :, here] = lam[EDGE : EDGE + rows]
            multipliers[k, :, here] = mu[EDGE : EDGE + rows]
            slope_out[k, :, here] = dl[EDGE : EDGE + rows]
            mult_out[k, :, here] = dm[EDGE : EDGE + rows]
            new = new + dl * dl + dm * dm
        return squares + new, worth + bound.total()

    squares, worth = lax.fori_loop(0, wide - 4, step, (zero, zero))
    lane = lax.broadcasted_iota(jnp.int32, (1, LANES), 1)
    first, fixed = (jnp.where(lane == j, value0[0:1, :], 0.0) for j in range(2))
    second = jnp.where(lane == 0, value1[0:1, :], 0.0)
    stats(stat, [own_rows(squares), first, second + fixed, own_rows(worth) + fixed])


def last_body(total, steps, duals, multipliers, slope, mult, bounds, duals_out, mult_out, *, cells):
    scale = jnp.broadcast_to(scale_of(total, steps[2], cells), (duals.shape[1], duals.shape[2]))
    for k in range(LAYERS - 1):
        duals_out[k] = duals[k] + scale * slope[k]
        mult_out[k] = multipliers[k] + scale * mult[k]
    bounds[...] = jnp.broadcast_to(summed(total) / cells, bounds.shape)


def everyone(partial):
    return lax.all_gather(partial, ("row", "col"), axis=0, tiled=True)


def shards(objective, center, radius, lower, upper, kernels, biases, steps):
    rows, cols = objective.shape
    pairs = cols // LANES
    wide = pairs + 4
    frame = rows + 2 * EDGE
    tall = -(-(rows + 2 * WIDE) // 8) * 8
    cells = rows * cols * lax.axis_size("row") * lax.axis_size("col")
    inputs = (objective, center, radius, lower, upper)
    flops = 3 * 2 * 3 * wide * frame * 4 * CH * 3 * LANES

    strip = shape(9 * rows, HALO_PAIRS * LANES)
    head, tail = call(sides_body, (strip, strip), [], inputs, 1 << 20)
    left, right = neighbours(head, tail, "col")
    fwd_hi, fwd_lo, bwd_hi, bwd_lo, bias = weights(kernels, biases)
    strip = shape(pairs + 2 * HALO_PAIRS, SENT, LANES)
    top, bottom = call(ends_body, (strip, strip), [], inputs + (left, right), 1 << 20)
    above, below = neighbours(top, bottom, "row")

    stat_shape = shape(8, LANES)
    spread = shape(1, LANES)
    box, back, slope0, mult0, stat0, value0 = call(
        first_body,
        (
            shape(8, wide, frame, LANES),
            shape(wide, frame, LANES),
            shape(3, wide, frame, LANES),
            shape(wide, frame, LANES),
            spread,
            stat_shape,
        ),
        [
            pltpu.VMEM((3, wide + 2, tall, LANES), F32),
            pltpu.VMEM((wide, frame, LANES), F32),
            pltpu.VMEM((3, wide + 3, tall, LANES), F32),
            pltpu.VMEM((3, 3, wide, tall, LANES), F32),
        ],
        inputs + (left, right, above, below, fwd_hi, fwd_lo, bwd_hi, bwd_lo, bias),
        2 * flops,
    )

    def pulled(slope):
        count = slope.shape[1]
        return call(
            second_pull_body,
            shape(3, count, frame, LANES),
            [
                pltpu.VMEM((3, count + 1, frame, LANES), F32),
                pltpu.VMEM((3, 3, count, frame, LANES), F32),
            ],
            (slope, bwd_hi, bwd_lo),
            flops,
        )

    total0 = everyone(stat0)
    pull0 = pulled(slope0)
    slope1, mult1, stat1, value1 = call(
        functools.partial(second_body, cells=cells),
        (shape(3, wide - 2, frame, LANES), shape(3, wide - 2, frame, LANES), spread, stat_shape),
        [
            pltpu.VMEM((2, wide, frame, LANES), F32),
            pltpu.VMEM((3, wide + 1, frame, LANES), F32),
            pltpu.VMEM((3, 3, wide - 2, frame, LANES), F32),
        ],
        (total0, steps, box, back, slope0, mult0, pull0, fwd_hi, fwd_lo, bias),
        flops,
        scalars=(1,),
    )
    total1 = everyone(stat1)
    pull1 = pulled(slope1)
    out = shape(3, rows, cols)
    duals, multipliers, slope2, mult2, stat2 = call(
        functools.partial(third_body, cells=cells),
        (out, out, out, out, spread),
        [
            pltpu.VMEM((2, wide - 2, frame, LANES), F32),
            pltpu.VMEM((3, wide - 1, frame, LANES), F32),
            pltpu.VMEM((3, 3, wide - 4, frame, LANES), F32),
        ],
        (
            total0, total1, steps, box, back, slope0, mult0, pull0, slope1, mult1, pull1,
            fwd_hi, fwd_lo, bias, value0, value1,
        ),
        flops,
        scalars=(2,),
    )
    total2 = everyone(stat2)
    bounds, final_duals, final_multipliers = call(
        functools.partial(last_body, cells=cells),
        (stat_shape, out, out),
        [],
        (total2, steps, duals, multipliers, slope2, mult2),
        1 << 20,
        scalars=(1,),
    )
    return bounds[0, 1 : 1 + ITERS], final_duals, final_multipliers


def solution(mesh):
    placed = (
        P("row", "col"),
        P("row", "col"),
        P("row", "col"),
        P(None, "row", "col"),
        P(None, "row", "col"),
        P(),
        P(),
        P(),
    )
    return jax.shard_map(
        shards,
        mesh=mesh,
        in_specs=placed,
        out_specs=(P(), P(None, "row", "col"), P(None, "row", "col")),
        check_vma=False,
    )
```

```python
import functools
import math

import jax
import jax.numpy as jnp
from jax import lax
from jax.experimental import pallas as pl
from jax.experimental.pallas import tpu as pltpu
from jax.sharding import PartitionSpec as P

CH = 64
LAYERS = 4
ITERS = 3
EPS = 1e-06
LANES = 2 * CH
HALO_PAIRS = 3
WIDE = 5
EDGE = 4
F32 = jnp.float32
BF16 = jnp.bfloat16

ROWS_SENT = (5, 5, 5, 4, 4, 4, 4, 3, 3)
ROW_START = tuple(sum(ROWS_SENT[:m]) for m in range(9))
SENT = 40
WINDOW = 4 * CH

VMEM = pl.BlockSpec(memory_space=pltpu.VMEM)
SMEM = pl.BlockSpec(memory_space=pltpu.SMEM)
HBM = pl.BlockSpec(memory_space=pltpu.HBM)


def call(body, outs, scratch, operands, flops, mem=20, scalars=(), far=(), scalar_outs=()):
    specs = [SMEM if j in scalars else HBM if j in far else VMEM for j in range(len(operands))]
    out_specs = tuple(SMEM if j in scalar_outs else VMEM for j in range(len(outs)))
    return pl.pallas_call(
        body,
        out_shape=outs,
        in_specs=specs,
        out_specs=out_specs,
        scratch_shapes=scratch,
        compiler_params=pltpu.CompilerParams(vmem_limit_bytes=mem << 20),
        cost_estimate=pl.CostEstimate(flops=flops, bytes_accessed=4 << 20, transcendentals=0),
    )(*operands)


def shape(*dims, dtype=F32):
    return jax.ShapeDtypeStruct(dims, dtype)


def copies(pairs, sem):
    made = [pltpu.make_async_copy(src, dst, sem.at[j]) for j, (src, dst) in enumerate(pairs)]
    for one in made:
        one.start()
    return made


def finish(made):
    for one in made:
        one.wait()


def split(value):
    high = value.astype(BF16)
    return high, (value - high.astype(F32)).astype(BF16)


def weights_body(kernels, biases, fwd, bwd, bias2):
    zero = jnp.zeros((CH, CH), F32)

    def put(dest, k, j, dh, first, second):
        high, low = split(jnp.concatenate([first, second], axis=1))
        for part, value in enumerate((low, high, high)):
            dest[k, pl.ds(WINDOW * part + CH * j, CH), pl.ds(LANES * dh, LANES)] = value

    for k in range(LAYERS):
        for dh in range(3):
            taps = [kernels[k * 9 + dh * 3 + dw] for dw in range(3)]
            if k < LAYERS - 1:
                for j in range(4):
                    put(fwd, k, j, dh, taps[j] if j < 3 else zero, taps[j - 1] if j > 0 else zero)
            flips = [tap.T for tap in taps]
            for j in range(4):
                put(bwd, k, j, 2 - dh, flips[2 - j] if j < 3 else zero, flips[3 - j] if j > 0 else zero)
    for k in range(LAYERS):
        row = biases[k : k + 1, :]
        bias2[k : k + 1, :] = jnp.concatenate([row, row], axis=1)


def weights(kernels, biases):
    size = (3 * WINDOW, 3 * LANES)
    return call(
        weights_body,
        (shape(LAYERS - 1, *size, dtype=BF16), shape(LAYERS, *size, dtype=BF16), shape(8, LANES)),
        [],
        (kernels.reshape(LAYERS * 9, CH, CH), biases),
        1 << 22,
    )


def sources(objective, center, radius, lower, upper):
    return [
        lambda cols: center[:, cols].astype(F32),
        lambda cols: upper[0, :, cols].astype(F32),
        lambda cols: upper[1, :, cols].astype(F32),
        lambda cols: upper[2, :, cols].astype(F32),
        lambda cols: lower[0, :, cols].astype(F32),
        lambda cols: lower[1, :, cols].astype(F32),
        lambda cols: lower[2, :, cols].astype(F32),
        lambda cols: radius[:, cols].astype(F32),
        lambda cols: objective[:, cols],
    ]


def sides_body(
    objective, center, radius, lower, upper, head, tail, top, bottom, *rest
):
    rows, cols = objective.shape
    pairs = cols // LANES
    strip = HALO_PAIRS * LANES
    held, sem = rest[:5], rest[5]
    finish(copies(list(zip((objective, center, radius, lower, upper), held)), sem))
    for m, read in enumerate(sources(*held)):
        head[pl.ds(m * rows, rows), :] = read(pl.ds(0, strip))
        tail[pl.ds(m * rows, rows), :] = read(pl.ds(cols - strip, strip))
    for q in range(pairs):
        ends_of([read(pl.ds(q * LANES, LANES)) for read in sources(*held)], top.at[q], bottom.at[q])


def ends_of(values, top, bottom):
    for m, value in enumerate(values):
        here = slice(ROW_START[m], ROW_START[m] + ROWS_SENT[m])
        top[here, :] = value[: ROWS_SENT[m]]
        bottom[here, :] = value[value.shape[0] - ROWS_SENT[m] :]
    spare = slice(sum(ROWS_SENT), SENT)
    blank = jnp.zeros((SENT - sum(ROWS_SENT), LANES), F32)
    top[spare, :] = blank
    bottom[spare, :] = blank


def corners_body(left, right, top, bottom):
    rows = left.shape[0] // 9
    for side, strip in enumerate((left, right)):
        for q in range(HALO_PAIRS):
            values = [strip[pl.ds(m * rows, rows), pl.ds(q * LANES, LANES)] for m in range(9)]
            at = side * HALO_PAIRS + q
            ends_of(values, top.at[at], bottom.at[at])


def column(reads, left, right, rows, pairs, m, q):
    if q < HALO_PAIRS:
        return left[m * rows : (m + 1) * rows, q * LANES : (q + 1) * LANES]
    if q >= HALO_PAIRS + pairs:
        q -= HALO_PAIRS + pairs
        return right[m * rows : (m + 1) * rows, q * LANES : (q + 1) * LANES]
    return reads[m](pl.ds((q - HALO_PAIRS) * LANES, LANES))


def halo(middle, corner, pairs, q, here):
    if q < HALO_PAIRS:
        return corner[q, here, :]
    if q >= HALO_PAIRS + pairs:
        return corner[q - pairs, here, :]
    return middle[q - HALO_PAIRS, here, :]


def neighbours(head, tail, axis):
    count = lax.axis_size(axis)
    before = lax.ppermute(tail, axis, [(i, i + 1) for i in range(count - 1)])
    after = lax.ppermute(head, axis, [(i + 1, i) for i in range(count - 1)])
    return before, after


def roll_rows(value, shift):
    return pltpu.roll(value, shift % value.shape[0], 0)


def slide(maps, count, store, produce):
    rows = store.shape[2]
    early = lax.broadcasted_iota(jnp.int32, (rows, LANES), 1) < CH
    zero = jnp.zeros((rows, LANES), F32)

    def step(q, carry):
        fresh = [pltpu.roll(value, CH, 1) for value in produce(q)]
        for k in range(maps):
            store[k, q] = jnp.where(early, carry[k], fresh[k])
        return tuple(fresh)

    last = lax.fori_loop(0, count, step, (zero,) * maps, unroll=2)
    for k in range(maps):
        store[k, count] = jnp.where(early, last[k], zero)


def multiply(store, k, first, count, weight, layer, sums, exact=False):
    rows = store.shape[2]
    left = store[k, pl.ds(first, count)].reshape(count * rows, LANES)
    right = store[k, pl.ds(first + 1, count)].reshape(count * rows, LANES)
    high, low = split(jnp.concatenate([left, right], axis=1))
    terms = [high, high] if exact else [high, high, low]
    result = jnp.dot(
        jnp.concatenate(terms, axis=1),
        weight[layer, 0 : WINDOW * len(terms), :],
        preferred_element_type=F32,
    )
    for d in range(3):
        sums[k, d, pl.ds(0, count)] = result[:, d * LANES : (d + 1) * LANES].reshape(count, rows, LANES)


def gathered(sums, k, q):
    return roll_rows(sums[k, 0, q], 1) + sums[k, 1, q] + roll_rows(sums[k, 2, q], -1)


def inner(sums, k, q, first, rows):
    parts = [roll_rows(sums[k, d, q], 1 - d - first)[:rows] for d in range(3)]
    return parts[0] + parts[1] + parts[2]


def summed(total):
    return jnp.sum(total[...], axis=0, keepdims=True)


def scale_of(total, step, cells, dims):
    squares = summed(total)[:, 0:1]
    return jnp.broadcast_to(step / jnp.sqrt(squares / (2 * (LAYERS - 1) * cells) + EPS), dims)


def soft(top, t):
    return 0.5 * top * (1.0 - jnp.tanh(t))


class Bound:
    def __init__(self, start):
        self.linear = start
        self.factor = None

    def add(self, t):
        self.linear = self.linear - jnp.maximum(-t, 0.0)
        factor = 1.0 + jnp.exp(-2.0 * jnp.abs(t))
        self.factor = factor if self.factor is None else self.factor * factor

    def total(self):
        return self.linear - 0.5 * jnp.log(self.factor)


def folded(value):
    return jnp.sum(value, axis=0, keepdims=True)


def own_rows(value):
    rows = value.shape[0]
    row = lax.broadcasted_iota(jnp.int32, value.shape, 0)
    return folded(jnp.where((row >= EDGE) & (row < rows - EDGE), value, 0.0))


def stats(out, rows):
    lane = lax.broadcasted_iota(jnp.int32, (1, LANES), 1)
    packed = jnp.zeros((1, LANES), F32)
    for j, row in enumerate(rows):
        packed = jnp.where(lane == j, jnp.sum(row, axis=1, keepdims=True), packed)
    out[...] = jnp.broadcast_to(packed, out.shape)


def first_body(
    objective, center, radius, lower, upper, left, right, above, below, above_corner, below_corner, fwd, bwd, bias,
    near_box, far_box, back, slope, mult, stat, value,
    raw, gaps, target, store, sums,
):
    rows, cols = objective.shape
    pairs = cols // LANES
    frame = rows + 2 * EDGE
    wide = pairs + 4
    reads = sources(objective, center, radius, lower, upper)
    for m in range(9):
        sent = ROWS_SENT[m]
        here = slice(ROW_START[m], ROW_START[m] + sent)
        for q in range(pairs + 2 * HALO_PAIRS):
            if m >= 3 and not 1 <= q < wide + 1:
                continue
            own = column(reads, left, right, rows, pairs, m, q)
            if m < 3:
                dest, at, edge = raw.at[m, q], 0, WIDE
            else:
                dest, at, edge = (target.at[q - 1] if m == 8 else gaps.at[m - 3, q - 1]), EDGE - sent, EDGE
                if at:
                    dest[0:EDGE, :] = jnp.zeros((EDGE, LANES), F32)
                    dest[EDGE + rows : frame, :] = jnp.zeros((EDGE, LANES), F32)
            dest[at : at + sent, :] = halo(above, above_corner, pairs, q, here)
            dest[edge : edge + rows, :] = own
            dest[edge + rows : edge + rows + sent, :] = halo(below, below_corner, pairs, q, here)
    raw[:, :, rows + 2 * WIDE :, :] = jnp.zeros((3, wide + 2, raw.shape[2] - rows - 2 * WIDE, LANES), F32)

    slide(3, wide + 2, store, lambda q: [raw[0, q], 0.5 * raw[1, q], 0.5 * raw[2, q]])
    tugged = store.at[3:4, :, 0:frame, :]
    slide(1, wide, tugged, lambda q: [target[q]])
    for k in range(3):
        multiply(store, k, 1, wide, fwd, k, sums, exact=True)
    short = sums.at[3:4, :, :, 0:frame, :]
    multiply(tugged, 0, 0, wide, bwd, LAYERS - 1, short)
    zero = jnp.zeros((frame, LANES), F32)

    def step(q, carry):
        squares, worth, fixed = carry
        near = [raw[m, q + 1][1 : 1 + frame] for m in range(3)] + [gaps[4, q]]
        far = [gaps[m, q] for m in range(4)]
        for m in range(4):
            near_box[m, q] = near[m].astype(BF16)
            far_box[m, q] = far[m].astype(BF16)
        new = zero
        for k in range(3):
            gap = near[1 + k] if k < 2 else far[0]
            dl = 0.5 * (gap - far[1 + k]) - inner(sums, k, q, 1, frame) - bias[k : k + 1, :]
            dl = jnp.where(gap > 0.0, dl, 0.0)
            slope[k, q] = dl
            new = new + dl * dl
        tug = gathered(short, 0, q)
        back[q] = tug
        t = tug * gap
        dm = -0.5 * gap * jnp.tanh(t)
        mult[q] = dm
        new = new + dm * dm
        bound = Bound(jnp.full((frame, LANES), -4.5 * math.log(2.0), F32))
        bound.add(t)
        own = (q >= 2) & (q < wide - 2)
        squares = squares + jnp.where(own, new, 0.0)
        worth = worth + jnp.where(own, bound.total(), 0.0)
        fixed = fixed + jnp.where(own, target[q] * bias[3:4, :], 0.0)
        return squares, worth, fixed

    squares, worth, fixed = lax.fori_loop(0, wide, step, (zero, zero, zero), unroll=2)
    fixed = own_rows(fixed)
    stats(stat, [own_rows(squares)])
    stats(value, [own_rows(worth) + fixed, fixed])


def second_body(
    total, steps, near_box, far_box, back, slope, mult, fwd, bwd, bias,
    base, slope_out, mult_out, duals, last_mult, last_slope, last_pull, stat, value,
    points, store, sums, *, cells,
):
    wide, frame = near_box.shape[1:3]
    inside = slice(EDGE, frame - EDGE)
    scale = scale_of(total, steps[0], cells, (frame, LANES))
    zero = jnp.zeros((frame, LANES), F32)
    slide(3, wide, store, lambda q: [slope[k, q] for k in range(3)])
    for k in range(3):
        multiply(store, k, 0, wide, bwd, k, sums)

    def produce(q):
        center, radius = near_box[0, q].astype(F32), near_box[3, q].astype(F32)
        g = -(scale * gathered(sums, 0, q))
        base[0, q] = g
        outs = [center - radius * jnp.tanh(2.0 * radius * g)]
        for k in (1, 2):
            gap = near_box[k, q].astype(F32)
            g = -(scale * gathered(sums, k, q))
            base[k, q] = g
            x = soft(gap, g * gap)
            points[k - 1, q] = x
            outs.append(x)
        return outs

    slide(3, wide, store, produce)
    for k in range(3):
        multiply(store, k, 1, wide - 2, fwd, k, sums)

    def step(j, carry):
        squares, worth = carry
        q = j + 1
        new = zero
        center, radius = near_box[0, q].astype(F32), near_box[3, q].astype(F32)
        g = base[0, q]
        bound = Bound(g * (center - radius))
        bound.add(2.0 * g * radius)
        for k in range(3):
            gap = (near_box[1 + k, q] if k < 2 else far_box[0, q]).astype(F32)
            low = far_box[1 + k, q].astype(F32)
            lam = scale * slope[k, q]
            if k < 2:
                bound.add(base[k + 1, q] * gap)
                x = points[k, q]
                tp = lam * gap
            else:
                mu = scale * mult[q]
                g = back[q] + mu
                t = g * gap
                bound.add(t)
                x = soft(gap, t)
                tp = (lam - mu) * gap
            tn = -lam * low
            bound.add(tp)
            bound.add(tn)
            bound.linear = bound.linear - lam * bias[k : k + 1, :]
            positive = soft(gap, tp)
            dl = positive - soft(low, tn) - gathered(sums, k, j) - bias[k : k + 1, :]
            dl = jnp.where(gap > 0.0, dl, 0.0)
            dm = x - positive
            slope_out[k, j] = dl
            duals[k, j] = lam[inside]
            if k < 2:
                mult_out[k, j] = dm
            else:
                last_mult[j] = mu[inside]
                last_slope[j] = dm[inside]
                last_pull[j] = g[inside]
            new = new + dl * dl + dm * dm
        own = (q >= 2) & (q < wide - 2)
        return squares + jnp.where(own, new, 0.0), worth + jnp.where(own, bound.total(), 0.0)

    squares, worth = lax.fori_loop(0, wide - 2, step, (zero, zero))
    stats(stat, [own_rows(squares)])
    stats(value, [own_rows(worth)])


def third_body(
    total, steps, near_box, base, mult, slope, duals1, last_mult, last_slope, last_pull,
    fwd, bwd, lower, upper, bias, value0, value1,
    duals, multipliers, slope_out, mult_out, stat,
    points, store, sums, *, cells,
):
    wide, frame = near_box.shape[1:3]
    rows = frame - 2 * EDGE
    inside = slice(EDGE, frame - EDGE)
    scale = scale_of(total, steps[1], cells, (frame, LANES))
    zero = jnp.zeros((frame, LANES), F32)
    slide(3, wide - 2, store, lambda j: [slope[k, j] for k in range(3)])
    for k in range(3):
        multiply(store, k, 0, wide - 2, bwd, k, sums)
    early = lax.broadcasted_iota(jnp.int32, (frame, LANES), 1) < CH

    def point(j, carry):
        q = j + 1
        center, radius = near_box[0, q].astype(F32), near_box[3, q].astype(F32)
        g = base[0, q] - scale * gathered(sums, 0, j)
        bound = Bound(g * (center - radius))
        t = 2.0 * radius * g
        bound.add(t)
        outs = [center - radius * jnp.tanh(t)]
        for k in (1, 2):
            gap = near_box[k, q].astype(F32)
            t = (base[k, q] + scale * (mult[k - 1, j] - gathered(sums, k, j))) * gap
            bound.add(t)
            x = soft(gap, t)
            points[k - 1, j] = x
            outs.append(x)
        own = (q >= 2) & (q < wide - 2)
        fresh = [pltpu.roll(value, CH, 1) for value in outs]
        for k in range(3):
            store[k, j] = jnp.where(early, carry[k], fresh[k])
        return tuple(fresh) + (carry[3] + jnp.where(own, bound.total(), 0.0),)

    framed = lax.fori_loop(0, wide - 2, point, (zero,) * 4)[3]
    for k in range(3):
        multiply(store, k, 1, wide - 4, fwd, k, sums)

    scale = scale[:rows]

    def step(i, carry):
        squares, worth = carry
        j = i + 1
        here = pl.ds(pl.multiple_of(i * LANES, LANES), LANES)
        bound = Bound(jnp.zeros((rows, LANES), F32))
        for k in range(3):
            gap = upper[k, :, here].astype(F32)
            low = lower[k, :, here].astype(F32)
            lam = duals1[k, j] + scale * slope[k, j, inside, :]
            bound.linear = bound.linear - lam * bias[k : k + 1, :]
            if k < 2:
                x = points[k, j, inside, :]
                mu = scale * mult[k, j, inside, :]
            else:
                change = scale * last_slope[j]
                mu = last_mult[j] + change
                t = (last_pull[j] + change) * gap
                x = soft(gap, t)
                bound.add(t)
            tp = (lam - mu) * gap
            tn = -lam * low
            bound.add(tp)
            bound.add(tn)
            positive = soft(gap, tp)
            dl = positive - soft(low, tn) - inner(sums, k, i, EDGE, rows) - bias[k : k + 1, :]
            dm = x - positive
            duals[k, :, here] = lam
            multipliers[k, :, here] = mu
            slope_out[k, :, here] = dl
            mult_out[k, :, here] = dm
            squares = squares + dl * dl + dm * dm
        return squares, worth + bound.total()

    zero = jnp.zeros((rows, LANES), F32)
    squares, worth = lax.fori_loop(0, wide - 4, step, (zero, zero), unroll=2)
    lane = lax.broadcasted_iota(jnp.int32, (1, LANES), 1)
    start, fixed = (jnp.where(lane == j, value0[0:1, :], 0.0) for j in range(2))
    middle = jnp.where(lane == 0, value1[0:1, :], 0.0)
    stats(stat, [folded(squares), start, middle + fixed, folded(worth) + own_rows(framed) + fixed])


def last_body(total, steps, duals, multipliers, slope, mult, duals_out, mult_out, bounds, *, cells):
    scale = scale_of(total, steps[2], cells, duals.shape[1:])
    for k in range(LAYERS - 1):
        duals_out[k] = duals[k] + scale * slope[k]
        mult_out[k] = multipliers[k] + scale * mult[k]
    values = summed(total) / cells
    lane = lax.broadcasted_iota(jnp.int32, (1, LANES), 1)
    for j in range(ITERS):
        bounds[j] = jnp.sum(jnp.where(lane == j + 1, values, 0.0))


def everyone(partial):
    return lax.all_to_all(partial, ("row", "col"), 0, 0, tiled=True)


def shards(objective, center, radius, lower, upper, kernels, biases, steps):
    rows, cols = objective.shape
    pairs = cols // LANES
    wide = pairs + 4
    frame = rows + 2 * EDGE
    tall = -(-(rows + 2 * WIDE) // 8) * 8
    cells = rows * cols * lax.axis_size("row") * lax.axis_size("col")
    inputs = (objective, center, radius, lower, upper)
    flops = 3 * 2 * 3 * wide * frame * 4 * CH * 3 * LANES
    spread = shape(lax.axis_size("row") * lax.axis_size("col"), LANES)
    small = shape(8, LANES)

    strip = shape(9 * rows, HALO_PAIRS * LANES)
    ends = shape(pairs, SENT, LANES)
    head, tail, top, bottom = call(
        sides_body,
        (strip, strip, ends, ends),
        [pltpu.VMEM(one.shape, one.dtype) for one in inputs] + [pltpu.SemaphoreType.DMA((5,))],
        inputs,
        1 << 20,
        mem=58,
        far=range(5),
    )
    left, right = neighbours(head, tail, "col")
    above, below = neighbours(top, bottom, "row")
    fwd, bwd, bias = weights(kernels, biases)
    corner = shape(2 * HALO_PAIRS, SENT, LANES)
    corner_top, corner_bottom = call(corners_body, (corner, corner), [], (left, right), 1 << 20)
    above_corner, below_corner = neighbours(corner_top, corner_bottom, "row")

    box = shape(4, wide, frame, LANES, dtype=BF16)
    full = shape(wide, frame, LANES)
    near_box, far_box, back, slope0, mult0, stat0, value0 = call(
        first_body,
        (box, box, full, shape(3, wide, frame, LANES), full, spread, small),
        [
            pltpu.VMEM((3, wide + 2, tall, LANES), F32),
            pltpu.VMEM((5, wide, frame, LANES), F32),
            pltpu.VMEM((wide, frame, LANES), F32),
            pltpu.VMEM((4, wide + 3, tall, LANES), F32),
            pltpu.VMEM((4, 3, wide, tall, LANES), F32),
        ],
        inputs + (left, right, above, below, above_corner, below_corner, fwd, bwd, bias),
        2 * flops,
    )

    total0 = everyone(stat0)
    tile = shape(wide - 2, rows, LANES)
    base, slope1, mult1, duals1, last_mult, last_slope, last_pull, stat1, value1 = call(
        functools.partial(second_body, cells=cells),
        (
            shape(3, wide, frame, LANES),
            shape(3, wide - 2, frame, LANES),
            shape(2, wide - 2, frame, LANES),
            shape(3, wide - 2, rows, LANES),
            tile,
            tile,
            tile,
            spread,
            small,
        ),
        [
            pltpu.VMEM((2, wide, frame, LANES), F32),
            pltpu.VMEM((3, wide + 1, frame, LANES), F32),
            pltpu.VMEM((3, 3, wide, frame, LANES), F32),
        ],
        (total0, steps, near_box, far_box, back, slope0, mult0, fwd, bwd, bias),
        2 * flops,
        scalars=(1,),
    )
    total1 = everyone(stat1)
    out = shape(3, rows, cols)
    duals, multipliers, slope2, mult2, stat2 = call(
        functools.partial(third_body, cells=cells),
        (out, out, out, out, spread),
        [
            pltpu.VMEM((2, wide - 2, frame, LANES), F32),
            pltpu.VMEM((3, wide - 1, frame, LANES), F32),
            pltpu.VMEM((3, 3, wide - 2, frame, LANES), F32),
        ],
        (
            total1, steps, near_box, base, mult1, slope1, duals1, last_mult, last_slope, last_pull,
            fwd, bwd, lower, upper, bias, value0, value1,
        ),
        2 * flops,
        scalars=(1,),
    )
    total2 = everyone(stat2)
    final_duals, final_multipliers, bounds = call(
        functools.partial(last_body, cells=cells),
        (out, out, shape(ITERS)),
        [],
        (total2, steps, duals, multipliers, slope2, mult2),
        1 << 20,
        scalar_outs=(2,),
        scalars=(1,),
    )
    return bounds, final_duals, final_multipliers


def solution(mesh):
    placed = (
        P("row", "col"),
        P("row", "col"),
        P("row", "col"),
        P(None, "row", "col"),
        P(None, "row", "col"),
        P(),
        P(),
        P(),
    )
    return jax.shard_map(
        shards,
        mesh=mesh,
        in_specs=placed,
        out_specs=(P(), P(None, "row", "col"), P(None, "row", "col")),
        check_vma=False,
    )
```

```python
import functools
import math

import jax
import jax.numpy as jnp
from jax import lax
from jax.experimental import pallas as pl
from jax.experimental.pallas import tpu as pltpu
from jax.sharding import PartitionSpec as P

CH = 64
LAYERS = 4
ITERS = 3
EPS = 1e-06
LANES = 2 * CH
HALO_PAIRS = 3
WIDE = 5
EDGE = 4
F32 = jnp.float32
BF16 = jnp.bfloat16

ROWS_SENT = (5, 5, 5, 4, 4, 4, 2, 3, 3)
ROW_START = tuple(sum(ROWS_SENT[:m]) for m in range(9))
SENT = sum(ROWS_SENT)
WINDOW = 4 * CH

VMEM = pl.BlockSpec(memory_space=pltpu.VMEM)
SMEM = pl.BlockSpec(memory_space=pltpu.SMEM)
HBM = pl.BlockSpec(memory_space=pltpu.HBM)


def call(body, outs, scratch, operands, flops, mem=20, scalars=(), far=(), scalar_outs=()):
    specs = [SMEM if j in scalars else HBM if j in far else VMEM for j in range(len(operands))]
    out_specs = tuple(SMEM if j in scalar_outs else VMEM for j in range(len(outs)))
    return pl.pallas_call(
        body,
        out_shape=outs,
        in_specs=specs,
        out_specs=out_specs,
        scratch_shapes=scratch,
        compiler_params=pltpu.CompilerParams(vmem_limit_bytes=mem << 20),
        cost_estimate=pl.CostEstimate(flops=flops, bytes_accessed=4 << 20, transcendentals=0),
    )(*operands)


def shape(*dims, dtype=F32):
    return jax.ShapeDtypeStruct(dims, dtype)


def copies(pairs, sem):
    made = [pltpu.make_async_copy(src, dst, sem.at[j]) for j, (src, dst) in enumerate(pairs)]
    for one in made:
        one.start()
    return made


def finish(made):
    for one in made:
        one.wait()


def split(value):
    high = value.astype(BF16)
    return high, (value - high.astype(F32)).astype(BF16)


def weights_body(kernels, biases, fwd, bwd, bias2):
    zero = jnp.zeros((CH, CH), F32)

    def put(dest, k, j, dh, first, second):
        high, low = split(jnp.concatenate([first, second], axis=1))
        for part, value in enumerate((low, high, high)):
            dest[k, pl.ds(WINDOW * part + CH * j, CH), pl.ds(LANES * dh, LANES)] = value

    for k in range(LAYERS):
        for dh in range(3):
            taps = [kernels[k * 9 + dh * 3 + dw] for dw in range(3)]
            if k < LAYERS - 1:
                for j in range(4):
                    put(fwd, k, j, dh, taps[j] if j < 3 else zero, taps[j - 1] if j > 0 else zero)
            flips = [tap.T for tap in taps]
            for j in range(4):
                put(bwd, k, j, 2 - dh, flips[2 - j] if j < 3 else zero, flips[3 - j] if j > 0 else zero)
    for k in range(LAYERS):
        row = biases[k : k + 1, :]
        bias2[k : k + 1, :] = jnp.concatenate([row, row], axis=1)


def weights(kernels, biases):
    size = (3 * WINDOW, 3 * LANES)
    return call(
        weights_body,
        (shape(LAYERS - 1, *size, dtype=BF16), shape(LAYERS, *size, dtype=BF16), shape(8, LANES)),
        [],
        (kernels.reshape(LAYERS * 9, CH, CH), biases),
        1 << 22,
    )


def sources(objective, center, radius, lower, upper):
    return [
        lambda cols: center[:, cols].astype(F32),
        lambda cols: upper[0, :, cols].astype(F32),
        lambda cols: upper[1, :, cols].astype(F32),
        lambda cols: upper[2, :, cols].astype(F32),
        lambda cols: lower[0, :, cols].astype(F32),
        lambda cols: lower[1, :, cols].astype(F32),
        lambda cols: lower[2, :, cols].astype(F32),
        lambda cols: radius[:, cols].astype(F32),
        lambda cols: objective[:, cols],
    ]


def sides_body(objective, center, radius, lower, upper, head, tail):
    rows, cols = objective.shape
    strip = HALO_PAIRS * LANES
    for m, read in enumerate(sources(objective, center, radius, lower, upper)):
        head[pl.ds(m * rows, rows), :] = read(pl.ds(0, strip))
        tail[pl.ds(m * rows, rows), :] = read(pl.ds(cols - strip, strip))


def ends_body(objective, center, radius, lower, upper, top, bottom, *rest):
    rows, cols = objective.shape
    held, sem = rest[:5], rest[5]
    finish(copies(list(zip((objective, center, radius, lower, upper), held)), sem))
    row = lax.broadcasted_iota(jnp.int32, (rows, LANES), 0)
    outer = (row >= 2) & (row < rows - 2)
    for q in range(cols // LANES):
        values = [read(pl.ds(q * LANES, LANES)) for read in sources(*held)]
        values[3] = jnp.where(outer, values[3] - values[6], values[3])
        for m, value in enumerate(values):
            here = pl.ds(q * SENT + ROW_START[m], ROWS_SENT[m])
            top[here, :] = value[: ROWS_SENT[m]]
            bottom[here, :] = value[rows - ROWS_SENT[m] :]


def corners_body(above, below, head, tail):
    count = HALO_PAIRS * SENT
    size = above.shape[0]
    for part, source in enumerate((above, below)):
        here = pl.ds(part * count, count)
        head[here, :] = source[0:count, :]
        tail[here, :] = source[size - count : size, :]


def column(reads, left, right, rows, pairs, m, q):
    if q < HALO_PAIRS:
        return left[m * rows : (m + 1) * rows, q * LANES : (q + 1) * LANES]
    if q >= HALO_PAIRS + pairs:
        q -= HALO_PAIRS + pairs
        return right[m * rows : (m + 1) * rows, q * LANES : (q + 1) * LANES]
    return reads[m](pl.ds((q - HALO_PAIRS) * LANES, LANES))


def halo(middle, left, right, part, pairs, q, m):
    if q < HALO_PAIRS:
        source, at = left, part * HALO_PAIRS + q
    elif q >= HALO_PAIRS + pairs:
        source, at = right, part * HALO_PAIRS + q - HALO_PAIRS - pairs
    else:
        source, at = middle, q - HALO_PAIRS
    return source[pl.ds(at * SENT + ROW_START[m], ROWS_SENT[m]), :]


def neighbours(head, tail, axis):
    count = lax.axis_size(axis)
    before = lax.ppermute(tail, axis, [(i, i + 1) for i in range(count - 1)])
    after = lax.ppermute(head, axis, [(i + 1, i) for i in range(count - 1)])
    return before, after


def roll_rows(value, shift):
    return pltpu.roll(value, shift % value.shape[0], 0)


def slide(maps, count, store, produce):
    rows = store.shape[2]
    early = lax.broadcasted_iota(jnp.int32, (rows, LANES), 1) < CH
    zero = jnp.zeros((rows, LANES), F32)

    def step(q, carry):
        fresh = [pltpu.roll(value, CH, 1) for value in produce(q)]
        for k in range(maps):
            store[k, q] = jnp.where(early, carry[k], fresh[k])
        return tuple(fresh)

    last = lax.fori_loop(0, count, step, (zero,) * maps, unroll=2)
    for k in range(maps):
        store[k, count] = jnp.where(early, last[k], zero)


def multiply(store, k, first, count, weight, layer, sums, exact=False):
    rows = store.shape[2]
    left = store[k, pl.ds(first, count)].reshape(count * rows, LANES)
    right = store[k, pl.ds(first + 1, count)].reshape(count * rows, LANES)
    high, low = split(jnp.concatenate([left, right], axis=1))
    terms = [high, high] if exact else [high, high, low]
    result = jnp.dot(
        jnp.concatenate(terms, axis=1),
        weight[layer, 0 : WINDOW * len(terms), :],
        preferred_element_type=F32,
    )
    for d in range(3):
        sums[k, d, pl.ds(0, count)] = result[:, d * LANES : (d + 1) * LANES].reshape(count, rows, LANES)


def gathered(sums, k, q):
    return roll_rows(sums[k, 0, q], 1) + sums[k, 1, q] + roll_rows(sums[k, 2, q], -1)


def inner(sums, k, q, first, rows):
    parts = [roll_rows(sums[k, d, q], 1 - d - first)[:rows] for d in range(3)]
    return parts[0] + parts[1] + parts[2]


def summed(total):
    return jnp.sum(total[...], axis=0, keepdims=True)


def scale_of(total, step, cells, dims):
    squares = summed(total)[:, 0:1]
    return jnp.broadcast_to(step / jnp.sqrt(squares / (2 * (LAYERS - 1) * cells) + EPS), dims)


def soft(top, t):
    return 0.5 * top * (1.0 - jnp.tanh(t))


class Bound:
    def __init__(self, start):
        self.linear = start
        self.factor = None

    def add(self, t):
        self.linear = self.linear - jnp.maximum(-t, 0.0)
        factor = 1.0 + jnp.exp(-2.0 * jnp.abs(t))
        self.factor = factor if self.factor is None else self.factor * factor

    def total(self):
        return self.linear - 0.5 * jnp.log(self.factor)


def folded(value):
    return jnp.sum(value, axis=0, keepdims=True)


def own_rows(value):
    rows = value.shape[0]
    row = lax.broadcasted_iota(jnp.int32, value.shape, 0)
    return folded(jnp.where((row >= EDGE) & (row < rows - EDGE), value, 0.0))


def stats(out, rows):
    lane = lax.broadcasted_iota(jnp.int32, (1, LANES), 1)
    packed = jnp.zeros((1, LANES), F32)
    for j, row in enumerate(rows):
        packed = jnp.where(lane == j, jnp.sum(row, axis=1, keepdims=True), packed)
    out[...] = jnp.broadcast_to(packed, out.shape)


def first_body(
    objective, center, radius, lower, upper, left, right, above, below, left_corner, right_corner, fwd, bwd, bias,
    near_box, far_box, back, slope, mult, stat, value,
    raw, gaps, target, store, sums,
):
    rows, cols = objective.shape
    pairs = cols // LANES
    frame = rows + 2 * EDGE
    wide = pairs + 4
    reads = sources(objective, center, radius, lower, upper)
    for m in range(9):
        sent = ROWS_SENT[m]
        for q in range(pairs + 2 * HALO_PAIRS):
            if m >= 3 and not 1 <= q < wide + 1:
                continue
            own = column(reads, left, right, rows, pairs, m, q)
            if m < 3:
                dest, at, edge = raw.at[m, q], 0, WIDE
            else:
                dest, at, edge = (target.at[q - 1] if m == 8 else gaps.at[m - 3, q - 1]), EDGE - sent, EDGE
                if at:
                    dest[0:EDGE, :] = jnp.zeros((EDGE, LANES), F32)
                    dest[EDGE + rows : frame, :] = jnp.zeros((EDGE, LANES), F32)
            dest[at : at + sent, :] = halo(above, left_corner, right_corner, 0, pairs, q, m)
            dest[edge : edge + rows, :] = own
            dest[edge + rows : edge + rows + sent, :] = halo(below, left_corner, right_corner, 1, pairs, q, m)
    raw[:, :, rows + 2 * WIDE :, :] = jnp.zeros((3, wide + 2, raw.shape[2] - rows - 2 * WIDE, LANES), F32)

    slide(3, wide + 2, store, lambda q: [raw[0, q], 0.5 * raw[1, q], 0.5 * raw[2, q]])
    tugged = store.at[3:4, :, 0:frame, :]
    slide(1, wide, tugged, lambda q: [target[q]])
    for k in range(3):
        multiply(store, k, 1, wide, fwd, k, sums, exact=True)
    short = sums.at[3:4, :, :, 0:frame, :]
    multiply(tugged, 0, 0, wide, bwd, LAYERS - 1, short)
    zero = jnp.zeros((frame, LANES), F32)

    def step(q, carry):
        squares, worth, fixed = carry
        near = [raw[m, q + 1][1 : 1 + frame] for m in range(3)] + [gaps[4, q]]
        far = [gaps[m, q] for m in range(4)]
        for m in range(4):
            near_box[m, q] = near[m].astype(BF16)
            far_box[m, q] = far[m].astype(BF16)
        new = zero
        for k in range(3):
            gap = near[1 + k] if k < 2 else far[0]
            dl = 0.5 * (gap - far[1 + k]) - inner(sums, k, q, 1, frame) - bias[k : k + 1, :]
            dl = jnp.where(near[1] > 0.0, dl, 0.0)
            slope[k, q] = dl
            new = new + dl * dl
        tug = gathered(short, 0, q)
        back[q] = tug
        t = tug * gap
        dm = -0.5 * gap * jnp.tanh(t)
        mult[q] = dm
        new = new + dm * dm
        bound = Bound(jnp.full((frame, LANES), -4.5 * math.log(2.0), F32))
        bound.add(t)
        own = (q >= 2) & (q < wide - 2)
        squares = squares + jnp.where(own, new, 0.0)
        worth = worth + jnp.where(own, bound.total(), 0.0)
        fixed = fixed + jnp.where(own, target[q] * bias[3:4, :], 0.0)
        return squares, worth, fixed

    squares, worth, fixed = lax.fori_loop(0, wide, step, (zero, zero, zero), unroll=2)
    fixed = own_rows(fixed)
    stats(stat, [own_rows(squares)])
    stats(value, [own_rows(worth) + fixed, fixed])


def second_body(
    total, steps, near_box, far_box, back, slope, mult, fwd, bwd, bias,
    base, slope_out, mult_out, duals, last_mult, last_slope, last_pull, stat, value,
    points, store, sums, *, cells,
):
    wide, frame = near_box.shape[1:3]
    inside = slice(EDGE, frame - EDGE)
    scale = scale_of(total, steps[0], cells, (frame, LANES))
    zero = jnp.zeros((frame, LANES), F32)
    slide(3, wide, store, lambda q: [slope[k, q] for k in range(3)])
    for k in range(3):
        multiply(store, k, 0, wide, bwd, k, sums)

    def produce(q):
        center, radius = near_box[0, q].astype(F32), near_box[3, q].astype(F32)
        g = -(scale * gathered(sums, 0, q))
        base[0, q] = g
        outs = [center - radius * jnp.tanh(2.0 * radius * g)]
        for k in (1, 2):
            gap = near_box[k, q].astype(F32)
            g = -(scale * gathered(sums, k, q))
            base[k, q] = g
            x = soft(gap, g * gap)
            points[k - 1, q] = x
            outs.append(x)
        return outs

    slide(3, wide, store, produce)
    for k in range(3):
        multiply(store, k, 1, wide - 2, fwd, k, sums)

    def step(j, carry):
        squares, worth = carry
        q = j + 1
        new = zero
        center, radius = near_box[0, q].astype(F32), near_box[3, q].astype(F32)
        g = base[0, q]
        bound = Bound(g * (center - radius))
        bound.add(2.0 * g * radius)
        for k in range(3):
            gap = (near_box[1 + k, q] if k < 2 else far_box[0, q]).astype(F32)
            low = far_box[1 + k, q].astype(F32)
            lam = scale * slope[k, q]
            if k < 2:
                bound.add(base[k + 1, q] * gap)
                x = points[k, q]
                tp = lam * gap
            else:
                mu = scale * mult[q]
                g = back[q] + mu
                t = g * gap
                bound.add(t)
                x = soft(gap, t)
                tp = (lam - mu) * gap
            tn = -lam * low
            bound.add(tp)
            bound.add(tn)
            bound.linear = bound.linear - lam * bias[k : k + 1, :]
            positive = soft(gap, tp)
            dl = positive - soft(low, tn) - gathered(sums, k, j) - bias[k : k + 1, :]
            dl = jnp.where(gap > 0.0, dl, 0.0)
            dm = x - positive
            slope_out[k, j] = dl
            duals[k, j] = lam[inside]
            if k < 2:
                mult_out[k, j] = dm
            else:
                last_mult[j] = mu[inside]
                last_slope[j] = dm[inside]
                last_pull[j] = g[inside]
            new = new + dl * dl + dm * dm
        own = (q >= 2) & (q < wide - 2)
        return squares + jnp.where(own, new, 0.0), worth + jnp.where(own, bound.total(), 0.0)

    squares, worth = lax.fori_loop(0, wide - 2, step, (zero, zero))
    stats(stat, [own_rows(squares)])
    stats(value, [own_rows(worth)])


def third_body(
    total, steps, near_box, base, mult, slope, duals1, last_mult, last_slope, last_pull,
    fwd, bwd, lower, upper, bias, value0, value1,
    duals, multipliers, slope_out, mult_out, stat,
    points, store, sums, *, cells,
):
    wide, frame = near_box.shape[1:3]
    rows = frame - 2 * EDGE
    inside = slice(EDGE, frame - EDGE)
    scale = scale_of(total, steps[1], cells, (frame, LANES))
    zero = jnp.zeros((frame, LANES), F32)
    slide(3, wide - 2, store, lambda j: [slope[k, j] for k in range(3)])
    for k in range(3):
        multiply(store, k, 0, wide - 2, bwd, k, sums)
    early = lax.broadcasted_iota(jnp.int32, (frame, LANES), 1) < CH

    def point(j, carry):
        q = j + 1
        center, radius = near_box[0, q].astype(F32), near_box[3, q].astype(F32)
        g = base[0, q] - scale * gathered(sums, 0, j)
        bound = Bound(g * (center - radius))
        t = 2.0 * radius * g
        bound.add(t)
        outs = [center - radius * jnp.tanh(t)]
        for k in (1, 2):
            gap = near_box[k, q].astype(F32)
            t = (base[k, q] + scale * (mult[k - 1, j] - gathered(sums, k, j))) * gap
            bound.add(t)
            x = soft(gap, t)
            points[k - 1, j] = x
            outs.append(x)
        own = (q >= 2) & (q < wide - 2)
        fresh = [pltpu.roll(value, CH, 1) for value in outs]
        for k in range(3):
            store[k, j] = jnp.where(early, carry[k], fresh[k])
        return tuple(fresh) + (carry[3] + jnp.where(own, bound.total(), 0.0),)

    framed = lax.fori_loop(0, wide - 2, point, (zero,) * 4)[3]
    for k in range(3):
        multiply(store, k, 1, wide - 4, fwd, k, sums)

    scale = scale[:rows]

    def step(i, carry):
        squares, worth = carry
        j = i + 1
        here = pl.ds(pl.multiple_of(i * LANES, LANES), LANES)
        bound = Bound(jnp.zeros((rows, LANES), F32))
        for k in range(3):
            gap = upper[k, :, here].astype(F32)
            low = lower[k, :, here].astype(F32)
            lam = duals1[k, j] + scale * slope[k, j, inside, :]
            bound.linear = bound.linear - lam * bias[k : k + 1, :]
            if k < 2:
                x = points[k, j, inside, :]
                mu = scale * mult[k, j, inside, :]
            else:
                change = scale * last_slope[j]
                mu = last_mult[j] + change
                t = (last_pull[j] + change) * gap
                x = soft(gap, t)
                bound.add(t)
            tp = (lam - mu) * gap
            tn = -lam * low
            bound.add(tp)
            bound.add(tn)
            positive = soft(gap, tp)
            dl = positive - soft(low, tn) - inner(sums, k, i, EDGE, rows) - bias[k : k + 1, :]
            dm = x - positive
            duals[k, :, here] = lam
            multipliers[k, :, here] = mu
            slope_out[k, :, here] = dl
            mult_out[k, :, here] = dm
            squares = squares + dl * dl + dm * dm
        return squares, worth + bound.total()

    zero = jnp.zeros((rows, LANES), F32)
    squares, worth = lax.fori_loop(0, wide - 4, step, (zero, zero), unroll=2)
    lane = lax.broadcasted_iota(jnp.int32, (1, LANES), 1)
    start, fixed = (jnp.where(lane == j, value0[0:1, :], 0.0) for j in range(2))
    middle = jnp.where(lane == 0, value1[0:1, :], 0.0)
    stats(stat, [folded(squares), start, middle + fixed, folded(worth) + own_rows(framed) + fixed])


def last_body(total, steps, duals, multipliers, slope, mult, duals_out, mult_out, bounds, *, cells):
    scale = scale_of(total, steps[2], cells, duals.shape[1:])
    for k in range(LAYERS - 1):
        duals_out[k] = duals[k] + scale * slope[k]
        mult_out[k] = multipliers[k] + scale * mult[k]
    values = summed(total) / cells
    lane = lax.broadcasted_iota(jnp.int32, (1, LANES), 1)
    for j in range(ITERS):
        bounds[j] = jnp.sum(jnp.where(lane == j + 1, values, 0.0))


def everyone(partial):
    return lax.all_to_all(partial, ("row", "col"), 0, 0, tiled=True)


def shards(objective, center, radius, lower, upper, kernels, biases, steps):
    rows, cols = objective.shape
    pairs = cols // LANES
    wide = pairs + 4
    frame = rows + 2 * EDGE
    tall = -(-(rows + 2 * WIDE) // 8) * 8
    cells = rows * cols * lax.axis_size("row") * lax.axis_size("col")
    inputs = (objective, center, radius, lower, upper)
    flops = 3 * 2 * 3 * wide * frame * 4 * CH * 3 * LANES
    spread = shape(lax.axis_size("row") * lax.axis_size("col"), LANES)
    small = shape(8, LANES)

    ends = shape(pairs * SENT, LANES)
    top, bottom = call(
        ends_body,
        (ends, ends),
        [pltpu.VMEM(one.shape, one.dtype) for one in inputs] + [pltpu.SemaphoreType.DMA((5,))],
        inputs,
        1 << 20,
        mem=58,
        far=range(5),
    )
    above, below = neighbours(top, bottom, "row")
    strip = shape(9 * rows, HALO_PAIRS * LANES)
    head, tail = call(sides_body, (strip, strip), [], inputs, 1 << 20)
    left, right = neighbours(head, tail, "col")
    fwd, bwd, bias = weights(kernels, biases)
    corner = shape(2 * HALO_PAIRS * SENT, LANES)
    corner_head, corner_tail = call(corners_body, (corner, corner), [], (above, below), 1 << 20)
    left_corner, right_corner = neighbours(corner_head, corner_tail, "col")

    box = shape(4, wide, frame, LANES, dtype=BF16)
    full = shape(wide, frame, LANES)
    near_box, far_box, back, slope0, mult0, stat0, value0 = call(
        first_body,
        (box, box, full, shape(3, wide, frame, LANES), full, spread, small),
        [
            pltpu.VMEM((3, wide + 2, tall, LANES), F32),
            pltpu.VMEM((5, wide, frame, LANES), F32),
            pltpu.VMEM((wide, frame, LANES), F32),
            pltpu.VMEM((4, wide + 3, tall, LANES), F32),
            pltpu.VMEM((4, 3, wide, tall, LANES), F32),
        ],
        inputs + (left, right, above, below, left_corner, right_corner, fwd, bwd, bias),
        2 * flops,
    )

    total0 = everyone(stat0)
    tile = shape(wide - 2, rows, LANES)
    base, slope1, mult1, duals1, last_mult, last_slope, last_pull, stat1, value1 = call(
        functools.partial(second_body, cells=cells),
        (
            shape(3, wide, frame, LANES),
            shape(3, wide - 2, frame, LANES),
            shape(2, wide - 2, frame, LANES),
            shape(3, wide - 2, rows, LANES),
            tile,
            tile,
            tile,
            spread,
            small,
        ),
        [
            pltpu.VMEM((2, wide, frame, LANES), F32),
            pltpu.VMEM((3, wide + 1, frame, LANES), F32),
            pltpu.VMEM((3, 3, wide, frame, LANES), F32),
        ],
        (total0, steps, near_box, far_box, back, slope0, mult0, fwd, bwd, bias),
        2 * flops,
        scalars=(1,),
    )
    total1 = everyone(stat1)
    out = shape(3, rows, cols)
    duals, multipliers, slope2, mult2, stat2 = call(
        functools.partial(third_body, cells=cells),
        (out, out, out, out, spread),
        [
            pltpu.VMEM((2, wide - 2, frame, LANES), F32),
            pltpu.VMEM((3, wide - 1, frame, LANES), F32),
            pltpu.VMEM((3, 3, wide - 2, frame, LANES), F32),
        ],
        (
            total1, steps, near_box, base, mult1, slope1, duals1, last_mult, last_slope, last_pull,
            fwd, bwd, lower, upper, bias, value0, value1,
        ),
        2 * flops,
        scalars=(1,),
    )
    total2 = everyone(stat2)
    final_duals, final_multipliers, bounds = call(
        functools.partial(last_body, cells=cells),
        (out, out, shape(ITERS)),
        [],
        (total2, steps, duals, multipliers, slope2, mult2),
        1 << 20,
        scalar_outs=(2,),
        scalars=(1,),
    )
    return bounds, final_duals, final_multipliers


def solution(mesh):
    placed = (
        P("row", "col"),
        P("row", "col"),
        P("row", "col"),
        P(None, "row", "col"),
        P(None, "row", "col"),
        P(),
        P(),
        P(),
    )
    return jax.shard_map(
        shards,
        mesh=mesh,
        in_specs=placed,
        out_specs=(P(), P(None, "row", "col"), P(None, "row", "col")),
        check_vma=False,
    )
```

```python
import functools
import math

import jax
import jax.numpy as jnp
from jax import lax
from jax.experimental import pallas as pl
from jax.experimental.pallas import tpu as pltpu
from jax.sharding import PartitionSpec as P

CH = 64
LAYERS = 4
ITERS = 3
EPS = 1e-06
LANES = 2 * CH
HALO_PAIRS = 3
WIDE = 5
EDGE = 4
F32 = jnp.float32
BF16 = jnp.bfloat16

ROWS_SENT = (5, 5, 5, 4, 4, 4, 2, 3, 3)
ROW_START = tuple(sum(ROWS_SENT[:m]) for m in range(9))
SENT = sum(ROWS_SENT)
WINDOW = 4 * CH

VMEM = pl.BlockSpec(memory_space=pltpu.VMEM)
SMEM = pl.BlockSpec(memory_space=pltpu.SMEM)
HBM = pl.BlockSpec(memory_space=pltpu.HBM)


def call(body, outs, scratch, operands, flops, mem=20, scalars=(), far=(), scalar_outs=()):
    specs = [SMEM if j in scalars else HBM if j in far else VMEM for j in range(len(operands))]
    out_specs = tuple(SMEM if j in scalar_outs else VMEM for j in range(len(outs)))
    return pl.pallas_call(
        body,
        out_shape=outs,
        in_specs=specs,
        out_specs=out_specs,
        scratch_shapes=scratch,
        compiler_params=pltpu.CompilerParams(vmem_limit_bytes=mem << 20),
        cost_estimate=pl.CostEstimate(flops=flops, bytes_accessed=4 << 20, transcendentals=0),
    )(*operands)


def shape(*dims, dtype=F32):
    return jax.ShapeDtypeStruct(dims, dtype)


def copies(pairs, sem):
    made = [pltpu.make_async_copy(src, dst, sem.at[j]) for j, (src, dst) in enumerate(pairs)]
    for one in made:
        one.start()
    return made


def finish(made):
    for one in made:
        one.wait()


def split(value):
    high = value.astype(BF16)
    return high, (value - high.astype(F32)).astype(BF16)


def weights_body(kernels, biases, fwd, bwd, bias2):
    zero = jnp.zeros((CH, CH), F32)

    def put(dest, k, j, dh, first, second):
        high, low = split(jnp.concatenate([first, second], axis=1))
        for part, value in enumerate((low, high, high)):
            dest[k, pl.ds(WINDOW * part + CH * j, CH), pl.ds(LANES * dh, LANES)] = value

    for k in range(LAYERS):
        for dh in range(3):
            taps = [kernels[k * 9 + dh * 3 + dw] for dw in range(3)]
            if k < LAYERS - 1:
                for j in range(4):
                    put(fwd, k, j, dh, taps[j] if j < 3 else zero, taps[j - 1] if j > 0 else zero)
            flips = [tap.T for tap in taps]
            for j in range(4):
                put(bwd, k, j, 2 - dh, flips[2 - j] if j < 3 else zero, flips[3 - j] if j > 0 else zero)
    for k in range(LAYERS):
        row = biases[k : k + 1, :]
        bias2[k : k + 1, :] = jnp.concatenate([row, row], axis=1)


def weights(kernels, biases):
    size = (3 * WINDOW, 3 * LANES)
    return call(
        weights_body,
        (shape(LAYERS - 1, *size, dtype=BF16), shape(LAYERS, *size, dtype=BF16), shape(8, LANES)),
        [],
        (kernels.reshape(LAYERS * 9, CH, CH), biases),
        1 << 22,
    )


def sources(objective, center, radius, lower, upper):
    return [
        lambda cols: center[:, cols].astype(F32),
        lambda cols: upper[0, :, cols].astype(F32),
        lambda cols: upper[1, :, cols].astype(F32),
        lambda cols: upper[2, :, cols].astype(F32),
        lambda cols: lower[0, :, cols].astype(F32),
        lambda cols: lower[1, :, cols].astype(F32),
        lambda cols: lower[2, :, cols].astype(F32),
        lambda cols: radius[:, cols].astype(F32),
        lambda cols: objective[:, cols],
    ]


def ends_body(objective, center, radius, lower, upper, top, bottom, head, tail, *rest):
    rows, cols = objective.shape
    held, sem = rest[:5], rest[5]
    finish(copies(list(zip((objective, center, radius, lower, upper), held)), sem))
    strip = HALO_PAIRS * LANES
    for m, read in enumerate(sources(*held)):
        head[pl.ds(m * rows, rows), :] = read(pl.ds(0, strip))
        tail[pl.ds(m * rows, rows), :] = read(pl.ds(cols - strip, strip))
    row = lax.broadcasted_iota(jnp.int32, (rows, LANES), 0)
    outer = (row >= 2) & (row < rows - 2)
    for q in range(cols // LANES):
        values = [read(pl.ds(q * LANES, LANES)) for read in sources(*held)]
        values[3] = jnp.where(outer, values[3] - values[6], values[3])
        for m, value in enumerate(values):
            here = pl.ds(q * SENT + ROW_START[m], ROWS_SENT[m])
            top[here, :] = value[: ROWS_SENT[m]]
            bottom[here, :] = value[rows - ROWS_SENT[m] :]


def corners_body(above, below, head, tail):
    count = HALO_PAIRS * SENT
    size = above.shape[0]
    for part, source in enumerate((above, below)):
        here = pl.ds(part * count, count)
        head[here, :] = source[0:count, :]
        tail[here, :] = source[size - count : size, :]


def column(reads, left, right, rows, pairs, m, q):
    if q < HALO_PAIRS:
        return left[m * rows : (m + 1) * rows, q * LANES : (q + 1) * LANES]
    if q >= HALO_PAIRS + pairs:
        q -= HALO_PAIRS + pairs
        return right[m * rows : (m + 1) * rows, q * LANES : (q + 1) * LANES]
    return reads[m](pl.ds((q - HALO_PAIRS) * LANES, LANES))


def halo(middle, left, right, part, pairs, q, m):
    if q < HALO_PAIRS:
        source, at = left, part * HALO_PAIRS + q
    elif q >= HALO_PAIRS + pairs:
        source, at = right, part * HALO_PAIRS + q - HALO_PAIRS - pairs
    else:
        source, at = middle, q - HALO_PAIRS
    return source[pl.ds(at * SENT + ROW_START[m], ROWS_SENT[m]), :]


def neighbours(head, tail, axis):
    count = lax.axis_size(axis)
    before = lax.ppermute(tail, axis, [(i, i + 1) for i in range(count - 1)])
    after = lax.ppermute(head, axis, [(i + 1, i) for i in range(count - 1)])
    return before, after


def roll_rows(value, shift):
    return pltpu.roll(value, shift % value.shape[0], 0)


def slide(maps, count, store, produce):
    rows = store.shape[2]
    early = lax.broadcasted_iota(jnp.int32, (rows, LANES), 1) < CH
    zero = jnp.zeros((rows, LANES), F32)

    def step(q, carry):
        fresh = [pltpu.roll(value, CH, 1) for value in produce(q)]
        for k in range(maps):
            store[k, q] = jnp.where(early, carry[k], fresh[k])
        return tuple(fresh)

    last = lax.fori_loop(0, count, step, (zero,) * maps, unroll=2)
    for k in range(maps):
        store[k, count] = jnp.where(early, last[k], zero)


def multiply(store, k, first, count, weight, layer, sums, exact=False):
    rows = store.shape[2]
    left = store[k, pl.ds(first, count)].reshape(count * rows, LANES)
    right = store[k, pl.ds(first + 1, count)].reshape(count * rows, LANES)
    high, low = split(jnp.concatenate([left, right], axis=1))
    terms = [high, high] if exact else [high, high, low]
    result = jnp.dot(
        jnp.concatenate(terms, axis=1),
        weight[layer, 0 : WINDOW * len(terms), :],
        preferred_element_type=F32,
    )
    for d in range(3):
        sums[k, d, pl.ds(0, count)] = result[:, d * LANES : (d + 1) * LANES].reshape(count, rows, LANES)


def gathered(sums, k, q):
    return roll_rows(sums[k, 0, q], 1) + sums[k, 1, q] + roll_rows(sums[k, 2, q], -1)


def inner(sums, k, q, first, rows):
    parts = [roll_rows(sums[k, d, q], 1 - d - first)[:rows] for d in range(3)]
    return parts[0] + parts[1] + parts[2]


def summed(total):
    return jnp.sum(total[...], axis=0, keepdims=True)


def scale_of(total, step, cells, dims):
    squares = summed(total)[:, 0:1]
    return jnp.broadcast_to(step / jnp.sqrt(squares / (2 * (LAYERS - 1) * cells) + EPS), dims)


def soft(top, bend):
    return 0.5 * top * (1.0 - bend)


class Bound:
    def __init__(self, start):
        self.linear = start
        self.factor = None

    def add(self, t):
        bend = jnp.tanh(t)
        self.linear = self.linear + (jnp.minimum(t, 0.0) - 0.5 * math.log(2.0))
        factor = 1.0 + jnp.abs(bend)
        self.factor = factor if self.factor is None else self.factor * factor
        return bend

    def total(self):
        return self.linear + 0.5 * jnp.log(self.factor)


def folded(value):
    return jnp.sum(value, axis=0, keepdims=True)


def own_rows(value):
    rows = value.shape[0]
    row = lax.broadcasted_iota(jnp.int32, value.shape, 0)
    return folded(jnp.where((row >= EDGE) & (row < rows - EDGE), value, 0.0))


def stats(out, rows):
    lane = lax.broadcasted_iota(jnp.int32, (1, LANES), 1)
    packed = jnp.zeros((1, LANES), F32)
    for j, row in enumerate(rows):
        packed = jnp.where(lane == j, jnp.sum(row, axis=1, keepdims=True), packed)
    out[...] = jnp.broadcast_to(packed, out.shape)


def first_body(
    objective, center, radius, lower, upper, left, right, above, below, left_corner, right_corner, fwd, bwd, bias,
    near_box, far_box, back, slope, mult, stat, value,
    raw, gaps, target, store, sums,
):
    rows, cols = objective.shape
    pairs = cols // LANES
    frame = rows + 2 * EDGE
    wide = pairs + 4
    reads = sources(objective, center, radius, lower, upper)
    for m in range(9):
        sent = ROWS_SENT[m]
        for q in range(pairs + 2 * HALO_PAIRS):
            if m >= 3 and not 1 <= q < wide + 1:
                continue
            own = column(reads, left, right, rows, pairs, m, q)
            if m < 3:
                dest, at, edge = raw.at[m, q], 0, WIDE
            else:
                dest, at, edge = (target.at[q - 1] if m == 8 else gaps.at[m - 3, q - 1]), EDGE - sent, EDGE
                if at:
                    dest[0:EDGE, :] = jnp.zeros((EDGE, LANES), F32)
                    dest[EDGE + rows : frame, :] = jnp.zeros((EDGE, LANES), F32)
            dest[at : at + sent, :] = halo(above, left_corner, right_corner, 0, pairs, q, m)
            dest[edge : edge + rows, :] = own
            dest[edge + rows : edge + rows + sent, :] = halo(below, left_corner, right_corner, 1, pairs, q, m)
    raw[:, :, rows + 2 * WIDE :, :] = jnp.zeros((3, wide + 2, raw.shape[2] - rows - 2 * WIDE, LANES), F32)

    slide(3, wide + 2, store, lambda q: [raw[0, q], 0.5 * raw[1, q], 0.5 * raw[2, q]])
    tugged = store.at[3:4, :, 0:frame, :]
    slide(1, wide, tugged, lambda q: [target[q]])
    for k in range(3):
        multiply(store, k, 1, wide, fwd, k, sums, exact=True)
    short = sums.at[3:4, :, :, 0:frame, :]
    multiply(tugged, 0, 0, wide, bwd, LAYERS - 1, short)
    zero = jnp.zeros((frame, LANES), F32)

    def step(q, carry):
        squares, worth, fixed = carry
        near = [raw[m, q + 1][1 : 1 + frame] for m in range(3)] + [gaps[4, q]]
        far = [gaps[m, q] for m in range(4)]
        for m in range(4):
            near_box[m, q] = near[m].astype(BF16)
            far_box[m, q] = far[m].astype(BF16)
        new = zero
        for k in range(3):
            gap = near[1 + k] if k < 2 else far[0]
            dl = 0.5 * (gap - far[1 + k]) - inner(sums, k, q, 1, frame) - bias[k : k + 1, :]
            dl = jnp.where(near[1] > 0.0, dl, 0.0)
            slope[k, q] = dl
            new = new + dl * dl
        tug = gathered(short, 0, q)
        back[q] = tug
        bound = Bound(jnp.full((frame, LANES), -4.5 * math.log(2.0), F32))
        dm = -0.5 * gap * bound.add(tug * gap)
        mult[q] = dm
        new = new + dm * dm
        own = (q >= 2) & (q < wide - 2)
        squares = squares + jnp.where(own, new, 0.0)
        worth = worth + jnp.where(own, bound.total(), 0.0)
        fixed = fixed + jnp.where(own, target[q] * bias[3:4, :], 0.0)
        return squares, worth, fixed

    squares, worth, fixed = lax.fori_loop(0, wide, step, (zero, zero, zero), unroll=2)
    fixed = own_rows(fixed)
    stats(stat, [own_rows(squares)])
    stats(value, [own_rows(worth) + fixed, fixed])


def second_body(
    total, steps, near_box, far_box, back, slope, mult, fwd, bwd, bias,
    base, slope_out, mult_out, duals, last_mult, last_slope, last_pull, stat, value,
    points, worths, store, sums, *, cells,
):
    wide, frame = near_box.shape[1:3]
    inside = slice(EDGE, frame - EDGE)
    scale = scale_of(total, steps[0], cells, (frame, LANES))
    zero = jnp.zeros((frame, LANES), F32)
    slide(3, wide, store, lambda q: [slope[k, q] for k in range(3)])
    for k in range(3):
        multiply(store, k, 0, wide, bwd, k, sums)

    def produce(q):
        center, radius = near_box[0, q].astype(F32), near_box[3, q].astype(F32)
        g = -(scale * gathered(sums, 0, q))
        base[0, q] = g
        bound = Bound(g * (center - radius))
        outs = [center - radius * bound.add(2.0 * radius * g)]
        for k in (1, 2):
            gap = near_box[k, q].astype(F32)
            g = -(scale * gathered(sums, k, q))
            base[k, q] = g
            x = soft(gap, bound.add(g * gap))
            points[k - 1, q] = x
            outs.append(x)
        worths[q] = bound.total()
        return outs

    slide(3, wide, store, produce)
    for k in range(3):
        multiply(store, k, 1, wide - 2, fwd, k, sums)

    def step(j, carry):
        squares, worth = carry
        q = j + 1
        new = zero
        bound = Bound(worths[q])
        for k in range(3):
            gap = (near_box[1 + k, q] if k < 2 else far_box[0, q]).astype(F32)
            low = far_box[1 + k, q].astype(F32)
            lam = scale * slope[k, q]
            if k < 2:
                x = points[k, q]
                tp = lam * gap
            else:
                mu = scale * mult[q]
                g = back[q] + mu
                x = soft(gap, bound.add(g * gap))
                tp = (lam - mu) * gap
            positive = soft(gap, bound.add(tp))
            negative = soft(low, bound.add(-lam * low))
            bound.linear = bound.linear - lam * bias[k : k + 1, :]
            dl = positive - negative - gathered(sums, k, j) - bias[k : k + 1, :]
            dl = jnp.where(gap > 0.0, dl, 0.0)
            dm = x - positive
            slope_out[k, j] = dl
            duals[k, j] = lam[inside]
            if k < 2:
                mult_out[k, j] = dm
            else:
                last_mult[j] = mu[inside]
                last_slope[j] = dm[inside]
                last_pull[j] = g[inside]
            new = new + dl * dl + dm * dm
        own = (q >= 2) & (q < wide - 2)
        return squares + jnp.where(own, new, 0.0), worth + jnp.where(own, bound.total(), 0.0)

    squares, worth = lax.fori_loop(0, wide - 2, step, (zero, zero), unroll=2)
    stats(stat, [own_rows(squares)])
    stats(value, [own_rows(worth)])


def third_body(
    total, steps, near_box, base, mult, slope, duals1, last_mult, last_slope, last_pull,
    fwd, bwd, lower, upper, bias, value0, value1,
    duals, multipliers, slope_out, mult_out, stat,
    points, store, sums, *, cells,
):
    wide, frame = near_box.shape[1:3]
    rows = frame - 2 * EDGE
    inside = slice(EDGE, frame - EDGE)
    scale = scale_of(total, steps[1], cells, (frame, LANES))
    zero = jnp.zeros((frame, LANES), F32)
    slide(3, wide - 2, store, lambda j: [slope[k, j] for k in range(3)])
    for k in range(3):
        multiply(store, k, 0, wide - 2, bwd, k, sums)
    early = lax.broadcasted_iota(jnp.int32, (frame, LANES), 1) < CH

    def point(j, carry):
        q = j + 1
        center, radius = near_box[0, q].astype(F32), near_box[3, q].astype(F32)
        g = base[0, q] - scale * gathered(sums, 0, j)
        bound = Bound(g * (center - radius))
        outs = [center - radius * bound.add(2.0 * radius * g)]
        for k in (1, 2):
            gap = near_box[k, q].astype(F32)
            t = (base[k, q] + scale * (mult[k - 1, j] - gathered(sums, k, j))) * gap
            x = soft(gap, bound.add(t))
            points[k - 1, j] = x
            outs.append(x)
        own = (q >= 2) & (q < wide - 2)
        fresh = [pltpu.roll(value, CH, 1) for value in outs]
        for k in range(3):
            store[k, j] = jnp.where(early, carry[k], fresh[k])
        return tuple(fresh) + (carry[3] + jnp.where(own, bound.total(), 0.0),)

    framed = lax.fori_loop(0, wide - 2, point, (zero,) * 4, unroll=2)[3]
    for k in range(3):
        multiply(store, k, 1, wide - 4, fwd, k, sums)

    scale = scale[:rows]

    def step(i, carry):
        squares, worth = carry
        j = i + 1
        here = pl.ds(pl.multiple_of(i * LANES, LANES), LANES)
        bound = Bound(jnp.zeros((rows, LANES), F32))
        for k in range(3):
            gap = upper[k, :, here].astype(F32)
            low = lower[k, :, here].astype(F32)
            lam = duals1[k, j] + scale * slope[k, j, inside, :]
            bound.linear = bound.linear - lam * bias[k : k + 1, :]
            if k < 2:
                x = points[k, j, inside, :]
                mu = scale * mult[k, j, inside, :]
            else:
                change = scale * last_slope[j]
                mu = last_mult[j] + change
                x = soft(gap, bound.add((last_pull[j] + change) * gap))
            positive = soft(gap, bound.add((lam - mu) * gap))
            negative = soft(low, bound.add(-lam * low))
            dl = positive - negative - inner(sums, k, i, EDGE, rows) - bias[k : k + 1, :]
            dm = x - positive
            duals[k, :, here] = lam
            multipliers[k, :, here] = mu
            slope_out[k, :, here] = dl
            mult_out[k, :, here] = dm
            squares = squares + dl * dl + dm * dm
        return squares, worth + bound.total()

    zero = jnp.zeros((rows, LANES), F32)
    squares, worth = lax.fori_loop(0, wide - 4, step, (zero, zero), unroll=2)
    lane = lax.broadcasted_iota(jnp.int32, (1, LANES), 1)
    start, fixed = (jnp.where(lane == j, value0[0:1, :], 0.0) for j in range(2))
    middle = jnp.where(lane == 0, value1[0:1, :], 0.0)
    stats(stat, [folded(squares), start, middle + fixed, folded(worth) + own_rows(framed) + fixed])


def last_body(total, steps, duals, multipliers, slope, mult, duals_out, mult_out, bounds, *, cells):
    scale = scale_of(total, steps[2], cells, duals.shape[1:])
    for k in range(LAYERS - 1):
        duals_out[k] = duals[k] + scale * slope[k]
        mult_out[k] = multipliers[k] + scale * mult[k]
    values = summed(total) / cells
    lane = lax.broadcasted_iota(jnp.int32, (1, LANES), 1)
    for j in range(ITERS):
        bounds[j] = jnp.sum(jnp.where(lane == j + 1, values, 0.0))


def everyone(partial):
    return lax.all_to_all(partial, ("row", "col"), 0, 0, tiled=True)


def shards(objective, center, radius, lower, upper, kernels, biases, steps):
    rows, cols = objective.shape
    pairs = cols // LANES
    wide = pairs + 4
    frame = rows + 2 * EDGE
    tall = -(-(rows + 2 * WIDE) // 8) * 8
    cells = rows * cols * lax.axis_size("row") * lax.axis_size("col")
    inputs = (objective, center, radius, lower, upper)
    flops = 3 * 2 * 3 * wide * frame * 4 * CH * 3 * LANES
    spread = shape(lax.axis_size("row") * lax.axis_size("col"), LANES)
    small = shape(8, LANES)

    ends = shape(pairs * SENT, LANES)
    strip = shape(9 * rows, HALO_PAIRS * LANES)
    top, bottom, head, tail = call(
        ends_body,
        (ends, ends, strip, strip),
        [pltpu.VMEM(one.shape, one.dtype) for one in inputs] + [pltpu.SemaphoreType.DMA((5,))],
        inputs,
        1 << 20,
        mem=58,
        far=range(5),
    )
    above, below = neighbours(top, bottom, "row")
    left, right = neighbours(head, tail, "col")
    fwd, bwd, bias = weights(kernels, biases)
    corner = shape(2 * HALO_PAIRS * SENT, LANES)
    corner_head, corner_tail = call(corners_body, (corner, corner), [], (above, below), 1 << 20)
    left_corner, right_corner = neighbours(corner_head, corner_tail, "col")

    box = shape(4, wide, frame, LANES, dtype=BF16)
    full = shape(wide, frame, LANES)
    near_box, far_box, back, slope0, mult0, stat0, value0 = call(
        first_body,
        (box, box, full, shape(3, wide, frame, LANES), full, spread, small),
        [
            pltpu.VMEM((3, wide + 2, tall, LANES), F32),
            pltpu.VMEM((5, wide, frame, LANES), F32),
            pltpu.VMEM((wide, frame, LANES), F32),
            pltpu.VMEM((4, wide + 3, tall, LANES), F32),
            pltpu.VMEM((4, 3, wide, tall, LANES), F32),
        ],
        inputs + (left, right, above, below, left_corner, right_corner, fwd, bwd, bias),
        2 * flops,
    )

    total0 = everyone(stat0)
    tile = shape(wide - 2, rows, LANES)
    base, slope1, mult1, duals1, last_mult, last_slope, last_pull, stat1, value1 = call(
        functools.partial(second_body, cells=cells),
        (
            shape(3, wide, frame, LANES),
            shape(3, wide - 2, frame, LANES),
            shape(2, wide - 2, frame, LANES),
            shape(3, wide - 2, rows, LANES),
            tile,
            tile,
            tile,
            spread,
            small,
        ),
        [
            pltpu.VMEM((2, wide, frame, LANES), F32),
            pltpu.VMEM((wide, frame, LANES), F32),
            pltpu.VMEM((3, wide + 1, frame, LANES), F32),
            pltpu.VMEM((3, 3, wide, frame, LANES), F32),
        ],
        (total0, steps, near_box, far_box, back, slope0, mult0, fwd, bwd, bias),
        2 * flops,
        scalars=(1,),
    )
    total1 = everyone(stat1)
    out = shape(3, rows, cols)
    duals, multipliers, slope2, mult2, stat2 = call(
        functools.partial(third_body, cells=cells),
        (out, out, out, out, spread),
        [
            pltpu.VMEM((2, wide - 2, frame, LANES), F32),
            pltpu.VMEM((3, wide - 1, frame, LANES), F32),
            pltpu.VMEM((3, 3, wide - 2, frame, LANES), F32),
        ],
        (
            total1, steps, near_box, base, mult1, slope1, duals1, last_mult, last_slope, last_pull,
            fwd, bwd, lower, upper, bias, value0, value1,
        ),
        2 * flops,
        scalars=(1,),
    )
    total2 = everyone(stat2)
    final_duals, final_multipliers, bounds = call(
        functools.partial(last_body, cells=cells),
        (out, out, shape(ITERS)),
        [],
        (total2, steps, duals, multipliers, slope2, mult2),
        1 << 20,
        scalar_outs=(2,),
        scalars=(1,),
    )
    return bounds, final_duals, final_multipliers


def solution(mesh):
    placed = (
        P("row", "col"),
        P("row", "col"),
        P("row", "col"),
        P(None, "row", "col"),
        P(None, "row", "col"),
        P(),
        P(),
        P(),
    )
    return jax.shard_map(
        shards,
        mesh=mesh,
        in_specs=placed,
        out_specs=(P(), P(None, "row", "col"), P(None, "row", "col")),
        check_vma=False,
    )
```

```python
import functools
import math

import jax
import jax.numpy as jnp
from jax import lax
from jax.experimental import pallas as pl
from jax.experimental.pallas import tpu as pltpu
from jax.sharding import PartitionSpec as P

CH = 64
LAYERS = 4
ITERS = 3
EPS = 1e-06
LANES = 2 * CH
HALO_PAIRS = 3
WIDE = 5
EDGE = 4
F32 = jnp.float32
BF16 = jnp.bfloat16

ROWS_SENT = (5, 5, 5, 4, 4, 4, 2, 3, 3)
ROW_START = tuple(sum(ROWS_SENT[:m]) for m in range(9))
SENT = sum(ROWS_SENT)
WINDOW = 4 * CH

VMEM = pl.BlockSpec(memory_space=pltpu.VMEM)
SMEM = pl.BlockSpec(memory_space=pltpu.SMEM)
HBM = pl.BlockSpec(memory_space=pltpu.HBM)


def call(body, outs, scratch, operands, flops, mem=20, scalars=(), far=(), scalar_outs=()):
    specs = [SMEM if j in scalars else HBM if j in far else VMEM for j in range(len(operands))]
    out_specs = tuple(SMEM if j in scalar_outs else VMEM for j in range(len(outs)))
    return pl.pallas_call(
        body,
        out_shape=outs,
        in_specs=specs,
        out_specs=out_specs,
        scratch_shapes=scratch,
        compiler_params=pltpu.CompilerParams(vmem_limit_bytes=mem << 20),
        cost_estimate=pl.CostEstimate(flops=flops, bytes_accessed=4 << 20, transcendentals=0),
    )(*operands)


def shape(*dims, dtype=F32):
    return jax.ShapeDtypeStruct(dims, dtype)


def copies(pairs, sem):
    made = [pltpu.make_async_copy(src, dst, sem.at[j]) for j, (src, dst) in enumerate(pairs)]
    for one in made:
        one.start()
    return made


def finish(made):
    for one in made:
        one.wait()


def split(value):
    high = value.astype(BF16)
    return high, (value - high.astype(F32)).astype(BF16)


def weights_body(kernels, biases, fwd, bwd, bias2):
    zero = jnp.zeros((CH, CH), F32)

    def put(dest, k, j, dh, first, second):
        high, low = split(jnp.concatenate([first, second], axis=1))
        for part, value in enumerate((low, high, high)):
            dest[k, pl.ds(WINDOW * part + CH * j, CH), pl.ds(LANES * dh, LANES)] = value

    for k in range(LAYERS):
        for dh in range(3):
            taps = [kernels[k * 9 + dh * 3 + dw] for dw in range(3)]
            if k < LAYERS - 1:
                for j in range(4):
                    put(fwd, k, j, dh, taps[j] if j < 3 else zero, taps[j - 1] if j > 0 else zero)
            flips = [tap.T for tap in taps]
            for j in range(4):
                put(bwd, k, j, 2 - dh, flips[2 - j] if j < 3 else zero, flips[3 - j] if j > 0 else zero)
    for k in range(LAYERS):
        row = biases[k : k + 1, :]
        bias2[k : k + 1, :] = jnp.concatenate([row, row], axis=1)


def weights(kernels, biases):
    size = (3 * WINDOW, 3 * LANES)
    return call(
        weights_body,
        (shape(LAYERS - 1, *size, dtype=BF16), shape(LAYERS, *size, dtype=BF16), shape(8, LANES)),
        [],
        (kernels.reshape(LAYERS * 9, CH, CH), biases),
        1 << 22,
    )


def sources(objective, center, radius, lower, upper):
    return [
        lambda cols: center[:, cols].astype(F32),
        lambda cols: upper[0, :, cols].astype(F32),
        lambda cols: upper[1, :, cols].astype(F32),
        lambda cols: upper[2, :, cols].astype(F32),
        lambda cols: lower[0, :, cols].astype(F32),
        lambda cols: lower[1, :, cols].astype(F32),
        lambda cols: lower[2, :, cols].astype(F32),
        lambda cols: radius[:, cols].astype(F32),
        lambda cols: objective[:, cols],
    ]


def ends_body(objective, center, radius, lower, upper, top, bottom, head, tail, *rest):
    rows, cols = objective.shape
    held, sem = rest[:5], rest[5]
    finish(copies(list(zip((objective, center, radius, lower, upper), held)), sem))
    strip = HALO_PAIRS * LANES
    for m, read in enumerate(sources(*held)):
        head[pl.ds(m * rows, rows), :] = read(pl.ds(0, strip))
        tail[pl.ds(m * rows, rows), :] = read(pl.ds(cols - strip, strip))
    row = lax.broadcasted_iota(jnp.int32, (rows, LANES), 0)
    outer = (row >= 2) & (row < rows - 2)
    for q in range(cols // LANES):
        values = [read(pl.ds(q * LANES, LANES)) for read in sources(*held)]
        values[3] = jnp.where(outer, values[3] - values[6], values[3])
        for m, value in enumerate(values):
            here = pl.ds(q * SENT + ROW_START[m], ROWS_SENT[m])
            top[here, :] = value[: ROWS_SENT[m]]
            bottom[here, :] = value[rows - ROWS_SENT[m] :]


def corners_body(above, below, after, head, tail):
    del after
    count = HALO_PAIRS * SENT
    size = above.shape[0]
    for part, source in enumerate((above, below)):
        here = pl.ds(part * count, count)
        head[here, :] = source[0:count, :]
        tail[here, :] = source[size - count : size, :]


def column(reads, left, right, rows, pairs, m, q):
    if q < HALO_PAIRS:
        return left[m * rows : (m + 1) * rows, q * LANES : (q + 1) * LANES]
    if q >= HALO_PAIRS + pairs:
        q -= HALO_PAIRS + pairs
        return right[m * rows : (m + 1) * rows, q * LANES : (q + 1) * LANES]
    return reads[m](pl.ds((q - HALO_PAIRS) * LANES, LANES))


def halo(middle, left, right, part, pairs, q, m):
    if q < HALO_PAIRS:
        source, at = left, part * HALO_PAIRS + q
    elif q >= HALO_PAIRS + pairs:
        source, at = right, part * HALO_PAIRS + q - HALO_PAIRS - pairs
    else:
        source, at = middle, q - HALO_PAIRS
    return source[pl.ds(at * SENT + ROW_START[m], ROWS_SENT[m]), :]


def neighbours(head, tail, axis):
    count = lax.axis_size(axis)
    before = lax.ppermute(tail, axis, [(i, i + 1) for i in range(count - 1)])
    after = lax.ppermute(head, axis, [(i + 1, i) for i in range(count - 1)])
    return before, after


def roll_rows(value, shift):
    return pltpu.roll(value, shift % value.shape[0], 0)


def slide(maps, count, store, produce):
    rows = store.shape[2]
    early = lax.broadcasted_iota(jnp.int32, (rows, LANES), 1) < CH
    zero = jnp.zeros((rows, LANES), F32)

    def step(q, carry):
        fresh = [pltpu.roll(value, CH, 1) for value in produce(q)]
        for k in range(maps):
            store[k, q] = jnp.where(early, carry[k], fresh[k])
        return tuple(fresh)

    last = lax.fori_loop(0, count, step, (zero,) * maps, unroll=2)
    for k in range(maps):
        store[k, count] = jnp.where(early, last[k], zero)


def multiply(store, k, first, count, weight, layer, sums, exact=False):
    rows = store.shape[2]
    left = store[k, pl.ds(first, count)].reshape(count * rows, LANES)
    right = store[k, pl.ds(first + 1, count)].reshape(count * rows, LANES)
    high, low = split(jnp.concatenate([left, right], axis=1))
    terms = [high, high] if exact else [high, high, low]
    result = jnp.dot(
        jnp.concatenate(terms, axis=1),
        weight[layer, 0 : WINDOW * len(terms), :],
        preferred_element_type=F32,
    )
    for d in range(3):
        sums[k, d, pl.ds(0, count)] = result[:, d * LANES : (d + 1) * LANES].reshape(count, rows, LANES)


def gathered(sums, k, q):
    return roll_rows(sums[k, 0, q], 1) + sums[k, 1, q] + roll_rows(sums[k, 2, q], -1)


def inner(sums, k, q, first, rows):
    parts = [roll_rows(sums[k, d, q], 1 - d - first)[:rows] for d in range(3)]
    return parts[0] + parts[1] + parts[2]


def summed(total):
    return jnp.sum(total[...], axis=0, keepdims=True)


def scale_of(total, step, cells, dims):
    squares = summed(total)[:, 0:1]
    return jnp.broadcast_to(step / jnp.sqrt(squares / (2 * (LAYERS - 1) * cells) + EPS), dims)


def soft(top, bend):
    return 0.5 * top * (1.0 - bend)


class Bound:
    def __init__(self, start):
        self.linear = start
        self.factor = None

    def add(self, t):
        bend = jnp.tanh(t)
        self.linear = self.linear + (jnp.minimum(t, 0.0) - 0.5 * math.log(2.0))
        factor = 1.0 + jnp.abs(bend)
        self.factor = factor if self.factor is None else self.factor * factor
        return bend

    def total(self):
        return self.linear + 0.5 * jnp.log(self.factor)


def folded(value):
    return jnp.sum(value, axis=0, keepdims=True)


def own_rows(value):
    rows = value.shape[0]
    row = lax.broadcasted_iota(jnp.int32, value.shape, 0)
    return folded(jnp.where((row >= EDGE) & (row < rows - EDGE), value, 0.0))


def stats(out, rows):
    lane = lax.broadcasted_iota(jnp.int32, (1, LANES), 1)
    packed = jnp.zeros((1, LANES), F32)
    for j, row in enumerate(rows):
        packed = jnp.where(lane == j, jnp.sum(row, axis=1, keepdims=True), packed)
    out[...] = jnp.broadcast_to(packed, out.shape)


def assemble(reads, above, below, left, right, corners, slots, rows, pairs, raw, gaps, target):
    frame = rows + 2 * EDGE
    blank = jnp.zeros((EDGE, LANES), F32)
    for slot, q in enumerate(slots):
        outside = not 1 <= q < pairs + 2 * HALO_PAIRS - 1
        for m in range(9):
            sent = ROWS_SENT[m]
            if m < 3:
                dest, at, edge = raw.at[m, slot], 0, WIDE
            else:
                dest, at, edge = (target.at[slot] if m == 8 else gaps.at[m - 3, slot]), EDGE - sent, EDGE
                if outside:
                    dest[...] = jnp.zeros((frame, LANES), F32)
                    continue
                if at:
                    dest[0:EDGE, :] = blank
                    dest[EDGE + rows : frame, :] = blank
            dest[at : at + sent, :] = halo(above, *corners, 0, pairs, q, m)
            dest[edge : edge + rows, :] = column(reads, left, right, rows, pairs, m, q)
            dest[edge + rows : edge + rows + sent, :] = halo(below, *corners, 1, pairs, q, m)
    count = len(slots)
    spare = raw.shape[2] - rows - 2 * WIDE
    raw[:, :, rows + 2 * WIDE :, :] = jnp.zeros((3, count, spare, LANES), F32)


def start_convs(raw, target, store, sums, fwd, bwd, frame):
    count = raw.shape[1]
    slide(3, count, store, lambda q: [raw[0, q], 0.5 * raw[1, q], 0.5 * raw[2, q]])
    tugged = store.at[3:4, :, 0:frame, :]
    slide(1, count, tugged, lambda q: [target[q]])
    for k in range(3):
        multiply(store, k, 1, count - 2, fwd, k, sums, exact=True)
    multiply(tugged, 0, 1, count - 2, bwd, LAYERS - 1, sums.at[3:4, :, :, 0:frame, :])


def start_step(slot, out, raw, gaps, target, sums, bias, near_box, far_box, back, slope, mult):
    frame = gaps.shape[2]
    near = [raw[m, slot][1 : 1 + frame] for m in range(3)] + [gaps[4, slot]]
    far = [gaps[m, slot] for m in range(4)]
    for m in range(4):
        near_box[m, out] = near[m].astype(BF16)
        far_box[m, out] = far[m].astype(BF16)
    new = jnp.zeros((frame, LANES), F32)
    for k in range(3):
        gap = near[1 + k] if k < 2 else far[0]
        dl = 0.5 * (gap - far[1 + k]) - inner(sums, k, slot - 1, 1, frame) - bias[k : k + 1, :]
        dl = jnp.where(near[1] > 0.0, dl, 0.0)
        slope[k, out] = dl
        new = new + dl * dl
    tug = gathered(sums.at[3:4, :, :, 0:frame, :], 0, slot - 1)
    back[out] = tug
    bound = Bound(jnp.full((frame, LANES), -4.5 * math.log(2.0), F32))
    dm = -0.5 * gap * bound.add(tug * gap)
    mult[out] = dm
    return new + dm * dm, bound.total(), target[slot] * bias[3:4, :]


def middle_body(
    objective, center, radius, lower, upper, above, below, fwd, bwd, bias,
    near_box, far_box, back, slope, mult, totals,
    raw, gaps, target, store, sums,
):
    rows, cols = objective.shape
    pairs = cols // LANES
    frame = rows + 2 * EDGE
    reads = sources(objective, center, radius, lower, upper)
    slots = range(HALO_PAIRS, HALO_PAIRS + pairs)
    assemble(reads, above, below, None, None, (None, None), slots, rows, pairs, raw, gaps, target)
    start_convs(raw, target, store, sums, fwd, bwd, frame)

    def step(q, carry):
        new = start_step(q + 1, q, raw, gaps, target, sums, bias, near_box, far_box, back, slope, mult)
        return tuple(old + one for old, one in zip(carry, new))

    zero = jnp.zeros((frame, LANES), F32)
    sizes = lax.fori_loop(0, pairs - 2, step, (zero, zero, zero), unroll=2)
    for j in range(3):
        totals[j] = sizes[j]


def first_body(
    objective, center, radius, lower, upper, left, right, above, below, left_corner, right_corner, fwd, bwd, bias,
    near_in, far_in, back_in, slope_in, mult_in, totals,
    near_box, far_box, back, slope, mult, stat, value,
    raw, gaps, target, store, sums,
):
    rows, cols = objective.shape
    pairs = cols // LANES
    frame = rows + 2 * EDGE
    wide = pairs + 4
    reads = sources(objective, center, radius, lower, upper)
    corners = (left_corner, right_corner)
    slots = list(range(5)) + list(range(wide - 3, wide + 2))
    assemble(reads, above, below, left, right, corners, slots, rows, pairs, raw, gaps, target)
    start_convs(raw, target, store, sums, fwd, bwd, frame)
    here = slice(3, wide - 3)
    near_box[:, here] = near_in[...]
    far_box[:, here] = far_in[...]
    back[here] = back_in[...]
    slope[:, here] = slope_in[...]
    mult[here] = mult_in[...]
    sizes = [totals[j] for j in range(3)]
    for slot, q in ((1, 0), (2, 1), (3, 2), (6, wide - 3), (7, wide - 2), (8, wide - 1)):
        new = start_step(slot, q, raw, gaps, target, sums, bias, near_box, far_box, back, slope, mult)
        if 2 <= q < wide - 2:
            sizes = [old + one for old, one in zip(sizes, new)]
    squares, worth, fixed = (own_rows(one) for one in sizes)
    stats(stat, [squares])
    stats(value, [worth + fixed, fixed])


def second_body(
    total, steps, near_box, far_box, back, slope, mult, fwd, bwd, bias,
    base, slope_out, mult_out, duals, last_mult, last_slope, last_pull, stat, value,
    points, worths, store, sums, *, cells,
):
    wide, frame = near_box.shape[1:3]
    inside = slice(EDGE, frame - EDGE)
    scale = scale_of(total, steps[0], cells, (frame, LANES))
    zero = jnp.zeros((frame, LANES), F32)
    slide(3, wide, store, lambda q: [slope[k, q] for k in range(3)])
    for k in range(3):
        multiply(store, k, 0, wide, bwd, k, sums)

    def produce(q):
        center, radius = near_box[0, q].astype(F32), near_box[3, q].astype(F32)
        g = -(scale * gathered(sums, 0, q))
        base[0, q] = g
        bound = Bound(g * (center - radius))
        outs = [center - radius * bound.add(2.0 * radius * g)]
        for k in (1, 2):
            gap = near_box[k, q].astype(F32)
            g = -(scale * gathered(sums, k, q))
            base[k, q] = g
            x = soft(gap, bound.add(g * gap))
            points[k - 1, q] = x
            outs.append(x)
        worths[q] = bound.total()
        return outs

    slide(3, wide, store, produce)
    for k in range(3):
        multiply(store, k, 1, wide - 2, fwd, k, sums)

    def step(j, carry):
        squares, worth = carry
        q = j + 1
        new = zero
        bound = Bound(worths[q])
        for k in range(3):
            gap = (near_box[1 + k, q] if k < 2 else far_box[0, q]).astype(F32)
            low = far_box[1 + k, q].astype(F32)
            lam = scale * slope[k, q]
            if k < 2:
                x = points[k, q]
                tp = lam * gap
            else:
                mu = scale * mult[q]
                g = back[q] + mu
                x = soft(gap, bound.add(g * gap))
                tp = (lam - mu) * gap
            positive = soft(gap, bound.add(tp))
            negative = soft(low, bound.add(-lam * low))
            bound.linear = bound.linear - lam * bias[k : k + 1, :]
            dl = positive - negative - gathered(sums, k, j) - bias[k : k + 1, :]
            dl = jnp.where(gap > 0.0, dl, 0.0)
            dm = x - positive
            slope_out[k, j] = dl
            duals[k, j] = lam[inside]
            if k < 2:
                mult_out[k, j] = dm
            else:
                last_mult[j] = mu[inside]
                last_slope[j] = dm[inside]
                last_pull[j] = g[inside]
            new = new + dl * dl + dm * dm
        own = (q >= 2) & (q < wide - 2)
        return squares + jnp.where(own, new, 0.0), worth + jnp.where(own, bound.total(), 0.0)

    squares, worth = lax.fori_loop(0, wide - 2, step, (zero, zero), unroll=2)
    stats(stat, [own_rows(squares)])
    stats(value, [own_rows(worth)])


def third_body(
    total, steps, near_box, base, mult, slope, duals1, last_mult, last_slope, last_pull,
    fwd, bwd, lower, upper, bias, value0, value1,
    duals, multipliers, slope_out, mult_out, stat,
    points, store, sums, *, cells,
):
    wide, frame = near_box.shape[1:3]
    rows = frame - 2 * EDGE
    inside = slice(EDGE, frame - EDGE)
    scale = scale_of(total, steps[1], cells, (frame, LANES))
    zero = jnp.zeros((frame, LANES), F32)
    slide(3, wide - 2, store, lambda j: [slope[k, j] for k in range(3)])
    for k in range(3):
        multiply(store, k, 0, wide - 2, bwd, k, sums)
    early = lax.broadcasted_iota(jnp.int32, (frame, LANES), 1) < CH

    def point(j, carry):
        q = j + 1
        center, radius = near_box[0, q].astype(F32), near_box[3, q].astype(F32)
        g = base[0, q] - scale * gathered(sums, 0, j)
        bound = Bound(g * (center - radius))
        outs = [center - radius * bound.add(2.0 * radius * g)]
        for k in (1, 2):
            gap = near_box[k, q].astype(F32)
            t = (base[k, q] + scale * (mult[k - 1, j] - gathered(sums, k, j))) * gap
            x = soft(gap, bound.add(t))
            points[k - 1, j] = x
            outs.append(x)
        own = (q >= 2) & (q < wide - 2)
        fresh = [pltpu.roll(value, CH, 1) for value in outs]
        for k in range(3):
            store[k, j] = jnp.where(early, carry[k], fresh[k])
        return tuple(fresh) + (carry[3] + jnp.where(own, bound.total(), 0.0),)

    framed = lax.fori_loop(0, wide - 2, point, (zero,) * 4, unroll=2)[3]
    for k in range(3):
        multiply(store, k, 1, wide - 4, fwd, k, sums)

    scale = scale[:rows]

    def step(i, carry):
        squares, worth = carry
        j = i + 1
        here = pl.ds(pl.multiple_of(i * LANES, LANES), LANES)
        bound = Bound(jnp.zeros((rows, LANES), F32))
        for k in range(3):
            gap = upper[k, :, here].astype(F32)
            low = lower[k, :, here].astype(F32)
            lam = duals1[k, j] + scale * slope[k, j, inside, :]
            bound.linear = bound.linear - lam * bias[k : k + 1, :]
            if k < 2:
                x = points[k, j, inside, :]
                mu = scale * mult[k, j, inside, :]
            else:
                change = scale * last_slope[j]
                mu = last_mult[j] + change
                x = soft(gap, bound.add((last_pull[j] + change) * gap))
            positive = soft(gap, bound.add((lam - mu) * gap))
            negative = soft(low, bound.add(-lam * low))
            dl = positive - negative - inner(sums, k, i, EDGE, rows) - bias[k : k + 1, :]
            dm = x - positive
            duals[k, :, here] = lam
            multipliers[k, :, here] = mu
            slope_out[k, :, here] = dl
            mult_out[k, :, here] = dm
            squares = squares + dl * dl + dm * dm
        return squares, worth + bound.total()

    zero = jnp.zeros((rows, LANES), F32)
    squares, worth = lax.fori_loop(0, wide - 4, step, (zero, zero), unroll=2)
    lane = lax.broadcasted_iota(jnp.int32, (1, LANES), 1)
    start, fixed = (jnp.where(lane == j, value0[0:1, :], 0.0) for j in range(2))
    middle = jnp.where(lane == 0, value1[0:1, :], 0.0)
    stats(stat, [folded(squares), start, middle + fixed, folded(worth) + own_rows(framed) + fixed])


def last_body(total, steps, duals, multipliers, slope, mult, duals_out, mult_out, bounds, *, cells):
    scale = scale_of(total, steps[2], cells, duals.shape[1:])
    for k in range(LAYERS - 1):
        duals_out[k] = duals[k] + scale * slope[k]
        mult_out[k] = multipliers[k] + scale * mult[k]
    values = summed(total) / cells
    lane = lax.broadcasted_iota(jnp.int32, (1, LANES), 1)
    for j in range(ITERS):
        bounds[j] = jnp.sum(jnp.where(lane == j + 1, values, 0.0))


def everyone(partial):
    return lax.all_to_all(partial, ("row", "col"), 0, 0, tiled=True)


def shards(objective, center, radius, lower, upper, kernels, biases, steps):
    rows, cols = objective.shape
    pairs = cols // LANES
    wide = pairs + 4
    frame = rows + 2 * EDGE
    tall = -(-(rows + 2 * WIDE) // 8) * 8
    cells = rows * cols * lax.axis_size("row") * lax.axis_size("col")
    inputs = (objective, center, radius, lower, upper)
    flops = 3 * 2 * 3 * wide * frame * 4 * CH * 3 * LANES
    spread = shape(lax.axis_size("row") * lax.axis_size("col"), LANES)
    small = shape(8, LANES)

    ends = shape(pairs * SENT, LANES)
    strip = shape(9 * rows, HALO_PAIRS * LANES)
    top, bottom, head, tail = call(
        ends_body,
        (ends, ends, strip, strip),
        [pltpu.VMEM(one.shape, one.dtype) for one in inputs] + [pltpu.SemaphoreType.DMA((5,))],
        inputs,
        1 << 20,
        mem=58,
        far=range(5),
    )
    above, below = neighbours(top, bottom, "row")
    left, right = neighbours(head, tail, "col")
    fwd, bwd, bias = weights(kernels, biases)
    corner = shape(2 * HALO_PAIRS * SENT, LANES)
    corner_head, corner_tail = call(corners_body, (corner, corner), [], (above, below, bias), 1 << 20)
    left_corner, right_corner = neighbours(corner_head, corner_tail, "col")

    def start_scratch(count):
        return [
            pltpu.VMEM((3, count, tall, LANES), F32),
            pltpu.VMEM((5, count, frame, LANES), F32),
            pltpu.VMEM((count, frame, LANES), F32),
            pltpu.VMEM((4, count + 1, tall, LANES), F32),
            pltpu.VMEM((4, 3, count - 2, tall, LANES), F32),
        ]

    def start_shapes(count):
        box = shape(4, count, frame, LANES, dtype=BF16)
        full = shape(count, frame, LANES)
        return box, box, full, shape(3, count, frame, LANES), full

    middle = call(
        middle_body,
        start_shapes(pairs - 2) + (shape(3, frame, LANES),),
        start_scratch(pairs),
        inputs + (above, below, fwd, bwd, bias),
        flops,
    )
    near_box, far_box, back, slope0, mult0, stat0, value0 = call(
        first_body,
        start_shapes(wide) + (spread, small),
        start_scratch(10),
        inputs + (left, right, above, below, left_corner, right_corner, fwd, bwd, bias) + tuple(middle),
        flops,
    )

    total0 = everyone(stat0)
    tile = shape(wide - 2, rows, LANES)
    base, slope1, mult1, duals1, last_mult, last_slope, last_pull, stat1, value1 = call(
        functools.partial(second_body, cells=cells),
        (
            shape(3, wide, frame, LANES),
            shape(3, wide - 2, frame, LANES),
            shape(2, wide - 2, frame, LANES),
            shape(3, wide - 2, rows, LANES),
            tile,
            tile,
            tile,
            spread,
            small,
        ),
        [
            pltpu.VMEM((2, wide, frame, LANES), F32),
            pltpu.VMEM((wide, frame, LANES), F32),
            pltpu.VMEM((3, wide + 1, frame, LANES), F32),
            pltpu.VMEM((3, 3, wide, frame, LANES), F32),
        ],
        (total0, steps, near_box, far_box, back, slope0, mult0, fwd, bwd, bias),
        2 * flops,
        scalars=(1,),
    )
    total1 = everyone(stat1)
    out = shape(3, rows, cols)
    duals, multipliers, slope2, mult2, stat2 = call(
        functools.partial(third_body, cells=cells),
        (out, out, out, out, spread),
        [
            pltpu.VMEM((2, wide - 2, frame, LANES), F32),
            pltpu.VMEM((3, wide - 1, frame, LANES), F32),
            pltpu.VMEM((3, 3, wide - 2, frame, LANES), F32),
        ],
        (
            total1, steps, near_box, base, mult1, slope1, duals1, last_mult, last_slope, last_pull,
            fwd, bwd, lower, upper, bias, value0, value1,
        ),
        2 * flops,
        scalars=(1,),
    )
    total2 = everyone(stat2)
    final_duals, final_multipliers, bounds = call(
        functools.partial(last_body, cells=cells),
        (out, out, shape(ITERS)),
        [],
        (total2, steps, duals, multipliers, slope2, mult2),
        1 << 20,
        scalar_outs=(2,),
        scalars=(1,),
    )
    return bounds, final_duals, final_multipliers


def solution(mesh):
    placed = (
        P("row", "col"),
        P("row", "col"),
        P("row", "col"),
        P(None, "row", "col"),
        P(None, "row", "col"),
        P(),
        P(),
        P(),
    )
    return jax.shard_map(
        shards,
        mesh=mesh,
        in_specs=placed,
        out_specs=(P(), P(None, "row", "col"), P(None, "row", "col")),
        check_vma=False,
    )
```

```python
import functools
import math

import jax
import jax.numpy as jnp
from jax import lax
from jax.experimental import pallas as pl
from jax.experimental.pallas import tpu as pltpu
from jax.sharding import PartitionSpec as P

CH = 64
LAYERS = 4
ITERS = 3
EPS = 1e-06
LANES = 2 * CH
HALO_PAIRS = 3
WIDE = 5
EDGE = 4
F32 = jnp.float32
BF16 = jnp.bfloat16

ROWS_SENT = (5, 5, 5, 4, 4, 4, 2, 3, 3)
ROW_START = tuple(sum(ROWS_SENT[:m]) for m in range(9))
SENT = sum(ROWS_SENT)
OUTER = 3 * WIDE
CORNER = (0, OUTER, OUTER + SENT, OUTER + 2 * SENT, OUTER + 3 * SENT, OUTER + 4 * SENT, 2 * OUTER + 4 * SENT)
WINDOW = 4 * CH

VMEM = pl.BlockSpec(memory_space=pltpu.VMEM)
SMEM = pl.BlockSpec(memory_space=pltpu.SMEM)
HBM = pl.BlockSpec(memory_space=pltpu.HBM)


def call(body, outs, scratch, operands, flops, mem=20, scalars=(), far=(), scalar_outs=()):
    specs = [SMEM if j in scalars else HBM if j in far else VMEM for j in range(len(operands))]
    out_specs = tuple(SMEM if j in scalar_outs else VMEM for j in range(len(outs)))
    return pl.pallas_call(
        body,
        out_shape=outs,
        in_specs=specs,
        out_specs=out_specs,
        scratch_shapes=scratch,
        compiler_params=pltpu.CompilerParams(vmem_limit_bytes=mem << 20),
        cost_estimate=pl.CostEstimate(flops=flops, bytes_accessed=4 << 20, transcendentals=0),
    )(*operands)


def shape(*dims, dtype=F32):
    return jax.ShapeDtypeStruct(dims, dtype)


def copies(pairs, sem):
    made = [pltpu.make_async_copy(src, dst, sem.at[j]) for j, (src, dst) in enumerate(pairs)]
    for one in made:
        one.start()
    return made


def finish(made):
    for one in made:
        one.wait()


def split(value):
    high = value.astype(BF16)
    return high, (value - high.astype(F32)).astype(BF16)


def weights_body(kernels, biases, fwd, bwd, bias2):
    zero = jnp.zeros((CH, CH), F32)

    def put(dest, k, j, dh, first, second):
        high, low = split(jnp.concatenate([first, second], axis=1))
        for part, value in enumerate((low, high, high)):
            dest[k, pl.ds(WINDOW * part + CH * j, CH), pl.ds(LANES * dh, LANES)] = value

    for k in range(LAYERS):
        for dh in range(3):
            taps = [kernels[k * 9 + dh * 3 + dw] for dw in range(3)]
            if k < LAYERS - 1:
                for j in range(4):
                    put(fwd, k, j, dh, taps[j] if j < 3 else zero, taps[j - 1] if j > 0 else zero)
            flips = [tap.T for tap in taps]
            for j in range(4):
                put(bwd, k, j, 2 - dh, flips[2 - j] if j < 3 else zero, flips[3 - j] if j > 0 else zero)
    for k in range(LAYERS):
        row = biases[k : k + 1, :]
        bias2[k : k + 1, :] = jnp.concatenate([row, row], axis=1)


def weights(kernels, biases):
    size = (3 * WINDOW, 3 * LANES)
    return call(
        weights_body,
        (shape(LAYERS - 1, *size, dtype=BF16), shape(LAYERS, *size, dtype=BF16), shape(8, LANES)),
        [],
        (kernels.reshape(LAYERS * 9, CH, CH), biases),
        1 << 22,
    )


def sources(objective, center, radius, lower, upper):
    return [
        lambda cols: center[:, cols].astype(F32),
        lambda cols: upper[0, :, cols].astype(F32),
        lambda cols: upper[1, :, cols].astype(F32),
        lambda cols: upper[2, :, cols].astype(F32),
        lambda cols: lower[0, :, cols].astype(F32),
        lambda cols: lower[1, :, cols].astype(F32),
        lambda cols: lower[2, :, cols].astype(F32),
        lambda cols: radius[:, cols].astype(F32),
        lambda cols: objective[:, cols],
    ]


def ends_body(objective, center, radius, lower, upper, top, bottom, head, tail, *rest):
    rows, cols = objective.shape
    held, sem = rest[:5], rest[5]
    finish(copies(list(zip((objective, center, radius, lower, upper), held)), sem))
    strip = HALO_PAIRS * LANES
    for m, read in enumerate(sources(*held)):
        head[pl.ds(m * rows, rows), :] = read(pl.ds(0, strip))
        tail[pl.ds(m * rows, rows), :] = read(pl.ds(cols - strip, strip))
    for q in range(cols // LANES):
        ends_of([read(pl.ds(q * LANES, LANES)) for read in sources(*held)], top, bottom, q * SENT)


def ends_of(values, top, bottom, start):
    rows = values[0].shape[0]
    if len(values) > 3:
        row = lax.broadcasted_iota(jnp.int32, (rows, LANES), 0)
        outer = (row >= 2) & (row < rows - 2)
        values[3] = jnp.where(outer, values[3] - values[6], values[3])
    for m, value in enumerate(values):
        here = pl.ds(start + ROW_START[m], ROWS_SENT[m])
        top[here, :] = value[: ROWS_SENT[m]]
        bottom[here, :] = value[rows - ROWS_SENT[m] :]


def corners_body(left, right, top, bottom):
    rows = left.shape[0] // 9
    for j in range(2 * HALO_PAIRS):
        strip, q = (left, j) if j < HALO_PAIRS else (right, j - HALO_PAIRS)
        maps = 3 if j in (0, 2 * HALO_PAIRS - 1) else 9
        values = [strip[pl.ds(m * rows, rows), pl.ds(q * LANES, LANES)] for m in range(maps)]
        ends_of(values, top, bottom, CORNER[j])


def column(reads, left, right, rows, pairs, m, q):
    if q < HALO_PAIRS:
        return left[m * rows : (m + 1) * rows, q * LANES : (q + 1) * LANES]
    if q >= HALO_PAIRS + pairs:
        q -= HALO_PAIRS + pairs
        return right[m * rows : (m + 1) * rows, q * LANES : (q + 1) * LANES]
    return reads[m](pl.ds((q - HALO_PAIRS) * LANES, LANES))


def halo(middle, corner, pairs, q, m):
    if HALO_PAIRS <= q < HALO_PAIRS + pairs:
        source, start = middle, (q - HALO_PAIRS) * SENT
    else:
        source, start = corner, CORNER[q if q < HALO_PAIRS else q - pairs]
    return source[pl.ds(start + ROW_START[m], ROWS_SENT[m]), :]


def neighbours(head, tail, axis):
    count = lax.axis_size(axis)
    before = lax.ppermute(tail, axis, [(i, i + 1) for i in range(count - 1)])
    after = lax.ppermute(head, axis, [(i + 1, i) for i in range(count - 1)])
    return before, after


def roll_rows(value, shift):
    return pltpu.roll(value, shift % value.shape[0], 0)


def slide(maps, count, store, produce):
    rows = store.shape[2]
    early = lax.broadcasted_iota(jnp.int32, (rows, LANES), 1) < CH
    zero = jnp.zeros((rows, LANES), F32)

    def step(q, carry):
        fresh = [pltpu.roll(value, CH, 1) for value in produce(q)]
        for k in range(maps):
            store[k, q] = jnp.where(early, carry[k], fresh[k])
        return tuple(fresh)

    last = lax.fori_loop(0, count, step, (zero,) * maps, unroll=2)
    for k in range(maps):
        store[k, count] = jnp.where(early, last[k], zero)


def multiply(store, k, first, count, weight, layer, sums, exact=False):
    rows = store.shape[2]
    left = store[k, pl.ds(first, count)].reshape(count * rows, LANES)
    right = store[k, pl.ds(first + 1, count)].reshape(count * rows, LANES)
    high, low = split(jnp.concatenate([left, right], axis=1))
    terms = [high, high] if exact else [high, high, low]
    result = jnp.dot(
        jnp.concatenate(terms, axis=1),
        weight[layer, 0 : WINDOW * len(terms), :],
        preferred_element_type=F32,
    )
    for d in range(3):
        sums[k, d, pl.ds(0, count)] = result[:, d * LANES : (d + 1) * LANES].reshape(count, rows, LANES)


def gathered(sums, k, q):
    return roll_rows(sums[k, 0, q], 1) + sums[k, 1, q] + roll_rows(sums[k, 2, q], -1)


def inner(sums, k, q, first, rows):
    parts = [roll_rows(sums[k, d, q], 1 - d - first)[:rows] for d in range(3)]
    return parts[0] + parts[1] + parts[2]


def summed(total):
    return jnp.sum(total[...], axis=0, keepdims=True)


def scale_of(total, step, cells, dims):
    squares = summed(total)[:, 0:1]
    return jnp.broadcast_to(step / jnp.sqrt(squares / (2 * (LAYERS - 1) * cells) + EPS), dims)


def soft(top, bend):
    return 0.5 * top * (1.0 - bend)


class Bound:
    def __init__(self, start):
        self.linear = start
        self.factor = None

    def add(self, t):
        bend = jnp.tanh(t)
        self.linear = self.linear + (jnp.minimum(t, 0.0) - 0.5 * math.log(2.0))
        factor = 1.0 + jnp.abs(bend)
        self.factor = factor if self.factor is None else self.factor * factor
        return bend

    def total(self):
        return self.linear + 0.5 * jnp.log(self.factor)


def folded(value):
    return jnp.sum(value, axis=0, keepdims=True)


def own_rows(value):
    rows = value.shape[0]
    row = lax.broadcasted_iota(jnp.int32, value.shape, 0)
    return folded(jnp.where((row >= EDGE) & (row < rows - EDGE), value, 0.0))


def stats(out, rows):
    lane = lax.broadcasted_iota(jnp.int32, (1, LANES), 1)
    packed = jnp.zeros((1, LANES), F32)
    for j, row in enumerate(rows):
        packed = jnp.where(lane == j, jnp.sum(row, axis=1, keepdims=True), packed)
    out[...] = jnp.broadcast_to(packed, out.shape)


def assemble(reads, above, below, left, right, corners, slots, rows, pairs, raw, gaps, target):
    frame = rows + 2 * EDGE
    blank = jnp.zeros((EDGE, LANES), F32)
    for slot, q in enumerate(slots):
        outside = not 1 <= q < pairs + 2 * HALO_PAIRS - 1
        for m in range(9):
            sent = ROWS_SENT[m]
            if m < 3:
                dest, at, edge = raw.at[m, slot], 0, WIDE
            else:
                dest, at, edge = (target.at[slot] if m == 8 else gaps.at[m - 3, slot]), EDGE - sent, EDGE
                if outside:
                    dest[...] = jnp.zeros((frame, LANES), F32)
                    continue
                if at:
                    dest[0:EDGE, :] = blank
                    dest[EDGE + rows : frame, :] = blank
            dest[at : at + sent, :] = halo(above, corners[0], pairs, q, m)
            dest[edge : edge + rows, :] = column(reads, left, right, rows, pairs, m, q)
            dest[edge + rows : edge + rows + sent, :] = halo(below, corners[1], pairs, q, m)
    count = len(slots)
    spare = raw.shape[2] - rows - 2 * WIDE
    raw[:, :, rows + 2 * WIDE :, :] = jnp.zeros((3, count, spare, LANES), F32)


def start_convs(raw, target, store, sums, fwd, bwd, frame):
    count = raw.shape[1]
    slide(3, count, store, lambda q: [raw[0, q], 0.5 * raw[1, q], 0.5 * raw[2, q]])
    tugged = store.at[3:4, :, 0:frame, :]
    slide(1, count, tugged, lambda q: [target[q]])
    for k in range(3):
        multiply(store, k, 1, count - 2, fwd, k, sums, exact=True)
    multiply(tugged, 0, 1, count - 2, bwd, LAYERS - 1, sums.at[3:4, :, :, 0:frame, :])


def start_step(slot, out, raw, gaps, target, sums, bias, near_box, far_box, back, slope, mult):
    frame = gaps.shape[2]
    near = [raw[m, slot][1 : 1 + frame] for m in range(3)] + [gaps[4, slot]]
    far = [gaps[m, slot] for m in range(4)]
    for m in range(4):
        near_box[m, out] = near[m].astype(BF16)
        far_box[m, out] = far[m].astype(BF16)
    new = jnp.zeros((frame, LANES), F32)
    for k in range(3):
        gap = near[1 + k] if k < 2 else far[0]
        dl = 0.5 * (gap - far[1 + k]) - inner(sums, k, slot - 1, 1, frame) - bias[k : k + 1, :]
        dl = jnp.where(near[1] > 0.0, dl, 0.0)
        slope[k, out] = dl
        new = new + dl * dl
    tug = gathered(sums.at[3:4, :, :, 0:frame, :], 0, slot - 1)
    back[out] = tug
    bound = Bound(jnp.full((frame, LANES), -4.5 * math.log(2.0), F32))
    dm = -0.5 * gap * bound.add(tug * gap)
    mult[out] = dm
    return new + dm * dm, bound.total(), target[slot] * bias[3:4, :]


def middle_body(
    objective, center, radius, lower, upper, above, below, fwd, bwd, bias,
    near_box, far_box, back, slope, mult, totals,
    raw, gaps, target, store, sums,
):
    rows, cols = objective.shape
    pairs = cols // LANES
    frame = rows + 2 * EDGE
    reads = sources(objective, center, radius, lower, upper)
    slots = range(HALO_PAIRS, HALO_PAIRS + pairs)
    assemble(reads, above, below, None, None, (None, None), slots, rows, pairs, raw, gaps, target)
    start_convs(raw, target, store, sums, fwd, bwd, frame)

    def step(q, carry):
        new = start_step(q + 1, q, raw, gaps, target, sums, bias, near_box, far_box, back, slope, mult)
        return tuple(old + one for old, one in zip(carry, new))

    zero = jnp.zeros((frame, LANES), F32)
    sizes = lax.fori_loop(0, pairs - 2, step, (zero, zero, zero), unroll=2)
    for j in range(3):
        totals[j] = sizes[j]


def first_body(
    objective, center, radius, lower, upper, left, right, above, below, above_corner, below_corner, fwd, bwd, bias,
    near_in, far_in, back_in, slope_in, mult_in, totals,
    near_box, far_box, back, slope, mult, stat, value,
    raw, gaps, target, store, sums,
):
    rows, cols = objective.shape
    pairs = cols // LANES
    frame = rows + 2 * EDGE
    wide = pairs + 4
    reads = sources(objective, center, radius, lower, upper)
    corners = (above_corner, below_corner)
    slots = list(range(5)) + list(range(wide - 3, wide + 2))
    assemble(reads, above, below, left, right, corners, slots, rows, pairs, raw, gaps, target)
    start_convs(raw, target, store, sums, fwd, bwd, frame)
    here = slice(3, wide - 3)
    near_box[:, here] = near_in[...]
    far_box[:, here] = far_in[...]
    back[here] = back_in[...]
    slope[:, here] = slope_in[...]
    mult[here] = mult_in[...]
    sizes = [totals[j] for j in range(3)]
    for slot, q in ((1, 0), (2, 1), (3, 2), (6, wide - 3), (7, wide - 2), (8, wide - 1)):
        new = start_step(slot, q, raw, gaps, target, sums, bias, near_box, far_box, back, slope, mult)
        if 2 <= q < wide - 2:
            sizes = [old + one for old, one in zip(sizes, new)]
    squares, worth, fixed = (own_rows(one) for one in sizes)
    stats(stat, [squares])
    stats(value, [worth + fixed, fixed])


def second_body(
    total, steps, near_box, far_box, back, slope, mult, fwd, bwd, bias,
    base, slope_out, mult_out, duals, last_mult, last_slope, last_pull, stat, value,
    points, worths, store, sums, *, cells,
):
    wide, frame = near_box.shape[1:3]
    inside = slice(EDGE, frame - EDGE)
    scale = scale_of(total, steps[0], cells, (frame, LANES))
    zero = jnp.zeros((frame, LANES), F32)
    slide(3, wide, store, lambda q: [slope[k, q] for k in range(3)])
    for k in range(3):
        multiply(store, k, 0, wide, bwd, k, sums)

    def produce(q):
        center, radius = near_box[0, q].astype(F32), near_box[3, q].astype(F32)
        g = -(scale * gathered(sums, 0, q))
        base[0, q] = g
        bound = Bound(g * (center - radius))
        outs = [center - radius * bound.add(2.0 * radius * g)]
        for k in (1, 2):
            gap = near_box[k, q].astype(F32)
            g = -(scale * gathered(sums, k, q))
            base[k, q] = g
            x = soft(gap, bound.add(g * gap))
            points[k - 1, q] = x
            outs.append(x)
        worths[q] = bound.total()
        return outs

    slide(3, wide, store, produce)
    for k in range(3):
        multiply(store, k, 1, wide - 2, fwd, k, sums)

    def step(j, carry):
        squares, worth = carry
        q = j + 1
        new = zero
        bound = Bound(worths[q])
        for k in range(3):
            gap = (near_box[1 + k, q] if k < 2 else far_box[0, q]).astype(F32)
            low = far_box[1 + k, q].astype(F32)
            lam = scale * slope[k, q]
            if k < 2:
                x = points[k, q]
                tp = lam * gap
            else:
                mu = scale * mult[q]
                g = back[q] + mu
                x = soft(gap, bound.add(g * gap))
                tp = (lam - mu) * gap
            positive = soft(gap, bound.add(tp))
            negative = soft(low, bound.add(-lam * low))
            bound.linear = bound.linear - lam * bias[k : k + 1, :]
            dl = positive - negative - gathered(sums, k, j) - bias[k : k + 1, :]
            dl = jnp.where(gap > 0.0, dl, 0.0)
            dm = x - positive
            slope_out[k, j] = dl
            duals[k, j] = lam[inside]
            if k < 2:
                mult_out[k, j] = dm
            else:
                last_mult[j] = mu[inside]
                last_slope[j] = dm[inside]
                last_pull[j] = g[inside]
            new = new + dl * dl + dm * dm
        own = (q >= 2) & (q < wide - 2)
        return squares + jnp.where(own, new, 0.0), worth + jnp.where(own, bound.total(), 0.0)

    squares, worth = lax.fori_loop(0, wide - 2, step, (zero, zero), unroll=2)
    stats(stat, [own_rows(squares)])
    stats(value, [own_rows(worth)])


def third_body(
    total, steps, near_box, base, mult, slope, duals1, last_mult, last_slope, last_pull,
    fwd, bwd, lower, upper, bias, value0, value1,
    duals, multipliers, slope_out, mult_out, stat,
    points, store, sums, *, cells,
):
    wide, frame = near_box.shape[1:3]
    rows = frame - 2 * EDGE
    inside = slice(EDGE, frame - EDGE)
    scale = scale_of(total, steps[1], cells, (frame, LANES))
    zero = jnp.zeros((frame, LANES), F32)
    slide(3, wide - 2, store, lambda j: [slope[k, j] for k in range(3)])
    for k in range(3):
        multiply(store, k, 0, wide - 2, bwd, k, sums)
    early = lax.broadcasted_iota(jnp.int32, (frame, LANES), 1) < CH

    def point(j, carry):
        q = j + 1
        center, radius = near_box[0, q].astype(F32), near_box[3, q].astype(F32)
        g = base[0, q] - scale * gathered(sums, 0, j)
        bound = Bound(g * (center - radius))
        outs = [center - radius * bound.add(2.0 * radius * g)]
        for k in (1, 2):
            gap = near_box[k, q].astype(F32)
            t = (base[k, q] + scale * (mult[k - 1, j] - gathered(sums, k, j))) * gap
            x = soft(gap, bound.add(t))
            points[k - 1, j] = x
            outs.append(x)
        own = (q >= 2) & (q < wide - 2)
        fresh = [pltpu.roll(value, CH, 1) for value in outs]
        for k in range(3):
            store[k, j] = jnp.where(early, carry[k], fresh[k])
        return tuple(fresh) + (carry[3] + jnp.where(own, bound.total(), 0.0),)

    framed = lax.fori_loop(0, wide - 2, point, (zero,) * 4, unroll=2)[3]
    for k in range(3):
        multiply(store, k, 1, wide - 4, fwd, k, sums)

    scale = scale[:rows]

    def step(i, carry):
        squares, worth = carry
        j = i + 1
        here = pl.ds(pl.multiple_of(i * LANES, LANES), LANES)
        bound = Bound(jnp.zeros((rows, LANES), F32))
        for k in range(3):
            gap = upper[k, :, here].astype(F32)
            low = lower[k, :, here].astype(F32)
            lam = duals1[k, j] + scale * slope[k, j, inside, :]
            bound.linear = bound.linear - lam * bias[k : k + 1, :]
            if k < 2:
                x = points[k, j, inside, :]
                mu = scale * mult[k, j, inside, :]
            else:
                change = scale * last_slope[j]
                mu = last_mult[j] + change
                x = soft(gap, bound.add((last_pull[j] + change) * gap))
            positive = soft(gap, bound.add((lam - mu) * gap))
            negative = soft(low, bound.add(-lam * low))
            dl = positive - negative - inner(sums, k, i, EDGE, rows) - bias[k : k + 1, :]
            dm = x - positive
            duals[k, :, here] = lam
            multipliers[k, :, here] = mu
            slope_out[k, :, here] = dl
            mult_out[k, :, here] = dm
            squares = squares + dl * dl + dm * dm
        return squares, worth + bound.total()

    zero = jnp.zeros((rows, LANES), F32)
    squares, worth = lax.fori_loop(0, wide - 4, step, (zero, zero), unroll=2)
    lane = lax.broadcasted_iota(jnp.int32, (1, LANES), 1)
    start, fixed = (jnp.where(lane == j, value0[0:1, :], 0.0) for j in range(2))
    middle = jnp.where(lane == 0, value1[0:1, :], 0.0)
    stats(stat, [folded(squares), start, middle + fixed, folded(worth) + own_rows(framed) + fixed])


def last_body(total, steps, duals, multipliers, slope, mult, duals_out, mult_out, bounds, *, cells):
    scale = scale_of(total, steps[2], cells, duals.shape[1:])
    for k in range(LAYERS - 1):
        duals_out[k] = duals[k] + scale * slope[k]
        mult_out[k] = multipliers[k] + scale * mult[k]
    values = summed(total) / cells
    lane = lax.broadcasted_iota(jnp.int32, (1, LANES), 1)
    for j in range(ITERS):
        bounds[j] = jnp.sum(jnp.where(lane == j + 1, values, 0.0))


def everyone(partial):
    return lax.all_to_all(partial, ("row", "col"), 0, 0, tiled=True)


def shards(objective, center, radius, lower, upper, kernels, biases, steps):
    rows, cols = objective.shape
    pairs = cols // LANES
    wide = pairs + 4
    frame = rows + 2 * EDGE
    tall = -(-(rows + 2 * WIDE) // 8) * 8
    cells = rows * cols * lax.axis_size("row") * lax.axis_size("col")
    inputs = (objective, center, radius, lower, upper)
    flops = 3 * 2 * 3 * wide * frame * 4 * CH * 3 * LANES
    spread = shape(lax.axis_size("row") * lax.axis_size("col"), LANES)
    small = shape(8, LANES)

    ends = shape(pairs * SENT, LANES)
    strip = shape(9 * rows, HALO_PAIRS * LANES)
    top, bottom, head, tail = call(
        ends_body,
        (ends, ends, strip, strip),
        [pltpu.VMEM(one.shape, one.dtype) for one in inputs] + [pltpu.SemaphoreType.DMA((5,))],
        inputs,
        1 << 20,
        mem=58,
        far=range(5),
    )
    above, below = neighbours(top, bottom, "row")
    left, right = neighbours(head, tail, "col")
    fwd, bwd, bias = weights(kernels, biases)
    corner = shape(CORNER[-1], LANES)
    corner_top, corner_bottom = call(corners_body, (corner, corner), [], (left, right), 1 << 20)
    above_corner, below_corner = neighbours(corner_top, corner_bottom, "row")

    def start_scratch(count):
        return [
            pltpu.VMEM((3, count, tall, LANES), F32),
            pltpu.VMEM((5, count, frame, LANES), F32),
            pltpu.VMEM((count, frame, LANES), F32),
            pltpu.VMEM((4, count + 1, tall, LANES), F32),
            pltpu.VMEM((4, 3, count - 2, tall, LANES), F32),
        ]

    def start_shapes(count):
        box = shape(4, count, frame, LANES, dtype=BF16)
        full = shape(count, frame, LANES)
        return box, box, full, shape(3, count, frame, LANES), full

    middle = call(
        middle_body,
        start_shapes(pairs - 2) + (shape(3, frame, LANES),),
        start_scratch(pairs),
        inputs + (above, below, fwd, bwd, bias),
        flops,
    )
    near_box, far_box, back, slope0, mult0, stat0, value0 = call(
        first_body,
        start_shapes(wide) + (spread, small),
        start_scratch(10),
        inputs + (left, right, above, below, above_corner, below_corner, fwd, bwd, bias) + tuple(middle),
        flops,
    )

    total0 = everyone(stat0)
    tile = shape(wide - 2, rows, LANES)
    base, slope1, mult1, duals1, last_mult, last_slope, last_pull, stat1, value1 = call(
        functools.partial(second_body, cells=cells),
        (
            shape(3, wide, frame, LANES),
            shape(3, wide - 2, frame, LANES),
            shape(2, wide - 2, frame, LANES),
            shape(3, wide - 2, rows, LANES),
            tile,
            tile,
            tile,
            spread,
            small,
        ),
        [
            pltpu.VMEM((2, wide, frame, LANES), F32),
            pltpu.VMEM((wide, frame, LANES), F32),
            pltpu.VMEM((3, wide + 1, frame, LANES), F32),
            pltpu.VMEM((3, 3, wide, frame, LANES), F32),
        ],
        (total0, steps, near_box, far_box, back, slope0, mult0, fwd, bwd, bias),
        2 * flops,
        scalars=(1,),
    )
    total1 = everyone(stat1)
    out = shape(3, rows, cols)
    duals, multipliers, slope2, mult2, stat2 = call(
        functools.partial(third_body, cells=cells),
        (out, out, out, out, spread),
        [
            pltpu.VMEM((2, wide - 2, frame, LANES), F32),
            pltpu.VMEM((3, wide - 1, frame, LANES), F32),
            pltpu.VMEM((3, 3, wide - 2, frame, LANES), F32),
        ],
        (
            total1, steps, near_box, base, mult1, slope1, duals1, last_mult, last_slope, last_pull,
            fwd, bwd, lower, upper, bias, value0, value1,
        ),
        2 * flops,
        scalars=(1,),
    )
    total2 = everyone(stat2)
    final_duals, final_multipliers, bounds = call(
        functools.partial(last_body, cells=cells),
        (out, out, shape(ITERS)),
        [],
        (total2, steps, duals, multipliers, slope2, mult2),
        1 << 20,
        scalar_outs=(2,),
        scalars=(1,),
    )
    return bounds, final_duals, final_multipliers


def solution(mesh):
    placed = (
        P("row", "col"),
        P("row", "col"),
        P("row", "col"),
        P(None, "row", "col"),
        P(None, "row", "col"),
        P(),
        P(),
        P(),
    )
    return jax.shard_map(
        shards,
        mesh=mesh,
        in_specs=placed,
        out_specs=(P(), P(None, "row", "col"), P(None, "row", "col")),
        check_vma=False,
    )
```

```python
import functools
import math

import jax
import jax.numpy as jnp
from jax import lax
from jax.experimental import pallas as pl
from jax.experimental.pallas import tpu as pltpu
from jax.sharding import PartitionSpec as P

CH = 64
LAYERS = 4
ITERS = 3
EPS = 1e-06
LANES = 2 * CH
HALO_PAIRS = 3
WIDE = 5
EDGE = 4
F32 = jnp.float32
BF16 = jnp.bfloat16

ROWS_SENT = (5, 5, 5, 4, 4, 4, 2, 3, 3)
ROW_START = tuple(sum(ROWS_SENT[:m]) for m in range(9))
SENT = sum(ROWS_SENT)
WINDOW = 4 * CH

VMEM = pl.BlockSpec(memory_space=pltpu.VMEM)
SMEM = pl.BlockSpec(memory_space=pltpu.SMEM)
HBM = pl.BlockSpec(memory_space=pltpu.HBM)


def call(body, outs, scratch, operands, flops, mem=20, scalars=(), far=(), scalar_outs=()):
    specs = [SMEM if j in scalars else HBM if j in far else VMEM for j in range(len(operands))]
    out_specs = tuple(SMEM if j in scalar_outs else VMEM for j in range(len(outs)))
    return pl.pallas_call(
        body,
        out_shape=outs,
        in_specs=specs,
        out_specs=out_specs,
        scratch_shapes=scratch,
        compiler_params=pltpu.CompilerParams(vmem_limit_bytes=mem << 20),
        cost_estimate=pl.CostEstimate(flops=flops, bytes_accessed=4 << 20, transcendentals=0),
    )(*operands)


def shape(*dims, dtype=F32):
    return jax.ShapeDtypeStruct(dims, dtype)


def copies(pairs, sem):
    made = [pltpu.make_async_copy(src, dst, sem.at[j]) for j, (src, dst) in enumerate(pairs)]
    for one in made:
        one.start()
    return made


def finish(made):
    for one in made:
        one.wait()


def split(value):
    high = value.astype(BF16)
    return high, (value - high.astype(F32)).astype(BF16)


def weights_body(kernels, biases, fwd, bwd, bias2):
    zero = jnp.zeros((CH, CH), F32)

    def put(dest, k, j, dh, first, second):
        high, low = split(jnp.concatenate([first, second], axis=1))
        for part, value in enumerate((low, high, high)):
            dest[k, pl.ds(WINDOW * part + CH * j, CH), pl.ds(LANES * dh, LANES)] = value

    for k in range(LAYERS):
        for dh in range(3):
            taps = [kernels[k * 9 + dh * 3 + dw] for dw in range(3)]
            if k < LAYERS - 1:
                for j in range(4):
                    put(fwd, k, j, dh, taps[j] if j < 3 else zero, taps[j - 1] if j > 0 else zero)
            flips = [tap.T for tap in taps]
            for j in range(4):
                put(bwd, k, j, 2 - dh, flips[2 - j] if j < 3 else zero, flips[3 - j] if j > 0 else zero)
    for k in range(LAYERS):
        row = biases[k : k + 1, :]
        bias2[k : k + 1, :] = jnp.concatenate([row, row], axis=1)


def weights(kernels, biases):
    size = (3 * WINDOW, 3 * LANES)
    return call(
        weights_body,
        (shape(LAYERS - 1, *size, dtype=BF16), shape(LAYERS, *size, dtype=BF16), shape(8, LANES)),
        [],
        (kernels.reshape(LAYERS * 9, CH, CH), biases),
        1 << 22,
    )


def sources(objective, center, radius, lower, upper):
    return [
        lambda cols: center[:, cols].astype(F32),
        lambda cols: upper[0, :, cols].astype(F32),
        lambda cols: upper[1, :, cols].astype(F32),
        lambda cols: upper[2, :, cols].astype(F32),
        lambda cols: lower[0, :, cols].astype(F32),
        lambda cols: lower[1, :, cols].astype(F32),
        lambda cols: lower[2, :, cols].astype(F32),
        lambda cols: radius[:, cols].astype(F32),
        lambda cols: objective[:, cols],
    ]


def ends_body(objective, center, radius, lower, upper, top, bottom, head, tail, *rest):
    rows, cols = objective.shape
    held, sem = rest[:5], rest[5]
    finish(copies(list(zip((objective, center, radius, lower, upper), held)), sem))
    strip = HALO_PAIRS * LANES
    for m, read in enumerate(sources(*held)):
        head[pl.ds(m * rows, rows), :] = read(pl.ds(0, strip))
        tail[pl.ds(m * rows, rows), :] = read(pl.ds(cols - strip, strip))
    row = lax.broadcasted_iota(jnp.int32, (rows, LANES), 0)
    outer = (row >= 2) & (row < rows - 2)
    for q in range(cols // LANES):
        values = [read(pl.ds(q * LANES, LANES)) for read in sources(*held)]
        values[3] = jnp.where(outer, values[3] - values[6], values[3])
        for m, value in enumerate(values):
            here = pl.ds(q * SENT + ROW_START[m], ROWS_SENT[m])
            top[here, :] = value[: ROWS_SENT[m]]
            bottom[here, :] = value[rows - ROWS_SENT[m] :]


def corners_body(above, below, after, head, tail):
    del after
    count = HALO_PAIRS * SENT
    size = above.shape[0]
    for part, source in enumerate((above, below)):
        here = pl.ds(part * count, count)
        head[here, :] = source[0:count, :]
        tail[here, :] = source[size - count : size, :]


def column(reads, left, right, rows, pairs, m, q):
    if q < HALO_PAIRS:
        return left[m * rows : (m + 1) * rows, q * LANES : (q + 1) * LANES]
    if q >= HALO_PAIRS + pairs:
        q -= HALO_PAIRS + pairs
        return right[m * rows : (m + 1) * rows, q * LANES : (q + 1) * LANES]
    return reads[m](pl.ds((q - HALO_PAIRS) * LANES, LANES))


def halo(middle, left, right, part, pairs, q, m):
    if q < HALO_PAIRS:
        source, at = left, part * HALO_PAIRS + q
    elif q >= HALO_PAIRS + pairs:
        source, at = right, part * HALO_PAIRS + q - HALO_PAIRS - pairs
    else:
        source, at = middle, q - HALO_PAIRS
    return source[pl.ds(at * SENT + ROW_START[m], ROWS_SENT[m]), :]


def neighbours(head, tail, axis):
    count = lax.axis_size(axis)
    before = lax.ppermute(tail, axis, [(i, i + 1) for i in range(count - 1)])
    after = lax.ppermute(head, axis, [(i + 1, i) for i in range(count - 1)])
    return before, after


def roll_rows(value, shift):
    return pltpu.roll(value, shift % value.shape[0], 0)


def unrolled(count, most):
    return max(n for n in range(1, most + 1) if count % n == 0)


def slide(maps, count, store, produce, most=32):
    rows = store.shape[2]
    early = lax.broadcasted_iota(jnp.int32, (rows, LANES), 1) < CH
    zero = jnp.zeros((rows, LANES), F32)

    def step(q, carry):
        fresh = [pltpu.roll(value, CH, 1) for value in produce(q)]
        for k in range(maps):
            store[k, q] = jnp.where(early, carry[k], fresh[k])
        return tuple(fresh)

    last = lax.fori_loop(0, count, step, (zero,) * maps, unroll=unrolled(count, most))
    for k in range(maps):
        store[k, count] = jnp.where(early, last[k], zero)


def multiply(store, k, first, count, weight, layer, sums, exact=False):
    rows = store.shape[2]
    left = store[k, pl.ds(first, count)].reshape(count * rows, LANES)
    right = store[k, pl.ds(first + 1, count)].reshape(count * rows, LANES)
    high, low = split(jnp.concatenate([left, right], axis=1))
    terms = [high, high] if exact else [high, high, low]
    result = jnp.dot(
        jnp.concatenate(terms, axis=1),
        weight[layer, 0 : WINDOW * len(terms), :],
        preferred_element_type=F32,
    )
    for d in range(3):
        sums[k, d, pl.ds(0, count)] = result[:, d * LANES : (d + 1) * LANES].reshape(count, rows, LANES)


def gathered(sums, k, q):
    return roll_rows(sums[k, 0, q], 1) + sums[k, 1, q] + roll_rows(sums[k, 2, q], -1)


def inner(sums, k, q, first, rows):
    parts = [roll_rows(sums[k, d, q], 1 - d - first)[:rows] for d in range(3)]
    return parts[0] + parts[1] + parts[2]


def summed(total):
    return jnp.sum(total[...], axis=0, keepdims=True)


def scale_of(total, step, cells, dims):
    squares = summed(total)[:, 0:1]
    return jnp.broadcast_to(step / jnp.sqrt(squares / (2 * (LAYERS - 1) * cells) + EPS), dims)


def soft(top, bend):
    return 0.5 * top * (1.0 - bend)


class Bound:
    def __init__(self, start):
        self.linear = start
        self.factor = None

    def add(self, t):
        bend = jnp.tanh(t)
        self.linear = self.linear + (jnp.minimum(t, 0.0) - 0.5 * math.log(2.0))
        factor = 1.0 + jnp.abs(bend)
        self.factor = factor if self.factor is None else self.factor * factor
        return bend

    def total(self):
        return self.linear + 0.5 * jnp.log(self.factor)


def folded(value):
    return jnp.sum(value, axis=0, keepdims=True)


def own_rows(value):
    rows = value.shape[0]
    row = lax.broadcasted_iota(jnp.int32, value.shape, 0)
    return folded(jnp.where((row >= EDGE) & (row < rows - EDGE), value, 0.0))


def stats(out, rows):
    lane = lax.broadcasted_iota(jnp.int32, (1, LANES), 1)
    packed = jnp.zeros((1, LANES), F32)
    for j, row in enumerate(rows):
        packed = jnp.where(lane == j, jnp.sum(row, axis=1, keepdims=True), packed)
    out[...] = jnp.broadcast_to(packed, out.shape)


def assemble(reads, above, below, left, right, corners, slots, rows, pairs, raw, gaps, target):
    frame = rows + 2 * EDGE
    blank = jnp.zeros((EDGE, LANES), F32)
    for slot, q in enumerate(slots):
        outside = not 1 <= q < pairs + 2 * HALO_PAIRS - 1
        for m in range(9):
            sent = ROWS_SENT[m]
            if m < 3:
                dest, at, edge = raw.at[m, slot], 0, WIDE
            else:
                dest, at, edge = (target.at[slot] if m == 8 else gaps.at[m - 3, slot]), EDGE - sent, EDGE
                if outside:
                    dest[...] = jnp.zeros((frame, LANES), F32)
                    continue
                if at:
                    dest[0:EDGE, :] = blank
                    dest[EDGE + rows : frame, :] = blank
            dest[at : at + sent, :] = halo(above, *corners, 0, pairs, q, m)
            dest[edge : edge + rows, :] = column(reads, left, right, rows, pairs, m, q)
            dest[edge + rows : edge + rows + sent, :] = halo(below, *corners, 1, pairs, q, m)
    count = len(slots)
    spare = raw.shape[2] - rows - 2 * WIDE
    raw[:, :, rows + 2 * WIDE :, :] = jnp.zeros((3, count, spare, LANES), F32)


def start_convs(raw, target, store, sums, fwd, bwd, frame):
    count = raw.shape[1]
    slide(3, count, store, lambda q: [raw[0, q], 0.5 * raw[1, q], 0.5 * raw[2, q]])
    tugged = store.at[3:4, :, 0:frame, :]
    slide(1, count, tugged, lambda q: [target[q]])
    for k in range(3):
        multiply(store, k, 1, count - 2, fwd, k, sums, exact=True)
    multiply(tugged, 0, 1, count - 2, bwd, LAYERS - 1, sums.at[3:4, :, :, 0:frame, :])


def start_step(slot, out, raw, gaps, target, sums, bias, near_box, far_box, back, slope, mult):
    frame = gaps.shape[2]
    near = [raw[m, slot][1 : 1 + frame] for m in range(3)] + [gaps[4, slot]]
    far = [gaps[m, slot] for m in range(4)]
    for m in range(4):
        near_box[m, out] = near[m].astype(BF16)
        far_box[m, out] = far[m].astype(BF16)
    new = jnp.zeros((frame, LANES), F32)
    for k in range(3):
        gap = near[1 + k] if k < 2 else far[0]
        dl = 0.5 * (gap - far[1 + k]) - inner(sums, k, slot - 1, 1, frame) - bias[k : k + 1, :]
        dl = jnp.where(near[1] > 0.0, dl, 0.0)
        slope[k, out] = dl
        new = new + dl * dl
    tug = gathered(sums.at[3:4, :, :, 0:frame, :], 0, slot - 1)
    back[out] = tug
    bound = Bound(jnp.full((frame, LANES), -4.5 * math.log(2.0), F32))
    dm = -0.5 * gap * bound.add(tug * gap)
    mult[out] = dm
    return new + dm * dm, bound.total(), target[slot] * bias[3:4, :]


def middle_body(
    objective, center, radius, lower, upper, above, below, fwd, bwd, bias,
    near_box, far_box, back, slope, mult, totals,
    raw, gaps, target, store, sums,
):
    rows, cols = objective.shape
    pairs = cols // LANES
    frame = rows + 2 * EDGE
    reads = sources(objective, center, radius, lower, upper)
    slots = range(HALO_PAIRS, HALO_PAIRS + pairs)
    assemble(reads, above, below, None, None, (None, None), slots, rows, pairs, raw, gaps, target)
    start_convs(raw, target, store, sums, fwd, bwd, frame)

    def step(q, carry):
        new = start_step(q + 1, q, raw, gaps, target, sums, bias, near_box, far_box, back, slope, mult)
        return tuple(old + one for old, one in zip(carry, new))

    zero = jnp.zeros((frame, LANES), F32)
    sizes = lax.fori_loop(0, pairs - 2, step, (zero, zero, zero), unroll=unrolled(pairs - 2, 7))
    for j in range(3):
        totals[j] = sizes[j]


def first_body(
    objective, center, radius, lower, upper, left, right, above, below, left_corner, right_corner, fwd, bwd, bias,
    near_in, far_in, back_in, slope_in, mult_in, totals,
    near_box, far_box, back, slope, mult, stat, value,
    raw, gaps, target, store, sums,
):
    rows, cols = objective.shape
    pairs = cols // LANES
    frame = rows + 2 * EDGE
    wide = pairs + 4
    reads = sources(objective, center, radius, lower, upper)
    corners = (left_corner, right_corner)
    slots = list(range(5)) + list(range(wide - 3, wide + 2))
    assemble(reads, above, below, left, right, corners, slots, rows, pairs, raw, gaps, target)
    start_convs(raw, target, store, sums, fwd, bwd, frame)
    here = slice(3, wide - 3)
    near_box[:, here] = near_in[...]
    far_box[:, here] = far_in[...]
    back[here] = back_in[...]
    slope[:, here] = slope_in[...]
    mult[here] = mult_in[...]
    sizes = [totals[j] for j in range(3)]
    for slot, q in ((1, 0), (2, 1), (3, 2), (6, wide - 3), (7, wide - 2), (8, wide - 1)):
        new = start_step(slot, q, raw, gaps, target, sums, bias, near_box, far_box, back, slope, mult)
        if 2 <= q < wide - 2:
            sizes = [old + one for old, one in zip(sizes, new)]
    squares, worth, fixed = (own_rows(one) for one in sizes)
    stats(stat, [squares])
    stats(value, [worth + fixed, fixed])


def second_body(
    total, steps, near_box, far_box, back, slope, mult, fwd, bwd, bias,
    base, slope_out, mult_out, duals, last_mult, last_slope, last_pull, stat, value,
    points, worths, store, sums, *, cells,
):
    wide, frame = near_box.shape[1:3]
    inside = slice(EDGE, frame - EDGE)
    scale = scale_of(total, steps[0], cells, (frame, LANES))
    zero = jnp.zeros((frame, LANES), F32)
    slide(3, wide, store, lambda q: [slope[k, q] for k in range(3)])
    for k in range(3):
        multiply(store, k, 0, wide, bwd, k, sums)

    def produce(q):
        center, radius = near_box[0, q].astype(F32), near_box[3, q].astype(F32)
        g = -(scale * gathered(sums, 0, q))
        base[0, q] = g
        bound = Bound(g * (center - radius))
        outs = [center - radius * bound.add(2.0 * radius * g)]
        for k in (1, 2):
            gap = near_box[k, q].astype(F32)
            g = -(scale * gathered(sums, k, q))
            base[k, q] = g
            x = soft(gap, bound.add(g * gap))
            points[k - 1, q] = x
            outs.append(x)
        worths[q] = bound.total()
        return outs

    slide(3, wide, store, produce, most=5)
    for k in range(3):
        multiply(store, k, 1, wide - 2, fwd, k, sums)

    def step(j, carry):
        squares, worth = carry
        q = j + 1
        new = zero
        bound = Bound(worths[q])
        for k in range(3):
            gap = (near_box[1 + k, q] if k < 2 else far_box[0, q]).astype(F32)
            low = far_box[1 + k, q].astype(F32)
            lam = scale * slope[k, q]
            if k < 2:
                x = points[k, q]
                tp = lam * gap
            else:
                mu = scale * mult[q]
                g = back[q] + mu
                x = soft(gap, bound.add(g * gap))
                tp = (lam - mu) * gap
            positive = soft(gap, bound.add(tp))
            negative = soft(low, bound.add(-lam * low))
            bound.linear = bound.linear - lam * bias[k : k + 1, :]
            dl = positive - negative - gathered(sums, k, j) - bias[k : k + 1, :]
            dl = jnp.where(gap > 0.0, dl, 0.0)
            dm = x - positive
            slope_out[k, j] = dl
            duals[k, j] = lam[inside]
            if k < 2:
                mult_out[k, j] = dm
            else:
                last_mult[j] = mu[inside]
                last_slope[j] = dm[inside]
                last_pull[j] = g[inside]
            new = new + dl * dl + dm * dm
        own = (q >= 2) & (q < wide - 2)
        return squares + jnp.where(own, new, 0.0), worth + jnp.where(own, bound.total(), 0.0)

    squares, worth = lax.fori_loop(0, wide - 2, step, (zero, zero), unroll=unrolled(wide - 2, 3))
    stats(stat, [own_rows(squares)])
    stats(value, [own_rows(worth)])


def third_body(
    total, steps, near_box, base, mult, slope, duals1, last_mult, last_slope, last_pull,
    fwd, bwd, lower, upper, bias, value0, value1,
    duals, multipliers, slope_out, mult_out, stat,
    points, store, sums, *, cells,
):
    wide, frame = near_box.shape[1:3]
    rows = frame - 2 * EDGE
    inside = slice(EDGE, frame - EDGE)
    scale = scale_of(total, steps[1], cells, (frame, LANES))
    zero = jnp.zeros((frame, LANES), F32)
    slide(3, wide - 2, store, lambda j: [slope[k, j] for k in range(3)])
    for k in range(3):
        multiply(store, k, 0, wide - 2, bwd, k, sums)
    early = lax.broadcasted_iota(jnp.int32, (frame, LANES), 1) < CH

    def point(j, carry):
        q = j + 1
        center, radius = near_box[0, q].astype(F32), near_box[3, q].astype(F32)
        g = base[0, q] - scale * gathered(sums, 0, j)
        bound = Bound(g * (center - radius))
        outs = [center - radius * bound.add(2.0 * radius * g)]
        for k in (1, 2):
            gap = near_box[k, q].astype(F32)
            t = (base[k, q] + scale * (mult[k - 1, j] - gathered(sums, k, j))) * gap
            x = soft(gap, bound.add(t))
            points[k - 1, j] = x
            outs.append(x)
        own = (q >= 2) & (q < wide - 2)
        fresh = [pltpu.roll(value, CH, 1) for value in outs]
        for k in range(3):
            store[k, j] = jnp.where(early, carry[k], fresh[k])
        return tuple(fresh) + (carry[3] + jnp.where(own, bound.total(), 0.0),)

    framed = lax.fori_loop(0, wide - 2, point, (zero,) * 4, unroll=unrolled(wide - 2, 6))[3]
    for k in range(3):
        multiply(store, k, 1, wide - 4, fwd, k, sums)

    scale = scale[:rows]

    def step(i, carry):
        squares, worth = carry
        j = i + 1
        here = pl.ds(pl.multiple_of(i * LANES, LANES), LANES)
        bound = Bound(jnp.zeros((rows, LANES), F32))
        for k in range(3):
            gap = upper[k, :, here].astype(F32)
            low = lower[k, :, here].astype(F32)
            lam = duals1[k, j] + scale * slope[k, j, inside, :]
            bound.linear = bound.linear - lam * bias[k : k + 1, :]
            if k < 2:
                x = points[k, j, inside, :]
                mu = scale * mult[k, j, inside, :]
            else:
                change = scale * last_slope[j]
                mu = last_mult[j] + change
                x = soft(gap, bound.add((last_pull[j] + change) * gap))
            positive = soft(gap, bound.add((lam - mu) * gap))
            negative = soft(low, bound.add(-lam * low))
            dl = positive - negative - inner(sums, k, i, EDGE, rows) - bias[k : k + 1, :]
            dm = x - positive
            duals[k, :, here] = lam
            multipliers[k, :, here] = mu
            slope_out[k, :, here] = dl
            mult_out[k, :, here] = dm
            squares = squares + dl * dl + dm * dm
        return squares, worth + bound.total()

    zero = jnp.zeros((rows, LANES), F32)
    squares, worth = lax.fori_loop(0, wide - 4, step, (zero, zero), unroll=unrolled(wide - 4, 4))
    lane = lax.broadcasted_iota(jnp.int32, (1, LANES), 1)
    start, fixed = (jnp.where(lane == j, value0[0:1, :], 0.0) for j in range(2))
    middle = jnp.where(lane == 0, value1[0:1, :], 0.0)
    stats(stat, [folded(squares), start, middle + fixed, folded(worth) + own_rows(framed) + fixed])


def last_body(total, steps, duals, multipliers, slope, mult, duals_out, mult_out, bounds, *, cells):
    scale = scale_of(total, steps[2], cells, duals.shape[1:])
    for k in range(LAYERS - 1):
        duals_out[k] = duals[k] + scale * slope[k]
        mult_out[k] = multipliers[k] + scale * mult[k]
    values = summed(total) / cells
    lane = lax.broadcasted_iota(jnp.int32, (1, LANES), 1)
    for j in range(ITERS):
        bounds[j] = jnp.sum(jnp.where(lane == j + 1, values, 0.0))


def everyone(partial):
    return lax.all_to_all(partial, ("row", "col"), 0, 0, tiled=True)


def shards(objective, center, radius, lower, upper, kernels, biases, steps):
    rows, cols = objective.shape
    pairs = cols // LANES
    wide = pairs + 4
    frame = rows + 2 * EDGE
    tall = -(-(rows + 2 * WIDE) // 8) * 8
    cells = rows * cols * lax.axis_size("row") * lax.axis_size("col")
    inputs = (objective, center, radius, lower, upper)
    flops = 3 * 2 * 3 * wide * frame * 4 * CH * 3 * LANES
    spread = shape(lax.axis_size("row") * lax.axis_size("col"), LANES)
    small = shape(8, LANES)

    ends = shape(pairs * SENT, LANES)
    strip = shape(9 * rows, HALO_PAIRS * LANES)
    top, bottom, head, tail = call(
        ends_body,
        (ends, ends, strip, strip),
        [pltpu.VMEM(one.shape, one.dtype) for one in inputs] + [pltpu.SemaphoreType.DMA((5,))],
        inputs,
        1 << 20,
        mem=58,
        far=range(5),
    )
    above, below = neighbours(top, bottom, "row")
    left, right = neighbours(head, tail, "col")
    fwd, bwd, bias = weights(kernels, biases)
    corner = shape(2 * HALO_PAIRS * SENT, LANES)
    corner_head, corner_tail = call(corners_body, (corner, corner), [], (above, below, bias), 1 << 20)
    left_corner, right_corner = neighbours(corner_head, corner_tail, "col")

    def start_scratch(count):
        return [
            pltpu.VMEM((3, count, tall, LANES), F32),
            pltpu.VMEM((5, count, frame, LANES), F32),
            pltpu.VMEM((count, frame, LANES), F32),
            pltpu.VMEM((4, count + 1, tall, LANES), F32),
            pltpu.VMEM((4, 3, count - 2, tall, LANES), F32),
        ]

    def start_shapes(count):
        box = shape(4, count, frame, LANES, dtype=BF16)
        full = shape(count, frame, LANES)
        return box, box, full, shape(3, count, frame, LANES), full

    middle = call(
        middle_body,
        start_shapes(pairs - 2) + (shape(3, frame, LANES),),
        start_scratch(pairs),
        inputs + (above, below, fwd, bwd, bias),
        flops,
    )
    near_box, far_box, back, slope0, mult0, stat0, value0 = call(
        first_body,
        start_shapes(wide) + (spread, small),
        start_scratch(10),
        inputs + (left, right, above, below, left_corner, right_corner, fwd, bwd, bias) + tuple(middle),
        flops,
    )

    total0 = everyone(stat0)
    tile = shape(wide - 2, rows, LANES)
    base, slope1, mult1, duals1, last_mult, last_slope, last_pull, stat1, value1 = call(
        functools.partial(second_body, cells=cells),
        (
            shape(3, wide, frame, LANES),
            shape(3, wide - 2, frame, LANES),
            shape(2, wide - 2, frame, LANES),
            shape(3, wide - 2, rows, LANES),
            tile,
            tile,
            tile,
            spread,
            small,
        ),
        [
            pltpu.VMEM((2, wide, frame, LANES), F32),
            pltpu.VMEM((wide, frame, LANES), F32),
            pltpu.VMEM((3, wide + 1, frame, LANES), F32),
            pltpu.VMEM((3, 3, wide, frame, LANES), F32),
        ],
        (total0, steps, near_box, far_box, back, slope0, mult0, fwd, bwd, bias),
        2 * flops,
        scalars=(1,),
    )
    total1 = everyone(stat1)
    out = shape(3, rows, cols)
    duals, multipliers, slope2, mult2, stat2 = call(
        functools.partial(third_body, cells=cells),
        (out, out, out, out, spread),
        [
            pltpu.VMEM((2, wide - 2, frame, LANES), F32),
            pltpu.VMEM((3, wide - 1, frame, LANES), F32),
            pltpu.VMEM((3, 3, wide - 2, frame, LANES), F32),
        ],
        (
            total1, steps, near_box, base, mult1, slope1, duals1, last_mult, last_slope, last_pull,
            fwd, bwd, lower, upper, bias, value0, value1,
        ),
        2 * flops,
        scalars=(1,),
    )
    total2 = everyone(stat2)
    final_duals, final_multipliers, bounds = call(
        functools.partial(last_body, cells=cells),
        (out, out, shape(ITERS)),
        [],
        (total2, steps, duals, multipliers, slope2, mult2),
        1 << 20,
        scalar_outs=(2,),
        scalars=(1,),
    )
    return bounds, final_duals, final_multipliers


def solution(mesh):
    placed = (
        P("row", "col"),
        P("row", "col"),
        P("row", "col"),
        P(None, "row", "col"),
        P(None, "row", "col"),
        P(),
        P(),
        P(),
    )
    return jax.shard_map(
        shards,
        mesh=mesh,
        in_specs=placed,
        out_specs=(P(), P(None, "row", "col"), P(None, "row", "col")),
        check_vma=False,
    )
```

```python
import functools
import math

import jax
import jax.numpy as jnp
from jax import lax
from jax.experimental import pallas as pl
from jax.experimental.pallas import tpu as pltpu
from jax.sharding import PartitionSpec as P

CH = 64
LAYERS = 4
ITERS = 3
EPS = 1e-06
LANES = 2 * CH
HALO_PAIRS = 3
WIDE = 5
EDGE = 4
F32 = jnp.float32
BF16 = jnp.bfloat16

ROWS_SENT = (5, 5, 5, 4, 4, 4, 2, 3, 3)
ROW_START = tuple(sum(ROWS_SENT[:m]) for m in range(9))
SENT = sum(ROWS_SENT)
WINDOW = 4 * CH

VMEM = pl.BlockSpec(memory_space=pltpu.VMEM)
SMEM = pl.BlockSpec(memory_space=pltpu.SMEM)
HBM = pl.BlockSpec(memory_space=pltpu.HBM)


def call(body, outs, scratch, operands, flops, mem=20, scalars=(), far=(), scalar_outs=()):
    specs = [SMEM if j in scalars else HBM if j in far else VMEM for j in range(len(operands))]
    out_specs = tuple(SMEM if j in scalar_outs else VMEM for j in range(len(outs)))
    return pl.pallas_call(
        body,
        out_shape=outs,
        in_specs=specs,
        out_specs=out_specs,
        scratch_shapes=scratch,
        compiler_params=pltpu.CompilerParams(vmem_limit_bytes=mem << 20),
        cost_estimate=pl.CostEstimate(flops=flops, bytes_accessed=4 << 20, transcendentals=0),
    )(*operands)


def shape(*dims, dtype=F32):
    return jax.ShapeDtypeStruct(dims, dtype)


def copies(pairs, sem):
    made = [pltpu.make_async_copy(src, dst, sem.at[j]) for j, (src, dst) in enumerate(pairs)]
    for one in made:
        one.start()
    return made


def finish(made):
    for one in made:
        one.wait()


def split(value):
    high = value.astype(BF16)
    return high, (value - high.astype(F32)).astype(BF16)


def weights_body(kernels, biases, fwd, bwd, bias2):
    zero = jnp.zeros((CH, CH), F32)

    def put(dest, k, j, dh, first, second):
        high, low = split(jnp.concatenate([first, second], axis=1))
        for part, value in enumerate((low, high, high)):
            dest[k, pl.ds(WINDOW * part + CH * j, CH), pl.ds(LANES * dh, LANES)] = value

    for k in range(LAYERS):
        for dh in range(3):
            taps = [kernels[k * 9 + dh * 3 + dw] for dw in range(3)]
            if k < LAYERS - 1:
                for j in range(4):
                    put(fwd, k, j, dh, taps[j] if j < 3 else zero, taps[j - 1] if j > 0 else zero)
            flips = [tap.T for tap in taps]
            for j in range(4):
                put(bwd, k, j, 2 - dh, flips[2 - j] if j < 3 else zero, flips[3 - j] if j > 0 else zero)
    for k in range(LAYERS):
        row = biases[k : k + 1, :]
        bias2[k : k + 1, :] = jnp.concatenate([row, row], axis=1)


def weights(kernels, biases):
    size = (3 * WINDOW, 3 * LANES)
    return call(
        weights_body,
        (shape(LAYERS - 1, *size, dtype=BF16), shape(LAYERS, *size, dtype=BF16), shape(8, LANES)),
        [],
        (kernels.reshape(LAYERS * 9, CH, CH), biases),
        1 << 22,
    )


def sources(objective, center, radius, lower, upper):
    return [
        lambda cols: center[:, cols].astype(F32),
        lambda cols: upper[0, :, cols].astype(F32),
        lambda cols: upper[1, :, cols].astype(F32),
        lambda cols: upper[2, :, cols].astype(F32),
        lambda cols: lower[0, :, cols].astype(F32),
        lambda cols: lower[1, :, cols].astype(F32),
        lambda cols: lower[2, :, cols].astype(F32),
        lambda cols: radius[:, cols].astype(F32),
        lambda cols: objective[:, cols],
    ]


def ends_body(objective, center, radius, lower, upper, top, bottom, head, tail, *rest):
    rows, cols = objective.shape
    held, sem = rest[:5], rest[5]
    finish(copies(list(zip((objective, center, radius, lower, upper), held)), sem))
    strip = HALO_PAIRS * LANES
    for m, read in enumerate(sources(*held)):
        head[pl.ds(m * rows, rows), :] = read(pl.ds(0, strip))
        tail[pl.ds(m * rows, rows), :] = read(pl.ds(cols - strip, strip))
    row = lax.broadcasted_iota(jnp.int32, (rows, LANES), 0)
    outer = (row >= 2) & (row < rows - 2)
    for q in range(cols // LANES):
        values = [read(pl.ds(q * LANES, LANES)) for read in sources(*held)]
        values[3] = jnp.where(outer, values[3] - values[6], values[3])
        for m, value in enumerate(values):
            here = pl.ds(q * SENT + ROW_START[m], ROWS_SENT[m])
            top[here, :] = value[: ROWS_SENT[m]]
            bottom[here, :] = value[rows - ROWS_SENT[m] :]


def corners_body(above, below, after, head, tail):
    del after
    count = HALO_PAIRS * SENT
    size = above.shape[0]
    for part, source in enumerate((above, below)):
        here = pl.ds(part * count, count)
        head[here, :] = source[0:count, :]
        tail[here, :] = source[size - count : size, :]


def column(reads, left, right, rows, pairs, m, q):
    if q < HALO_PAIRS:
        return left[m * rows : (m + 1) * rows, q * LANES : (q + 1) * LANES]
    if q >= HALO_PAIRS + pairs:
        q -= HALO_PAIRS + pairs
        return right[m * rows : (m + 1) * rows, q * LANES : (q + 1) * LANES]
    return reads[m](pl.ds((q - HALO_PAIRS) * LANES, LANES))


def halo(middle, left, right, part, pairs, q, m):
    if q < HALO_PAIRS:
        source, at = left, part * HALO_PAIRS + q
    elif q >= HALO_PAIRS + pairs:
        source, at = right, part * HALO_PAIRS + q - HALO_PAIRS - pairs
    else:
        source, at = middle, q - HALO_PAIRS
    return source[pl.ds(at * SENT + ROW_START[m], ROWS_SENT[m]), :]


def neighbours(head, tail, axis):
    count = lax.axis_size(axis)
    before = lax.ppermute(tail, axis, [(i, i + 1) for i in range(count - 1)])
    after = lax.ppermute(head, axis, [(i + 1, i) for i in range(count - 1)])
    return before, after


def roll_rows(value, shift):
    return pltpu.roll(value, shift % value.shape[0], 0)


def slide(maps, count, store, produce):
    rows = store.shape[2]
    early = lax.broadcasted_iota(jnp.int32, (rows, LANES), 1) < CH
    zero = jnp.zeros((rows, LANES), F32)

    def step(q, carry):
        fresh = [pltpu.roll(value, CH, 1) for value in produce(q)]
        for k in range(maps):
            store[k, q] = jnp.where(early, carry[k], fresh[k])
        return tuple(fresh)

    last = lax.fori_loop(0, count, step, (zero,) * maps, unroll=True)
    for k in range(maps):
        store[k, count] = jnp.where(early, last[k], zero)


def multiply(store, k, first, count, weight, layer, sums, exact=False):
    rows = store.shape[2]
    left = store[k, pl.ds(first, count)].reshape(count * rows, LANES)
    right = store[k, pl.ds(first + 1, count)].reshape(count * rows, LANES)
    high, low = split(jnp.concatenate([left, right], axis=1))
    terms = [high, high] if exact else [high, high, low]
    result = jnp.dot(
        jnp.concatenate(terms, axis=1),
        weight[layer, 0 : WINDOW * len(terms), :],
        preferred_element_type=F32,
    )
    for d in range(3):
        sums[k, d, pl.ds(0, count)] = result[:, d * LANES : (d + 1) * LANES].reshape(count, rows, LANES)


def gathered(sums, k, q):
    return roll_rows(sums[k, 0, q], 1) + sums[k, 1, q] + roll_rows(sums[k, 2, q], -1)


def inner(sums, k, q, first, rows):
    parts = [roll_rows(sums[k, d, q], 1 - d - first)[:rows] for d in range(3)]
    return parts[0] + parts[1] + parts[2]


def summed(total):
    return jnp.sum(total[...], axis=0, keepdims=True)


def scale_of(total, step, cells, dims):
    squares = summed(total)[:, 0:1]
    return jnp.broadcast_to(step / jnp.sqrt(squares / (2 * (LAYERS - 1) * cells) + EPS), dims)


def soft(top, bend):
    return 0.5 * top * (1.0 - bend)


class Bound:
    def __init__(self, start):
        self.linear = start
        self.factor = None

    def add(self, t):
        bend = jnp.tanh(t)
        self.linear = self.linear + (jnp.minimum(t, 0.0) - 0.5 * math.log(2.0))
        factor = 1.0 + jnp.abs(bend)
        self.factor = factor if self.factor is None else self.factor * factor
        return bend

    def total(self):
        return self.linear + 0.5 * jnp.log(self.factor)


def folded(value):
    return jnp.sum(value, axis=0, keepdims=True)


def own_rows(value):
    rows = value.shape[0]
    row = lax.broadcasted_iota(jnp.int32, value.shape, 0)
    return folded(jnp.where((row >= EDGE) & (row < rows - EDGE), value, 0.0))


def stats(out, rows):
    lane = lax.broadcasted_iota(jnp.int32, (1, LANES), 1)
    packed = jnp.zeros((1, LANES), F32)
    for j, row in enumerate(rows):
        packed = jnp.where(lane == j, jnp.sum(row, axis=1, keepdims=True), packed)
    out[...] = jnp.broadcast_to(packed, out.shape)


def assemble(reads, above, below, left, right, corners, slots, rows, pairs, raw, gaps, target):
    frame = rows + 2 * EDGE
    blank = jnp.zeros((EDGE, LANES), F32)
    for slot, q in enumerate(slots):
        outside = not 1 <= q < pairs + 2 * HALO_PAIRS - 1
        for m in range(9):
            sent = ROWS_SENT[m]
            if m < 3:
                dest, at, edge = raw.at[m, slot], 0, WIDE
            else:
                dest, at, edge = (target.at[slot] if m == 8 else gaps.at[m - 3, slot]), EDGE - sent, EDGE
                if outside:
                    dest[...] = jnp.zeros((frame, LANES), F32)
                    continue
                if at:
                    dest[0:EDGE, :] = blank
                    dest[EDGE + rows : frame, :] = blank
            dest[at : at + sent, :] = halo(above, *corners, 0, pairs, q, m)
            dest[edge : edge + rows, :] = column(reads, left, right, rows, pairs, m, q)
            dest[edge + rows : edge + rows + sent, :] = halo(below, *corners, 1, pairs, q, m)
    count = len(slots)
    spare = raw.shape[2] - rows - 2 * WIDE
    raw[:, :, rows + 2 * WIDE :, :] = jnp.zeros((3, count, spare, LANES), F32)


def start_convs(raw, target, store, sums, fwd, bwd, frame):
    count = raw.shape[1]
    slide(3, count, store, lambda q: [raw[0, q], 0.5 * raw[1, q], 0.5 * raw[2, q]])
    tugged = store.at[3:4, :, 0:frame, :]
    slide(1, count, tugged, lambda q: [target[q]])
    for k in range(3):
        multiply(store, k, 1, count - 2, fwd, k, sums, exact=True)
    multiply(tugged, 0, 1, count - 2, bwd, LAYERS - 1, sums.at[3:4, :, :, 0:frame, :])


def start_step(slot, out, raw, gaps, target, sums, bias, near_box, far_box, back, slope, mult):
    frame = gaps.shape[2]
    near = [raw[m, slot][1 : 1 + frame] for m in range(3)] + [gaps[4, slot]]
    far = [gaps[m, slot] for m in range(4)]
    for m in range(4):
        near_box[m, out] = near[m].astype(BF16)
        far_box[m, out] = far[m].astype(BF16)
    new = jnp.zeros((frame, LANES), F32)
    for k in range(3):
        gap = near[1 + k] if k < 2 else far[0]
        dl = 0.5 * (gap - far[1 + k]) - inner(sums, k, slot - 1, 1, frame) - bias[k : k + 1, :]
        dl = jnp.where(near[1] > 0.0, dl, 0.0)
        slope[k, out] = dl
        new = new + dl * dl
    tug = gathered(sums.at[3:4, :, :, 0:frame, :], 0, slot - 1)
    back[out] = tug
    bound = Bound(jnp.full((frame, LANES), -4.5 * math.log(2.0), F32))
    dm = -0.5 * gap * bound.add(tug * gap)
    mult[out] = dm
    return new + dm * dm, bound.total(), target[slot] * bias[3:4, :]


def middle_body(
    objective, center, radius, lower, upper, above, below, fwd, bwd, bias,
    near_box, far_box, back, slope, mult, totals,
    raw, gaps, target, store, sums,
):
    rows, cols = objective.shape
    pairs = cols // LANES
    frame = rows + 2 * EDGE
    reads = sources(objective, center, radius, lower, upper)
    slots = range(HALO_PAIRS, HALO_PAIRS + pairs)
    assemble(reads, above, below, None, None, (None, None), slots, rows, pairs, raw, gaps, target)
    start_convs(raw, target, store, sums, fwd, bwd, frame)

    def step(q, carry):
        new = start_step(q + 1, q, raw, gaps, target, sums, bias, near_box, far_box, back, slope, mult)
        return tuple(old + one for old, one in zip(carry, new))

    zero = jnp.zeros((frame, LANES), F32)
    sizes = lax.fori_loop(0, pairs - 2, step, (zero, zero, zero), unroll=True)
    for j in range(3):
        totals[j] = sizes[j]


def first_body(
    objective, center, radius, lower, upper, left, right, above, below, left_corner, right_corner, fwd, bwd, bias,
    near_in, far_in, back_in, slope_in, mult_in, totals,
    near_box, far_box, back, slope, mult, stat, value,
    raw, gaps, target, store, sums,
):
    rows, cols = objective.shape
    pairs = cols // LANES
    frame = rows + 2 * EDGE
    wide = pairs + 4
    reads = sources(objective, center, radius, lower, upper)
    corners = (left_corner, right_corner)
    slots = list(range(5)) + list(range(wide - 3, wide + 2))
    assemble(reads, above, below, left, right, corners, slots, rows, pairs, raw, gaps, target)
    start_convs(raw, target, store, sums, fwd, bwd, frame)
    here = slice(3, wide - 3)
    near_box[:, here] = near_in[...]
    far_box[:, here] = far_in[...]
    back[here] = back_in[...]
    slope[:, here] = slope_in[...]
    mult[here] = mult_in[...]
    sizes = [totals[j] for j in range(3)]
    for slot, q in ((1, 0), (2, 1), (3, 2), (6, wide - 3), (7, wide - 2), (8, wide - 1)):
        new = start_step(slot, q, raw, gaps, target, sums, bias, near_box, far_box, back, slope, mult)
        if 2 <= q < wide - 2:
            sizes = [old + one for old, one in zip(sizes, new)]
    squares, worth, fixed = (own_rows(one) for one in sizes)
    stats(stat, [squares])
    stats(value, [worth + fixed, fixed])


def second_body(
    total, steps, near_box, far_box, back, slope, mult, fwd, bwd, bias,
    base, slope_out, mult_out, duals, last_mult, last_slope, last_pull, stat, value,
    points, worths, store, sums, *, cells,
):
    wide, frame = near_box.shape[1:3]
    inside = slice(EDGE, frame - EDGE)
    scale = scale_of(total, steps[0], cells, (frame, LANES))
    zero = jnp.zeros((frame, LANES), F32)
    slide(3, wide, store, lambda q: [slope[k, q] for k in range(3)])
    for k in range(3):
        multiply(store, k, 0, wide, bwd, k, sums)

    def produce(q):
        center, radius = near_box[0, q].astype(F32), near_box[3, q].astype(F32)
        g = -(scale * gathered(sums, 0, q))
        base[0, q] = g
        bound = Bound(g * (center - radius))
        outs = [center - radius * bound.add(2.0 * radius * g)]
        for k in (1, 2):
            gap = near_box[k, q].astype(F32)
            g = -(scale * gathered(sums, k, q))
            base[k, q] = g
            x = soft(gap, bound.add(g * gap))
            points[k - 1, q] = x
            outs.append(x)
        worths[q] = bound.total()
        return outs

    slide(3, wide, store, produce)
    for k in range(3):
        multiply(store, k, 1, wide - 2, fwd, k, sums)

    def step(j, carry):
        squares, worth = carry
        q = j + 1
        new = zero
        bound = Bound(worths[q])
        for k in range(3):
            gap = (near_box[1 + k, q] if k < 2 else far_box[0, q]).astype(F32)
            low = far_box[1 + k, q].astype(F32)
            lam = scale * slope[k, q]
            if k < 2:
                x = points[k, q]
                tp = lam * gap
            else:
                mu = scale * mult[q]
                g = back[q] + mu
                x = soft(gap, bound.add(g * gap))
                tp = (lam - mu) * gap
            positive = soft(gap, bound.add(tp))
            negative = soft(low, bound.add(-lam * low))
            bound.linear = bound.linear - lam * bias[k : k + 1, :]
            dl = positive - negative - gathered(sums, k, j) - bias[k : k + 1, :]
            dl = jnp.where(gap > 0.0, dl, 0.0)
            dm = x - positive
            slope_out[k, j] = dl
            duals[k, j] = lam[inside]
            if k < 2:
                mult_out[k, j] = dm
            else:
                last_mult[j] = mu[inside]
                last_slope[j] = dm[inside]
                last_pull[j] = g[inside]
            new = new + dl * dl + dm * dm
        own = (q >= 2) & (q < wide - 2)
        return squares + jnp.where(own, new, 0.0), worth + jnp.where(own, bound.total(), 0.0)

    squares, worth = lax.fori_loop(0, wide - 2, step, (zero, zero), unroll=True)
    stats(stat, [own_rows(squares)])
    stats(value, [own_rows(worth)])


def third_body(
    total, steps, near_box, base, mult, slope, duals1, last_mult, last_slope, last_pull,
    fwd, bwd, lower, upper, bias, value0, value1,
    duals, multipliers, slope_out, mult_out, stat,
    points, store, sums, *, cells,
):
    wide, frame = near_box.shape[1:3]
    rows = frame - 2 * EDGE
    inside = slice(EDGE, frame - EDGE)
    scale = scale_of(total, steps[1], cells, (frame, LANES))
    zero = jnp.zeros((frame, LANES), F32)
    slide(3, wide - 2, store, lambda j: [slope[k, j] for k in range(3)])
    for k in range(3):
        multiply(store, k, 0, wide - 2, bwd, k, sums)
    early = lax.broadcasted_iota(jnp.int32, (frame, LANES), 1) < CH

    def point(j, carry):
        q = j + 1
        center, radius = near_box[0, q].astype(F32), near_box[3, q].astype(F32)
        g = base[0, q] - scale * gathered(sums, 0, j)
        bound = Bound(g * (center - radius))
        outs = [center - radius * bound.add(2.0 * radius * g)]
        for k in (1, 2):
            gap = near_box[k, q].astype(F32)
            t = (base[k, q] + scale * (mult[k - 1, j] - gathered(sums, k, j))) * gap
            x = soft(gap, bound.add(t))
            points[k - 1, j] = x
            outs.append(x)
        own = (q >= 2) & (q < wide - 2)
        fresh = [pltpu.roll(value, CH, 1) for value in outs]
        for k in range(3):
            store[k, j] = jnp.where(early, carry[k], fresh[k])
        return tuple(fresh) + (carry[3] + jnp.where(own, bound.total(), 0.0),)

    framed = lax.fori_loop(0, wide - 2, point, (zero,) * 4, unroll=True)[3]
    for k in range(3):
        multiply(store, k, 1, wide - 4, fwd, k, sums)

    scale = scale[:rows]

    def step(i, carry):
        squares, worth = carry
        j = i + 1
        here = pl.ds(pl.multiple_of(i * LANES, LANES), LANES)
        bound = Bound(jnp.zeros((rows, LANES), F32))
        for k in range(3):
            gap = upper[k, :, here].astype(F32)
            low = lower[k, :, here].astype(F32)
            lam = duals1[k, j] + scale * slope[k, j, inside, :]
            bound.linear = bound.linear - lam * bias[k : k + 1, :]
            if k < 2:
                x = points[k, j, inside, :]
                mu = scale * mult[k, j, inside, :]
            else:
                change = scale * last_slope[j]
                mu = last_mult[j] + change
                x = soft(gap, bound.add((last_pull[j] + change) * gap))
            positive = soft(gap, bound.add((lam - mu) * gap))
            negative = soft(low, bound.add(-lam * low))
            dl = positive - negative - inner(sums, k, i, EDGE, rows) - bias[k : k + 1, :]
            dm = x - positive
            duals[k, :, here] = lam
            multipliers[k, :, here] = mu
            slope_out[k, :, here] = dl
            mult_out[k, :, here] = dm
            squares = squares + dl * dl + dm * dm
        return squares, worth + bound.total()

    zero = jnp.zeros((rows, LANES), F32)
    squares, worth = lax.fori_loop(0, wide - 4, step, (zero, zero), unroll=True)
    lane = lax.broadcasted_iota(jnp.int32, (1, LANES), 1)
    start, fixed = (jnp.where(lane == j, value0[0:1, :], 0.0) for j in range(2))
    middle = jnp.where(lane == 0, value1[0:1, :], 0.0)
    stats(stat, [folded(squares), start, middle + fixed, folded(worth) + own_rows(framed) + fixed])


def last_body(total, steps, duals, multipliers, slope, mult, duals_out, mult_out, bounds, *, cells):
    scale = scale_of(total, steps[2], cells, duals.shape[1:])
    for k in range(LAYERS - 1):
        duals_out[k] = duals[k] + scale * slope[k]
        mult_out[k] = multipliers[k] + scale * mult[k]
    values = summed(total) / cells
    lane = lax.broadcasted_iota(jnp.int32, (1, LANES), 1)
    for j in range(ITERS):
        bounds[j] = jnp.sum(jnp.where(lane == j + 1, values, 0.0))


def everyone(partial):
    return lax.all_to_all(partial, ("row", "col"), 0, 0, tiled=True)


def shards(objective, center, radius, lower, upper, kernels, biases, steps):
    rows, cols = objective.shape
    pairs = cols // LANES
    wide = pairs + 4
    frame = rows + 2 * EDGE
    tall = -(-(rows + 2 * WIDE) // 8) * 8
    cells = rows * cols * lax.axis_size("row") * lax.axis_size("col")
    inputs = (objective, center, radius, lower, upper)
    flops = 3 * 2 * 3 * wide * frame * 4 * CH * 3 * LANES
    spread = shape(lax.axis_size("row") * lax.axis_size("col"), LANES)
    small = shape(8, LANES)

    ends = shape(pairs * SENT, LANES)
    strip = shape(9 * rows, HALO_PAIRS * LANES)
    top, bottom, head, tail = call(
        ends_body,
        (ends, ends, strip, strip),
        [pltpu.VMEM(one.shape, one.dtype) for one in inputs] + [pltpu.SemaphoreType.DMA((5,))],
        inputs,
        1 << 20,
        mem=58,
        far=range(5),
    )
    above, below = neighbours(top, bottom, "row")
    left, right = neighbours(head, tail, "col")
    fwd, bwd, bias = weights(kernels, biases)
    corner = shape(2 * HALO_PAIRS * SENT, LANES)
    corner_head, corner_tail = call(corners_body, (corner, corner), [], (above, below, bias), 1 << 20)
    left_corner, right_corner = neighbours(corner_head, corner_tail, "col")

    def start_scratch(count):
        return [
            pltpu.VMEM((3, count, tall, LANES), F32),
            pltpu.VMEM((5, count, frame, LANES), F32),
            pltpu.VMEM((count, frame, LANES), F32),
            pltpu.VMEM((4, count + 1, tall, LANES), F32),
            pltpu.VMEM((4, 3, count - 2, tall, LANES), F32),
        ]

    def start_shapes(count):
        box = shape(4, count, frame, LANES, dtype=BF16)
        full = shape(count, frame, LANES)
        return box, box, full, shape(3, count, frame, LANES), full

    middle = call(
        middle_body,
        start_shapes(pairs - 2) + (shape(3, frame, LANES),),
        start_scratch(pairs),
        inputs + (above, below, fwd, bwd, bias),
        flops,
    )
    near_box, far_box, back, slope0, mult0, stat0, value0 = call(
        first_body,
        start_shapes(wide) + (spread, small),
        start_scratch(10),
        inputs + (left, right, above, below, left_corner, right_corner, fwd, bwd, bias) + tuple(middle),
        flops,
    )

    total0 = everyone(stat0)
    tile = shape(wide - 2, rows, LANES)
    base, slope1, mult1, duals1, last_mult, last_slope, last_pull, stat1, value1 = call(
        functools.partial(second_body, cells=cells),
        (
            shape(3, wide, frame, LANES),
            shape(3, wide - 2, frame, LANES),
            shape(2, wide - 2, frame, LANES),
            shape(3, wide - 2, rows, LANES),
            tile,
            tile,
            tile,
            spread,
            small,
        ),
        [
            pltpu.VMEM((2, wide, frame, LANES), F32),
            pltpu.VMEM((wide, frame, LANES), F32),
            pltpu.VMEM((3, wide + 1, frame, LANES), F32),
            pltpu.VMEM((3, 3, wide, frame, LANES), F32),
        ],
        (total0, steps, near_box, far_box, back, slope0, mult0, fwd, bwd, bias),
        2 * flops,
        scalars=(1,),
    )
    total1 = everyone(stat1)
    out = shape(3, rows, cols)
    duals, multipliers, slope2, mult2, stat2 = call(
        functools.partial(third_body, cells=cells),
        (out, out, out, out, spread),
        [
            pltpu.VMEM((2, wide - 2, frame, LANES), F32),
            pltpu.VMEM((3, wide - 1, frame, LANES), F32),
            pltpu.VMEM((3, 3, wide - 2, frame, LANES), F32),
        ],
        (
            total1, steps, near_box, base, mult1, slope1, duals1, last_mult, last_slope, last_pull,
            fwd, bwd, lower, upper, bias, value0, value1,
        ),
        2 * flops,
        scalars=(1,),
    )
    total2 = everyone(stat2)
    final_duals, final_multipliers, bounds = call(
        functools.partial(last_body, cells=cells),
        (out, out, shape(ITERS)),
        [],
        (total2, steps, duals, multipliers, slope2, mult2),
        1 << 20,
        scalar_outs=(2,),
        scalars=(1,),
    )
    return bounds, final_duals, final_multipliers


def solution(mesh):
    placed = (
        P("row", "col"),
        P("row", "col"),
        P("row", "col"),
        P(None, "row", "col"),
        P(None, "row", "col"),
        P(),
        P(),
        P(),
    )
    return jax.shard_map(
        shards,
        mesh=mesh,
        in_specs=placed,
        out_specs=(P(), P(None, "row", "col"), P(None, "row", "col")),
        check_vma=False,
    )
```

```python
import functools
import math

import jax
import jax.numpy as jnp
from jax import lax
from jax.experimental import pallas as pl
from jax.experimental.pallas import tpu as pltpu
from jax.sharding import PartitionSpec as P

CH = 64
LAYERS = 4
ITERS = 3
EPS = 1e-06
LANES = 2 * CH
HALO_PAIRS = 3
WIDE = 5
EDGE = 4
F32 = jnp.float32
BF16 = jnp.bfloat16

ROWS_SENT = (5, 5, 5, 4, 4, 4, 2, 3, 3)
ROW_START = tuple(sum(ROWS_SENT[:m]) for m in range(9))
SENT = sum(ROWS_SENT)
WINDOW = 4 * CH

VMEM = pl.BlockSpec(memory_space=pltpu.VMEM)
SMEM = pl.BlockSpec(memory_space=pltpu.SMEM)
HBM = pl.BlockSpec(memory_space=pltpu.HBM)


def call(body, outs, scratch, operands, flops, mem=20, scalars=(), far=(), scalar_outs=()):
    specs = [SMEM if j in scalars else HBM if j in far else VMEM for j in range(len(operands))]
    out_specs = tuple(SMEM if j in scalar_outs else VMEM for j in range(len(outs)))
    return pl.pallas_call(
        body,
        out_shape=outs,
        in_specs=specs,
        out_specs=out_specs,
        scratch_shapes=scratch,
        compiler_params=pltpu.CompilerParams(vmem_limit_bytes=mem << 20),
        cost_estimate=pl.CostEstimate(flops=flops, bytes_accessed=4 << 20, transcendentals=0),
    )(*operands)


def shape(*dims, dtype=F32):
    return jax.ShapeDtypeStruct(dims, dtype)


def copies(pairs, sem):
    made = [pltpu.make_async_copy(src, dst, sem.at[j]) for j, (src, dst) in enumerate(pairs)]
    for one in made:
        one.start()
    return made


def finish(made):
    for one in made:
        one.wait()


def split(value):
    high = value.astype(BF16)
    return high, (value - high.astype(F32)).astype(BF16)


def weights_body(kernels, biases, fwd, bwd, bias2):
    zero = jnp.zeros((CH, CH), F32)

    def put(dest, k, j, dh, first, second):
        high, low = split(jnp.concatenate([first, second], axis=1))
        for part, value in enumerate((low, high, high)):
            dest[k, pl.ds(WINDOW * part + CH * j, CH), pl.ds(LANES * dh, LANES)] = value

    for k in range(LAYERS):
        for dh in range(3):
            taps = [kernels[k * 9 + dh * 3 + dw] for dw in range(3)]
            if k < LAYERS - 1:
                for j in range(4):
                    put(fwd, k, j, dh, taps[j] if j < 3 else zero, taps[j - 1] if j > 0 else zero)
            flips = [tap.T for tap in taps]
            for j in range(4):
                put(bwd, k, j, 2 - dh, flips[2 - j] if j < 3 else zero, flips[3 - j] if j > 0 else zero)
    for k in range(LAYERS):
        row = biases[k : k + 1, :]
        bias2[k : k + 1, :] = jnp.concatenate([row, row], axis=1)


def weights(kernels, biases):
    size = (3 * WINDOW, 3 * LANES)
    return call(
        weights_body,
        (shape(LAYERS - 1, *size, dtype=BF16), shape(LAYERS, *size, dtype=BF16), shape(8, LANES)),
        [],
        (kernels.reshape(LAYERS * 9, CH, CH), biases),
        1 << 22,
    )


def sources(objective, center, radius, lower, upper):
    return [
        lambda cols: center[:, cols].astype(F32),
        lambda cols: upper[0, :, cols].astype(F32),
        lambda cols: upper[1, :, cols].astype(F32),
        lambda cols: upper[2, :, cols].astype(F32),
        lambda cols: lower[0, :, cols].astype(F32),
        lambda cols: lower[1, :, cols].astype(F32),
        lambda cols: lower[2, :, cols].astype(F32),
        lambda cols: radius[:, cols].astype(F32),
        lambda cols: objective[:, cols],
    ]


def ends_body(objective, center, radius, lower, upper, top, bottom, far, near, *rest):
    rows, cols = objective.shape
    held, sem = rest[:5], rest[5]
    finish(copies(list(zip((objective, center, radius, lower, upper), held)), sem))
    strip = HALO_PAIRS * LANES
    for m, read in enumerate(sources(*held)):
        here = pl.ds(m * rows, rows)
        sorted_strips(read(pl.ds(0, strip)), read(pl.ds(cols - strip, strip)), far.at[here], near.at[here])
    row = lax.broadcasted_iota(jnp.int32, (rows, LANES), 0)
    outer = (row >= 2) & (row < rows - 2)
    for q in range(cols // LANES):
        values = [read(pl.ds(q * LANES, LANES)) for read in sources(*held)]
        values[3] = jnp.where(outer, values[3] - values[6], values[3])
        for m, value in enumerate(values):
            here = pl.ds(q * SENT + ROW_START[m], ROWS_SENT[m])
            top[here, :] = value[: ROWS_SENT[m]]
            bottom[here, :] = value[rows - ROWS_SENT[m] :]


def odd_column():
    return lax.axis_index("col") % 2 == 1


def sorted_strips(first, last, far, near):
    odd = odd_column()
    far[...] = jnp.where(odd, last, first)
    near[...] = jnp.where(odd, first, last)


class Side:
    def __init__(self, far, near, right):
        self.far, self.near, self.right = far, near, right

    def __getitem__(self, index):
        odd = odd_column()
        other = jnp.logical_not(odd) if self.right else odd
        return jnp.where(other, self.near[index], self.far[index])


def corners_body(above, below, after, far, near):
    del after
    count = HALO_PAIRS * SENT
    size = above.shape[0]
    for part, source in enumerate((above, below)):
        here = pl.ds(part * count, count)
        sorted_strips(source[0:count, :], source[size - count : size, :], far.at[here], near.at[here])


def column(reads, left, right, rows, pairs, m, q):
    if q < HALO_PAIRS:
        return left[m * rows : (m + 1) * rows, q * LANES : (q + 1) * LANES]
    if q >= HALO_PAIRS + pairs:
        q -= HALO_PAIRS + pairs
        return right[m * rows : (m + 1) * rows, q * LANES : (q + 1) * LANES]
    return reads[m](pl.ds((q - HALO_PAIRS) * LANES, LANES))


def halo(middle, left, right, part, pairs, q, m):
    if q < HALO_PAIRS:
        source, at = left, part * HALO_PAIRS + q
    elif q >= HALO_PAIRS + pairs:
        source, at = right, part * HALO_PAIRS + q - HALO_PAIRS - pairs
    else:
        source, at = middle, q - HALO_PAIRS
    return source[pl.ds(at * SENT + ROW_START[m], ROWS_SENT[m]), :]


def neighbours(head, tail, axis):
    count = lax.axis_size(axis)
    before = lax.ppermute(tail, axis, [(i, i + 1) for i in range(count - 1)])
    after = lax.ppermute(head, axis, [(i + 1, i) for i in range(count - 1)])
    return before, after


def partners(far, near, axis):
    count = lax.axis_size(axis)

    def pairs(first):
        return [(i + a, i + 1 - a) for i in range(first, count - 1, 2) for a in (0, 1)]

    return lax.ppermute(far, axis, pairs(1)), lax.ppermute(near, axis, pairs(0))


def roll_rows(value, shift):
    return pltpu.roll(value, shift % value.shape[0], 0)


def slide(maps, count, store, produce):
    rows = store.shape[2]
    early = lax.broadcasted_iota(jnp.int32, (rows, LANES), 1) < CH
    zero = jnp.zeros((rows, LANES), F32)

    def step(q, carry):
        fresh = [pltpu.roll(value, CH, 1) for value in produce(q)]
        for k in range(maps):
            store[k, q] = jnp.where(early, carry[k], fresh[k])
        return tuple(fresh)

    last = lax.fori_loop(0, count, step, (zero,) * maps, unroll=True)
    for k in range(maps):
        store[k, count] = jnp.where(early, last[k], zero)


def multiply(store, k, first, count, weight, layer, sums, exact=False):
    rows = store.shape[2]
    left = store[k, pl.ds(first, count)].reshape(count * rows, LANES)
    right = store[k, pl.ds(first + 1, count)].reshape(count * rows, LANES)
    high, low = split(jnp.concatenate([left, right], axis=1))
    terms = [high, high] if exact else [high, high, low]
    result = jnp.dot(
        jnp.concatenate(terms, axis=1),
        weight[layer, 0 : WINDOW * len(terms), :],
        preferred_element_type=F32,
    )
    for d in range(3):
        sums[k, d, pl.ds(0, count)] = result[:, d * LANES : (d + 1) * LANES].reshape(count, rows, LANES)


def gathered(sums, k, q):
    return roll_rows(sums[k, 0, q], 1) + sums[k, 1, q] + roll_rows(sums[k, 2, q], -1)


def inner(sums, k, q, first, rows):
    parts = [roll_rows(sums[k, d, q], 1 - d - first)[:rows] for d in range(3)]
    return parts[0] + parts[1] + parts[2]


def summed(total):
    return jnp.sum(total[...], axis=0, keepdims=True)


def scale_of(total, step, cells, dims):
    squares = summed(total)[:, 0:1]
    return jnp.broadcast_to(step / jnp.sqrt(squares / (2 * (LAYERS - 1) * cells) + EPS), dims)


def soft(top, bend):
    return 0.5 * top * (1.0 - bend)


class Bound:
    def __init__(self, start):
        self.linear = start
        self.factor = None

    def add(self, t):
        bend = jnp.tanh(t)
        self.linear = self.linear + (jnp.minimum(t, 0.0) - 0.5 * math.log(2.0))
        factor = 1.0 + jnp.abs(bend)
        self.factor = factor if self.factor is None else self.factor * factor
        return bend

    def total(self):
        return self.linear + 0.5 * jnp.log(self.factor)


def folded(value):
    return jnp.sum(value, axis=0, keepdims=True)


def own_rows(value):
    rows = value.shape[0]
    row = lax.broadcasted_iota(jnp.int32, value.shape, 0)
    return folded(jnp.where((row >= EDGE) & (row < rows - EDGE), value, 0.0))


def stats(out, rows):
    lane = lax.broadcasted_iota(jnp.int32, (1, LANES), 1)
    packed = jnp.zeros((1, LANES), F32)
    for j, row in enumerate(rows):
        packed = jnp.where(lane == j, jnp.sum(row, axis=1, keepdims=True), packed)
    out[...] = jnp.broadcast_to(packed, out.shape)


def assemble(reads, above, below, left, right, corners, slots, rows, pairs, raw, gaps, target):
    frame = rows + 2 * EDGE
    blank = jnp.zeros((EDGE, LANES), F32)
    for slot, q in enumerate(slots):
        outside = not 1 <= q < pairs + 2 * HALO_PAIRS - 1
        for m in range(9):
            sent = ROWS_SENT[m]
            if m < 3:
                dest, at, edge = raw.at[m, slot], 0, WIDE
            else:
                dest, at, edge = (target.at[slot] if m == 8 else gaps.at[m - 3, slot]), EDGE - sent, EDGE
                if outside:
                    dest[...] = jnp.zeros((frame, LANES), F32)
                    continue
                if at:
                    dest[0:EDGE, :] = blank
                    dest[EDGE + rows : frame, :] = blank
            dest[at : at + sent, :] = halo(above, *corners, 0, pairs, q, m)
            dest[edge : edge + rows, :] = column(reads, left, right, rows, pairs, m, q)
            dest[edge + rows : edge + rows + sent, :] = halo(below, *corners, 1, pairs, q, m)
    count = len(slots)
    spare = raw.shape[2] - rows - 2 * WIDE
    raw[:, :, rows + 2 * WIDE :, :] = jnp.zeros((3, count, spare, LANES), F32)


def start_convs(raw, target, store, sums, fwd, bwd, frame):
    count = raw.shape[1]
    slide(3, count, store, lambda q: [raw[0, q], 0.5 * raw[1, q], 0.5 * raw[2, q]])
    tugged = store.at[3:4, :, 0:frame, :]
    slide(1, count, tugged, lambda q: [target[q]])
    for k in range(3):
        multiply(store, k, 1, count - 2, fwd, k, sums, exact=True)
    multiply(tugged, 0, 1, count - 2, bwd, LAYERS - 1, sums.at[3:4, :, :, 0:frame, :])


def start_step(slot, out, raw, gaps, target, sums, bias, near_box, far_box, back, slope, mult):
    frame = gaps.shape[2]
    near = [raw[m, slot][1 : 1 + frame] for m in range(3)] + [gaps[4, slot]]
    far = [gaps[m, slot] for m in range(4)]
    for m in range(4):
        near_box[m, out] = near[m].astype(BF16)
        far_box[m, out] = far[m].astype(BF16)
    new = jnp.zeros((frame, LANES), F32)
    for k in range(3):
        gap = near[1 + k] if k < 2 else far[0]
        dl = 0.5 * (gap - far[1 + k]) - inner(sums, k, slot - 1, 1, frame) - bias[k : k + 1, :]
        dl = jnp.where(near[1] > 0.0, dl, 0.0)
        slope[k, out] = dl
        new = new + dl * dl
    tug = gathered(sums.at[3:4, :, :, 0:frame, :], 0, slot - 1)
    back[out] = tug
    bound = Bound(jnp.full((frame, LANES), -4.5 * math.log(2.0), F32))
    dm = -0.5 * gap * bound.add(tug * gap)
    mult[out] = dm
    return new + dm * dm, bound.total(), target[slot] * bias[3:4, :]


def middle_body(
    objective, center, radius, lower, upper, above, below, fwd, bwd, bias,
    near_box, far_box, back, slope, mult, totals,
    raw, gaps, target, store, sums,
):
    rows, cols = objective.shape
    pairs = cols // LANES
    frame = rows + 2 * EDGE
    reads = sources(objective, center, radius, lower, upper)
    slots = range(HALO_PAIRS, HALO_PAIRS + pairs)
    assemble(reads, above, below, None, None, (None, None), slots, rows, pairs, raw, gaps, target)
    start_convs(raw, target, store, sums, fwd, bwd, frame)

    def step(q, carry):
        new = start_step(q + 1, q, raw, gaps, target, sums, bias, near_box, far_box, back, slope, mult)
        return tuple(old + one for old, one in zip(carry, new))

    zero = jnp.zeros((frame, LANES), F32)
    sizes = lax.fori_loop(0, pairs - 2, step, (zero, zero, zero), unroll=True)
    for j in range(3):
        totals[j] = sizes[j]


def first_body(
    objective, center, radius, lower, upper, far, near, above, below, far_corner, near_corner, fwd, bwd, bias,
    near_in, far_in, back_in, slope_in, mult_in, totals,
    near_box, far_box, back, slope, mult, stat, value,
    raw, gaps, target, store, sums,
):
    rows, cols = objective.shape
    pairs = cols // LANES
    frame = rows + 2 * EDGE
    wide = pairs + 4
    reads = sources(objective, center, radius, lower, upper)
    left, right = (Side(far, near, right) for right in (False, True))
    corners = tuple(Side(far_corner, near_corner, right) for right in (False, True))
    slots = list(range(5)) + list(range(wide - 3, wide + 2))
    assemble(reads, above, below, left, right, corners, slots, rows, pairs, raw, gaps, target)
    start_convs(raw, target, store, sums, fwd, bwd, frame)
    here = slice(3, wide - 3)
    near_box[:, here] = near_in[...]
    far_box[:, here] = far_in[...]
    back[here] = back_in[...]
    slope[:, here] = slope_in[...]
    mult[here] = mult_in[...]
    sizes = [totals[j] for j in range(3)]
    for slot, q in ((1, 0), (2, 1), (3, 2), (6, wide - 3), (7, wide - 2), (8, wide - 1)):
        new = start_step(slot, q, raw, gaps, target, sums, bias, near_box, far_box, back, slope, mult)
        if 2 <= q < wide - 2:
            sizes = [old + one for old, one in zip(sizes, new)]
    squares, worth, fixed = (own_rows(one) for one in sizes)
    stats(stat, [squares])
    stats(value, [worth + fixed, fixed])


def second_body(
    total, steps, near_box, far_box, back, slope, mult, fwd, bwd, bias,
    base, slope_out, mult_out, duals, last_mult, last_slope, last_pull, stat, value,
    points, worths, store, sums, *, cells,
):
    wide, frame = near_box.shape[1:3]
    inside = slice(EDGE, frame - EDGE)
    scale = scale_of(total, steps[0], cells, (frame, LANES))
    zero = jnp.zeros((frame, LANES), F32)
    slide(3, wide, store, lambda q: [slope[k, q] for k in range(3)])
    for k in range(3):
        multiply(store, k, 0, wide, bwd, k, sums)

    def produce(q):
        center, radius = near_box[0, q].astype(F32), near_box[3, q].astype(F32)
        g = -(scale * gathered(sums, 0, q))
        base[0, q] = g
        bound = Bound(g * (center - radius))
        outs = [center - radius * bound.add(2.0 * radius * g)]
        for k in (1, 2):
            gap = near_box[k, q].astype(F32)
            g = -(scale * gathered(sums, k, q))
            base[k, q] = g
            x = soft(gap, bound.add(g * gap))
            points[k - 1, q] = x
            outs.append(x)
        worths[q] = bound.total()
        return outs

    slide(3, wide, store, produce)
    for k in range(3):
        multiply(store, k, 1, wide - 2, fwd, k, sums)

    def step(j, carry):
        squares, worth = carry
        q = j + 1
        new = zero
        bound = Bound(worths[q])
        for k in range(3):
            gap = (near_box[1 + k, q] if k < 2 else far_box[0, q]).astype(F32)
            low = far_box[1 + k, q].astype(F32)
            lam = scale * slope[k, q]
            if k < 2:
                x = points[k, q]
                tp = lam * gap
            else:
                mu = scale * mult[q]
                g = back[q] + mu
                x = soft(gap, bound.add(g * gap))
                tp = (lam - mu) * gap
            positive = soft(gap, bound.add(tp))
            negative = soft(low, bound.add(-lam * low))
            bound.linear = bound.linear - lam * bias[k : k + 1, :]
            dl = positive - negative - gathered(sums, k, j) - bias[k : k + 1, :]
            dl = jnp.where(gap > 0.0, dl, 0.0)
            dm = x - positive
            slope_out[k, j] = dl
            duals[k, j] = lam[inside]
            if k < 2:
                mult_out[k, j] = dm
            else:
                last_mult[j] = mu[inside]
                last_slope[j] = dm[inside]
                last_pull[j] = g[inside]
            new = new + dl * dl + dm * dm
        own = (q >= 2) & (q < wide - 2)
        return squares + jnp.where(own, new, 0.0), worth + jnp.where(own, bound.total(), 0.0)

    squares, worth = lax.fori_loop(0, wide - 2, step, (zero, zero), unroll=True)
    stats(stat, [own_rows(squares)])
    stats(value, [own_rows(worth)])


def third_body(
    total, steps, near_box, base, mult, slope, duals1, last_mult, last_slope, last_pull,
    fwd, bwd, lower, upper, bias, value0, value1,
    duals, multipliers, slope_out, mult_out, stat,
    points, store, sums, *, cells,
):
    wide, frame = near_box.shape[1:3]
    rows = frame - 2 * EDGE
    inside = slice(EDGE, frame - EDGE)
    scale = scale_of(total, steps[1], cells, (frame, LANES))
    zero = jnp.zeros((frame, LANES), F32)
    slide(3, wide - 2, store, lambda j: [slope[k, j] for k in range(3)])
    for k in range(3):
        multiply(store, k, 0, wide - 2, bwd, k, sums)
    early = lax.broadcasted_iota(jnp.int32, (frame, LANES), 1) < CH

    def point(j, carry):
        q = j + 1
        center, radius = near_box[0, q].astype(F32), near_box[3, q].astype(F32)
        g = base[0, q] - scale * gathered(sums, 0, j)
        bound = Bound(g * (center - radius))
        outs = [center - radius * bound.add(2.0 * radius * g)]
        for k in (1, 2):
            gap = near_box[k, q].astype(F32)
            t = (base[k, q] + scale * (mult[k - 1, j] - gathered(sums, k, j))) * gap
            x = soft(gap, bound.add(t))
            points[k - 1, j] = x
            outs.append(x)
        own = (q >= 2) & (q < wide - 2)
        fresh = [pltpu.roll(value, CH, 1) for value in outs]
        for k in range(3):
            store[k, j] = jnp.where(early, carry[k], fresh[k])
        return tuple(fresh) + (carry[3] + jnp.where(own, bound.total(), 0.0),)

    framed = lax.fori_loop(0, wide - 2, point, (zero,) * 4, unroll=True)[3]
    for k in range(3):
        multiply(store, k, 1, wide - 4, fwd, k, sums)

    scale = scale[:rows]

    def step(i, carry):
        squares, worth = carry
        j = i + 1
        here = pl.ds(pl.multiple_of(i * LANES, LANES), LANES)
        bound = Bound(jnp.zeros((rows, LANES), F32))
        for k in range(3):
            gap = upper[k, :, here].astype(F32)
            low = lower[k, :, here].astype(F32)
            lam = duals1[k, j] + scale * slope[k, j, inside, :]
            bound.linear = bound.linear - lam * bias[k : k + 1, :]
            if k < 2:
                x = points[k, j, inside, :]
                mu = scale * mult[k, j, inside, :]
            else:
                change = scale * last_slope[j]
                mu = last_mult[j] + change
                x = soft(gap, bound.add((last_pull[j] + change) * gap))
            positive = soft(gap, bound.add((lam - mu) * gap))
            negative = soft(low, bound.add(-lam * low))
            dl = positive - negative - inner(sums, k, i, EDGE, rows) - bias[k : k + 1, :]
            dm = x - positive
            duals[k, :, here] = lam
            multipliers[k, :, here] = mu
            slope_out[k, :, here] = dl
            mult_out[k, :, here] = dm
            squares = squares + dl * dl + dm * dm
        return squares, worth + bound.total()

    zero = jnp.zeros((rows, LANES), F32)
    squares, worth = lax.fori_loop(0, wide - 4, step, (zero, zero), unroll=True)
    lane = lax.broadcasted_iota(jnp.int32, (1, LANES), 1)
    start, fixed = (jnp.where(lane == j, value0[0:1, :], 0.0) for j in range(2))
    middle = jnp.where(lane == 0, value1[0:1, :], 0.0)
    stats(stat, [folded(squares), start, middle + fixed, folded(worth) + own_rows(framed) + fixed])


def last_body(total, steps, duals, multipliers, slope, mult, duals_out, mult_out, bounds, *, cells):
    scale = scale_of(total, steps[2], cells, duals.shape[1:])
    for k in range(LAYERS - 1):
        duals_out[k] = duals[k] + scale * slope[k]
        mult_out[k] = multipliers[k] + scale * mult[k]
    values = summed(total) / cells
    lane = lax.broadcasted_iota(jnp.int32, (1, LANES), 1)
    for j in range(ITERS):
        bounds[j] = jnp.sum(jnp.where(lane == j + 1, values, 0.0))


def everyone(partial):
    return lax.all_to_all(partial, ("row", "col"), 0, 0, tiled=True)


def shards(objective, center, radius, lower, upper, kernels, biases, steps):
    rows, cols = objective.shape
    pairs = cols // LANES
    wide = pairs + 4
    frame = rows + 2 * EDGE
    tall = -(-(rows + 2 * WIDE) // 8) * 8
    cells = rows * cols * lax.axis_size("row") * lax.axis_size("col")
    inputs = (objective, center, radius, lower, upper)
    flops = 3 * 2 * 3 * wide * frame * 4 * CH * 3 * LANES
    spread = shape(lax.axis_size("row") * lax.axis_size("col"), LANES)
    small = shape(8, LANES)

    ends = shape(pairs * SENT, LANES)
    strip = shape(9 * rows, HALO_PAIRS * LANES)
    top, bottom, far, near = call(
        ends_body,
        (ends, ends, strip, strip),
        [pltpu.VMEM(one.shape, one.dtype) for one in inputs] + [pltpu.SemaphoreType.DMA((5,))],
        inputs,
        1 << 20,
        mem=58,
        far=range(5),
    )
    above, below = neighbours(top, bottom, "row")
    far, near = partners(far, near, "col")
    fwd, bwd, bias = weights(kernels, biases)
    corner = shape(2 * HALO_PAIRS * SENT, LANES)
    far_corner, near_corner = call(corners_body, (corner, corner), [], (above, below, bias), 1 << 20)
    far_corner, near_corner = partners(far_corner, near_corner, "col")

    def start_scratch(count):
        return [
            pltpu.VMEM((3, count, tall, LANES), F32),
            pltpu.VMEM((5, count, frame, LANES), F32),
            pltpu.VMEM((count, frame, LANES), F32),
            pltpu.VMEM((4, count + 1, tall, LANES), F32),
            pltpu.VMEM((4, 3, count - 2, tall, LANES), F32),
        ]

    def start_shapes(count):
        box = shape(4, count, frame, LANES, dtype=BF16)
        full = shape(count, frame, LANES)
        return box, box, full, shape(3, count, frame, LANES), full

    middle = call(
        middle_body,
        start_shapes(pairs - 2) + (shape(3, frame, LANES),),
        start_scratch(pairs),
        inputs + (above, below, fwd, bwd, bias),
        flops,
    )
    near_box, far_box, back, slope0, mult0, stat0, value0 = call(
        first_body,
        start_shapes(wide) + (spread, small),
        start_scratch(10),
        inputs + (far, near, above, below, far_corner, near_corner, fwd, bwd, bias) + tuple(middle),
        flops,
    )

    total0 = everyone(stat0)
    tile = shape(wide - 2, rows, LANES)
    base, slope1, mult1, duals1, last_mult, last_slope, last_pull, stat1, value1 = call(
        functools.partial(second_body, cells=cells),
        (
            shape(3, wide, frame, LANES),
            shape(3, wide - 2, frame, LANES),
            shape(2, wide - 2, frame, LANES),
            shape(3, wide - 2, rows, LANES),
            tile,
            tile,
            tile,
            spread,
            small,
        ),
        [
            pltpu.VMEM((2, wide, frame, LANES), F32),
            pltpu.VMEM((wide, frame, LANES), F32),
            pltpu.VMEM((3, wide + 1, frame, LANES), F32),
            pltpu.VMEM((3, 3, wide, frame, LANES), F32),
        ],
        (total0, steps, near_box, far_box, back, slope0, mult0, fwd, bwd, bias),
        2 * flops,
        scalars=(1,),
    )
    total1 = everyone(stat1)
    out = shape(3, rows, cols)
    duals, multipliers, slope2, mult2, stat2 = call(
        functools.partial(third_body, cells=cells),
        (out, out, out, out, spread),
        [
            pltpu.VMEM((2, wide - 2, frame, LANES), F32),
            pltpu.VMEM((3, wide - 1, frame, LANES), F32),
            pltpu.VMEM((3, 3, wide - 2, frame, LANES), F32),
        ],
        (
            total1, steps, near_box, base, mult1, slope1, duals1, last_mult, last_slope, last_pull,
            fwd, bwd, lower, upper, bias, value0, value1,
        ),
        2 * flops,
        scalars=(1,),
    )
    total2 = everyone(stat2)
    final_duals, final_multipliers, bounds = call(
        functools.partial(last_body, cells=cells),
        (out, out, shape(ITERS)),
        [],
        (total2, steps, duals, multipliers, slope2, mult2),
        1 << 20,
        scalar_outs=(2,),
        scalars=(1,),
    )
    return bounds, final_duals, final_multipliers


def solution(mesh):
    placed = (
        P("row", "col"),
        P("row", "col"),
        P("row", "col"),
        P(None, "row", "col"),
        P(None, "row", "col"),
        P(),
        P(),
        P(),
    )
    return jax.shard_map(
        shards,
        mesh=mesh,
        in_specs=placed,
        out_specs=(P(), P(None, "row", "col"), P(None, "row", "col")),
        check_vma=False,
    )
```

```python
import functools
import math

import jax
import jax.numpy as jnp
from jax import lax
from jax.experimental import pallas as pl
from jax.experimental.pallas import tpu as pltpu
from jax.sharding import PartitionSpec as P

CH = 64
LAYERS = 4
ITERS = 3
EPS = 1e-06
LANES = 2 * CH
HALO_PAIRS = 3
WIDE = 5
EDGE = 4
F32 = jnp.float32
BF16 = jnp.bfloat16

ROWS_SENT = (5, 5, 5, 4, 4, 4, 2, 3, 3)
ROW_START = tuple(sum(ROWS_SENT[:m]) for m in range(9))
SENT = sum(ROWS_SENT)
WINDOW = 4 * CH

VMEM = pl.BlockSpec(memory_space=pltpu.VMEM)
SMEM = pl.BlockSpec(memory_space=pltpu.SMEM)
HBM = pl.BlockSpec(memory_space=pltpu.HBM)


def call(body, outs, scratch, operands, flops, mem=20, scalars=(), far=(), scalar_outs=(), far_outs=()):
    specs = [SMEM if j in scalars else HBM if j in far else VMEM for j in range(len(operands))]
    out_specs = tuple(SMEM if j in scalar_outs else HBM if j in far_outs else VMEM for j in range(len(outs)))
    return pl.pallas_call(
        body,
        out_shape=outs,
        in_specs=specs,
        out_specs=out_specs,
        scratch_shapes=scratch,
        compiler_params=pltpu.CompilerParams(vmem_limit_bytes=mem << 20),
        cost_estimate=pl.CostEstimate(flops=flops, bytes_accessed=4 << 20, transcendentals=0),
    )(*operands)


def shape(*dims, dtype=F32):
    return jax.ShapeDtypeStruct(dims, dtype)


def copies(pairs, sem):
    made = [pltpu.make_async_copy(src, dst, sem.at[j]) for j, (src, dst) in enumerate(pairs)]
    for one in made:
        one.start()
    return made


def finish(made):
    for one in made:
        one.wait()


def split(value):
    high = value.astype(BF16)
    return high, (value - high.astype(F32)).astype(BF16)


def weights_body(kernels, biases, fwd, bwd, bias2):
    zero = jnp.zeros((CH, CH), F32)

    def put(dest, k, j, dh, first, second):
        high, low = split(jnp.concatenate([first, second], axis=1))
        for part, value in enumerate((low, high, high)):
            dest[k, pl.ds(WINDOW * part + CH * j, CH), pl.ds(LANES * dh, LANES)] = value

    for k in range(LAYERS):
        for dh in range(3):
            taps = [kernels[k * 9 + dh * 3 + dw] for dw in range(3)]
            if k < LAYERS - 1:
                for j in range(4):
                    put(fwd, k, j, dh, taps[j] if j < 3 else zero, taps[j - 1] if j > 0 else zero)
            flips = [tap.T for tap in taps]
            for j in range(4):
                put(bwd, k, j, 2 - dh, flips[2 - j] if j < 3 else zero, flips[3 - j] if j > 0 else zero)
    for k in range(LAYERS):
        row = biases[k : k + 1, :]
        bias2[k : k + 1, :] = jnp.concatenate([row, row], axis=1)


def weights(kernels, biases):
    size = (3 * WINDOW, 3 * LANES)
    return call(
        weights_body,
        (shape(LAYERS - 1, *size, dtype=BF16), shape(LAYERS, *size, dtype=BF16), shape(8, LANES)),
        [],
        (kernels.reshape(LAYERS * 9, CH, CH), biases),
        1 << 22,
    )


def sources(objective, center, radius, lower, upper):
    return [
        lambda cols: center[:, cols].astype(F32),
        lambda cols: upper[0, :, cols].astype(F32),
        lambda cols: upper[1, :, cols].astype(F32),
        lambda cols: upper[2, :, cols].astype(F32),
        lambda cols: lower[0, :, cols].astype(F32),
        lambda cols: lower[1, :, cols].astype(F32),
        lambda cols: lower[2, :, cols].astype(F32),
        lambda cols: radius[:, cols].astype(F32),
        lambda cols: objective[:, cols],
    ]


def ends_body(objective, center, radius, lower, upper, *rest):
    rows, cols = objective.shape
    outs, held, made, sem = rest[:4], rest[4:9], rest[9:13], rest[13]
    arrivals = copies(list(zip((objective, center, radius, lower, upper), held)), sem)
    finish(arrivals)
    strip = HALO_PAIRS * LANES
    for q in range(cols // LANES):
        values = [read(pl.ds(q * LANES, LANES)) for read in sources(*held)]
        ends_of(values, made[0], made[1], q * SENT)
    leaving = copies(list(zip(made[:2], outs[:2])), sem)
    for m, read in enumerate(sources(*held)):
        here = pl.ds(m * rows, rows)
        sorted_strips(
            "col", read(pl.ds(0, strip)), read(pl.ds(cols - strip, strip)), made[2].at[here], made[3].at[here]
        )
    finish(leaving + copies(list(zip(made[2:], outs[2:])), sem.at[2:4]))


def ends_of(values, far, near, start):
    rows = values[0].shape[0]
    row = lax.broadcasted_iota(jnp.int32, (rows, LANES), 0)
    outer = (row >= 2) & (row < rows - 2)
    values[3] = jnp.where(outer, values[3] - values[6], values[3])
    for m, value in enumerate(values):
        here = pl.ds(start + ROW_START[m], ROWS_SENT[m])
        sorted_strips("row", value[: ROWS_SENT[m]], value[rows - ROWS_SENT[m] :], far.at[here], near.at[here])


def odd_index(axis):
    return lax.axis_index(axis) % 2 == 1


def sorted_strips(axis, first, last, far, near):
    odd = odd_index(axis)
    far[...] = jnp.where(odd, last, first)
    near[...] = jnp.where(odd, first, last)


class Side:
    def __init__(self, axis, far, near, after):
        self.axis, self.far, self.near, self.after = axis, far, near, after
        self.shape = far.shape

    def __getitem__(self, index):
        odd = odd_index(self.axis)
        near = jnp.logical_not(odd) if self.after else odd
        return jnp.where(near, self.near[index], self.far[index])


def sides(axis, far, near):
    return Side(axis, far, near, False), Side(axis, far, near, True)


def corners_body(far_rows, near_rows, after, far, near):
    del after
    count = HALO_PAIRS * SENT
    size = far_rows.shape[0]
    for part, source in enumerate(sides("row", far_rows, near_rows)):
        here = pl.ds(part * count, count)
        sorted_strips("col", source[0:count, :], source[size - count : size, :], far.at[here], near.at[here])


def column(reads, left, right, rows, pairs, m, q):
    if q < HALO_PAIRS:
        return left[m * rows : (m + 1) * rows, q * LANES : (q + 1) * LANES]
    if q >= HALO_PAIRS + pairs:
        q -= HALO_PAIRS + pairs
        return right[m * rows : (m + 1) * rows, q * LANES : (q + 1) * LANES]
    return reads[m](pl.ds((q - HALO_PAIRS) * LANES, LANES))


def halo(middle, left, right, part, pairs, q, m):
    if q < HALO_PAIRS:
        source, at = left, part * HALO_PAIRS + q
    elif q >= HALO_PAIRS + pairs:
        source, at = right, part * HALO_PAIRS + q - HALO_PAIRS - pairs
    else:
        source, at = middle, q - HALO_PAIRS
    return source[pl.ds(at * SENT + ROW_START[m], ROWS_SENT[m]), :]


def partners(far, near, axis):
    count = lax.axis_size(axis)

    def pairs(first):
        return [(i + a, i + 1 - a) for i in range(first, count - 1, 2) for a in (0, 1)]

    return lax.ppermute(far, axis, pairs(1)), lax.ppermute(near, axis, pairs(0))


def roll_rows(value, shift):
    return pltpu.roll(value, shift % value.shape[0], 0)


def slide(maps, count, store, produce):
    rows = store.shape[2]
    early = lax.broadcasted_iota(jnp.int32, (rows, LANES), 1) < CH
    zero = jnp.zeros((rows, LANES), F32)

    def step(q, carry):
        fresh = [pltpu.roll(value, CH, 1) for value in produce(q)]
        for k in range(maps):
            store[k, q] = jnp.where(early, carry[k], fresh[k])
        return tuple(fresh)

    last = lax.fori_loop(0, count, step, (zero,) * maps, unroll=True)
    for k in range(maps):
        store[k, count] = jnp.where(early, last[k], zero)


def multiply(store, k, first, count, weight, layer, sums, exact=False):
    rows = store.shape[2]
    left = store[k, pl.ds(first, count)].reshape(count * rows, LANES)
    right = store[k, pl.ds(first + 1, count)].reshape(count * rows, LANES)
    high, low = split(jnp.concatenate([left, right], axis=1))
    terms = [high, high] if exact else [high, high, low]
    result = jnp.dot(
        jnp.concatenate(terms, axis=1),
        weight[layer, 0 : WINDOW * len(terms), :],
        preferred_element_type=F32,
    )
    for d in range(3):
        sums[k, d, pl.ds(0, count)] = result[:, d * LANES : (d + 1) * LANES].reshape(count, rows, LANES)


def gathered(sums, k, q):
    return roll_rows(sums[k, 0, q], 1) + sums[k, 1, q] + roll_rows(sums[k, 2, q], -1)


def inner(sums, k, q, first, rows):
    parts = [roll_rows(sums[k, d, q], 1 - d - first)[:rows] for d in range(3)]
    return parts[0] + parts[1] + parts[2]


def summed(total):
    return jnp.sum(total[...], axis=0, keepdims=True)


def scale_of(total, step, cells, dims):
    squares = summed(total)[:, 0:1]
    return jnp.broadcast_to(step / jnp.sqrt(squares / (2 * (LAYERS - 1) * cells) + EPS), dims)


def soft(top, bend):
    return 0.5 * top * (1.0 - bend)


class Bound:
    def __init__(self, start):
        self.linear = start
        self.factor = None

    def add(self, t):
        bend = jnp.tanh(t)
        self.linear = self.linear + (jnp.minimum(t, 0.0) - 0.5 * math.log(2.0))
        factor = 1.0 + jnp.abs(bend)
        self.factor = factor if self.factor is None else self.factor * factor
        return bend

    def total(self):
        return self.linear + 0.5 * jnp.log(self.factor)


def folded(value):
    return jnp.sum(value, axis=0, keepdims=True)


def own_rows(value):
    rows = value.shape[0]
    row = lax.broadcasted_iota(jnp.int32, value.shape, 0)
    return folded(jnp.where((row >= EDGE) & (row < rows - EDGE), value, 0.0))


def stats(out, rows):
    lane = lax.broadcasted_iota(jnp.int32, (1, LANES), 1)
    packed = jnp.zeros((1, LANES), F32)
    for j, row in enumerate(rows):
        packed = jnp.where(lane == j, jnp.sum(row, axis=1, keepdims=True), packed)
    out[...] = jnp.broadcast_to(packed, out.shape)


def assemble(reads, above, below, left, right, corners, slots, rows, pairs, raw, gaps, target):
    frame = rows + 2 * EDGE
    blank = jnp.zeros((EDGE, LANES), F32)
    for slot, q in enumerate(slots):
        outside = not 1 <= q < pairs + 2 * HALO_PAIRS - 1
        for m in range(9):
            sent = ROWS_SENT[m]
            if m < 3:
                dest, at, edge = raw.at[m, slot], 0, WIDE
            else:
                dest, at, edge = (target.at[slot] if m == 8 else gaps.at[m - 3, slot]), EDGE - sent, EDGE
                if outside:
                    dest[...] = jnp.zeros((frame, LANES), F32)
                    continue
                if at:
                    dest[0:EDGE, :] = blank
                    dest[EDGE + rows : frame, :] = blank
            dest[at : at + sent, :] = halo(above, *corners, 0, pairs, q, m)
            dest[edge : edge + rows, :] = column(reads, left, right, rows, pairs, m, q)
            dest[edge + rows : edge + rows + sent, :] = halo(below, *corners, 1, pairs, q, m)
    count = len(slots)
    spare = raw.shape[2] - rows - 2 * WIDE
    raw[:, :, rows + 2 * WIDE :, :] = jnp.zeros((3, count, spare, LANES), F32)


def start_convs(raw, target, store, sums, fwd, bwd, frame):
    count = raw.shape[1]
    slide(3, count, store, lambda q: [raw[0, q], 0.5 * raw[1, q], 0.5 * raw[2, q]])
    tugged = store.at[3:4, :, 0:frame, :]
    slide(1, count, tugged, lambda q: [target[q]])
    for k in range(3):
        multiply(store, k, 1, count - 2, fwd, k, sums, exact=True)
    multiply(tugged, 0, 1, count - 2, bwd, LAYERS - 1, sums.at[3:4, :, :, 0:frame, :])


def start_step(slot, out, raw, gaps, target, sums, bias, near_box, far_box, back, slope, mult):
    frame = gaps.shape[2]
    near = [raw[m, slot][1 : 1 + frame] for m in range(3)] + [gaps[4, slot]]
    far = [gaps[m, slot] for m in range(4)]
    for m in range(4):
        near_box[m, out] = near[m].astype(BF16)
        far_box[m, out] = far[m].astype(BF16)
    new = jnp.zeros((frame, LANES), F32)
    for k in range(3):
        gap = near[1 + k] if k < 2 else far[0]
        dl = 0.5 * (gap - far[1 + k]) - inner(sums, k, slot - 1, 1, frame) - bias[k : k + 1, :]
        dl = jnp.where(near[1] > 0.0, dl, 0.0)
        slope[k, out] = dl
        new = new + dl * dl
    tug = gathered(sums.at[3:4, :, :, 0:frame, :], 0, slot - 1)
    back[out] = tug
    bound = Bound(jnp.full((frame, LANES), -4.5 * math.log(2.0), F32))
    dm = -0.5 * gap * bound.add(tug * gap)
    mult[out] = dm
    return new + dm * dm, bound.total(), target[slot] * bias[3:4, :]


def middle_body(
    objective, center, radius, lower, upper, far_rows, near_rows, fwd, bwd, bias,
    near_box, far_box, back, slope, mult, totals,
    raw, gaps, target, store, sums,
):
    rows, cols = objective.shape
    pairs = cols // LANES
    frame = rows + 2 * EDGE
    reads = sources(objective, center, radius, lower, upper)
    above, below = sides("row", far_rows, near_rows)
    slots = range(HALO_PAIRS, HALO_PAIRS + pairs)
    assemble(reads, above, below, None, None, (None, None), slots, rows, pairs, raw, gaps, target)
    start_convs(raw, target, store, sums, fwd, bwd, frame)

    def step(q, carry):
        new = start_step(q + 1, q, raw, gaps, target, sums, bias, near_box, far_box, back, slope, mult)
        return tuple(old + one for old, one in zip(carry, new))

    zero = jnp.zeros((frame, LANES), F32)
    sizes = lax.fori_loop(0, pairs - 2, step, (zero, zero, zero), unroll=True)
    for j in range(3):
        totals[j] = sizes[j]


def first_body(
    objective, center, radius, lower, upper, far_cols, near_cols, far_rows, near_rows, far_corner, near_corner, fwd, bwd, bias,
    near_in, far_in, back_in, slope_in, mult_in, totals,
    near_box, far_box, back, slope, mult, stat, value,
    raw, gaps, target, store, sums,
):
    rows, cols = objective.shape
    pairs = cols // LANES
    frame = rows + 2 * EDGE
    wide = pairs + 4
    reads = sources(objective, center, radius, lower, upper)
    above, below = sides("row", far_rows, near_rows)
    left, right = sides("col", far_cols, near_cols)
    corners = sides("col", far_corner, near_corner)
    slots = list(range(5)) + list(range(wide - 3, wide + 2))
    assemble(reads, above, below, left, right, corners, slots, rows, pairs, raw, gaps, target)
    start_convs(raw, target, store, sums, fwd, bwd, frame)
    here = slice(3, wide - 3)
    near_box[:, here] = near_in[...]
    far_box[:, here] = far_in[...]
    back[here] = back_in[...]
    slope[:, here] = slope_in[...]
    mult[here] = mult_in[...]
    sizes = [totals[j] for j in range(3)]
    for slot, q in ((1, 0), (2, 1), (3, 2), (6, wide - 3), (7, wide - 2), (8, wide - 1)):
        new = start_step(slot, q, raw, gaps, target, sums, bias, near_box, far_box, back, slope, mult)
        if 2 <= q < wide - 2:
            sizes = [old + one for old, one in zip(sizes, new)]
    squares, worth, fixed = (own_rows(one) for one in sizes)
    stats(stat, [squares])
    stats(value, [worth + fixed, fixed])


def second_body(
    total, steps, near_box, far_box, back, slope, mult, fwd, bwd, bias,
    base, slope_out, mult_out, duals, last_mult, last_slope, last_pull, stat, value,
    points, worths, store, sums, *, cells,
):
    wide, frame = near_box.shape[1:3]
    inside = slice(EDGE, frame - EDGE)
    scale = scale_of(total, steps[0], cells, (frame, LANES))
    zero = jnp.zeros((frame, LANES), F32)
    slide(3, wide, store, lambda q: [slope[k, q] for k in range(3)])
    for k in range(3):
        multiply(store, k, 0, wide, bwd, k, sums)

    def produce(q):
        center, radius = near_box[0, q].astype(F32), near_box[3, q].astype(F32)
        g = -(scale * gathered(sums, 0, q))
        base[0, q] = g
        bound = Bound(g * (center - radius))
        outs = [center - radius * bound.add(2.0 * radius * g)]
        for k in (1, 2):
            gap = near_box[k, q].astype(F32)
            g = -(scale * gathered(sums, k, q))
            base[k, q] = g
            x = soft(gap, bound.add(g * gap))
            points[k - 1, q] = x
            outs.append(x)
        worths[q] = bound.total()
        return outs

    slide(3, wide, store, produce)
    for k in range(3):
        multiply(store, k, 1, wide - 2, fwd, k, sums)

    def step(j, carry):
        squares, worth = carry
        q = j + 1
        new = zero
        bound = Bound(worths[q])
        for k in range(3):
            gap = (near_box[1 + k, q] if k < 2 else far_box[0, q]).astype(F32)
            low = far_box[1 + k, q].astype(F32)
            lam = scale * slope[k, q]
            if k < 2:
                x = points[k, q]
                tp = lam * gap
            else:
                mu = scale * mult[q]
                g = back[q] + mu
                x = soft(gap, bound.add(g * gap))
                tp = (lam - mu) * gap
            positive = soft(gap, bound.add(tp))
            negative = soft(low, bound.add(-lam * low))
            bound.linear = bound.linear - lam * bias[k : k + 1, :]
            dl = positive - negative - gathered(sums, k, j) - bias[k : k + 1, :]
            dl = jnp.where(gap > 0.0, dl, 0.0)
            dm = x - positive
            slope_out[k, j] = dl
            duals[k, j] = lam[inside]
            if k < 2:
                mult_out[k, j] = dm
            else:
                last_mult[j] = mu[inside]
                last_slope[j] = dm[inside]
                last_pull[j] = g[inside]
            new = new + dl * dl + dm * dm
        own = (q >= 2) & (q < wide - 2)
        return squares + jnp.where(own, new, 0.0), worth + jnp.where(own, bound.total(), 0.0)

    squares, worth = lax.fori_loop(0, wide - 2, step, (zero, zero), unroll=True)
    stats(stat, [own_rows(squares)])
    stats(value, [own_rows(worth)])


def third_body(
    total, steps, near_box, base, mult, slope, duals1, last_mult, last_slope, last_pull,
    fwd, bwd, lower, upper, bias, value0, value1,
    duals, multipliers, slope_out, mult_out, stat,
    points, store, sums, *, cells,
):
    wide, frame = near_box.shape[1:3]
    rows = frame - 2 * EDGE
    inside = slice(EDGE, frame - EDGE)
    scale = scale_of(total, steps[1], cells, (frame, LANES))
    zero = jnp.zeros((frame, LANES), F32)
    slide(3, wide - 2, store, lambda j: [slope[k, j] for k in range(3)])
    for k in range(3):
        multiply(store, k, 0, wide - 2, bwd, k, sums)
    early = lax.broadcasted_iota(jnp.int32, (frame, LANES), 1) < CH

    def point(j, carry):
        q = j + 1
        center, radius = near_box[0, q].astype(F32), near_box[3, q].astype(F32)
        g = base[0, q] - scale * gathered(sums, 0, j)
        bound = Bound(g * (center - radius))
        outs = [center - radius * bound.add(2.0 * radius * g)]
        for k in (1, 2):
            gap = near_box[k, q].astype(F32)
            t = (base[k, q] + scale * (mult[k - 1, j] - gathered(sums, k, j))) * gap
            x = soft(gap, bound.add(t))
            points[k - 1, j] = x
            outs.append(x)
        own = (q >= 2) & (q < wide - 2)
        fresh = [pltpu.roll(value, CH, 1) for value in outs]
        for k in range(3):
            store[k, j] = jnp.where(early, carry[k], fresh[k])
        return tuple(fresh) + (carry[3] + jnp.where(own, bound.total(), 0.0),)

    framed = lax.fori_loop(0, wide - 2, point, (zero,) * 4, unroll=True)[3]
    for k in range(3):
        multiply(store, k, 1, wide - 4, fwd, k, sums)

    scale = scale[:rows]

    def step(i, carry):
        squares, worth = carry
        j = i + 1
        here = pl.ds(pl.multiple_of(i * LANES, LANES), LANES)
        bound = Bound(jnp.zeros((rows, LANES), F32))
        for k in range(3):
            gap = upper[k, :, here].astype(F32)
            low = lower[k, :, here].astype(F32)
            lam = duals1[k, j] + scale * slope[k, j, inside, :]
            bound.linear = bound.linear - lam * bias[k : k + 1, :]
            if k < 2:
                x = points[k, j, inside, :]
                mu = scale * mult[k, j, inside, :]
            else:
                change = scale * last_slope[j]
                mu = last_mult[j] + change
                x = soft(gap, bound.add((last_pull[j] + change) * gap))
            positive = soft(gap, bound.add((lam - mu) * gap))
            negative = soft(low, bound.add(-lam * low))
            dl = positive - negative - inner(sums, k, i, EDGE, rows) - bias[k : k + 1, :]
            dm = x - positive
            duals[k, :, here] = lam
            multipliers[k, :, here] = mu
            slope_out[k, :, here] = dl
            mult_out[k, :, here] = dm
            squares = squares + dl * dl + dm * dm
        return squares, worth + bound.total()

    zero = jnp.zeros((rows, LANES), F32)
    squares, worth = lax.fori_loop(0, wide - 4, step, (zero, zero), unroll=True)
    lane = lax.broadcasted_iota(jnp.int32, (1, LANES), 1)
    start, fixed = (jnp.where(lane == j, value0[0:1, :], 0.0) for j in range(2))
    middle = jnp.where(lane == 0, value1[0:1, :], 0.0)
    stats(stat, [folded(squares), start, middle + fixed, folded(worth) + own_rows(framed) + fixed])


def last_body(
    total, steps, duals, multipliers, slope, mult, duals_far, mult_far, bounds,
    duals_out, mult_out, sem, *, cells,
):
    scale = scale_of(total, steps[2], cells, duals.shape[1:])
    leaving = []
    for k in range(LAYERS - 1):
        duals_out[k] = duals[k] + scale * slope[k]
        mult_out[k] = multipliers[k] + scale * mult[k]
        moves = [(duals_out.at[k], duals_far.at[k]), (mult_out.at[k], mult_far.at[k])]
        leaving += copies(moves, sem.at[2 * k : 2 * k + 2])
    values = summed(total) / cells
    lane = lax.broadcasted_iota(jnp.int32, (1, LANES), 1)
    for j in range(ITERS):
        bounds[j] = jnp.sum(jnp.where(lane == j + 1, values, 0.0))
    finish(leaving)


def everyone(partial):
    return lax.all_to_all(partial, ("row", "col"), 0, 0, tiled=True)


def shards(objective, center, radius, lower, upper, kernels, biases, steps):
    rows, cols = objective.shape
    pairs = cols // LANES
    wide = pairs + 4
    frame = rows + 2 * EDGE
    tall = -(-(rows + 2 * WIDE) // 8) * 8
    cells = rows * cols * lax.axis_size("row") * lax.axis_size("col")
    inputs = (objective, center, radius, lower, upper)
    flops = 3 * 2 * 3 * wide * frame * 4 * CH * 3 * LANES
    spread = shape(lax.axis_size("row") * lax.axis_size("col"), LANES)
    small = shape(8, LANES)

    ends = shape(pairs * SENT, LANES)
    strip = shape(9 * rows, HALO_PAIRS * LANES)
    made = (ends, ends, strip, strip)
    far_rows, near_rows, far_cols, near_cols = call(
        ends_body,
        made,
        [pltpu.VMEM(one.shape, one.dtype) for one in inputs + made] + [pltpu.SemaphoreType.DMA((5,))],
        inputs,
        1 << 20,
        mem=58,
        far=range(5),
        far_outs=range(4),
    )
    far_rows, near_rows = partners(far_rows, near_rows, "row")
    far_cols, near_cols = partners(far_cols, near_cols, "col")
    fwd, bwd, bias = weights(kernels, biases)
    corner = shape(2 * HALO_PAIRS * SENT, LANES)
    far_corner, near_corner = call(corners_body, (corner, corner), [], (far_rows, near_rows, bias), 1 << 20)
    far_corner, near_corner = partners(far_corner, near_corner, "col")

    def start_scratch(count):
        return [
            pltpu.VMEM((3, count, tall, LANES), F32),
            pltpu.VMEM((5, count, frame, LANES), F32),
            pltpu.VMEM((count, frame, LANES), F32),
            pltpu.VMEM((4, count + 1, tall, LANES), F32),
            pltpu.VMEM((4, 3, count - 2, tall, LANES), F32),
        ]

    def start_shapes(count):
        box = shape(4, count, frame, LANES, dtype=BF16)
        full = shape(count, frame, LANES)
        return box, box, full, shape(3, count, frame, LANES), full

    middle = call(
        middle_body,
        start_shapes(pairs - 2) + (shape(3, frame, LANES),),
        start_scratch(pairs),
        inputs + (far_rows, near_rows, fwd, bwd, bias),
        flops,
    )
    near_box, far_box, back, slope0, mult0, stat0, value0 = call(
        first_body,
        start_shapes(wide) + (spread, small),
        start_scratch(10),
        inputs
        + (far_cols, near_cols, far_rows, near_rows, far_corner, near_corner, fwd, bwd, bias)
        + tuple(middle),
        flops,
    )

    total0 = everyone(stat0)
    tile = shape(wide - 2, rows, LANES)
    base, slope1, mult1, duals1, last_mult, last_slope, last_pull, stat1, value1 = call(
        functools.partial(second_body, cells=cells),
        (
            shape(3, wide, frame, LANES),
            shape(3, wide - 2, frame, LANES),
            shape(2, wide - 2, frame, LANES),
            shape(3, wide - 2, rows, LANES),
            tile,
            tile,
            tile,
            spread,
            small,
        ),
        [
            pltpu.VMEM((2, wide, frame, LANES), F32),
            pltpu.VMEM((wide, frame, LANES), F32),
            pltpu.VMEM((3, wide + 1, frame, LANES), F32),
            pltpu.VMEM((3, 3, wide, frame, LANES), F32),
        ],
        (total0, steps, near_box, far_box, back, slope0, mult0, fwd, bwd, bias),
        2 * flops,
        scalars=(1,),
    )
    total1 = everyone(stat1)
    out = shape(3, rows, cols)
    duals, multipliers, slope2, mult2, stat2 = call(
        functools.partial(third_body, cells=cells),
        (out, out, out, out, spread),
        [
            pltpu.VMEM((2, wide - 2, frame, LANES), F32),
            pltpu.VMEM((3, wide - 1, frame, LANES), F32),
            pltpu.VMEM((3, 3, wide - 2, frame, LANES), F32),
        ],
        (
            total1, steps, near_box, base, mult1, slope1, duals1, last_mult, last_slope, last_pull,
            fwd, bwd, lower, upper, bias, value0, value1,
        ),
        2 * flops,
        scalars=(1,),
    )
    total2 = everyone(stat2)
    final_duals, final_multipliers, bounds = call(
        functools.partial(last_body, cells=cells),
        (out, out, shape(ITERS)),
        [pltpu.VMEM(out.shape, F32), pltpu.VMEM(out.shape, F32), pltpu.SemaphoreType.DMA((6,))],
        (total2, steps, duals, multipliers, slope2, mult2),
        1 << 20,
        scalar_outs=(2,),
        far_outs=(0, 1),
        scalars=(1,),
    )
    return bounds, final_duals, final_multipliers


def solution(mesh):
    placed = (
        P("row", "col"),
        P("row", "col"),
        P("row", "col"),
        P(None, "row", "col"),
        P(None, "row", "col"),
        P(),
        P(),
        P(),
    )
    return jax.shard_map(
        shards,
        mesh=mesh,
        in_specs=placed,
        out_specs=(P(), P(None, "row", "col"), P(None, "row", "col")),
        check_vma=False,
    )
```

```python
import functools
import math

import jax
import jax.numpy as jnp
from jax import lax
from jax.experimental import pallas as pl
from jax.experimental.pallas import tpu as pltpu
from jax.sharding import PartitionSpec as P

CH = 64
LAYERS = 4
ITERS = 3
EPS = 1e-06
LANES = 2 * CH
HALO_PAIRS = 3
WIDE = 5
EDGE = 4
F32 = jnp.float32
BF16 = jnp.bfloat16

ROWS_SENT = (5, 5, 5, 4, 4, 4, 2, 3, 3)
ROW_START = tuple(sum(ROWS_SENT[:m]) for m in range(9))
SENT = sum(ROWS_SENT)
OUTER = 3 * WIDE
CORNER = (0, OUTER, OUTER + SENT, OUTER + 2 * SENT, OUTER + 3 * SENT, OUTER + 4 * SENT, 2 * OUTER + 4 * SENT)
WINDOW = 4 * CH

VMEM = pl.BlockSpec(memory_space=pltpu.VMEM)
SMEM = pl.BlockSpec(memory_space=pltpu.SMEM)
HBM = pl.BlockSpec(memory_space=pltpu.HBM)


def call(body, outs, scratch, operands, flops, mem=20, scalars=(), far=(), scalar_outs=()):
    specs = [SMEM if j in scalars else HBM if j in far else VMEM for j in range(len(operands))]
    out_specs = tuple(SMEM if j in scalar_outs else VMEM for j in range(len(outs)))
    return pl.pallas_call(
        body,
        out_shape=outs,
        in_specs=specs,
        out_specs=out_specs,
        scratch_shapes=scratch,
        compiler_params=pltpu.CompilerParams(vmem_limit_bytes=mem << 20),
        cost_estimate=pl.CostEstimate(flops=flops, bytes_accessed=4 << 20, transcendentals=0),
    )(*operands)


def shape(*dims, dtype=F32):
    return jax.ShapeDtypeStruct(dims, dtype)


def copies(pairs, sem):
    made = [pltpu.make_async_copy(src, dst, sem.at[j]) for j, (src, dst) in enumerate(pairs)]
    for one in made:
        one.start()
    return made


def finish(made):
    for one in made:
        one.wait()


def split(value):
    high = value.astype(BF16)
    return high, (value - high.astype(F32)).astype(BF16)


def weights_body(kernels, biases, fwd, bwd, bias2):
    zero = jnp.zeros((CH, CH), F32)

    def put(dest, k, j, dh, first, second):
        high, low = split(jnp.concatenate([first, second], axis=1))
        for part, value in enumerate((low, high, high)):
            dest[k, pl.ds(WINDOW * part + CH * j, CH), pl.ds(LANES * dh, LANES)] = value

    for k in range(LAYERS):
        for dh in range(3):
            taps = [kernels[k * 9 + dh * 3 + dw] for dw in range(3)]
            if k < LAYERS - 1:
                for j in range(4):
                    put(fwd, k, j, dh, taps[j] if j < 3 else zero, taps[j - 1] if j > 0 else zero)
            flips = [tap.T for tap in taps]
            for j in range(4):
                put(bwd, k, j, 2 - dh, flips[2 - j] if j < 3 else zero, flips[3 - j] if j > 0 else zero)
    for k in range(LAYERS):
        row = biases[k : k + 1, :]
        bias2[k : k + 1, :] = jnp.concatenate([row, row], axis=1)


def weights(kernels, biases):
    size = (3 * WINDOW, 3 * LANES)
    return call(
        weights_body,
        (shape(LAYERS - 1, *size, dtype=BF16), shape(LAYERS, *size, dtype=BF16), shape(8, LANES)),
        [],
        (kernels.reshape(LAYERS * 9, CH, CH), biases),
        1 << 22,
    )


def sources(objective, center, radius, lower, upper):
    return [
        lambda cols: center[:, cols].astype(F32),
        lambda cols: upper[0, :, cols].astype(F32),
        lambda cols: upper[1, :, cols].astype(F32),
        lambda cols: upper[2, :, cols].astype(F32),
        lambda cols: lower[0, :, cols].astype(F32),
        lambda cols: lower[1, :, cols].astype(F32),
        lambda cols: lower[2, :, cols].astype(F32),
        lambda cols: radius[:, cols].astype(F32),
        lambda cols: objective[:, cols],
    ]


def ends_body(objective, center, radius, lower, upper, far_rows, near_rows, far_cols, near_cols, *rest):
    rows, cols = objective.shape
    held, sem = rest[:5], rest[5]
    finish(copies(list(zip((objective, center, radius, lower, upper), held)), sem))
    strip = HALO_PAIRS * LANES
    for m, read in enumerate(sources(*held)):
        here = pl.ds(m * rows, rows)
        sorted_strips(
            "col", read(pl.ds(0, strip)), read(pl.ds(cols - strip, strip)), far_cols.at[here], near_cols.at[here]
        )
    for q in range(cols // LANES):
        values = [read(pl.ds(q * LANES, LANES)) for read in sources(*held)]
        ends_of(values, far_rows, near_rows, q * SENT)


def ends_of(values, far, near, start):
    rows = values[0].shape[0]
    row = lax.broadcasted_iota(jnp.int32, (rows, LANES), 0)
    outer = (row >= 2) & (row < rows - 2)
    if len(values) > 3:
        values[3] = jnp.where(outer, values[3] - values[6], values[3])
    for m, value in enumerate(values):
        here = pl.ds(start + ROW_START[m], ROWS_SENT[m])
        sorted_strips("row", value[: ROWS_SENT[m]], value[rows - ROWS_SENT[m] :], far.at[here], near.at[here])


def odd_index(axis):
    return lax.axis_index(axis) % 2 == 1


def sorted_strips(axis, first, last, far, near):
    odd = odd_index(axis)
    far[...] = jnp.where(odd, last, first)
    near[...] = jnp.where(odd, first, last)


class Side:
    def __init__(self, axis, far, near, after):
        self.axis, self.far, self.near, self.after = axis, far, near, after
        self.shape = far.shape

    def __getitem__(self, index):
        odd = odd_index(self.axis)
        near = jnp.logical_not(odd) if self.after else odd
        return jnp.where(near, self.near[index], self.far[index])


def sides(axis, far, near):
    return Side(axis, far, near, False), Side(axis, far, near, True)


def corners_body(far_cols, near_cols, far, near):
    rows = far_cols.shape[0] // 9
    left, right = sides("col", far_cols, near_cols)
    for j in range(2 * HALO_PAIRS):
        strip, q = (left, j) if j < HALO_PAIRS else (right, j - HALO_PAIRS)
        maps = 3 if j in (0, 2 * HALO_PAIRS - 1) else 9
        values = [strip[pl.ds(m * rows, rows), pl.ds(q * LANES, LANES)] for m in range(maps)]
        ends_of(values, far, near, CORNER[j])


def column(reads, left, right, rows, pairs, m, q):
    if q < HALO_PAIRS:
        return left[m * rows : (m + 1) * rows, q * LANES : (q + 1) * LANES]
    if q >= HALO_PAIRS + pairs:
        q -= HALO_PAIRS + pairs
        return right[m * rows : (m + 1) * rows, q * LANES : (q + 1) * LANES]
    return reads[m](pl.ds((q - HALO_PAIRS) * LANES, LANES))


def halo(middle, corner, pairs, q, m):
    if HALO_PAIRS <= q < HALO_PAIRS + pairs:
        source, start = middle, (q - HALO_PAIRS) * SENT
    else:
        source, start = corner, CORNER[q if q < HALO_PAIRS else q - pairs]
    return source[pl.ds(start + ROW_START[m], ROWS_SENT[m]), :]


def partners(far, near, axis):
    count = lax.axis_size(axis)

    def pairs(first):
        return [(i + a, i + 1 - a) for i in range(first, count - 1, 2) for a in (0, 1)]

    return lax.ppermute(far, axis, pairs(1)), lax.ppermute(near, axis, pairs(0))


def roll_rows(value, shift):
    return pltpu.roll(value, shift % value.shape[0], 0)


def slide(maps, count, store, produce):
    rows = store.shape[2]
    early = lax.broadcasted_iota(jnp.int32, (rows, LANES), 1) < CH
    zero = jnp.zeros((rows, LANES), F32)

    def step(q, carry):
        fresh = [pltpu.roll(value, CH, 1) for value in produce(q)]
        for k in range(maps):
            store[k, q] = jnp.where(early, carry[k], fresh[k])
        return tuple(fresh)

    last = lax.fori_loop(0, count, step, (zero,) * maps, unroll=True)
    for k in range(maps):
        store[k, count] = jnp.where(early, last[k], zero)


def multiply(store, k, first, count, weight, layer, sums, exact=False):
    rows = store.shape[2]
    left = store[k, pl.ds(first, count)].reshape(count * rows, LANES)
    right = store[k, pl.ds(first + 1, count)].reshape(count * rows, LANES)
    high, low = split(jnp.concatenate([left, right], axis=1))
    terms = [high, high] if exact else [high, high, low]
    result = jnp.dot(
        jnp.concatenate(terms, axis=1),
        weight[layer, 0 : WINDOW * len(terms), :],
        preferred_element_type=F32,
    )
    for d in range(3):
        sums[k, d, pl.ds(0, count)] = result[:, d * LANES : (d + 1) * LANES].reshape(count, rows, LANES)


def gathered(sums, k, q):
    return roll_rows(sums[k, 0, q], 1) + sums[k, 1, q] + roll_rows(sums[k, 2, q], -1)


def inner(sums, k, q, first, rows):
    parts = [roll_rows(sums[k, d, q], 1 - d - first)[:rows] for d in range(3)]
    return parts[0] + parts[1] + parts[2]


def summed(total):
    return jnp.sum(total[...], axis=0, keepdims=True)


def scale_of(total, step, cells, dims):
    squares = summed(total)[:, 0:1]
    return jnp.broadcast_to(step / jnp.sqrt(squares / (2 * (LAYERS - 1) * cells) + EPS), dims)


def soft(top, bend):
    return 0.5 * top * (1.0 - bend)


class Bound:
    def __init__(self, start):
        self.linear = start
        self.factor = None

    def add(self, t):
        bend = jnp.tanh(t)
        self.linear = self.linear + (jnp.minimum(t, 0.0) - 0.5 * math.log(2.0))
        factor = 1.0 + jnp.abs(bend)
        self.factor = factor if self.factor is None else self.factor * factor
        return bend

    def total(self):
        return self.linear + 0.5 * jnp.log(self.factor)


def folded(value):
    return jnp.sum(value, axis=0, keepdims=True)


def own_rows(value):
    rows = value.shape[0]
    row = lax.broadcasted_iota(jnp.int32, value.shape, 0)
    return folded(jnp.where((row >= EDGE) & (row < rows - EDGE), value, 0.0))


def stats(out, rows):
    lane = lax.broadcasted_iota(jnp.int32, (1, LANES), 1)
    packed = jnp.zeros((1, LANES), F32)
    for j, row in enumerate(rows):
        packed = jnp.where(lane == j, jnp.sum(row, axis=1, keepdims=True), packed)
    out[...] = jnp.broadcast_to(packed, out.shape)


def assemble(reads, above, below, left, right, corners, slots, rows, pairs, raw, gaps, target):
    frame = rows + 2 * EDGE
    blank = jnp.zeros((EDGE, LANES), F32)
    for slot, q in enumerate(slots):
        outside = not 1 <= q < pairs + 2 * HALO_PAIRS - 1
        for m in range(9):
            sent = ROWS_SENT[m]
            if m < 3:
                dest, at, edge = raw.at[m, slot], 0, WIDE
            else:
                dest, at, edge = (target.at[slot] if m == 8 else gaps.at[m - 3, slot]), EDGE - sent, EDGE
                if outside:
                    dest[...] = jnp.zeros((frame, LANES), F32)
                    continue
                if at:
                    dest[0:EDGE, :] = blank
                    dest[EDGE + rows : frame, :] = blank
            dest[at : at + sent, :] = halo(above, corners[0], pairs, q, m)
            dest[edge : edge + rows, :] = column(reads, left, right, rows, pairs, m, q)
            dest[edge + rows : edge + rows + sent, :] = halo(below, corners[1], pairs, q, m)
    count = len(slots)
    spare = raw.shape[2] - rows - 2 * WIDE
    raw[:, :, rows + 2 * WIDE :, :] = jnp.zeros((3, count, spare, LANES), F32)


def start_convs(raw, target, store, sums, fwd, bwd, frame):
    count = raw.shape[1]
    slide(3, count, store, lambda q: [raw[0, q], 0.5 * raw[1, q], 0.5 * raw[2, q]])
    tugged = store.at[3:4, :, 0:frame, :]
    slide(1, count, tugged, lambda q: [target[q]])
    for k in range(3):
        multiply(store, k, 1, count - 2, fwd, k, sums, exact=True)
    multiply(tugged, 0, 1, count - 2, bwd, LAYERS - 1, sums.at[3:4, :, :, 0:frame, :])


def start_step(slot, out, raw, gaps, target, sums, bias, near_box, far_box, back, slope, mult):
    frame = gaps.shape[2]
    near = [raw[m, slot][1 : 1 + frame] for m in range(3)] + [gaps[4, slot]]
    far = [gaps[m, slot] for m in range(4)]
    for m in range(4):
        near_box[m, out] = near[m].astype(BF16)
        far_box[m, out] = far[m].astype(BF16)
    new = jnp.zeros((frame, LANES), F32)
    for k in range(3):
        gap = near[1 + k] if k < 2 else far[0]
        dl = 0.5 * (gap - far[1 + k]) - inner(sums, k, slot - 1, 1, frame) - bias[k : k + 1, :]
        dl = jnp.where(near[1] > 0.0, dl, 0.0)
        slope[k, out] = dl
        new = new + dl * dl
    tug = gathered(sums.at[3:4, :, :, 0:frame, :], 0, slot - 1)
    back[out] = tug
    bound = Bound(jnp.full((frame, LANES), -4.5 * math.log(2.0), F32))
    dm = -0.5 * gap * bound.add(tug * gap)
    mult[out] = dm
    return new + dm * dm, bound.total(), target[slot] * bias[3:4, :]


def middle_body(
    objective, center, radius, lower, upper, far_rows, near_rows, fwd, bwd, bias,
    near_box, far_box, back, slope, mult, totals,
    raw, gaps, target, store, sums,
):
    rows, cols = objective.shape
    pairs = cols // LANES
    frame = rows + 2 * EDGE
    reads = sources(objective, center, radius, lower, upper)
    above, below = sides("row", far_rows, near_rows)
    slots = range(HALO_PAIRS, HALO_PAIRS + pairs)
    assemble(reads, above, below, None, None, (None, None), slots, rows, pairs, raw, gaps, target)
    start_convs(raw, target, store, sums, fwd, bwd, frame)

    def step(q, carry):
        new = start_step(q + 1, q, raw, gaps, target, sums, bias, near_box, far_box, back, slope, mult)
        return tuple(old + one for old, one in zip(carry, new))

    zero = jnp.zeros((frame, LANES), F32)
    sizes = lax.fori_loop(0, pairs - 2, step, (zero, zero, zero), unroll=True)
    for j in range(3):
        totals[j] = sizes[j]


def first_body(
    objective, center, radius, lower, upper, far_cols, near_cols, far_rows, near_rows, far_corner, near_corner, fwd, bwd, bias,
    near_in, far_in, back_in, slope_in, mult_in, totals,
    near_box, far_box, back, slope, mult, stat, value,
    raw, gaps, target, store, sums,
):
    rows, cols = objective.shape
    pairs = cols // LANES
    frame = rows + 2 * EDGE
    wide = pairs + 4
    reads = sources(objective, center, radius, lower, upper)
    above, below = sides("row", far_rows, near_rows)
    left, right = sides("col", far_cols, near_cols)
    corners = sides("row", far_corner, near_corner)
    slots = list(range(5)) + list(range(wide - 3, wide + 2))
    assemble(reads, above, below, left, right, corners, slots, rows, pairs, raw, gaps, target)
    start_convs(raw, target, store, sums, fwd, bwd, frame)
    here = slice(3, wide - 3)
    near_box[:, here] = near_in[...]
    far_box[:, here] = far_in[...]
    back[here] = back_in[...]
    slope[:, here] = slope_in[...]
    mult[here] = mult_in[...]
    sizes = [totals[j] for j in range(3)]
    for slot, q in ((1, 0), (2, 1), (3, 2), (6, wide - 3), (7, wide - 2), (8, wide - 1)):
        new = start_step(slot, q, raw, gaps, target, sums, bias, near_box, far_box, back, slope, mult)
        if 2 <= q < wide - 2:
            sizes = [old + one for old, one in zip(sizes, new)]
    squares, worth, fixed = (own_rows(one) for one in sizes)
    stats(stat, [squares])
    stats(value, [worth + fixed, fixed])


def second_body(
    total, steps, near_box, far_box, back, slope, mult, fwd, bwd, bias,
    base, slope_out, mult_out, duals, last_mult, last_slope, last_pull, stat, value,
    points, worths, store, sums, *, cells,
):
    wide, frame = near_box.shape[1:3]
    inside = slice(EDGE, frame - EDGE)
    scale = scale_of(total, steps[0], cells, (frame, LANES))
    zero = jnp.zeros((frame, LANES), F32)
    slide(3, wide, store, lambda q: [slope[k, q] for k in range(3)])
    for k in range(3):
        multiply(store, k, 0, wide, bwd, k, sums)

    def produce(q):
        center, radius = near_box[0, q].astype(F32), near_box[3, q].astype(F32)
        g = -(scale * gathered(sums, 0, q))
        base[0, q] = g
        bound = Bound(g * (center - radius))
        outs = [center - radius * bound.add(2.0 * radius * g)]
        for k in (1, 2):
            gap = near_box[k, q].astype(F32)
            g = -(scale * gathered(sums, k, q))
            base[k, q] = g
            x = soft(gap, bound.add(g * gap))
            points[k - 1, q] = x
            outs.append(x)
        worths[q] = bound.total()
        return outs

    slide(3, wide, store, produce)
    for k in range(3):
        multiply(store, k, 1, wide - 2, fwd, k, sums)

    def step(j, carry):
        squares, worth = carry
        q = j + 1
        new = zero
        bound = Bound(worths[q])
        for k in range(3):
            gap = (near_box[1 + k, q] if k < 2 else far_box[0, q]).astype(F32)
            low = far_box[1 + k, q].astype(F32)
            lam = scale * slope[k, q]
            if k < 2:
                x = points[k, q]
                tp = lam * gap
            else:
                mu = scale * mult[q]
                g = back[q] + mu
                x = soft(gap, bound.add(g * gap))
                tp = (lam - mu) * gap
            positive = soft(gap, bound.add(tp))
            negative = soft(low, bound.add(-lam * low))
            bound.linear = bound.linear - lam * bias[k : k + 1, :]
            dl = positive - negative - gathered(sums, k, j) - bias[k : k + 1, :]
            dl = jnp.where(gap > 0.0, dl, 0.0)
            dm = x - positive
            slope_out[k, j] = dl
            duals[k, j] = lam[inside]
            if k < 2:
                mult_out[k, j] = dm
            else:
                last_mult[j] = mu[inside]
                last_slope[j] = dm[inside]
                last_pull[j] = g[inside]
            new = new + dl * dl + dm * dm
        own = (q >= 2) & (q < wide - 2)
        return squares + jnp.where(own, new, 0.0), worth + jnp.where(own, bound.total(), 0.0)

    squares, worth = lax.fori_loop(0, wide - 2, step, (zero, zero), unroll=True)
    stats(stat, [own_rows(squares)])
    stats(value, [own_rows(worth)])


def third_body(
    total, steps, near_box, base, mult, slope, duals1, last_mult, last_slope, last_pull,
    fwd, bwd, lower, upper, bias, value0, value1,
    duals, multipliers, slope_out, mult_out, stat,
    points, store, sums, *, cells,
):
    wide, frame = near_box.shape[1:3]
    rows = frame - 2 * EDGE
    inside = slice(EDGE, frame - EDGE)
    scale = scale_of(total, steps[1], cells, (frame, LANES))
    zero = jnp.zeros((frame, LANES), F32)
    slide(3, wide - 2, store, lambda j: [slope[k, j] for k in range(3)])
    for k in range(3):
        multiply(store, k, 0, wide - 2, bwd, k, sums)
    early = lax.broadcasted_iota(jnp.int32, (frame, LANES), 1) < CH

    def point(j, carry):
        q = j + 1
        center, radius = near_box[0, q].astype(F32), near_box[3, q].astype(F32)
        g = base[0, q] - scale * gathered(sums, 0, j)
        bound = Bound(g * (center - radius))
        outs = [center - radius * bound.add(2.0 * radius * g)]
        for k in (1, 2):
            gap = near_box[k, q].astype(F32)
            t = (base[k, q] + scale * (mult[k - 1, j] - gathered(sums, k, j))) * gap
            x = soft(gap, bound.add(t))
            points[k - 1, j] = x
            outs.append(x)
        own = (q >= 2) & (q < wide - 2)
        fresh = [pltpu.roll(value, CH, 1) for value in outs]
        for k in range(3):
            store[k, j] = jnp.where(early, carry[k], fresh[k])
        return tuple(fresh) + (carry[3] + jnp.where(own, bound.total(), 0.0),)

    framed = lax.fori_loop(0, wide - 2, point, (zero,) * 4, unroll=True)[3]
    for k in range(3):
        multiply(store, k, 1, wide - 4, fwd, k, sums)

    scale = scale[:rows]

    def step(i, carry):
        squares, worth = carry
        j = i + 1
        here = pl.ds(pl.multiple_of(i * LANES, LANES), LANES)
        bound = Bound(jnp.zeros((rows, LANES), F32))
        for k in range(3):
            gap = upper[k, :, here].astype(F32)
            low = lower[k, :, here].astype(F32)
            lam = duals1[k, j] + scale * slope[k, j, inside, :]
            bound.linear = bound.linear - lam * bias[k : k + 1, :]
            if k < 2:
                x = points[k, j, inside, :]
                mu = scale * mult[k, j, inside, :]
            else:
                change = scale * last_slope[j]
                mu = last_mult[j] + change
                x = soft(gap, bound.add((last_pull[j] + change) * gap))
            positive = soft(gap, bound.add((lam - mu) * gap))
            negative = soft(low, bound.add(-lam * low))
            dl = positive - negative - inner(sums, k, i, EDGE, rows) - bias[k : k + 1, :]
            dm = x - positive
            duals[k, :, here] = lam
            multipliers[k, :, here] = mu
            slope_out[k, :, here] = dl
            mult_out[k, :, here] = dm
            squares = squares + dl * dl + dm * dm
        return squares, worth + bound.total()

    zero = jnp.zeros((rows, LANES), F32)
    squares, worth = lax.fori_loop(0, wide - 4, step, (zero, zero), unroll=True)
    lane = lax.broadcasted_iota(jnp.int32, (1, LANES), 1)
    start, fixed = (jnp.where(lane == j, value0[0:1, :], 0.0) for j in range(2))
    middle = jnp.where(lane == 0, value1[0:1, :], 0.0)
    stats(stat, [folded(squares), start, middle + fixed, folded(worth) + own_rows(framed) + fixed])


def last_body(total, steps, duals, multipliers, slope, mult, duals_out, mult_out, bounds, *, cells):
    scale = scale_of(total, steps[2], cells, duals.shape[1:])
    for k in range(LAYERS - 1):
        duals_out[k] = duals[k] + scale * slope[k]
        mult_out[k] = multipliers[k] + scale * mult[k]
    values = summed(total) / cells
    lane = lax.broadcasted_iota(jnp.int32, (1, LANES), 1)
    for j in range(ITERS):
        bounds[j] = jnp.sum(jnp.where(lane == j + 1, values, 0.0))


def everyone(partial):
    return lax.all_to_all(partial, ("row", "col"), 0, 0, tiled=True)


def shards(objective, center, radius, lower, upper, kernels, biases, steps):
    rows, cols = objective.shape
    pairs = cols // LANES
    wide = pairs + 4
    frame = rows + 2 * EDGE
    tall = -(-(rows + 2 * WIDE) // 8) * 8
    cells = rows * cols * lax.axis_size("row") * lax.axis_size("col")
    inputs = (objective, center, radius, lower, upper)
    flops = 3 * 2 * 3 * wide * frame * 4 * CH * 3 * LANES
    spread = shape(lax.axis_size("row") * lax.axis_size("col"), LANES)
    small = shape(8, LANES)

    ends = shape(pairs * SENT, LANES)
    strip = shape(9 * rows, HALO_PAIRS * LANES)
    made = (ends, ends, strip, strip)
    far_rows, near_rows, far_cols, near_cols = call(
        ends_body,
        made,
        [pltpu.VMEM(one.shape, one.dtype) for one in inputs] + [pltpu.SemaphoreType.DMA((5,))],
        inputs,
        1 << 20,
        mem=58,
        far=range(5),
    )
    far_rows, near_rows = partners(far_rows, near_rows, "row")
    far_cols, near_cols = partners(far_cols, near_cols, "col")
    fwd, bwd, bias = weights(kernels, biases)
    corner = shape(CORNER[-1], LANES)
    far_corner, near_corner = call(corners_body, (corner, corner), [], (far_cols, near_cols), 1 << 20)
    far_corner, near_corner = partners(far_corner, near_corner, "row")

    def start_scratch(count):
        return [
            pltpu.VMEM((3, count, tall, LANES), F32),
            pltpu.VMEM((5, count, frame, LANES), F32),
            pltpu.VMEM((count, frame, LANES), F32),
            pltpu.VMEM((4, count + 1, tall, LANES), F32),
            pltpu.VMEM((4, 3, count - 2, tall, LANES), F32),
        ]

    def start_shapes(count):
        box = shape(4, count, frame, LANES, dtype=BF16)
        full = shape(count, frame, LANES)
        return box, box, full, shape(3, count, frame, LANES), full

    middle = call(
        middle_body,
        start_shapes(pairs - 2) + (shape(3, frame, LANES),),
        start_scratch(pairs),
        inputs + (far_rows, near_rows, fwd, bwd, bias),
        flops,
    )
    near_box, far_box, back, slope0, mult0, stat0, value0 = call(
        first_body,
        start_shapes(wide) + (spread, small),
        start_scratch(10),
        inputs
        + (far_cols, near_cols, far_rows, near_rows, far_corner, near_corner, fwd, bwd, bias)
        + tuple(middle),
        flops,
    )

    total0 = everyone(stat0)
    tile = shape(wide - 2, rows, LANES)
    base, slope1, mult1, duals1, last_mult, last_slope, last_pull, stat1, value1 = call(
        functools.partial(second_body, cells=cells),
        (
            shape(3, wide, frame, LANES),
            shape(3, wide - 2, frame, LANES),
            shape(2, wide - 2, frame, LANES),
            shape(3, wide - 2, rows, LANES),
            tile,
            tile,
            tile,
            spread,
            small,
        ),
        [
            pltpu.VMEM((2, wide, frame, LANES), F32),
            pltpu.VMEM((wide, frame, LANES), F32),
            pltpu.VMEM((3, wide + 1, frame, LANES), F32),
            pltpu.VMEM((3, 3, wide, frame, LANES), F32),
        ],
        (total0, steps, near_box, far_box, back, slope0, mult0, fwd, bwd, bias),
        2 * flops,
        scalars=(1,),
    )
    total1 = everyone(stat1)
    out = shape(3, rows, cols)
    duals, multipliers, slope2, mult2, stat2 = call(
        functools.partial(third_body, cells=cells),
        (out, out, out, out, spread),
        [
            pltpu.VMEM((2, wide - 2, frame, LANES), F32),
            pltpu.VMEM((3, wide - 1, frame, LANES), F32),
            pltpu.VMEM((3, 3, wide - 2, frame, LANES), F32),
        ],
        (
            total1, steps, near_box, base, mult1, slope1, duals1, last_mult, last_slope, last_pull,
            fwd, bwd, lower, upper, bias, value0, value1,
        ),
        2 * flops,
        scalars=(1,),
    )
    total2 = everyone(stat2)
    final_duals, final_multipliers, bounds = call(
        functools.partial(last_body, cells=cells),
        (out, out, shape(ITERS)),
        [],
        (total2, steps, duals, multipliers, slope2, mult2),
        1 << 20,
        scalar_outs=(2,),
        scalars=(1,),
    )
    return bounds, final_duals, final_multipliers


def solution(mesh):
    placed = (
        P("row", "col"),
        P("row", "col"),
        P("row", "col"),
        P(None, "row", "col"),
        P(None, "row", "col"),
        P(),
        P(),
        P(),
    )
    return jax.shard_map(
        shards,
        mesh=mesh,
        in_specs=placed,
        out_specs=(P(), P(None, "row", "col"), P(None, "row", "col")),
        check_vma=False,
    )
```

```python
import functools
import math

import jax
import jax.numpy as jnp
from jax import lax
from jax.experimental import pallas as pl
from jax.experimental.pallas import tpu as pltpu
from jax.sharding import PartitionSpec as P

CH = 64
LAYERS = 4
ITERS = 3
EPS = 1e-06
LANES = 2 * CH
HALO_PAIRS = 3
WIDE = 5
EDGE = 4
F32 = jnp.float32
BF16 = jnp.bfloat16

ROWS_SENT = (5, 5, 5, 4, 4, 4, 2, 3, 3)
ROW_START = tuple(sum(ROWS_SENT[:m]) for m in range(9))
SENT = sum(ROWS_SENT)
OUTER = 3 * WIDE
CORNER = (0, OUTER, OUTER + SENT, OUTER + 2 * SENT, OUTER + 3 * SENT, OUTER + 4 * SENT, 2 * OUTER + 4 * SENT)
WINDOW = 4 * CH

VMEM = pl.BlockSpec(memory_space=pltpu.VMEM)
SMEM = pl.BlockSpec(memory_space=pltpu.SMEM)
HBM = pl.BlockSpec(memory_space=pltpu.HBM)


def call(body, outs, scratch, operands, flops, mem=20, scalars=(), far=(), scalar_outs=()):
    specs = [SMEM if j in scalars else HBM if j in far else VMEM for j in range(len(operands))]
    out_specs = tuple(SMEM if j in scalar_outs else VMEM for j in range(len(outs)))
    return pl.pallas_call(
        body,
        out_shape=outs,
        in_specs=specs,
        out_specs=out_specs,
        scratch_shapes=scratch,
        compiler_params=pltpu.CompilerParams(vmem_limit_bytes=mem << 20),
        cost_estimate=pl.CostEstimate(flops=flops, bytes_accessed=4 << 20, transcendentals=0),
    )(*operands)


def shape(*dims, dtype=F32):
    return jax.ShapeDtypeStruct(dims, dtype)


def copies(pairs, sem):
    made = [pltpu.make_async_copy(src, dst, sem.at[j]) for j, (src, dst) in enumerate(pairs)]
    for one in made:
        one.start()
    return made


def finish(made):
    for one in made:
        one.wait()


def split(value):
    high = value.astype(BF16)
    return high, (value - high.astype(F32)).astype(BF16)


def weights_body(kernels, biases, fwd, bwd, bias2):
    zero = jnp.zeros((CH, CH), F32)

    def put(dest, k, j, dh, first, second):
        high, low = split(jnp.concatenate([first, second], axis=1))
        for part, value in enumerate((low, high, high)):
            dest[k, pl.ds(WINDOW * part + CH * j, CH), pl.ds(LANES * dh, LANES)] = value

    for k in range(LAYERS):
        for dh in range(3):
            taps = [kernels[k * 9 + dh * 3 + dw] for dw in range(3)]
            if k < LAYERS - 1:
                for j in range(4):
                    put(fwd, k, j, dh, taps[j] if j < 3 else zero, taps[j - 1] if j > 0 else zero)
            flips = [tap.T for tap in taps]
            for j in range(4):
                put(bwd, k, j, 2 - dh, flips[2 - j] if j < 3 else zero, flips[3 - j] if j > 0 else zero)
    for k in range(LAYERS):
        row = biases[k : k + 1, :]
        bias2[k : k + 1, :] = jnp.concatenate([row, row], axis=1)


def weights(kernels, biases):
    size = (3 * WINDOW, 3 * LANES)
    return call(
        weights_body,
        (shape(LAYERS - 1, *size, dtype=BF16), shape(LAYERS, *size, dtype=BF16), shape(8, LANES)),
        [],
        (kernels.reshape(LAYERS * 9, CH, CH), biases),
        1 << 22,
    )


def sources(objective, center, radius, lower, upper):
    return [
        lambda cols: center[:, cols].astype(F32),
        lambda cols: upper[0, :, cols].astype(F32),
        lambda cols: upper[1, :, cols].astype(F32),
        lambda cols: upper[2, :, cols].astype(F32),
        lambda cols: lower[0, :, cols].astype(F32),
        lambda cols: lower[1, :, cols].astype(F32),
        lambda cols: lower[2, :, cols].astype(F32),
        lambda cols: radius[:, cols].astype(F32),
        lambda cols: objective[:, cols],
    ]


def pairs_of(m):
    return HALO_PAIRS if m < 3 else HALO_PAIRS - 1


def block_of(m, j):
    return sum(pairs_of(n) for n in range(m)) + j


BLOCKS = block_of(9, 0)


def ends_body(objective, center, radius, lower, upper, far_rows, near_rows, far_cols, near_cols, *rest):
    rows, cols = objective.shape
    held, sem = rest[:5], rest[5]
    finish(copies(list(zip((objective, center, radius, lower, upper), held)), sem))
    for m, read in enumerate(sources(*held)):
        for j in range(pairs_of(m)):
            here = pl.ds(block_of(m, j) * rows, rows)
            first = read(pl.ds(j * LANES, LANES))
            last = read(pl.ds(cols - (pairs_of(m) - j) * LANES, LANES))
            sorted_strips("col", first, last, far_cols.at[here], near_cols.at[here])
    for q in range(cols // LANES):
        values = [read(pl.ds(q * LANES, LANES)) for read in sources(*held)]
        ends_of(values, far_rows, near_rows, q * SENT)


def ends_of(values, far, near, start):
    rows = values[0].shape[0]
    row = lax.broadcasted_iota(jnp.int32, (rows, LANES), 0)
    outer = (row >= 2) & (row < rows - 2)
    if len(values) > 3:
        values[3] = jnp.where(outer, values[3] - values[6], values[3])
    for m, value in enumerate(values):
        here = pl.ds(start + ROW_START[m], ROWS_SENT[m])
        sorted_strips("row", value[: ROWS_SENT[m]], value[rows - ROWS_SENT[m] :], far.at[here], near.at[here])


def odd_index(axis):
    return lax.axis_index(axis) % 2 == 1


def sorted_strips(axis, first, last, far, near):
    odd = odd_index(axis)
    far[...] = jnp.where(odd, last, first)
    near[...] = jnp.where(odd, first, last)


class Side:
    def __init__(self, axis, far, near, after):
        self.axis, self.far, self.near, self.after = axis, far, near, after
        self.shape = far.shape

    def __getitem__(self, index):
        odd = odd_index(self.axis)
        near = jnp.logical_not(odd) if self.after else odd
        return jnp.where(near, self.near[index], self.far[index])


def sides(axis, far, near):
    return Side(axis, far, near, False), Side(axis, far, near, True)


def corners_body(far_cols, near_cols, after, far, near):
    del after
    rows = far_cols.shape[0] // BLOCKS
    left, right = sides("col", far_cols, near_cols)
    for j in range(2 * HALO_PAIRS):
        maps = 3 if j in (0, 2 * HALO_PAIRS - 1) else 9
        values = [column(None, left, right, rows, 0, m, j) for m in range(maps)]
        ends_of(values, far, near, CORNER[j])


def column(reads, left, right, rows, pairs, m, q):
    if q < HALO_PAIRS:
        at = block_of(m, q - HALO_PAIRS + pairs_of(m)) * rows
        return left[at : at + rows, :]
    if q >= HALO_PAIRS + pairs:
        at = block_of(m, q - HALO_PAIRS - pairs) * rows
        return right[at : at + rows, :]
    return reads[m](pl.ds((q - HALO_PAIRS) * LANES, LANES))


def halo(middle, corner, pairs, q, m):
    if HALO_PAIRS <= q < HALO_PAIRS + pairs:
        source, start = middle, (q - HALO_PAIRS) * SENT
    else:
        source, start = corner, CORNER[q if q < HALO_PAIRS else q - pairs]
    return source[pl.ds(start + ROW_START[m], ROWS_SENT[m]), :]


def partners(far, near, axis):
    count = lax.axis_size(axis)

    def pairs(first):
        return [(i + a, i + 1 - a) for i in range(first, count - 1, 2) for a in (0, 1)]

    return lax.ppermute(far, axis, pairs(1)), lax.ppermute(near, axis, pairs(0))


def roll_rows(value, shift):
    return pltpu.roll(value, shift % value.shape[0], 0)


def slide(maps, count, store, produce):
    rows = store.shape[2]
    early = lax.broadcasted_iota(jnp.int32, (rows, LANES), 1) < CH
    zero = jnp.zeros((rows, LANES), F32)

    last = (zero,) * maps
    for q in range(count):
        fresh = [pltpu.roll(value, CH, 1) for value in produce(q)]
        for k in range(maps):
            store[k, q] = jnp.where(early, last[k], fresh[k])
        last = fresh
    for k in range(maps):
        store[k, count] = jnp.where(early, last[k], zero)


def multiply(store, k, first, count, weight, layer, sums, exact=False):
    rows = store.shape[2]
    left = store[k, pl.ds(first, count)].reshape(count * rows, LANES)
    right = store[k, pl.ds(first + 1, count)].reshape(count * rows, LANES)
    high, low = split(jnp.concatenate([left, right], axis=1))
    terms = [high, high] if exact else [high, high, low]
    result = jnp.dot(
        jnp.concatenate(terms, axis=1),
        weight[layer, 0 : WINDOW * len(terms), :],
        preferred_element_type=F32,
    )
    for d in range(3):
        sums[k, d, pl.ds(0, count)] = result[:, d * LANES : (d + 1) * LANES].reshape(count, rows, LANES)


def gathered(sums, k, q):
    return roll_rows(sums[k, 0, q], 1) + sums[k, 1, q] + roll_rows(sums[k, 2, q], -1)


def inner(sums, k, q, first, rows):
    parts = [roll_rows(sums[k, d, q], 1 - d - first)[:rows] for d in range(3)]
    return parts[0] + parts[1] + parts[2]


def summed(total):
    return jnp.sum(total[...], axis=0, keepdims=True)


def scale_of(total, step, cells, dims):
    squares = summed(total)[:, 0:1]
    return jnp.broadcast_to(step / jnp.sqrt(squares / (2 * (LAYERS - 1) * cells) + EPS), dims)


def soft(top, bend):
    return 0.5 * top * (1.0 - bend)


class Bound:
    def __init__(self, start, counted=True):
        self.linear = start
        self.factor = None
        self.counted = counted

    def add(self, t):
        bend = jnp.tanh(t)
        if self.counted:
            self.linear = self.linear + (jnp.minimum(t, 0.0) - 0.5 * math.log(2.0))
            factor = 1.0 + jnp.abs(bend)
            self.factor = factor if self.factor is None else self.factor * factor
        return bend

    def less(self, term):
        if self.counted:
            self.linear = self.linear - term

    def total(self):
        return self.linear + 0.5 * jnp.log(self.factor)


def folded(value):
    return jnp.sum(value, axis=0, keepdims=True)


def own_rows(value):
    rows = value.shape[0]
    row = lax.broadcasted_iota(jnp.int32, value.shape, 0)
    return folded(jnp.where((row >= EDGE) & (row < rows - EDGE), value, 0.0))


def stats(out, rows):
    lane = lax.broadcasted_iota(jnp.int32, (1, LANES), 1)
    packed = jnp.zeros((1, LANES), F32)
    for j, row in enumerate(rows):
        packed = jnp.where(lane == j, jnp.sum(row, axis=1, keepdims=True), packed)
    out[...] = jnp.broadcast_to(packed, out.shape)


def assemble(reads, above, below, left, right, corners, slots, rows, pairs, raw, gaps, target):
    frame = rows + 2 * EDGE
    blank = jnp.zeros((EDGE, LANES), F32)
    for slot, q in enumerate(slots):
        outside = not 1 <= q < pairs + 2 * HALO_PAIRS - 1
        for m in range(9):
            sent = ROWS_SENT[m]
            if m < 3:
                dest, at, edge = raw.at[m, slot], 0, WIDE
            else:
                dest, at, edge = (target.at[slot] if m == 8 else gaps.at[m - 3, slot]), EDGE - sent, EDGE
                if outside:
                    dest[...] = jnp.zeros((frame, LANES), F32)
                    continue
                if at:
                    dest[0:EDGE, :] = blank
                    dest[EDGE + rows : frame, :] = blank
            dest[at : at + sent, :] = halo(above, corners[0], pairs, q, m)
            dest[edge : edge + rows, :] = column(reads, left, right, rows, pairs, m, q)
            dest[edge + rows : edge + rows + sent, :] = halo(below, corners[1], pairs, q, m)
    count = len(slots)
    spare = raw.shape[2] - rows - 2 * WIDE
    raw[:, :, rows + 2 * WIDE :, :] = jnp.zeros((3, count, spare, LANES), F32)


def start_convs(raw, target, store, sums, fwd, bwd, frame):
    count = raw.shape[1]
    slide(3, count, store, lambda q: [raw[0, q], 0.5 * raw[1, q], 0.5 * raw[2, q]])
    tugged = store.at[3:4, :, 0:frame, :]
    slide(1, count, tugged, lambda q: [target[q]])
    for k in range(3):
        multiply(store, k, 1, count - 2, fwd, k, sums, exact=True)
    multiply(tugged, 0, 1, count - 2, bwd, LAYERS - 1, sums.at[3:4, :, :, 0:frame, :])


def start_step(slot, out, raw, gaps, target, sums, bias, near_box, far_box, back, slope, mult):
    frame = gaps.shape[2]
    near = [raw[m, slot][1 : 1 + frame] for m in range(3)] + [gaps[4, slot]]
    far = [gaps[m, slot] for m in range(4)]
    for m in range(4):
        near_box[m, out] = near[m].astype(BF16)
        far_box[m, out] = far[m].astype(BF16)
    new = jnp.zeros((frame, LANES), F32)
    for k in range(3):
        gap = near[1 + k] if k < 2 else far[0]
        dl = 0.5 * (gap - far[1 + k]) - inner(sums, k, slot - 1, 1, frame) - bias[k : k + 1, :]
        dl = jnp.where(near[1] > 0.0, dl, 0.0)
        slope[k, out] = dl
        new = new + dl * dl
    tug = gathered(sums.at[3:4, :, :, 0:frame, :], 0, slot - 1)
    back[out] = tug
    bound = Bound(jnp.full((frame, LANES), -4.5 * math.log(2.0), F32))
    dm = -0.5 * gap * bound.add(tug * gap)
    mult[out] = dm
    return new + dm * dm, bound.total(), target[slot] * bias[3:4, :]


def middle_body(
    objective, center, radius, lower, upper, far_rows, near_rows, fwd, bwd, bias,
    near_box, far_box, back, slope, mult, totals,
    raw, gaps, target, store, sums,
):
    rows, cols = objective.shape
    pairs = cols // LANES
    frame = rows + 2 * EDGE
    reads = sources(objective, center, radius, lower, upper)
    above, below = sides("row", far_rows, near_rows)
    slots = range(HALO_PAIRS, HALO_PAIRS + pairs)
    assemble(reads, above, below, None, None, (None, None), slots, rows, pairs, raw, gaps, target)
    start_convs(raw, target, store, sums, fwd, bwd, frame)

    def step(q, carry):
        new = start_step(q + 1, q, raw, gaps, target, sums, bias, near_box, far_box, back, slope, mult)
        return tuple(old + one for old, one in zip(carry, new))

    zero = jnp.zeros((frame, LANES), F32)
    sizes = lax.fori_loop(0, pairs - 2, step, (zero, zero, zero), unroll=True)
    for j in range(3):
        totals[j] = sizes[j]


def first_body(
    objective, center, radius, lower, upper, far_cols, near_cols, far_rows, near_rows, far_corner, near_corner, fwd, bwd, bias,
    near_in, far_in, back_in, slope_in, mult_in, totals,
    near_box, far_box, back, slope, mult, stat, value,
    raw, gaps, target, store, sums,
):
    rows, cols = objective.shape
    pairs = cols // LANES
    frame = rows + 2 * EDGE
    wide = pairs + 4
    reads = sources(objective, center, radius, lower, upper)
    above, below = sides("row", far_rows, near_rows)
    left, right = sides("col", far_cols, near_cols)
    corners = sides("row", far_corner, near_corner)
    slots = list(range(5)) + list(range(wide - 3, wide + 2))
    assemble(reads, above, below, left, right, corners, slots, rows, pairs, raw, gaps, target)
    start_convs(raw, target, store, sums, fwd, bwd, frame)
    here = slice(3, wide - 3)
    near_box[:, here] = near_in[...]
    far_box[:, here] = far_in[...]
    back[here] = back_in[...]
    slope[:, here] = slope_in[...]
    mult[here] = mult_in[...]
    sizes = [totals[j] for j in range(3)]
    for slot, q in ((1, 0), (2, 1), (3, 2), (6, wide - 3), (7, wide - 2), (8, wide - 1)):
        new = start_step(slot, q, raw, gaps, target, sums, bias, near_box, far_box, back, slope, mult)
        if 2 <= q < wide - 2:
            sizes = [old + one for old, one in zip(sizes, new)]
    squares, worth, fixed = (own_rows(one) for one in sizes)
    stats(stat, [squares])
    stats(value, [worth + fixed, fixed])


def second_body(
    total, steps, near_box, far_box, back, slope, mult, fwd, bwd, bias,
    base, slope_out, mult_out, duals, last_mult, last_slope, last_pull, stat, value,
    points, worths, store, sums, *, cells,
):
    wide, frame = near_box.shape[1:3]
    inside = slice(EDGE, frame - EDGE)
    scale = scale_of(total, steps[0], cells, (frame, LANES))
    zero = jnp.zeros((frame, LANES), F32)
    slide(3, wide, store, lambda q: [slope[k, q] for k in range(3)])
    for k in range(3):
        multiply(store, k, 0, wide, bwd, k, sums)

    def produce(q):
        center, radius = near_box[0, q].astype(F32), near_box[3, q].astype(F32)
        g = -(scale * gathered(sums, 0, q))
        base[0, q] = g
        bound = Bound(g * (center - radius), 2 <= q < wide - 2)
        outs = [center - radius * bound.add(2.0 * radius * g)]
        for k in (1, 2):
            gap = near_box[k, q].astype(F32)
            g = -(scale * gathered(sums, k, q))
            base[k, q] = g
            x = soft(gap, bound.add(g * gap))
            points[k - 1, q] = x
            outs.append(x)
        if bound.counted:
            worths[q] = bound.total()
        return outs

    slide(3, wide, store, produce)
    for k in range(3):
        multiply(store, k, 1, wide - 2, fwd, k, sums)

    squares = worth = zero
    for j in range(wide - 2):
        q = j + 1
        own = 2 <= q < wide - 2
        new = zero
        bound = Bound(worths[q] if own else None, own)
        for k in range(3):
            gap = (near_box[1 + k, q] if k < 2 else far_box[0, q]).astype(F32)
            low = far_box[1 + k, q].astype(F32)
            lam = scale * slope[k, q]
            if k < 2:
                x = points[k, q]
                tp = lam * gap
            else:
                mu = scale * mult[q]
                g = back[q] + mu
                x = soft(gap, bound.add(g * gap))
                tp = (lam - mu) * gap
            positive = soft(gap, bound.add(tp))
            negative = soft(low, bound.add(-lam * low))
            bound.less(lam * bias[k : k + 1, :])
            dl = positive - negative - gathered(sums, k, j) - bias[k : k + 1, :]
            dl = jnp.where(gap > 0.0, dl, 0.0)
            dm = x - positive
            slope_out[k, j] = dl
            duals[k, j] = lam[inside]
            if k < 2:
                mult_out[k, j] = dm
            else:
                last_mult[j] = mu[inside]
                last_slope[j] = dm[inside]
                last_pull[j] = g[inside]
            new = new + dl * dl + dm * dm
        if own:
            squares = squares + new
            worth = worth + bound.total()
    stats(stat, [own_rows(squares)])
    stats(value, [own_rows(worth)])


def third_body(
    total, steps, near_box, base, mult, slope, duals1, last_mult, last_slope, last_pull,
    fwd, bwd, lower, upper, bias, value0, value1,
    duals, multipliers, slope_out, mult_out, stat,
    points, store, sums, *, cells,
):
    wide, frame = near_box.shape[1:3]
    rows = frame - 2 * EDGE
    inside = slice(EDGE, frame - EDGE)
    scale = scale_of(total, steps[1], cells, (frame, LANES))
    zero = jnp.zeros((frame, LANES), F32)
    slide(3, wide - 2, store, lambda j: [slope[k, j] for k in range(3)])
    for k in range(3):
        multiply(store, k, 0, wide - 2, bwd, k, sums)
    early = lax.broadcasted_iota(jnp.int32, (frame, LANES), 1) < CH

    framed = zero
    before = (zero,) * 3
    for j in range(wide - 2):
        q = j + 1
        own = 2 <= q < wide - 2
        center, radius = near_box[0, q].astype(F32), near_box[3, q].astype(F32)
        g = base[0, q] - scale * gathered(sums, 0, j)
        bound = Bound(g * (center - radius), own)
        outs = [center - radius * bound.add(2.0 * radius * g)]
        for k in (1, 2):
            gap = near_box[k, q].astype(F32)
            t = (base[k, q] + scale * (mult[k - 1, j] - gathered(sums, k, j))) * gap
            x = soft(gap, bound.add(t))
            points[k - 1, j] = x
            outs.append(x)
        fresh = [pltpu.roll(value, CH, 1) for value in outs]
        for k in range(3):
            store[k, j] = jnp.where(early, before[k], fresh[k])
        before = fresh
        if own:
            framed = framed + bound.total()

    for k in range(3):
        multiply(store, k, 1, wide - 4, fwd, k, sums)

    scale = scale[:rows]

    squares = worth = jnp.zeros((rows, LANES), F32)
    for i in range(wide - 4):
        j = i + 1
        here = pl.ds(i * LANES, LANES)
        bound = Bound(jnp.zeros((rows, LANES), F32))
        for k in range(3):
            gap = upper[k, :, here].astype(F32)
            low = lower[k, :, here].astype(F32)
            lam = duals1[k, j] + scale * slope[k, j, inside, :]
            bound.less(lam * bias[k : k + 1, :])
            if k < 2:
                x = points[k, j, inside, :]
                mu = scale * mult[k, j, inside, :]
            else:
                change = scale * last_slope[j]
                mu = last_mult[j] + change
                x = soft(gap, bound.add((last_pull[j] + change) * gap))
            positive = soft(gap, bound.add((lam - mu) * gap))
            negative = soft(low, bound.add(-lam * low))
            dl = positive - negative - inner(sums, k, i, EDGE, rows) - bias[k : k + 1, :]
            dm = x - positive
            duals[k, :, here] = lam
            multipliers[k, :, here] = mu
            slope_out[k, :, here] = dl
            mult_out[k, :, here] = dm
            squares = squares + dl * dl + dm * dm
        worth = worth + bound.total()

    lane = lax.broadcasted_iota(jnp.int32, (1, LANES), 1)
    start, fixed = (jnp.where(lane == j, value0[0:1, :], 0.0) for j in range(2))
    middle = jnp.where(lane == 0, value1[0:1, :], 0.0)
    stats(stat, [folded(squares), start, middle + fixed, folded(worth) + own_rows(framed) + fixed])


def last_body(total, steps, duals, multipliers, slope, mult, duals_out, mult_out, bounds, *, cells):
    scale = scale_of(total, steps[2], cells, duals.shape[1:])
    for k in range(LAYERS - 1):
        duals_out[k] = duals[k] + scale * slope[k]
        mult_out[k] = multipliers[k] + scale * mult[k]
    values = summed(total) / cells
    lane = lax.broadcasted_iota(jnp.int32, (1, LANES), 1)
    for j in range(ITERS):
        bounds[j] = jnp.sum(jnp.where(lane == j + 1, values, 0.0))


def everyone(partial):
    return lax.all_to_all(partial, ("row", "col"), 0, 0, tiled=True)


def shards(objective, center, radius, lower, upper, kernels, biases, steps):
    rows, cols = objective.shape
    pairs = cols // LANES
    wide = pairs + 4
    frame = rows + 2 * EDGE
    tall = -(-(rows + 2 * WIDE) // 8) * 8
    cells = rows * cols * lax.axis_size("row") * lax.axis_size("col")
    inputs = (objective, center, radius, lower, upper)
    flops = 3 * 2 * 3 * wide * frame * 4 * CH * 3 * LANES
    spread = shape(lax.axis_size("row") * lax.axis_size("col"), LANES)
    small = shape(8, LANES)

    ends = shape(pairs * SENT, LANES)
    strip = shape(BLOCKS * rows, LANES)
    made = (ends, ends, strip, strip)
    far_rows, near_rows, far_cols, near_cols = call(
        ends_body,
        made,
        [pltpu.VMEM(one.shape, one.dtype) for one in inputs] + [pltpu.SemaphoreType.DMA((5,))],
        inputs,
        1 << 20,
        mem=58,
        far=range(5),
    )
    far_rows, near_rows = partners(far_rows, near_rows, "row")
    far_cols, near_cols = partners(far_cols, near_cols, "col")
    fwd, bwd, bias = weights(kernels, biases)
    corner = shape(CORNER[-1], LANES)
    far_corner, near_corner = call(corners_body, (corner, corner), [], (far_cols, near_cols, bias), 1 << 20)
    far_corner, near_corner = partners(far_corner, near_corner, "row")

    def start_scratch(count):
        return [
            pltpu.VMEM((3, count, tall, LANES), F32),
            pltpu.VMEM((5, count, frame, LANES), F32),
            pltpu.VMEM((count, frame, LANES), F32),
            pltpu.VMEM((4, count + 1, tall, LANES), F32),
            pltpu.VMEM((4, 3, count - 2, tall, LANES), F32),
        ]

    def start_shapes(count):
        box = shape(4, count, frame, LANES, dtype=BF16)
        full = shape(count, frame, LANES)
        return box, box, full, shape(3, count, frame, LANES), full

    middle = call(
        middle_body,
        start_shapes(pairs - 2) + (shape(3, frame, LANES),),
        start_scratch(pairs),
        inputs + (far_rows, near_rows, fwd, bwd, bias),
        flops,
    )
    near_box, far_box, back, slope0, mult0, stat0, value0 = call(
        first_body,
        start_shapes(wide) + (spread, small),
        start_scratch(10),
        inputs
        + (far_cols, near_cols, far_rows, near_rows, far_corner, near_corner, fwd, bwd, bias)
        + tuple(middle),
        flops,
    )

    total0 = everyone(stat0)
    tile = shape(wide - 2, rows, LANES)
    base, slope1, mult1, duals1, last_mult, last_slope, last_pull, stat1, value1 = call(
        functools.partial(second_body, cells=cells),
        (
            shape(3, wide, frame, LANES),
            shape(3, wide - 2, frame, LANES),
            shape(2, wide - 2, frame, LANES),
            shape(3, wide - 2, rows, LANES),
            tile,
            tile,
            tile,
            spread,
            small,
        ),
        [
            pltpu.VMEM((2, wide, frame, LANES), F32),
            pltpu.VMEM((wide, frame, LANES), F32),
            pltpu.VMEM((3, wide + 1, frame, LANES), F32),
            pltpu.VMEM((3, 3, wide, frame, LANES), F32),
        ],
        (total0, steps, near_box, far_box, back, slope0, mult0, fwd, bwd, bias),
        2 * flops,
        scalars=(1,),
    )
    total1 = everyone(stat1)
    out = shape(3, rows, cols)
    duals, multipliers, slope2, mult2, stat2 = call(
        functools.partial(third_body, cells=cells),
        (out, out, out, out, spread),
        [
            pltpu.VMEM((2, wide - 2, frame, LANES), F32),
            pltpu.VMEM((3, wide - 1, frame, LANES), F32),
            pltpu.VMEM((3, 3, wide - 2, frame, LANES), F32),
        ],
        (
            total1, steps, near_box, base, mult1, slope1, duals1, last_mult, last_slope, last_pull,
            fwd, bwd, lower, upper, bias, value0, value1,
        ),
        2 * flops,
        scalars=(1,),
    )
    total2 = everyone(stat2)
    final_duals, final_multipliers, bounds = call(
        functools.partial(last_body, cells=cells),
        (out, out, shape(ITERS)),
        [],
        (total2, steps, duals, multipliers, slope2, mult2),
        1 << 20,
        scalar_outs=(2,),
        scalars=(1,),
    )
    return bounds, final_duals, final_multipliers


def solution(mesh):
    placed = (
        P("row", "col"),
        P("row", "col"),
        P("row", "col"),
        P(None, "row", "col"),
        P(None, "row", "col"),
        P(),
        P(),
        P(),
    )
    return jax.shard_map(
        shards,
        mesh=mesh,
        in_specs=placed,
        out_specs=(P(), P(None, "row", "col"), P(None, "row", "col")),
        check_vma=False,
    )
```

```python
import functools
import math

import jax
import jax.numpy as jnp
from jax import lax
from jax.experimental import pallas as pl
from jax.experimental.pallas import tpu as pltpu
from jax.sharding import PartitionSpec as P

CH = 64
LAYERS = 4
ITERS = 3
EPS = 1e-06
LANES = 2 * CH
HALO_PAIRS = 3
WIDE = 5
EDGE = 4
F32 = jnp.float32
BF16 = jnp.bfloat16

ROWS_SENT = (5, 5, 5, 4, 4, 4, 2, 3, 3)
ROW_START = tuple(sum(ROWS_SENT[:m]) for m in range(9))
SENT = sum(ROWS_SENT)
OUTER = 3 * WIDE
CORNER = (0, OUTER, OUTER + SENT, OUTER + 2 * SENT, OUTER + 3 * SENT, OUTER + 4 * SENT, 2 * OUTER + 4 * SENT)
WINDOW = 4 * CH

VMEM = pl.BlockSpec(memory_space=pltpu.VMEM)
SMEM = pl.BlockSpec(memory_space=pltpu.SMEM)
HBM = pl.BlockSpec(memory_space=pltpu.HBM)


def call(body, outs, scratch, operands, flops, mem=20, scalars=(), far=(), scalar_outs=()):
    specs = [SMEM if j in scalars else HBM if j in far else VMEM for j in range(len(operands))]
    out_specs = tuple(SMEM if j in scalar_outs else VMEM for j in range(len(outs)))
    return pl.pallas_call(
        body,
        out_shape=outs,
        in_specs=specs,
        out_specs=out_specs,
        scratch_shapes=scratch,
        compiler_params=pltpu.CompilerParams(vmem_limit_bytes=mem << 20),
        cost_estimate=pl.CostEstimate(flops=flops, bytes_accessed=4 << 20, transcendentals=0),
    )(*operands)


def shape(*dims, dtype=F32):
    return jax.ShapeDtypeStruct(dims, dtype)


def copies(pairs, sem):
    made = [pltpu.make_async_copy(src, dst, sem.at[j]) for j, (src, dst) in enumerate(pairs)]
    for one in made:
        one.start()
    return made


def finish(made):
    for one in made:
        one.wait()


def split(value):
    high = value.astype(BF16)
    return high, (value - high.astype(F32)).astype(BF16)


def weights_body(kernels, biases, fwd, bwd, bias2):
    zero = jnp.zeros((CH, CH), F32)

    def put(dest, k, j, dh, first, second):
        high, low = split(jnp.concatenate([first, second], axis=1))
        for part, value in enumerate((low, high, high)):
            dest[k, pl.ds(WINDOW * part + CH * j, CH), pl.ds(LANES * dh, LANES)] = value

    for k in range(LAYERS):
        for dh in range(3):
            taps = [kernels[k * 9 + dh * 3 + dw] for dw in range(3)]
            if k < LAYERS - 1:
                for j in range(4):
                    put(fwd, k, j, dh, taps[j] if j < 3 else zero, taps[j - 1] if j > 0 else zero)
            flips = [tap.T for tap in taps]
            for j in range(4):
                put(bwd, k, j, 2 - dh, flips[2 - j] if j < 3 else zero, flips[3 - j] if j > 0 else zero)
    for k in range(LAYERS):
        row = biases[k : k + 1, :]
        bias2[k : k + 1, :] = jnp.concatenate([row, row], axis=1)


def weights(kernels, biases):
    size = (3 * WINDOW, 3 * LANES)
    return call(
        weights_body,
        (shape(LAYERS - 1, *size, dtype=BF16), shape(LAYERS, *size, dtype=BF16), shape(8, LANES)),
        [],
        (kernels.reshape(LAYERS * 9, CH, CH), biases),
        1 << 22,
    )


def sources(objective, center, radius, lower, upper):
    return [
        lambda cols: center[:, cols].astype(F32),
        lambda cols: upper[0, :, cols].astype(F32),
        lambda cols: upper[1, :, cols].astype(F32),
        lambda cols: upper[2, :, cols].astype(F32),
        lambda cols: lower[0, :, cols].astype(F32),
        lambda cols: lower[1, :, cols].astype(F32),
        lambda cols: lower[2, :, cols].astype(F32),
        lambda cols: radius[:, cols].astype(F32),
        lambda cols: objective[:, cols],
    ]


def pairs_of(m):
    return HALO_PAIRS if m < 3 else HALO_PAIRS - 1


def block_of(m, j):
    return sum(pairs_of(n) for n in range(m)) + j


BLOCKS = block_of(9, 0)


def ends_body(objective, center, radius, lower, upper, far_rows, near_rows, far_cols, near_cols, *rest):
    rows, cols = objective.shape
    held, sem = rest[:5], rest[5]
    finish(copies(list(zip((objective, center, radius, lower, upper), held)), sem))
    for m, read in enumerate(sources(*held)):
        for j in range(pairs_of(m)):
            here = pl.ds(block_of(m, j) * rows, rows)
            first = read(pl.ds(j * LANES, LANES))
            last = read(pl.ds(cols - (pairs_of(m) - j) * LANES, LANES))
            sorted_strips("col", first, last, far_cols.at[here], near_cols.at[here])
    for q in range(cols // LANES):
        values = [read(pl.ds(q * LANES, LANES)) for read in sources(*held)]
        ends_of(values, far_rows, near_rows, q * SENT)


def ends_of(values, far, near, start):
    rows = values[0].shape[0]
    row = lax.broadcasted_iota(jnp.int32, (rows, LANES), 0)
    outer = (row >= 2) & (row < rows - 2)
    if len(values) > 3:
        values[3] = jnp.where(outer, values[3] - values[6], values[3])
    for m, value in enumerate(values):
        here = pl.ds(start + ROW_START[m], ROWS_SENT[m])
        sorted_strips("row", value[: ROWS_SENT[m]], value[rows - ROWS_SENT[m] :], far.at[here], near.at[here])


def odd_index(axis):
    return lax.axis_index(axis) % 2 == 1


def sorted_strips(axis, first, last, far, near):
    odd = odd_index(axis)
    far[...] = jnp.where(odd, last, first)
    near[...] = jnp.where(odd, first, last)


class Side:
    def __init__(self, axis, far, near, after):
        self.axis, self.far, self.near, self.after = axis, far, near, after
        self.shape = far.shape

    def __getitem__(self, index):
        odd = odd_index(self.axis)
        near = jnp.logical_not(odd) if self.after else odd
        return jnp.where(near, self.near[index], self.far[index])


def sides(axis, far, near):
    return Side(axis, far, near, False), Side(axis, far, near, True)


def corners_body(far_cols, near_cols, after, far, near):
    del after
    rows = far_cols.shape[0] // BLOCKS
    left, right = sides("col", far_cols, near_cols)
    for j in range(2 * HALO_PAIRS):
        maps = 3 if j in (0, 2 * HALO_PAIRS - 1) else 9
        values = [column(None, left, right, rows, 0, m, j) for m in range(maps)]
        ends_of(values, far, near, CORNER[j])


def column(reads, left, right, rows, pairs, m, q):
    if q < HALO_PAIRS:
        at = block_of(m, q - HALO_PAIRS + pairs_of(m)) * rows
        return left[at : at + rows, :]
    if q >= HALO_PAIRS + pairs:
        at = block_of(m, q - HALO_PAIRS - pairs) * rows
        return right[at : at + rows, :]
    return reads[m](pl.ds((q - HALO_PAIRS) * LANES, LANES))


def halo(middle, corner, pairs, q, m):
    if HALO_PAIRS <= q < HALO_PAIRS + pairs:
        source, start = middle, (q - HALO_PAIRS) * SENT
    else:
        source, start = corner, CORNER[q if q < HALO_PAIRS else q - pairs]
    return source[pl.ds(start + ROW_START[m], ROWS_SENT[m]), :]


def partners(far, near, axis):
    count = lax.axis_size(axis)

    def pairs(first):
        return [(i + a, i + 1 - a) for i in range(first, count - 1, 2) for a in (0, 1)]

    return lax.ppermute(far, axis, pairs(1)), lax.ppermute(near, axis, pairs(0))


def roll_rows(value, shift):
    return pltpu.roll(value, shift % value.shape[0], 0)


def slide(maps, count, store, produce):
    rows = store.shape[2]
    early = lax.broadcasted_iota(jnp.int32, (rows, LANES), 1) < CH
    zero = jnp.zeros((rows, LANES), F32)

    last = (zero,) * maps
    for q in range(count):
        fresh = [pltpu.roll(value, CH, 1) for value in produce(q)]
        for k in range(maps):
            store[k, q] = jnp.where(early, last[k], fresh[k])
        last = fresh
    for k in range(maps):
        store[k, count] = jnp.where(early, last[k], zero)


def multiply(store, k, first, count, weight, layer, sums, exact=False):
    rows = store.shape[2]
    left = store[k, pl.ds(first, count)].reshape(count * rows, LANES)
    right = store[k, pl.ds(first + 1, count)].reshape(count * rows, LANES)
    high, low = split(jnp.concatenate([left, right], axis=1))
    terms = [high, high] if exact else [high, high, low]
    result = jnp.dot(
        jnp.concatenate(terms, axis=1),
        weight[layer, 0 : WINDOW * len(terms), :],
        preferred_element_type=F32,
    )
    for d in range(3):
        sums[k, d, pl.ds(0, count)] = result[:, d * LANES : (d + 1) * LANES].reshape(count, rows, LANES)


def gathered(sums, k, q):
    return roll_rows(sums[k, 0, q], 1) + sums[k, 1, q] + roll_rows(sums[k, 2, q], -1)


def inner(sums, k, q, first, rows):
    parts = [roll_rows(sums[k, d, q], 1 - d - first)[:rows] for d in range(3)]
    return parts[0] + parts[1] + parts[2]


def summed(total):
    return jnp.sum(total[...], axis=0, keepdims=True)


def scale_of(total, step, cells, dims, packed=False):
    squares = summed(total)
    squares = squares[:, 0:1] if packed else jnp.sum(squares, axis=1, keepdims=True)
    return jnp.broadcast_to(step / jnp.sqrt(squares / (2 * (LAYERS - 1) * cells) + EPS), dims)


def soft(top, bend):
    return 0.5 * top * (1.0 - bend)


class Bound:
    def __init__(self, start, counted=True):
        self.linear = start
        self.factor = None
        self.counted = counted

    def add(self, t):
        bend = jnp.tanh(t)
        if self.counted:
            self.linear = self.linear + (jnp.minimum(t, 0.0) - 0.5 * math.log(2.0))
            factor = 1.0 + jnp.abs(bend)
            self.factor = factor if self.factor is None else self.factor * factor
        return bend

    def less(self, term):
        if self.counted:
            self.linear = self.linear - term

    def total(self):
        return self.linear + 0.5 * jnp.log(self.factor)


def folded(value):
    return jnp.sum(value, axis=0, keepdims=True)


def own_rows(value):
    rows = value.shape[0]
    row = lax.broadcasted_iota(jnp.int32, value.shape, 0)
    return folded(jnp.where((row >= EDGE) & (row < rows - EDGE), value, 0.0))


def stats(out, rows):
    lane = lax.broadcasted_iota(jnp.int32, (1, LANES), 1)
    packed = jnp.zeros((1, LANES), F32)
    for j, row in enumerate(rows):
        packed = jnp.where(lane == j, jnp.sum(row, axis=1, keepdims=True), packed)
    out[...] = jnp.broadcast_to(packed, out.shape)


def lanes(out, rows):
    out[...] = jnp.concatenate(rows + [jnp.zeros((8 - len(rows), LANES), F32)], axis=0)


class Joined:
    def __init__(self, middle, ends):
        self.middle, self.ends = middle, ends
        self.count = middle.shape[-3]

    def __getitem__(self, index):
        *lead, q = index if isinstance(index, tuple) else (index,)
        inner_pair = 3 <= q < 3 + self.count
        source, at = (self.middle, q - 3) if inner_pair else (self.ends, q if q < 3 else q - self.count)
        return source[tuple(lead) + (at,)]


def assemble(reads, above, below, left, right, corners, slots, rows, pairs, raw, gaps, target):
    frame = rows + 2 * EDGE
    blank = jnp.zeros((EDGE, LANES), F32)
    for slot, q in enumerate(slots):
        outside = not 1 <= q < pairs + 2 * HALO_PAIRS - 1
        for m in range(9):
            sent = ROWS_SENT[m]
            if m < 3:
                dest, at, edge = raw.at[m, slot], 0, WIDE
            else:
                dest, at, edge = (target.at[slot] if m == 8 else gaps.at[m - 3, slot]), EDGE - sent, EDGE
                if outside:
                    dest[...] = jnp.zeros((frame, LANES), F32)
                    continue
                if at:
                    dest[0:EDGE, :] = blank
                    dest[EDGE + rows : frame, :] = blank
            dest[at : at + sent, :] = halo(above, corners[0], pairs, q, m)
            dest[edge : edge + rows, :] = column(reads, left, right, rows, pairs, m, q)
            dest[edge + rows : edge + rows + sent, :] = halo(below, corners[1], pairs, q, m)
    count = len(slots)
    spare = raw.shape[2] - rows - 2 * WIDE
    raw[:, :, rows + 2 * WIDE :, :] = jnp.zeros((3, count, spare, LANES), F32)


def start_convs(raw, target, store, sums, fwd, bwd, frame):
    count = raw.shape[1]
    slide(3, count, store, lambda q: [raw[0, q], 0.5 * raw[1, q], 0.5 * raw[2, q]])
    tugged = store.at[3:4, :, 0:frame, :]
    slide(1, count, tugged, lambda q: [target[q]])
    for k in range(3):
        multiply(store, k, 1, count - 2, fwd, k, sums, exact=True)
    multiply(tugged, 0, 1, count - 2, bwd, LAYERS - 1, sums.at[3:4, :, :, 0:frame, :])


def start_step(slot, out, raw, gaps, target, sums, bias, near_box, far_box, back, slope, mult):
    frame = gaps.shape[2]
    near = [raw[m, slot][1 : 1 + frame] for m in range(3)] + [gaps[4, slot]]
    far = [gaps[m, slot] for m in range(4)]
    for m in range(4):
        near_box[m, out] = near[m].astype(BF16)
        far_box[m, out] = far[m].astype(BF16)
    new = jnp.zeros((frame, LANES), F32)
    for k in range(3):
        gap = near[1 + k] if k < 2 else far[0]
        dl = 0.5 * (gap - far[1 + k]) - inner(sums, k, slot - 1, 1, frame) - bias[k : k + 1, :]
        dl = jnp.where(near[1] > 0.0, dl, 0.0)
        slope[k, out] = dl
        new = new + dl * dl
    tug = gathered(sums.at[3:4, :, :, 0:frame, :], 0, slot - 1)
    back[out] = tug
    bound = Bound(jnp.full((frame, LANES), -4.5 * math.log(2.0), F32))
    dm = -0.5 * gap * bound.add(tug * gap)
    mult[out] = dm
    return new + dm * dm, bound.total(), target[slot] * bias[3:4, :]


def middle_body(
    objective, center, radius, lower, upper, far_rows, near_rows, fwd, bwd, bias,
    near_box, far_box, back, slope, mult, totals,
    raw, gaps, target, store, sums,
):
    rows, cols = objective.shape
    pairs = cols // LANES
    frame = rows + 2 * EDGE
    reads = sources(objective, center, radius, lower, upper)
    above, below = sides("row", far_rows, near_rows)
    slots = range(HALO_PAIRS, HALO_PAIRS + pairs)
    assemble(reads, above, below, None, None, (None, None), slots, rows, pairs, raw, gaps, target)
    start_convs(raw, target, store, sums, fwd, bwd, frame)

    def step(q, carry):
        new = start_step(q + 1, q, raw, gaps, target, sums, bias, near_box, far_box, back, slope, mult)
        return tuple(old + one for old, one in zip(carry, new))

    zero = jnp.zeros((frame, LANES), F32)
    sizes = lax.fori_loop(0, pairs - 2, step, (zero, zero, zero), unroll=True)
    for j in range(3):
        totals[j] = sizes[j]


def first_body(
    objective, center, radius, lower, upper, far_cols, near_cols, far_rows, near_rows, far_corner, near_corner, fwd, bwd, bias,
    totals,
    near_box, far_box, back, slope, mult, stat, value,
    raw, gaps, target, store, sums,
):
    rows, cols = objective.shape
    pairs = cols // LANES
    frame = rows + 2 * EDGE
    wide = pairs + 4
    reads = sources(objective, center, radius, lower, upper)
    above, below = sides("row", far_rows, near_rows)
    left, right = sides("col", far_cols, near_cols)
    corners = sides("row", far_corner, near_corner)
    slots = list(range(5)) + list(range(wide - 3, wide + 2))
    assemble(reads, above, below, left, right, corners, slots, rows, pairs, raw, gaps, target)
    start_convs(raw, target, store, sums, fwd, bwd, frame)
    sizes = [totals[j] for j in range(3)]
    for out, slot in enumerate((1, 2, 3, 6, 7, 8)):
        new = start_step(slot, out, raw, gaps, target, sums, bias, near_box, far_box, back, slope, mult)
        if out in (2, 3):
            sizes = [old + one for old, one in zip(sizes, new)]
    squares, worth, fixed = (own_rows(one) for one in sizes)
    stat[...] = jnp.broadcast_to(squares, stat.shape)
    lanes(value, [worth + fixed, fixed])


def second_body(
    total, steps, *rest, cells,
):
    start, rest = rest[:10], rest[10:]
    second_joined(total, steps, *(Joined(*two) for two in zip(start[:5], start[5:])), *rest, cells=cells)


def second_joined(
    total, steps, near_box, far_box, back, slope, mult, fwd, bwd, bias,
    base, slope_out, mult_out, duals, last_mult, last_slope, last_pull, stat, value,
    points, worths, store, sums, *, cells,
):
    wide, frame = base.shape[1:3]
    inside = slice(EDGE, frame - EDGE)
    scale = scale_of(total, steps[0], cells, (frame, LANES))
    zero = jnp.zeros((frame, LANES), F32)
    slide(3, wide, store, lambda q: [slope[k, q] for k in range(3)])
    for k in range(3):
        multiply(store, k, 0, wide, bwd, k, sums)

    def produce(q):
        center, radius = near_box[0, q].astype(F32), near_box[3, q].astype(F32)
        g = -(scale * gathered(sums, 0, q))
        base[0, q] = g
        bound = Bound(g * (center - radius), 2 <= q < wide - 2)
        outs = [center - radius * bound.add(2.0 * radius * g)]
        for k in (1, 2):
            gap = near_box[k, q].astype(F32)
            g = -(scale * gathered(sums, k, q))
            base[k, q] = g
            x = soft(gap, bound.add(g * gap))
            points[k - 1, q] = x
            outs.append(x)
        if bound.counted:
            worths[q] = bound.total()
        return outs

    slide(3, wide, store, produce)
    for k in range(3):
        multiply(store, k, 1, wide - 2, fwd, k, sums)

    squares = worth = zero
    for j in range(wide - 2):
        q = j + 1
        own = 2 <= q < wide - 2
        new = zero
        bound = Bound(worths[q] if own else None, own)
        for k in range(3):
            gap = (near_box[1 + k, q] if k < 2 else far_box[0, q]).astype(F32)
            low = far_box[1 + k, q].astype(F32)
            lam = scale * slope[k, q]
            if k < 2:
                x = points[k, q]
                tp = lam * gap
            else:
                mu = scale * mult[q]
                g = back[q] + mu
                x = soft(gap, bound.add(g * gap))
                tp = (lam - mu) * gap
            positive = soft(gap, bound.add(tp))
            negative = soft(low, bound.add(-lam * low))
            bound.less(lam * bias[k : k + 1, :])
            dl = positive - negative - gathered(sums, k, j) - bias[k : k + 1, :]
            dl = jnp.where(gap > 0.0, dl, 0.0)
            dm = x - positive
            slope_out[k, j] = dl
            duals[k, j] = lam[inside]
            if k < 2:
                mult_out[k, j] = dm
            else:
                last_mult[j] = mu[inside]
                last_slope[j] = dm[inside]
                last_pull[j] = g[inside]
            new = new + dl * dl + dm * dm
        if own:
            squares = squares + new
            worth = worth + bound.total()
    stat[...] = jnp.broadcast_to(own_rows(squares), stat.shape)
    lanes(value, [own_rows(worth)])


def third_body(
    total, steps, near_middle, near_ends, base, mult, slope, duals1, last_mult, last_slope, last_pull,
    fwd, bwd, lower, upper, bias, value0, value1,
    duals, multipliers, slope_out, mult_out, stat,
    points, store, sums, *, cells,
):
    near_box = Joined(near_middle, near_ends)
    wide, frame = base.shape[1:3]
    rows = frame - 2 * EDGE
    inside = slice(EDGE, frame - EDGE)
    scale = scale_of(total, steps[1], cells, (frame, LANES))
    zero = jnp.zeros((frame, LANES), F32)
    slide(3, wide - 2, store, lambda j: [slope[k, j] for k in range(3)])
    for k in range(3):
        multiply(store, k, 0, wide - 2, bwd, k, sums)
    early = lax.broadcasted_iota(jnp.int32, (frame, LANES), 1) < CH

    framed = zero
    before = (zero,) * 3
    for j in range(wide - 2):
        q = j + 1
        own = 2 <= q < wide - 2
        center, radius = near_box[0, q].astype(F32), near_box[3, q].astype(F32)
        g = base[0, q] - scale * gathered(sums, 0, j)
        bound = Bound(g * (center - radius), own)
        outs = [center - radius * bound.add(2.0 * radius * g)]
        for k in (1, 2):
            gap = near_box[k, q].astype(F32)
            t = (base[k, q] + scale * (mult[k - 1, j] - gathered(sums, k, j))) * gap
            x = soft(gap, bound.add(t))
            points[k - 1, j] = x
            outs.append(x)
        fresh = [pltpu.roll(value, CH, 1) for value in outs]
        for k in range(3):
            store[k, j] = jnp.where(early, before[k], fresh[k])
        before = fresh
        if own:
            framed = framed + bound.total()

    for k in range(3):
        multiply(store, k, 1, wide - 4, fwd, k, sums)

    scale = scale[:rows]

    squares = worth = jnp.zeros((rows, LANES), F32)
    for i in range(wide - 4):
        j = i + 1
        here = pl.ds(i * LANES, LANES)
        bound = Bound(jnp.zeros((rows, LANES), F32))
        for k in range(3):
            gap = upper[k, :, here].astype(F32)
            low = lower[k, :, here].astype(F32)
            lam = duals1[k, j] + scale * slope[k, j, inside, :]
            bound.less(lam * bias[k : k + 1, :])
            if k < 2:
                x = points[k, j, inside, :]
                mu = scale * mult[k, j, inside, :]
            else:
                change = scale * last_slope[j]
                mu = last_mult[j] + change
                x = soft(gap, bound.add((last_pull[j] + change) * gap))
            positive = soft(gap, bound.add((lam - mu) * gap))
            negative = soft(low, bound.add(-lam * low))
            dl = positive - negative - inner(sums, k, i, EDGE, rows) - bias[k : k + 1, :]
            dm = x - positive
            duals[k, :, here] = lam
            multipliers[k, :, here] = mu
            slope_out[k, :, here] = dl
            mult_out[k, :, here] = dm
            squares = squares + dl * dl + dm * dm
        worth = worth + bound.total()

    start, fixed = value0[0:1, :], value0[1:2, :]
    stats(stat, [folded(squares), start, value1[0:1, :] + fixed, folded(worth) + own_rows(framed) + fixed])


def last_body(total, steps, duals, multipliers, slope, mult, duals_out, mult_out, bounds, *, cells):
    scale = scale_of(total, steps[2], cells, duals.shape[1:], packed=True)
    for k in range(LAYERS - 1):
        duals_out[k] = duals[k] + scale * slope[k]
        mult_out[k] = multipliers[k] + scale * mult[k]
    values = summed(total) / cells
    lane = lax.broadcasted_iota(jnp.int32, (1, LANES), 1)
    for j in range(ITERS):
        bounds[j] = jnp.sum(jnp.where(lane == j + 1, values, 0.0))


def everyone(partial):
    return lax.all_to_all(partial, ("row", "col"), 0, 0, tiled=True)


def shards(objective, center, radius, lower, upper, kernels, biases, steps):
    rows, cols = objective.shape
    pairs = cols // LANES
    wide = pairs + 4
    frame = rows + 2 * EDGE
    tall = -(-(rows + 2 * WIDE) // 8) * 8
    cells = rows * cols * lax.axis_size("row") * lax.axis_size("col")
    inputs = (objective, center, radius, lower, upper)
    flops = 3 * 2 * 3 * wide * frame * 4 * CH * 3 * LANES
    spread = shape(lax.axis_size("row") * lax.axis_size("col"), LANES)
    small = shape(8, LANES)

    ends = shape(pairs * SENT, LANES)
    strip = shape(BLOCKS * rows, LANES)
    made = (ends, ends, strip, strip)
    far_rows, near_rows, far_cols, near_cols = call(
        ends_body,
        made,
        [pltpu.VMEM(one.shape, one.dtype) for one in inputs] + [pltpu.SemaphoreType.DMA((5,))],
        inputs,
        1 << 20,
        mem=58,
        far=range(5),
    )
    far_rows, near_rows = partners(far_rows, near_rows, "row")
    far_cols, near_cols = partners(far_cols, near_cols, "col")
    fwd, bwd, bias = weights(kernels, biases)
    corner = shape(CORNER[-1], LANES)
    far_corner, near_corner = call(corners_body, (corner, corner), [], (far_cols, near_cols, bias), 1 << 20)
    far_corner, near_corner = partners(far_corner, near_corner, "row")

    def start_scratch(count):
        return [
            pltpu.VMEM((3, count, tall, LANES), F32),
            pltpu.VMEM((5, count, frame, LANES), F32),
            pltpu.VMEM((count, frame, LANES), F32),
            pltpu.VMEM((4, count + 1, tall, LANES), F32),
            pltpu.VMEM((4, 3, count - 2, tall, LANES), F32),
        ]

    def start_shapes(count):
        box = shape(4, count, frame, LANES, dtype=BF16)
        full = shape(count, frame, LANES)
        return box, box, full, shape(3, count, frame, LANES), full

    *middle, totals = call(
        middle_body,
        start_shapes(pairs - 2) + (shape(3, frame, LANES),),
        start_scratch(pairs),
        inputs + (far_rows, near_rows, fwd, bwd, bias),
        flops,
    )
    *ends, stat0, value0 = call(
        first_body,
        start_shapes(6) + (spread, small),
        start_scratch(10),
        inputs
        + (far_cols, near_cols, far_rows, near_rows, far_corner, near_corner, fwd, bwd, bias)
        + (totals,),
        flops,
    )

    total0 = everyone(stat0)
    tile = shape(wide - 2, rows, LANES)
    base, slope1, mult1, duals1, last_mult, last_slope, last_pull, stat1, value1 = call(
        functools.partial(second_body, cells=cells),
        (
            shape(3, wide, frame, LANES),
            shape(3, wide - 2, frame, LANES),
            shape(2, wide - 2, frame, LANES),
            shape(3, wide - 2, rows, LANES),
            tile,
            tile,
            tile,
            spread,
            small,
        ),
        [
            pltpu.VMEM((2, wide, frame, LANES), F32),
            pltpu.VMEM((wide, frame, LANES), F32),
            pltpu.VMEM((3, wide + 1, frame, LANES), F32),
            pltpu.VMEM((3, 3, wide, frame, LANES), F32),
        ],
        (total0, steps, *middle, *ends, fwd, bwd, bias),
        2 * flops,
        scalars=(1,),
    )
    total1 = everyone(stat1)
    out = shape(3, rows, cols)
    duals, multipliers, slope2, mult2, stat2 = call(
        functools.partial(third_body, cells=cells),
        (out, out, out, out, spread),
        [
            pltpu.VMEM((2, wide - 2, frame, LANES), F32),
            pltpu.VMEM((3, wide - 1, frame, LANES), F32),
            pltpu.VMEM((3, 3, wide - 2, frame, LANES), F32),
        ],
        (
            total1, steps, middle[0], ends[0], base, mult1, slope1, duals1, last_mult, last_slope, last_pull,
            fwd, bwd, lower, upper, bias, value0, value1,
        ),
        2 * flops,
        scalars=(1,),
    )
    total2 = everyone(stat2)
    final_duals, final_multipliers, bounds = call(
        functools.partial(last_body, cells=cells),
        (out, out, shape(ITERS)),
        [],
        (total2, steps, duals, multipliers, slope2, mult2),
        1 << 20,
        scalar_outs=(2,),
        scalars=(1,),
    )
    return bounds, final_duals, final_multipliers


def solution(mesh):
    placed = (
        P("row", "col"),
        P("row", "col"),
        P("row", "col"),
        P(None, "row", "col"),
        P(None, "row", "col"),
        P(),
        P(),
        P(),
    )
    return jax.shard_map(
        shards,
        mesh=mesh,
        in_specs=placed,
        out_specs=(P(), P(None, "row", "col"), P(None, "row", "col")),
        check_vma=False,
    )
```

```python
import functools
import math

import jax
import jax.numpy as jnp
from jax import lax
from jax.experimental import pallas as pl
from jax.experimental.pallas import tpu as pltpu
from jax.sharding import PartitionSpec as P

CH = 64
LAYERS = 4
ITERS = 3
EPS = 1e-06
LANES = 2 * CH
HALO_PAIRS = 3
WIDE = 5
EDGE = 4
F32 = jnp.float32
BF16 = jnp.bfloat16

ROWS_SENT = (5, 5, 5, 4, 4, 4, 2, 3, 3)
ROW_START = tuple(sum(ROWS_SENT[:m]) for m in range(9))
SENT = sum(ROWS_SENT)
OUTER = 3 * WIDE
CORNER = (0, OUTER, OUTER + SENT, OUTER + 2 * SENT, OUTER + 3 * SENT, OUTER + 4 * SENT, 2 * OUTER + 4 * SENT)
WINDOW = 4 * CH

VMEM = pl.BlockSpec(memory_space=pltpu.VMEM)
SMEM = pl.BlockSpec(memory_space=pltpu.SMEM)
HBM = pl.BlockSpec(memory_space=pltpu.HBM)


def call(body, outs, scratch, operands, flops, mem=20, scalars=(), far=(), scalar_outs=()):
    specs = [SMEM if j in scalars else HBM if j in far else VMEM for j in range(len(operands))]
    out_specs = tuple(SMEM if j in scalar_outs else VMEM for j in range(len(outs)))
    return pl.pallas_call(
        body,
        out_shape=outs,
        in_specs=specs,
        out_specs=out_specs,
        scratch_shapes=scratch,
        compiler_params=pltpu.CompilerParams(vmem_limit_bytes=mem << 20),
        cost_estimate=pl.CostEstimate(flops=flops, bytes_accessed=4 << 20, transcendentals=0),
    )(*operands)


def shape(*dims, dtype=F32):
    return jax.ShapeDtypeStruct(dims, dtype)


def copies(pairs, sem):
    made = [pltpu.make_async_copy(src, dst, sem.at[j]) for j, (src, dst) in enumerate(pairs)]
    for one in made:
        one.start()
    return made


def finish(made):
    for one in made:
        one.wait()


def split(value):
    high = value.astype(BF16)
    return high, (value - high.astype(F32)).astype(BF16)


def weights_body(kernels, biases, fwd, bwd, bias2):
    zero = jnp.zeros((CH, CH), F32)

    def put(dest, k, j, dh, first, second):
        high, low = split(jnp.concatenate([first, second], axis=1))
        for part, value in enumerate((low, high, high)):
            dest[k, pl.ds(WINDOW * part + CH * j, CH), pl.ds(LANES * dh, LANES)] = value

    for k in range(LAYERS):
        for dh in range(3):
            taps = [kernels[k * 9 + dh * 3 + dw] for dw in range(3)]
            if k < LAYERS - 1:
                for j in range(4):
                    put(fwd, k, j, dh, taps[j] if j < 3 else zero, taps[j - 1] if j > 0 else zero)
            flips = [tap.T for tap in taps]
            for j in range(4):
                put(bwd, k, j, 2 - dh, flips[2 - j] if j < 3 else zero, flips[3 - j] if j > 0 else zero)
    for k in range(LAYERS):
        row = biases[k : k + 1, :]
        bias2[k : k + 1, :] = jnp.concatenate([row, row], axis=1)


def weights(kernels, biases):
    size = (3 * WINDOW, 3 * LANES)
    return call(
        weights_body,
        (shape(LAYERS - 1, *size, dtype=BF16), shape(LAYERS, *size, dtype=BF16), shape(8, LANES)),
        [],
        (kernels.reshape(LAYERS * 9, CH, CH), biases),
        1 << 22,
    )


def sources(objective, center, radius, lower, upper):
    return [
        lambda cols: center[:, cols].astype(F32),
        lambda cols: upper[0, :, cols].astype(F32),
        lambda cols: upper[1, :, cols].astype(F32),
        lambda cols: upper[2, :, cols].astype(F32),
        lambda cols: lower[0, :, cols].astype(F32),
        lambda cols: lower[1, :, cols].astype(F32),
        lambda cols: lower[2, :, cols].astype(F32),
        lambda cols: radius[:, cols].astype(F32),
        lambda cols: objective[:, cols],
    ]


def pairs_of(m):
    return HALO_PAIRS if m < 3 else HALO_PAIRS - 1


def block_of(m, j):
    return sum(pairs_of(n) for n in range(m)) + j


BLOCKS = block_of(9, 0)


def ends_body(objective, center, radius, lower, upper, far_rows, near_rows, far_cols, near_cols, *rest):
    rows, cols = objective.shape
    held, sem = rest[:5], rest[5]
    finish(copies(list(zip((objective, center, radius, lower, upper), held)), sem))
    for m, read in enumerate(sources(*held)):
        for j in range(pairs_of(m)):
            here = pl.ds(block_of(m, j) * rows, rows)
            first = read(pl.ds(j * LANES, LANES))
            last = read(pl.ds(cols - (pairs_of(m) - j) * LANES, LANES))
            sorted_strips("col", first, last, far_cols.at[here], near_cols.at[here])
    for q in range(cols // LANES):
        values = [read(pl.ds(q * LANES, LANES)) for read in sources(*held)]
        ends_of(values, far_rows, near_rows, q * SENT)


def ends_of(values, far, near, start):
    rows = values[0].shape[0]
    row = lax.broadcasted_iota(jnp.int32, (rows, LANES), 0)
    outer = (row >= 2) & (row < rows - 2)
    if len(values) > 3:
        values[3] = jnp.where(outer, values[3] - values[6], values[3])
    for m, value in enumerate(values):
        here = pl.ds(start + ROW_START[m], ROWS_SENT[m])
        sorted_strips("row", value[: ROWS_SENT[m]], value[rows - ROWS_SENT[m] :], far.at[here], near.at[here])


def odd_index(axis):
    return lax.axis_index(axis) % 2 == 1


def sorted_strips(axis, first, last, far, near):
    odd = odd_index(axis)
    far[...] = jnp.where(odd, last, first)
    near[...] = jnp.where(odd, first, last)


class Side:
    def __init__(self, axis, far, near, after):
        self.axis, self.far, self.near, self.after = axis, far, near, after
        self.shape = far.shape

    def __getitem__(self, index):
        odd = odd_index(self.axis)
        near = jnp.logical_not(odd) if self.after else odd
        return jnp.where(near, self.near[index], self.far[index])


def sides(axis, far, near):
    return Side(axis, far, near, False), Side(axis, far, near, True)


def corners_body(far_cols, near_cols, after, far, near):
    del after
    rows = far_cols.shape[0] // BLOCKS
    left, right = sides("col", far_cols, near_cols)
    for j in range(2 * HALO_PAIRS):
        maps = 3 if j in (0, 2 * HALO_PAIRS - 1) else 9
        values = [column(None, left, right, rows, 0, m, j) for m in range(maps)]
        ends_of(values, far, near, CORNER[j])


def column(reads, left, right, rows, pairs, m, q):
    if q < HALO_PAIRS:
        at = block_of(m, q - HALO_PAIRS + pairs_of(m)) * rows
        return left[at : at + rows, :]
    if q >= HALO_PAIRS + pairs:
        at = block_of(m, q - HALO_PAIRS - pairs) * rows
        return right[at : at + rows, :]
    return reads[m](pl.ds((q - HALO_PAIRS) * LANES, LANES))


def halo(middle, corner, pairs, q, m):
    if HALO_PAIRS <= q < HALO_PAIRS + pairs:
        source, start = middle, (q - HALO_PAIRS) * SENT
    else:
        source, start = corner, CORNER[q if q < HALO_PAIRS else q - pairs]
    return source[pl.ds(start + ROW_START[m], ROWS_SENT[m]), :]


def partners(far, near, axis):
    count = lax.axis_size(axis)

    def pairs(first):
        return [(i + a, i + 1 - a) for i in range(first, count - 1, 2) for a in (0, 1)]

    return lax.ppermute(far, axis, pairs(1)), lax.ppermute(near, axis, pairs(0))


def roll_rows(value, shift):
    return pltpu.roll(value, shift % value.shape[0], 0)


def slide(maps, count, store, produce):
    rows = store.shape[2]
    early = lax.broadcasted_iota(jnp.int32, (rows, LANES), 1) < CH
    zero = jnp.zeros((rows, LANES), F32)

    last = (zero,) * maps
    for q in range(count):
        fresh = [pltpu.roll(value, CH, 1) for value in produce(q)]
        for k in range(maps):
            store[k, q] = jnp.where(early, last[k], fresh[k])
        last = fresh
    for k in range(maps):
        store[k, count] = jnp.where(early, last[k], zero)


def multiply(store, k, first, count, weight, layer, sums, exact=False):
    rows = store.shape[2]
    left = store[k, pl.ds(first, count)].reshape(count * rows, LANES)
    right = store[k, pl.ds(first + 1, count)].reshape(count * rows, LANES)
    high, low = split(jnp.concatenate([left, right], axis=1))
    terms = [high, high] if exact else [high, high, low]
    result = jnp.dot(
        jnp.concatenate(terms, axis=1),
        weight[layer, 0 : WINDOW * len(terms), :],
        preferred_element_type=F32,
    )
    for d in range(3):
        sums[k, d, pl.ds(0, count)] = result[:, d * LANES : (d + 1) * LANES].reshape(count, rows, LANES)


def gathered(sums, k, q):
    return roll_rows(sums[k, 0, q], 1) + sums[k, 1, q] + roll_rows(sums[k, 2, q], -1)


def inner(sums, k, q, first, rows):
    parts = [roll_rows(sums[k, d, q], 1 - d - first)[:rows] for d in range(3)]
    return parts[0] + parts[1] + parts[2]


def summed(total):
    return jnp.sum(total[...], axis=0, keepdims=True)


def scale_of(total, step, cells, dims, packed=False):
    squares = summed(total)
    squares = squares[:, 0:1] if packed else jnp.sum(squares, axis=1, keepdims=True)
    return jnp.broadcast_to(step / jnp.sqrt(squares / (2 * (LAYERS - 1) * cells) + EPS), dims)


def soft(top, bend):
    return 0.5 * top * (1.0 - bend)


class Bound:
    def __init__(self, start, counted=True):
        self.linear = start
        self.factor = None
        self.counted = counted

    def add(self, t):
        bend = jnp.tanh(t)
        if self.counted:
            self.linear = self.linear + (jnp.minimum(t, 0.0) - 0.5 * math.log(2.0))
            factor = 1.0 + jnp.abs(bend)
            self.factor = factor if self.factor is None else self.factor * factor
        return bend

    def less(self, term):
        if self.counted:
            self.linear = self.linear - term

    def total(self):
        return self.linear + 0.5 * jnp.log(self.factor)


def folded(value):
    return jnp.sum(value, axis=0, keepdims=True)


def own_rows(value):
    rows = value.shape[0]
    row = lax.broadcasted_iota(jnp.int32, value.shape, 0)
    return folded(jnp.where((row >= EDGE) & (row < rows - EDGE), value, 0.0))


def stats(out, rows):
    lane = lax.broadcasted_iota(jnp.int32, (1, LANES), 1)
    packed = jnp.zeros((1, LANES), F32)
    for j, row in enumerate(rows):
        packed = jnp.where(lane == j, jnp.sum(row, axis=1, keepdims=True), packed)
    out[...] = jnp.broadcast_to(packed, out.shape)


class At:
    def __init__(self, box, pairs):
        self.box, self.pairs = box, pairs

    def __setitem__(self, index, value):
        self.box[index[0], self.pairs[index[1]]] = value


class Joined:
    def __init__(self, middle, ends):
        self.middle, self.ends = middle, ends
        self.count = middle.shape[-3]

    def __getitem__(self, index):
        *lead, q = index if isinstance(index, tuple) else (index,)
        inner_pair = 3 <= q < 3 + self.count
        source, at = (self.middle, q - 3) if inner_pair else (self.ends, q if q < 3 else q - self.count)
        return source[tuple(lead) + (at,)]


def assemble(reads, above, below, left, right, corners, slots, rows, pairs, raw, gaps, target):
    frame = rows + 2 * EDGE
    blank = jnp.zeros((EDGE, LANES), F32)
    for slot, q in enumerate(slots):
        outside = not 1 <= q < pairs + 2 * HALO_PAIRS - 1
        for m in range(9):
            sent = ROWS_SENT[m]
            if m < 3:
                dest, at, edge = raw.at[m, slot], 0, WIDE
            else:
                dest, at, edge = (target.at[slot] if m == 8 else gaps.at[m - 3, slot]), EDGE - sent, EDGE
                if outside:
                    dest[...] = jnp.zeros((frame, LANES), F32)
                    continue
                if at:
                    dest[0:EDGE, :] = blank
                    dest[EDGE + rows : frame, :] = blank
            dest[at : at + sent, :] = halo(above, corners[0], pairs, q, m)
            dest[edge : edge + rows, :] = column(reads, left, right, rows, pairs, m, q)
            dest[edge + rows : edge + rows + sent, :] = halo(below, corners[1], pairs, q, m)
    count = len(slots)
    spare = raw.shape[2] - rows - 2 * WIDE
    raw[:, :, rows + 2 * WIDE :, :] = jnp.zeros((3, count, spare, LANES), F32)


def start_convs(raw, target, store, sums, fwd, bwd, frame):
    count = raw.shape[1]
    slide(3, count, store, lambda q: [raw[0, q], 0.5 * raw[1, q], 0.5 * raw[2, q]])
    tugged = store.at[3:4, :, 0:frame, :]
    slide(1, count, tugged, lambda q: [target[q]])
    for k in range(3):
        multiply(store, k, 1, count - 2, fwd, k, sums, exact=True)
    multiply(tugged, 0, 1, count - 2, bwd, LAYERS - 1, sums.at[3:4, :, :, 0:frame, :])


def start_step(slot, out, raw, gaps, target, sums, bias, near_box, far_box, back, slope, mult):
    frame = gaps.shape[2]
    near = [raw[m, slot][1 : 1 + frame] for m in range(3)] + [gaps[4, slot]]
    far = [gaps[m, slot] for m in range(4)]
    for m in range(4):
        near_box[m, out] = near[m].astype(BF16)
        far_box[m, out] = far[m].astype(BF16)
    new = jnp.zeros((frame, LANES), F32)
    for k in range(3):
        gap = near[1 + k] if k < 2 else far[0]
        dl = 0.5 * (gap - far[1 + k]) - inner(sums, k, slot - 1, 1, frame) - bias[k : k + 1, :]
        dl = jnp.where(near[1] > 0.0, dl, 0.0)
        slope[k, out] = dl
        new = new + dl * dl
    tug = gathered(sums.at[3:4, :, :, 0:frame, :], 0, slot - 1)
    back[out] = tug
    bound = Bound(jnp.full((frame, LANES), -4.5 * math.log(2.0), F32))
    dm = -0.5 * gap * bound.add(tug * gap)
    mult[out] = dm
    return new + dm * dm, bound.total(), target[slot] * bias[3:4, :]


def middle_body(
    objective, center, radius, lower, upper, far_rows, near_rows, fwd, bwd, bias,
    near_box, far_box, back, slope, mult, totals,
    raw, gaps, target, store, sums,
):
    rows, cols = objective.shape
    pairs = cols // LANES
    frame = rows + 2 * EDGE
    reads = sources(objective, center, radius, lower, upper)
    above, below = sides("row", far_rows, near_rows)
    slots = range(HALO_PAIRS, HALO_PAIRS + pairs)
    assemble(reads, above, below, None, None, (None, None), slots, rows, pairs, raw, gaps, target)
    start_convs(raw, target, store, sums, fwd, bwd, frame)

    def step(q, carry):
        new = start_step(q + 1, q, raw, gaps, target, sums, bias, near_box, far_box, back, slope, mult)
        return tuple(old + one for old, one in zip(carry, new))

    zero = jnp.zeros((frame, LANES), F32)
    sizes = lax.fori_loop(0, pairs - 2, step, (zero, zero, zero), unroll=True)
    for j in range(3):
        totals[j] = sizes[j]


def first_body(
    objective, center, radius, lower, upper, far_cols, near_cols, far_rows, near_rows, far_corner, near_corner, fwd, bwd, bias,
    totals, near_in,
    near_box, far_box, back, slope, mult, stat, value,
    raw, gaps, target, store, sums,
):
    rows, cols = objective.shape
    pairs = cols // LANES
    frame = rows + 2 * EDGE
    wide = pairs + 4
    reads = sources(objective, center, radius, lower, upper)
    above, below = sides("row", far_rows, near_rows)
    left, right = sides("col", far_cols, near_cols)
    corners = sides("row", far_corner, near_corner)
    slots = list(range(5)) + list(range(wide - 3, wide + 2))
    assemble(reads, above, below, left, right, corners, slots, rows, pairs, raw, gaps, target)
    start_convs(raw, target, store, sums, fwd, bwd, frame)
    near_box[:, 3 : wide - 3] = near_in[...]
    ends_box = At(near_box, (0, 1, 2, wide - 3, wide - 2, wide - 1))
    sizes = [totals[j] for j in range(3)]
    for out, slot in enumerate((1, 2, 3, 6, 7, 8)):
        new = start_step(slot, out, raw, gaps, target, sums, bias, ends_box, far_box, back, slope, mult)
        if out in (2, 3):
            sizes = [old + one for old, one in zip(sizes, new)]
    squares, worth, fixed = (own_rows(one) for one in sizes)
    stat[...] = jnp.broadcast_to(squares, stat.shape)
    stats(value, [worth + fixed, fixed])


def second_body(
    total, steps, *rest, cells,
):
    start, rest = rest[:9], rest[9:]
    joined = [Joined(*two) for two in zip(start[1:5], start[5:])]
    second_joined(total, steps, start[0], *joined, *rest, cells=cells)


def second_joined(
    total, steps, near_box, far_box, back, slope, mult, fwd, bwd, bias,
    base, slope_out, mult_out, duals, last_mult, last_slope, last_pull, stat, value,
    points, worths, store, sums, *, cells,
):
    wide, frame = base.shape[1:3]
    inside = slice(EDGE, frame - EDGE)
    scale = scale_of(total, steps[0], cells, (frame, LANES))
    zero = jnp.zeros((frame, LANES), F32)
    slide(3, wide, store, lambda q: [slope[k, q] for k in range(3)])
    for k in range(3):
        multiply(store, k, 0, wide, bwd, k, sums)

    def produce(q):
        center, radius = near_box[0, q].astype(F32), near_box[3, q].astype(F32)
        g = -(scale * gathered(sums, 0, q))
        base[0, q] = g
        bound = Bound(g * (center - radius), 2 <= q < wide - 2)
        outs = [center - radius * bound.add(2.0 * radius * g)]
        for k in (1, 2):
            gap = near_box[k, q].astype(F32)
            g = -(scale * gathered(sums, k, q))
            base[k, q] = g
            x = soft(gap, bound.add(g * gap))
            points[k - 1, q] = x
            outs.append(x)
        if bound.counted:
            worths[q] = bound.total()
        return outs

    slide(3, wide, store, produce)
    for k in range(3):
        multiply(store, k, 1, wide - 2, fwd, k, sums)

    squares = worth = zero
    for j in range(wide - 2):
        q = j + 1
        own = 2 <= q < wide - 2
        new = zero
        bound = Bound(worths[q] if own else None, own)
        for k in range(3):
            gap = (near_box[1 + k, q] if k < 2 else far_box[0, q]).astype(F32)
            low = far_box[1 + k, q].astype(F32)
            lam = scale * slope[k, q]
            if k < 2:
                x = points[k, q]
                tp = lam * gap
            else:
                mu = scale * mult[q]
                g = back[q] + mu
                x = soft(gap, bound.add(g * gap))
                tp = (lam - mu) * gap
            positive = soft(gap, bound.add(tp))
            negative = soft(low, bound.add(-lam * low))
            bound.less(lam * bias[k : k + 1, :])
            dl = positive - negative - gathered(sums, k, j) - bias[k : k + 1, :]
            dl = jnp.where(gap > 0.0, dl, 0.0)
            dm = x - positive
            slope_out[k, j] = dl
            duals[k, j] = lam[inside]
            if k < 2:
                mult_out[k, j] = dm
            else:
                last_mult[j] = mu[inside]
                last_slope[j] = dm[inside]
                last_pull[j] = g[inside]
            new = new + dl * dl + dm * dm
        if own:
            squares = squares + new
            worth = worth + bound.total()
    stats(stat, [own_rows(squares)])
    stats(value, [own_rows(worth)])


def third_body(
    total, steps, near_box, base, mult, slope, duals1, last_mult, last_slope, last_pull,
    fwd, bwd, lower, upper, bias, value0, value1,
    duals, multipliers, slope_out, mult_out, stat,
    points, store, sums, *, cells,
):
    wide, frame = near_box.shape[1:3]
    rows = frame - 2 * EDGE
    inside = slice(EDGE, frame - EDGE)
    scale = scale_of(total, steps[1], cells, (frame, LANES), packed=True)
    zero = jnp.zeros((frame, LANES), F32)
    slide(3, wide - 2, store, lambda j: [slope[k, j] for k in range(3)])
    for k in range(3):
        multiply(store, k, 0, wide - 2, bwd, k, sums)
    early = lax.broadcasted_iota(jnp.int32, (frame, LANES), 1) < CH

    framed = zero
    before = (zero,) * 3
    for j in range(wide - 2):
        q = j + 1
        own = 2 <= q < wide - 2
        center, radius = near_box[0, q].astype(F32), near_box[3, q].astype(F32)
        g = base[0, q] - scale * gathered(sums, 0, j)
        bound = Bound(g * (center - radius), own)
        outs = [center - radius * bound.add(2.0 * radius * g)]
        for k in (1, 2):
            gap = near_box[k, q].astype(F32)
            t = (base[k, q] + scale * (mult[k - 1, j] - gathered(sums, k, j))) * gap
            x = soft(gap, bound.add(t))
            points[k - 1, j] = x
            outs.append(x)
        fresh = [pltpu.roll(value, CH, 1) for value in outs]
        for k in range(3):
            store[k, j] = jnp.where(early, before[k], fresh[k])
        before = fresh
        if own:
            framed = framed + bound.total()

    for k in range(3):
        multiply(store, k, 1, wide - 4, fwd, k, sums)

    scale = scale[:rows]

    squares = worth = jnp.zeros((rows, LANES), F32)
    for i in range(wide - 4):
        j = i + 1
        here = pl.ds(i * LANES, LANES)
        bound = Bound(jnp.zeros((rows, LANES), F32))
        for k in range(3):
            gap = upper[k, :, here].astype(F32)
            low = lower[k, :, here].astype(F32)
            lam = duals1[k, j] + scale * slope[k, j, inside, :]
            bound.less(lam * bias[k : k + 1, :])
            if k < 2:
                x = points[k, j, inside, :]
                mu = scale * mult[k, j, inside, :]
            else:
                change = scale * last_slope[j]
                mu = last_mult[j] + change
                x = soft(gap, bound.add((last_pull[j] + change) * gap))
            positive = soft(gap, bound.add((lam - mu) * gap))
            negative = soft(low, bound.add(-lam * low))
            dl = positive - negative - inner(sums, k, i, EDGE, rows) - bias[k : k + 1, :]
            dm = x - positive
            duals[k, :, here] = lam
            multipliers[k, :, here] = mu
            slope_out[k, :, here] = dl
            mult_out[k, :, here] = dm
            squares = squares + dl * dl + dm * dm
        worth = worth + bound.total()

    lane = lax.broadcasted_iota(jnp.int32, (1, LANES), 1)
    start, fixed = (jnp.where(lane == j, value0[0:1, :], 0.0) for j in range(2))
    middle = jnp.where(lane == 0, value1[0:1, :], 0.0)
    stats(stat, [folded(squares), start, middle + fixed, folded(worth) + own_rows(framed) + fixed])


def last_body(total, steps, duals, multipliers, slope, mult, duals_out, mult_out, bounds, *, cells):
    scale = scale_of(total, steps[2], cells, duals.shape[1:], packed=True)
    for k in range(LAYERS - 1):
        duals_out[k] = duals[k] + scale * slope[k]
        mult_out[k] = multipliers[k] + scale * mult[k]
    values = summed(total) / cells
    lane = lax.broadcasted_iota(jnp.int32, (1, LANES), 1)
    for j in range(ITERS):
        bounds[j] = jnp.sum(jnp.where(lane == j + 1, values, 0.0))


def everyone(partial):
    return lax.all_to_all(partial, ("row", "col"), 0, 0, tiled=True)


def shards(objective, center, radius, lower, upper, kernels, biases, steps):
    rows, cols = objective.shape
    pairs = cols // LANES
    wide = pairs + 4
    frame = rows + 2 * EDGE
    tall = -(-(rows + 2 * WIDE) // 8) * 8
    cells = rows * cols * lax.axis_size("row") * lax.axis_size("col")
    inputs = (objective, center, radius, lower, upper)
    flops = 3 * 2 * 3 * wide * frame * 4 * CH * 3 * LANES
    spread = shape(lax.axis_size("row") * lax.axis_size("col"), LANES)
    small = shape(8, LANES)

    ends = shape(pairs * SENT, LANES)
    strip = shape(BLOCKS * rows, LANES)
    made = (ends, ends, strip, strip)
    far_rows, near_rows, far_cols, near_cols = call(
        ends_body,
        made,
        [pltpu.VMEM(one.shape, one.dtype) for one in inputs] + [pltpu.SemaphoreType.DMA((5,))],
        inputs,
        1 << 20,
        mem=58,
        far=range(5),
    )
    far_rows, near_rows = partners(far_rows, near_rows, "row")
    far_cols, near_cols = partners(far_cols, near_cols, "col")
    fwd, bwd, bias = weights(kernels, biases)
    corner = shape(CORNER[-1], LANES)
    far_corner, near_corner = call(corners_body, (corner, corner), [], (far_cols, near_cols, bias), 1 << 20)
    far_corner, near_corner = partners(far_corner, near_corner, "row")

    def start_scratch(count):
        return [
            pltpu.VMEM((3, count, tall, LANES), F32),
            pltpu.VMEM((5, count, frame, LANES), F32),
            pltpu.VMEM((count, frame, LANES), F32),
            pltpu.VMEM((4, count + 1, tall, LANES), F32),
            pltpu.VMEM((4, 3, count - 2, tall, LANES), F32),
        ]

    def start_shapes(count):
        box = shape(4, count, frame, LANES, dtype=BF16)
        full = shape(count, frame, LANES)
        return box, box, full, shape(3, count, frame, LANES), full

    *middle, totals = call(
        middle_body,
        start_shapes(pairs - 2) + (shape(3, frame, LANES),),
        start_scratch(pairs),
        inputs + (far_rows, near_rows, fwd, bwd, bias),
        flops,
    )
    near_box, *ends, stat0, value0 = call(
        first_body,
        start_shapes(wide)[:1] + start_shapes(6)[1:] + (spread, small),
        start_scratch(10),
        inputs
        + (far_cols, near_cols, far_rows, near_rows, far_corner, near_corner, fwd, bwd, bias)
        + (totals, middle[0]),
        flops,
    )

    total0 = everyone(stat0)
    tile = shape(wide - 2, rows, LANES)
    base, slope1, mult1, duals1, last_mult, last_slope, last_pull, stat1, value1 = call(
        functools.partial(second_body, cells=cells),
        (
            shape(3, wide, frame, LANES),
            shape(3, wide - 2, frame, LANES),
            shape(2, wide - 2, frame, LANES),
            shape(3, wide - 2, rows, LANES),
            tile,
            tile,
            tile,
            spread,
            small,
        ),
        [
            pltpu.VMEM((2, wide, frame, LANES), F32),
            pltpu.VMEM((wide, frame, LANES), F32),
            pltpu.VMEM((3, wide + 1, frame, LANES), F32),
            pltpu.VMEM((3, 3, wide, frame, LANES), F32),
        ],
        (total0, steps, near_box, *middle[1:], *ends, fwd, bwd, bias),
        2 * flops,
        scalars=(1,),
    )
    total1 = everyone(stat1)
    out = shape(3, rows, cols)
    duals, multipliers, slope2, mult2, stat2 = call(
        functools.partial(third_body, cells=cells),
        (out, out, out, out, spread),
        [
            pltpu.VMEM((2, wide - 2, frame, LANES), F32),
            pltpu.VMEM((3, wide - 1, frame, LANES), F32),
            pltpu.VMEM((3, 3, wide - 2, frame, LANES), F32),
        ],
        (
            total1, steps, near_box, base, mult1, slope1, duals1, last_mult, last_slope, last_pull,
            fwd, bwd, lower, upper, bias, value0, value1,
        ),
        2 * flops,
        scalars=(1,),
    )
    total2 = everyone(stat2)
    final_duals, final_multipliers, bounds = call(
        functools.partial(last_body, cells=cells),
        (out, out, shape(ITERS)),
        [],
        (total2, steps, duals, multipliers, slope2, mult2),
        1 << 20,
        scalar_outs=(2,),
        scalars=(1,),
    )
    return bounds, final_duals, final_multipliers


def solution(mesh):
    placed = (
        P("row", "col"),
        P("row", "col"),
        P("row", "col"),
        P(None, "row", "col"),
        P(None, "row", "col"),
        P(),
        P(),
        P(),
    )
    return jax.shard_map(
        shards,
        mesh=mesh,
        in_specs=placed,
        out_specs=(P(), P(None, "row", "col"), P(None, "row", "col")),
        check_vma=False,
    )
```

```python
import functools
import math

import jax
import jax.numpy as jnp
from jax import lax
from jax.experimental import pallas as pl
from jax.experimental.pallas import tpu as pltpu
from jax.sharding import PartitionSpec as P

CH = 64
LAYERS = 4
ITERS = 3
EPS = 1e-06
LANES = 2 * CH
HALO_PAIRS = 3
WIDE = 5
EDGE = 4
F32 = jnp.float32
BF16 = jnp.bfloat16

ROWS_SENT = (5, 5, 5, 4, 4, 4, 2, 3, 3)
ROW_START = tuple(sum(ROWS_SENT[:m]) for m in range(9))
SENT = sum(ROWS_SENT)
OUTER = 3 * WIDE
CORNER = (0, OUTER, OUTER + SENT, OUTER + 2 * SENT, OUTER + 3 * SENT, OUTER + 4 * SENT, 2 * OUTER + 4 * SENT)
WINDOW = 4 * CH

VMEM = pl.BlockSpec(memory_space=pltpu.VMEM)
SMEM = pl.BlockSpec(memory_space=pltpu.SMEM)
HBM = pl.BlockSpec(memory_space=pltpu.HBM)


def call(body, outs, scratch, operands, flops, mem=20, scalars=(), far=(), scalar_outs=()):
    specs = [SMEM if j in scalars else HBM if j in far else VMEM for j in range(len(operands))]
    out_specs = tuple(SMEM if j in scalar_outs else VMEM for j in range(len(outs)))
    return pl.pallas_call(
        body,
        out_shape=outs,
        in_specs=specs,
        out_specs=out_specs,
        scratch_shapes=scratch,
        compiler_params=pltpu.CompilerParams(vmem_limit_bytes=mem << 20),
        cost_estimate=pl.CostEstimate(flops=flops, bytes_accessed=4 << 20, transcendentals=0),
    )(*operands)


def shape(*dims, dtype=F32):
    return jax.ShapeDtypeStruct(dims, dtype)


def copies(pairs, sem):
    made = [pltpu.make_async_copy(src, dst, sem.at[j]) for j, (src, dst) in enumerate(pairs)]
    for one in made:
        one.start()
    return made


def finish(made):
    for one in made:
        one.wait()


def split(value):
    high = value.astype(BF16)
    return high, (value - high.astype(F32)).astype(BF16)


def weights_body(kernels, biases, fwd, bwd, bias2):
    zero = jnp.zeros((CH, CH), F32)

    def put(dest, k, j, dh, first, second):
        high, low = split(jnp.concatenate([first, second], axis=1))
        for part, value in enumerate((low, high, high)):
            dest[k, pl.ds(WINDOW * part + CH * j, CH), pl.ds(LANES * dh, LANES)] = value

    for k in range(LAYERS):
        for dh in range(3):
            taps = [kernels[k * 9 + dh * 3 + dw] for dw in range(3)]
            if k < LAYERS - 1:
                for j in range(4):
                    put(fwd, k, j, dh, taps[j] if j < 3 else zero, taps[j - 1] if j > 0 else zero)
            flips = [tap.T for tap in taps]
            for j in range(4):
                put(bwd, k, j, 2 - dh, flips[2 - j] if j < 3 else zero, flips[3 - j] if j > 0 else zero)
    for k in range(LAYERS):
        row = biases[k : k + 1, :]
        bias2[k : k + 1, :] = jnp.concatenate([row, row], axis=1)


def weights(kernels, biases):
    size = (3 * WINDOW, 3 * LANES)
    return call(
        weights_body,
        (shape(LAYERS - 1, *size, dtype=BF16), shape(LAYERS, *size, dtype=BF16), shape(8, LANES)),
        [],
        (kernels.reshape(LAYERS * 9, CH, CH), biases),
        1 << 22,
    )


def sources(objective, center, radius, lower, upper):
    return [
        lambda cols: center[:, cols].astype(F32),
        lambda cols: upper[0, :, cols].astype(F32),
        lambda cols: upper[1, :, cols].astype(F32),
        lambda cols: upper[2, :, cols].astype(F32),
        lambda cols: lower[0, :, cols].astype(F32),
        lambda cols: lower[1, :, cols].astype(F32),
        lambda cols: lower[2, :, cols].astype(F32),
        lambda cols: radius[:, cols].astype(F32),
        lambda cols: objective[:, cols],
    ]


def pairs_of(m):
    return HALO_PAIRS if m < 3 else HALO_PAIRS - 1


def block_of(m, j):
    return sum(pairs_of(n) for n in range(m)) + j


BLOCKS = block_of(9, 0)


def ends_body(objective, center, radius, lower, upper, far_rows, near_rows, far_cols, near_cols, *rest):
    rows, cols = objective.shape
    held, sem = rest[:5], rest[5]
    finish(copies(list(zip((objective, center, radius, lower, upper), held)), sem))
    for m, read in enumerate(sources(*held)):
        for j in range(pairs_of(m)):
            here = pl.ds(block_of(m, j) * rows, rows)
            first = read(pl.ds(j * LANES, LANES))
            last = read(pl.ds(cols - (pairs_of(m) - j) * LANES, LANES))
            sorted_strips("col", first, last, far_cols.at[here], near_cols.at[here])
    for q in range(cols // LANES):
        values = [read(pl.ds(q * LANES, LANES)) for read in sources(*held)]
        ends_of(values, far_rows, near_rows, q * SENT)


def ends_of(values, far, near, start):
    rows = values[0].shape[0]
    row = lax.broadcasted_iota(jnp.int32, (rows, LANES), 0)
    outer = (row >= 2) & (row < rows - 2)
    if len(values) > 3:
        values[3] = jnp.where(outer, values[3] - values[6], values[3])
    for m, value in enumerate(values):
        here = pl.ds(start + ROW_START[m], ROWS_SENT[m])
        sorted_strips("row", value[: ROWS_SENT[m]], value[rows - ROWS_SENT[m] :], far.at[here], near.at[here])


def odd_index(axis):
    return lax.axis_index(axis) % 2 == 1


def sorted_strips(axis, first, last, far, near):
    odd = odd_index(axis)
    far[...] = jnp.where(odd, last, first)
    near[...] = jnp.where(odd, first, last)


class Side:
    def __init__(self, axis, far, near, after):
        self.axis, self.far, self.near, self.after = axis, far, near, after
        self.shape = far.shape

    def __getitem__(self, index):
        odd = odd_index(self.axis)
        near = jnp.logical_not(odd) if self.after else odd
        return jnp.where(near, self.near[index], self.far[index])


def sides(axis, far, near):
    return Side(axis, far, near, False), Side(axis, far, near, True)


def corners_body(far_cols, near_cols, after, far, near):
    del after
    rows = far_cols.shape[0] // BLOCKS
    left, right = sides("col", far_cols, near_cols)
    for j in range(2 * HALO_PAIRS):
        maps = 3 if j in (0, 2 * HALO_PAIRS - 1) else 9
        values = [column(None, left, right, rows, 0, m, j) for m in range(maps)]
        ends_of(values, far, near, CORNER[j])


def column(reads, left, right, rows, pairs, m, q):
    if q < HALO_PAIRS:
        at = block_of(m, q - HALO_PAIRS + pairs_of(m)) * rows
        return left[at : at + rows, :]
    if q >= HALO_PAIRS + pairs:
        at = block_of(m, q - HALO_PAIRS - pairs) * rows
        return right[at : at + rows, :]
    return reads[m](pl.ds((q - HALO_PAIRS) * LANES, LANES))


def halo(middle, corner, pairs, q, m):
    if HALO_PAIRS <= q < HALO_PAIRS + pairs:
        source, start = middle, (q - HALO_PAIRS) * SENT
    else:
        source, start = corner, CORNER[q if q < HALO_PAIRS else q - pairs]
    return source[pl.ds(start + ROW_START[m], ROWS_SENT[m]), :]


def partners(far, near, axis):
    count = lax.axis_size(axis)

    def pairs(first):
        return [(i + a, i + 1 - a) for i in range(first, count - 1, 2) for a in (0, 1)]

    return lax.ppermute(far, axis, pairs(1)), lax.ppermute(near, axis, pairs(0))


def roll_rows(value, shift):
    return pltpu.roll(value, shift % value.shape[0], 0)


def slide(maps, count, store, produce):
    rows = store.shape[2]
    early = lax.broadcasted_iota(jnp.int32, (rows, LANES), 1) < CH
    zero = jnp.zeros((rows, LANES), F32)

    last = (zero,) * maps
    for q in range(count):
        fresh = [pltpu.roll(value, CH, 1) for value in produce(q)]
        for k in range(maps):
            store[k, q] = jnp.where(early, last[k], fresh[k])
        last = fresh
    for k in range(maps):
        store[k, count] = jnp.where(early, last[k], zero)


def multiply(store, k, first, count, weight, layer, sums, exact=False):
    rows = store.shape[2]
    left = store[k, pl.ds(first, count)].reshape(count * rows, LANES)
    right = store[k, pl.ds(first + 1, count)].reshape(count * rows, LANES)
    high, low = split(jnp.concatenate([left, right], axis=1))
    terms = [high, high] if exact else [high, high, low]
    result = jnp.dot(
        jnp.concatenate(terms, axis=1),
        weight[layer, 0 : WINDOW * len(terms), :],
        preferred_element_type=F32,
    )
    for d in range(3):
        sums[k, d, pl.ds(0, count)] = result[:, d * LANES : (d + 1) * LANES].reshape(count, rows, LANES)


def gathered(sums, k, q):
    return roll_rows(sums[k, 0, q], 1) + sums[k, 1, q] + roll_rows(sums[k, 2, q], -1)


def inner(sums, k, q, first, rows):
    parts = [roll_rows(sums[k, d, q], 1 - d - first)[:rows] for d in range(3)]
    return parts[0] + parts[1] + parts[2]


def summed(total):
    return jnp.sum(total[...], axis=0, keepdims=True)


def scale_of(total, step, cells, dims, packed=False):
    squares = summed(total)
    squares = squares[:, 0:1] if packed else jnp.sum(squares, axis=1, keepdims=True)
    return jnp.broadcast_to(step / jnp.sqrt(squares / (2 * (LAYERS - 1) * cells) + EPS), dims)


def soft(top, bend):
    return 0.5 * top * (1.0 - bend)


class Bound:
    def __init__(self, start, counted=True):
        self.linear = start
        self.factor = None
        self.counted = counted

    def add(self, t):
        bend = jnp.tanh(t)
        if self.counted:
            self.linear = self.linear + (jnp.minimum(t, 0.0) - 0.5 * math.log(2.0))
            factor = 1.0 + jnp.abs(bend)
            self.factor = factor if self.factor is None else self.factor * factor
        return bend

    def less(self, term):
        if self.counted:
            self.linear = self.linear - term

    def total(self):
        return self.linear + 0.5 * jnp.log(self.factor)


def folded(value):
    return jnp.sum(value, axis=0, keepdims=True)


def own_rows(value):
    rows = value.shape[0]
    row = lax.broadcasted_iota(jnp.int32, value.shape, 0)
    return folded(jnp.where((row >= EDGE) & (row < rows - EDGE), value, 0.0))


def stats(out, rows):
    lane = lax.broadcasted_iota(jnp.int32, (1, LANES), 1)
    packed = jnp.zeros((1, LANES), F32)
    for j, row in enumerate(rows):
        packed = jnp.where(lane == j, jnp.sum(row, axis=1, keepdims=True), packed)
    out[...] = jnp.broadcast_to(packed, out.shape)


class At:
    def __init__(self, box, pairs):
        self.box, self.pairs = box, pairs

    def __setitem__(self, index, value):
        self.box[index[0], self.pairs[index[1]]] = value


class Joined:
    def __init__(self, middle, ends):
        self.middle, self.ends = middle, ends
        self.count = middle.shape[-3]

    def __getitem__(self, index):
        *lead, q = index if isinstance(index, tuple) else (index,)
        inner_pair = 3 <= q < 3 + self.count
        source, at = (self.middle, q - 3) if inner_pair else (self.ends, q if q < 3 else q - self.count)
        return source[tuple(lead) + (at,)]


def assemble(reads, above, below, left, right, corners, slots, rows, pairs, raw, gaps, target):
    frame = rows + 2 * EDGE
    blank = jnp.zeros((EDGE, LANES), F32)
    for slot, q in enumerate(slots):
        outside = not 1 <= q < pairs + 2 * HALO_PAIRS - 1
        for m in range(9):
            sent = ROWS_SENT[m]
            if m < 3:
                dest, at, edge = raw.at[m, slot], 0, WIDE
            else:
                dest, at, edge = (target.at[slot] if m == 8 else gaps.at[m - 3, slot]), EDGE - sent, EDGE
                if outside:
                    dest[...] = jnp.zeros((frame, LANES), F32)
                    continue
                if at:
                    dest[0:EDGE, :] = blank
                    dest[EDGE + rows : frame, :] = blank
            dest[at : at + sent, :] = halo(above, corners[0], pairs, q, m)
            dest[edge : edge + rows, :] = column(reads, left, right, rows, pairs, m, q)
            dest[edge + rows : edge + rows + sent, :] = halo(below, corners[1], pairs, q, m)
    count = len(slots)
    spare = raw.shape[2] - rows - 2 * WIDE
    raw[:, :, rows + 2 * WIDE :, :] = jnp.zeros((3, count, spare, LANES), F32)


def start_convs(raw, target, store, sums, fwd, bwd, frame):
    count = raw.shape[1]
    slide(3, count, store, lambda q: [raw[0, q], 0.5 * raw[1, q], 0.5 * raw[2, q]])
    tugged = store.at[3:4, :, 0:frame, :]
    slide(1, count, tugged, lambda q: [target[q]])
    for k in range(3):
        multiply(store, k, 1, count - 2, fwd, k, sums, exact=True)
    multiply(tugged, 0, 1, count - 2, bwd, LAYERS - 1, sums.at[3:4, :, :, 0:frame, :])


def start_step(slot, out, raw, gaps, target, sums, bias, near_box, far_box, back, slope, mult):
    frame = gaps.shape[2]
    near = [raw[m, slot][1 : 1 + frame] for m in range(3)] + [gaps[4, slot]]
    far = [gaps[m, slot] for m in range(4)]
    for m in range(4):
        near_box[m, out] = near[m].astype(BF16)
        far_box[m, out] = far[m].astype(BF16)
    new = jnp.zeros((frame, LANES), F32)
    for k in range(3):
        gap = near[1 + k] if k < 2 else far[0]
        dl = 0.5 * (gap - far[1 + k]) - inner(sums, k, slot - 1, 1, frame) - bias[k : k + 1, :]
        dl = jnp.where(near[1] > 0.0, dl, 0.0)
        slope[k, out] = dl
        new = new + dl * dl
    tug = gathered(sums.at[3:4, :, :, 0:frame, :], 0, slot - 1)
    back[out] = tug
    bound = Bound(jnp.full((frame, LANES), -4.5 * math.log(2.0), F32))
    dm = -0.5 * gap * bound.add(tug * gap)
    mult[out] = dm
    return new + dm * dm, bound.total(), target[slot] * bias[3:4, :]


def middle_body(
    objective, center, radius, lower, upper, far_rows, near_rows, fwd, bwd, bias,
    near_box, far_box, back, slope, mult, totals,
    raw, gaps, target, store, sums,
):
    rows, cols = objective.shape
    pairs = cols // LANES
    frame = rows + 2 * EDGE
    reads = sources(objective, center, radius, lower, upper)
    above, below = sides("row", far_rows, near_rows)
    slots = range(HALO_PAIRS, HALO_PAIRS + pairs)
    assemble(reads, above, below, None, None, (None, None), slots, rows, pairs, raw, gaps, target)
    start_convs(raw, target, store, sums, fwd, bwd, frame)

    def step(q, carry):
        new = start_step(q + 1, q, raw, gaps, target, sums, bias, near_box, far_box, back, slope, mult)
        return tuple(old + one for old, one in zip(carry, new))

    zero = jnp.zeros((frame, LANES), F32)
    sizes = lax.fori_loop(0, pairs - 2, step, (zero, zero, zero), unroll=True)
    for j in range(3):
        totals[j] = sizes[j]


def first_body(
    objective, center, radius, lower, upper, far_cols, near_cols, far_rows, near_rows, far_corner, near_corner, fwd, bwd, bias,
    totals, near_in,
    near_box, far_box, back, slope, mult, stat, value,
    raw, gaps, target, store, sums,
):
    rows, cols = objective.shape
    pairs = cols // LANES
    frame = rows + 2 * EDGE
    wide = pairs + 4
    reads = sources(objective, center, radius, lower, upper)
    above, below = sides("row", far_rows, near_rows)
    left, right = sides("col", far_cols, near_cols)
    corners = sides("row", far_corner, near_corner)
    slots = list(range(5)) + list(range(wide - 3, wide + 2))
    assemble(reads, above, below, left, right, corners, slots, rows, pairs, raw, gaps, target)
    start_convs(raw, target, store, sums, fwd, bwd, frame)
    near_box[:, 3 : wide - 3] = near_in[...]
    ends_box = At(near_box, (0, 1, 2, wide - 3, wide - 2, wide - 1))
    sizes = [totals[j] for j in range(3)]
    for out, slot in enumerate((1, 2, 3, 6, 7, 8)):
        new = start_step(slot, out, raw, gaps, target, sums, bias, ends_box, far_box, back, slope, mult)
        if out in (2, 3):
            sizes = [old + one for old, one in zip(sizes, new)]
    squares, worth, fixed = (own_rows(one) for one in sizes)
    stat[...] = jnp.broadcast_to(squares, stat.shape)
    stats(value, [worth + fixed, fixed])


def second_body(
    total, steps, *rest, cells,
):
    start, rest = rest[:9], rest[9:]
    joined = [Joined(*two) for two in zip(start[1:5], start[5:])]
    second_joined(total, steps, start[0], *joined, *rest, cells=cells)


def second_joined(
    total, steps, near_box, far_box, back, slope, mult, fwd, bwd, bias,
    base, slope_out, mult_out, duals, last_mult, last_slope, last_pull, stat, value,
    points, worths, store, sums, *, cells,
):
    wide, frame = base.shape[1:3]
    inside = slice(EDGE, frame - EDGE)
    scale = scale_of(total, steps[0], cells, (frame, LANES))
    zero = jnp.zeros((frame, LANES), F32)
    slide(3, wide, store, lambda q: [slope[k, q] for k in range(3)])
    for k in range(3):
        multiply(store, k, 0, wide, bwd, k, sums)

    def produce(q):
        center, radius = near_box[0, q].astype(F32), near_box[3, q].astype(F32)
        g = -(scale * gathered(sums, 0, q))
        base[0, q] = g
        bound = Bound(g * (center - radius), 2 <= q < wide - 2)
        outs = [center - radius * bound.add(2.0 * radius * g)]
        for k in (1, 2):
            gap = near_box[k, q].astype(F32)
            g = -(scale * gathered(sums, k, q))
            base[k, q] = g
            x = soft(gap, bound.add(g * gap))
            points[k - 1, q] = x
            outs.append(x)
        if bound.counted:
            worths[q] = bound.total()
        return outs

    slide(3, wide, store, produce)
    for k in range(3):
        multiply(store, k, 1, wide - 2, fwd, k, sums)

    squares = worth = zero
    for j in range(wide - 2):
        q = j + 1
        own = 2 <= q < wide - 2
        new = zero
        bound = Bound(worths[q] if own else None, own)
        for k in range(3):
            gap = (near_box[1 + k, q] if k < 2 else far_box[0, q]).astype(F32)
            low = far_box[1 + k, q].astype(F32)
            lam = scale * slope[k, q]
            if k < 2:
                x = points[k, q]
                tp = lam * gap
            else:
                mu = scale * mult[q]
                g = back[q] + mu
                x = soft(gap, bound.add(g * gap))
                tp = (lam - mu) * gap
            positive = soft(gap, bound.add(tp))
            negative = soft(low, bound.add(-lam * low))
            bound.less(lam * bias[k : k + 1, :])
            dl = positive - negative - gathered(sums, k, j) - bias[k : k + 1, :]
            dl = jnp.where(gap > 0.0, dl, 0.0)
            dm = x - positive
            slope_out[k, j] = dl
            duals[k, j] = lam[inside]
            if k < 2:
                mult_out[k, j] = dm
            else:
                last_mult[j] = mu[inside]
                last_slope[j] = dm[inside]
                last_pull[j] = g[inside]
            new = new + dl * dl + dm * dm
        if own:
            squares = squares + new
            worth = worth + bound.total()
    stat[...] = jnp.broadcast_to(own_rows(squares), stat.shape)
    stats(value, [own_rows(worth)])


def third_body(
    total, steps, near_box, base, mult, slope, duals1, last_mult, last_slope, last_pull,
    fwd, bwd, lower, upper, bias, value0, value1,
    duals, multipliers, slope_out, mult_out, stat,
    points, store, sums, *, cells,
):
    wide, frame = near_box.shape[1:3]
    rows = frame - 2 * EDGE
    inside = slice(EDGE, frame - EDGE)
    scale = scale_of(total, steps[1], cells, (frame, LANES))
    zero = jnp.zeros((frame, LANES), F32)
    slide(3, wide - 2, store, lambda j: [slope[k, j] for k in range(3)])
    for k in range(3):
        multiply(store, k, 0, wide - 2, bwd, k, sums)
    early = lax.broadcasted_iota(jnp.int32, (frame, LANES), 1) < CH

    framed = zero
    before = (zero,) * 3
    for j in range(wide - 2):
        q = j + 1
        own = 2 <= q < wide - 2
        center, radius = near_box[0, q].astype(F32), near_box[3, q].astype(F32)
        g = base[0, q] - scale * gathered(sums, 0, j)
        bound = Bound(g * (center - radius), own)
        outs = [center - radius * bound.add(2.0 * radius * g)]
        for k in (1, 2):
            gap = near_box[k, q].astype(F32)
            t = (base[k, q] + scale * (mult[k - 1, j] - gathered(sums, k, j))) * gap
            x = soft(gap, bound.add(t))
            points[k - 1, j] = x
            outs.append(x)
        fresh = [pltpu.roll(value, CH, 1) for value in outs]
        for k in range(3):
            store[k, j] = jnp.where(early, before[k], fresh[k])
        before = fresh
        if own:
            framed = framed + bound.total()

    for k in range(3):
        multiply(store, k, 1, wide - 4, fwd, k, sums)

    scale = scale[:rows]

    squares = worth = jnp.zeros((rows, LANES), F32)
    for i in range(wide - 4):
        j = i + 1
        here = pl.ds(i * LANES, LANES)
        bound = Bound(jnp.zeros((rows, LANES), F32))
        for k in range(3):
            gap = upper[k, :, here].astype(F32)
            low = lower[k, :, here].astype(F32)
            lam = duals1[k, j] + scale * slope[k, j, inside, :]
            bound.less(lam * bias[k : k + 1, :])
            if k < 2:
                x = points[k, j, inside, :]
                mu = scale * mult[k, j, inside, :]
            else:
                change = scale * last_slope[j]
                mu = last_mult[j] + change
                x = soft(gap, bound.add((last_pull[j] + change) * gap))
            positive = soft(gap, bound.add((lam - mu) * gap))
            negative = soft(low, bound.add(-lam * low))
            dl = positive - negative - inner(sums, k, i, EDGE, rows) - bias[k : k + 1, :]
            dm = x - positive
            duals[k, :, here] = lam
            multipliers[k, :, here] = mu
            slope_out[k, :, here] = dl
            mult_out[k, :, here] = dm
            squares = squares + dl * dl + dm * dm
        worth = worth + bound.total()

    lane = lax.broadcasted_iota(jnp.int32, (1, LANES), 1)
    start, fixed = (jnp.where(lane == j, value0[0:1, :], 0.0) for j in range(2))
    middle = jnp.where(lane == 0, value1[0:1, :], 0.0)
    stats(stat, [folded(squares), start, middle + fixed, folded(worth) + own_rows(framed) + fixed])


def last_body(total, steps, duals, multipliers, slope, mult, duals_out, mult_out, bounds, *, cells):
    scale = scale_of(total, steps[2], cells, duals.shape[1:], packed=True)
    for k in range(LAYERS - 1):
        duals_out[k] = duals[k] + scale * slope[k]
        mult_out[k] = multipliers[k] + scale * mult[k]
    values = summed(total) / cells
    lane = lax.broadcasted_iota(jnp.int32, (1, LANES), 1)
    for j in range(ITERS):
        bounds[j] = jnp.sum(jnp.where(lane == j + 1, values, 0.0))


def everyone(partial):
    return lax.all_to_all(partial, ("row", "col"), 0, 0, tiled=True)


def shards(objective, center, radius, lower, upper, kernels, biases, steps):
    rows, cols = objective.shape
    pairs = cols // LANES
    wide = pairs + 4
    frame = rows + 2 * EDGE
    tall = -(-(rows + 2 * WIDE) // 8) * 8
    cells = rows * cols * lax.axis_size("row") * lax.axis_size("col")
    inputs = (objective, center, radius, lower, upper)
    flops = 3 * 2 * 3 * wide * frame * 4 * CH * 3 * LANES
    spread = shape(lax.axis_size("row") * lax.axis_size("col"), LANES)
    small = shape(8, LANES)

    ends = shape(pairs * SENT, LANES)
    strip = shape(BLOCKS * rows, LANES)
    made = (ends, ends, strip, strip)
    far_rows, near_rows, far_cols, near_cols = call(
        ends_body,
        made,
        [pltpu.VMEM(one.shape, one.dtype) for one in inputs] + [pltpu.SemaphoreType.DMA((5,))],
        inputs,
        1 << 20,
        mem=58,
        far=range(5),
    )
    far_rows, near_rows = partners(far_rows, near_rows, "row")
    far_cols, near_cols = partners(far_cols, near_cols, "col")
    fwd, bwd, bias = weights(kernels, biases)
    corner = shape(CORNER[-1], LANES)
    far_corner, near_corner = call(corners_body, (corner, corner), [], (far_cols, near_cols, bias), 1 << 20)
    far_corner, near_corner = partners(far_corner, near_corner, "row")

    def start_scratch(count):
        return [
            pltpu.VMEM((3, count, tall, LANES), F32),
            pltpu.VMEM((5, count, frame, LANES), F32),
            pltpu.VMEM((count, frame, LANES), F32),
            pltpu.VMEM((4, count + 1, tall, LANES), F32),
            pltpu.VMEM((4, 3, count - 2, tall, LANES), F32),
        ]

    def start_shapes(count):
        box = shape(4, count, frame, LANES, dtype=BF16)
        full = shape(count, frame, LANES)
        return box, box, full, shape(3, count, frame, LANES), full

    *middle, totals = call(
        middle_body,
        start_shapes(pairs - 2) + (shape(3, frame, LANES),),
        start_scratch(pairs),
        inputs + (far_rows, near_rows, fwd, bwd, bias),
        flops,
    )
    near_box, *ends, stat0, value0 = call(
        first_body,
        start_shapes(wide)[:1] + start_shapes(6)[1:] + (spread, small),
        start_scratch(10),
        inputs
        + (far_cols, near_cols, far_rows, near_rows, far_corner, near_corner, fwd, bwd, bias)
        + (totals, middle[0]),
        flops,
    )

    total0 = everyone(stat0)
    tile = shape(wide - 2, rows, LANES)
    base, slope1, mult1, duals1, last_mult, last_slope, last_pull, stat1, value1 = call(
        functools.partial(second_body, cells=cells),
        (
            shape(3, wide, frame, LANES),
            shape(3, wide - 2, frame, LANES),
            shape(2, wide - 2, frame, LANES),
            shape(3, wide - 2, rows, LANES),
            tile,
            tile,
            tile,
            spread,
            small,
        ),
        [
            pltpu.VMEM((2, wide, frame, LANES), F32),
            pltpu.VMEM((wide, frame, LANES), F32),
            pltpu.VMEM((3, wide + 1, frame, LANES), F32),
            pltpu.VMEM((3, 3, wide, frame, LANES), F32),
        ],
        (total0, steps, near_box, *middle[1:], *ends, fwd, bwd, bias),
        2 * flops,
        scalars=(1,),
    )
    total1 = everyone(stat1)
    out = shape(3, rows, cols)
    duals, multipliers, slope2, mult2, stat2 = call(
        functools.partial(third_body, cells=cells),
        (out, out, out, out, spread),
        [
            pltpu.VMEM((2, wide - 2, frame, LANES), F32),
            pltpu.VMEM((3, wide - 1, frame, LANES), F32),
            pltpu.VMEM((3, 3, wide - 2, frame, LANES), F32),
        ],
        (
            total1, steps, near_box, base, mult1, slope1, duals1, last_mult, last_slope, last_pull,
            fwd, bwd, lower, upper, bias, value0, value1,
        ),
        2 * flops,
        scalars=(1,),
    )
    total2 = everyone(stat2)
    final_duals, final_multipliers, bounds = call(
        functools.partial(last_body, cells=cells),
        (out, out, shape(ITERS)),
        [],
        (total2, steps, duals, multipliers, slope2, mult2),
        1 << 20,
        scalar_outs=(2,),
        scalars=(1,),
    )
    return bounds, final_duals, final_multipliers


def solution(mesh):
    placed = (
        P("row", "col"),
        P("row", "col"),
        P("row", "col"),
        P(None, "row", "col"),
        P(None, "row", "col"),
        P(),
        P(),
        P(),
    )
    return jax.shard_map(
        shards,
        mesh=mesh,
        in_specs=placed,
        out_specs=(P(), P(None, "row", "col"), P(None, "row", "col")),
        check_vma=False,
    )
```
